32 devices in a mesh: kf: 4 (over z), lat: 8 (over y, x, core).
Axes of the slice: x: 2, y: 2, z: 4, core: 2. Of those that a mesh axis runs over, the one named last changes fastest.
Arguments:
- tokens: bfloat16 [4, 4096, 256], P('kf', 'lat'), may hold values from -6 to 6
- frame_ids: int32 [4, 4096], P('kf', 'lat'), may hold values from 0 to 31, as said below
- episodes: int32 [4, 32], P('kf'), may hold values from 0 to 10
- master: float32 [5619712], P('lat'), may hold values from -8 to 8
- moment_one: float32 [5619712], P('lat'), may hold values from -6 to 6
- moment_two: float32 [5619712], P('lat'), may hold values from 0.0001 to 0.003
- latent_grad: bfloat16 [4, 32, 512, 512], P('kf', None, 'lat'), may hold values from -6 to 6
Outputs:
- latents_out: bfloat16 [4, 32, 512, 512], P('kf', None, 'lat')
- token_grad: bfloat16 [4, 4096, 256], P('kf', 'lat')
- param_grad: float32 [5619712], P('lat')
- lamb_update: float32 [5619712], P('lat')
- new_moment_one: float32 [5619712], P('lat')
- new_moment_two: float32 [5619712], P('lat')
- trust: float32 [13], replicated
- bias_grad: float32 [2, 2048], replicated
The draws below stay inside these ranges and needn't reach their ends.
Inputs may be any that keep to these rules, and one draw needn't show every extreme that they name: `frame_ids`: every keyframe has 1 to 512 tokens in its group; in each group, exactly four keyframes have 512 tokens.
All inputs are finite; a program needn't handle non-finite values.
Results may differ from the reference program's by a relative error of at most 0.017.
Values may be sent and summed in bfloat16 or wider, within the bound.
A program may use at most 320 MiB of HBM per device.

```python
import math
import jax
import jax.numpy as jnp
from jax import lax

DIN = 256
D = 512
LAT = 512
CH = 64
HEADS = 8
HEAD_DIM = 64
FF = 2048
EPISODES = 11
FRAMES = 32
GROUPS = 4
GTOK = 4096
NPARAM = 5619712


def param_layout_drawn():
    return [('latent', (LAT, D)), ('episode', (EPISODES, D)), ('tok_norm', (2, DIN)), ('lat_norms', (8, D)), ('w_kv', (DIN, 2 * CH)), ('w_q', (D, CH)), ('w_o', (CH, D)), ('w_qkv', (D, 3 * D)), ('w_so', (D, D)), ('w_up', (2, D, FF)), ('w_down', (2, FF, D)), ('hid_bias', (2, FF)), ('out_bias', (4, D))]


def tensor_scale(tensor_name):
    table = {'latent': 1.0, 'episode': 0.5, 'tok_norm': 0.2, 'lat_norms': 0.2, 'w_kv': DIN ** (-0.5), 'w_q': D ** (-0.5), 'w_o': 2.0 * CH ** (-0.5), 'w_qkv': D ** (-0.5), 'w_so': (LAT // 3) ** 0.5 * D ** (-0.5), 'w_up': D ** (-0.5), 'w_down': 1.5 * FF ** (-0.5), 'hid_bias': 0.2, 'out_bias': 0.2}
    return table[tensor_name]


def draw_master(key, part):
    key = jax.random.fold_in(key, 11)
    layout = param_layout_drawn()
    total = 0
    for tensor_name, tensor_shape in layout:
        total += math.prod(tensor_shape)
    positions = jnp.arange(total, dtype=jnp.int32)
    noise = jnp.clip(jax.random.normal(key, (total,), jnp.float32), -6.0, 6.0)
    scale = jnp.zeros((total,), jnp.float32)
    shift = jnp.zeros((total,), jnp.float32)
    offset = 0
    for tensor_name, tensor_shape in layout:
        entries = math.prod(tensor_shape)
        inside = (positions >= offset) & (positions < offset + entries)
        scale = jnp.where(inside, tensor_scale(tensor_name), scale)
        if tensor_name == 'tok_norm':
            gain_row = (positions - offset) // DIN == 0
            shift = jnp.where(inside & gain_row, 1.0, shift)
        if tensor_name == 'lat_norms':
            gain_row = (positions - offset) // D % 2 == 0
            shift = jnp.where(inside & gain_row, 1.0, shift)
        offset += entries
    return shift + scale * noise


def draw_frame_ids(key, part):
    key = jax.random.fold_in(key, 23)
    stride = GTOK // FRAMES
    set_count = FRAMES // 8
    spare = 4 * stride - 7
    cuts = jnp.sort(jax.random.randint(jax.random.fold_in(key, 1), (GROUPS, set_count, 6), 0, spare + 1), axis=-1)
    edges = jnp.concatenate([jnp.zeros((GROUPS, set_count, 1), jnp.int32), cuts.astype(jnp.int32), jnp.full((GROUPS, set_count, 1), spare, jnp.int32)], axis=-1)
    small_counts = edges[..., 1:] - edges[..., :-1] + 1
    counts = jnp.concatenate([jnp.full((GROUPS, set_count, 1), 4 * stride, jnp.int32), small_counts], axis=-1)
    counts = counts.reshape(GROUPS, FRAMES)
    ends = jnp.cumsum(counts, axis=1)
    positions = jnp.arange(GTOK, dtype=jnp.int32)
    slots = jax.vmap(lambda end_row: jnp.searchsorted(end_row, positions, side='right'))(ends).astype(jnp.int32)
    order_keys = jax.random.split(jax.random.fold_in(key, 2), GROUPS)
    orders = jax.vmap(lambda sub_key: jax.random.permutation(sub_key, FRAMES))(order_keys).astype(jnp.int32)
    labels = jnp.take_along_axis(orders, slots, axis=1)
    place_keys = jax.random.split(jax.random.fold_in(key, 3), GROUPS)
    places = jax.vmap(lambda sub_key: jax.random.permutation(sub_key, GTOK))(place_keys).astype(jnp.int32)
    return jnp.take_along_axis(labels, places, axis=1).astype(jnp.int32)


def set_ends(values, own_key, low, high):
    dims = values.shape
    place = [jax.random.randint(jax.random.fold_in(own_key, axis), (), 0, dims[axis]) for axis in range(len(dims))]
    values = values.at[tuple(place)].set(low)
    longest = dims.index(max(dims))
    place[longest] = (place[longest] + 1) % dims[longest]
    return values.at[tuple(place)].set(high)


def steps_of(key, dims, shards, low, top_value):
    def one(dim, blocks):
        heights = jax.random.uniform(jax.random.fold_in(jax.random.fold_in(key, 6), dim), (blocks,), jnp.float32, low / len(shards), top_value / len(shards))
        return jnp.repeat(jnp.exp(heights), dims[dim] // blocks).reshape((-1,) + (1,) * (len(dims) - dim - 1))

    level = one(*shards[0])
    for cut in shards[1:]:
        level = level * one(*cut)
    return level


def scatter_about(rng, shape, width, most, shards=(), kind=jnp.bfloat16):
    level = steps_of(rng, shape, shards, -0.22, 0.18) if shards else 1.0
    values = jax.random.normal(rng, shape, jnp.float32) * width * level
    return jnp.minimum(jnp.maximum(values, -most), most).astype(kind)


def setup_inputs(seed: int = 0) -> dict:
    key_list = jax.random.split(jax.random.key(seed), 8)
    return {
        "tokens": scatter_about(key_list[0], (GROUPS, GTOK, DIN), 1.0, 6.0, ((0, 4), (1, 8))),
        "frame_ids": draw_frame_ids(jax.random.fold_in(key_list[7], 71), 0),
        "episodes": set_ends(jax.random.randint(key_list[2], (GROUPS, FRAMES), 0, EPISODES), jax.random.fold_in(key_list[2], 1), 0, EPISODES - 1).astype(jnp.int32),
        "master": draw_master(jax.random.fold_in(key_list[7], 71), 0),
        "moment_one": scatter_about(key_list[4], (NPARAM,), 0.5, 6.0, ((0, 8),), jnp.float32),
        "moment_two": jnp.clip(jnp.exp(math.log(0.003) - 3.4011974 * jax.random.uniform(key_list[5], (NPARAM,), jnp.float32) ** steps_of(key_list[5], (NPARAM,), ((0, 8),), -0.2, 0.2)), 0.0001, 0.003),
        "latent_grad": scatter_about(key_list[6], (GROUPS, FRAMES, LAT, D), 1.0, 6.0, ((0, 4), (2, 8))),
    }


@jax.custom_vjp
def low(v):
    return lax.optimization_barrier(v.astype(jnp.bfloat16)).astype(jnp.float32)

@jax.custom_vjp
def low_back(v):
    return v

def low_keep(v):
    return (low(v), None)

def low_pass(kept, grad):
    return (grad,)

def back_keep(v):
    return (v, None)

def back_low(kept, grad):
    return (low(grad),)
low.defvjp(low_keep, low_pass)
low_back.defvjp(back_keep, back_low)
norm_eps = 1e-05
masked_fill = -1e+30
beta_one = 0.9
beta_two = 0.999
adam_eps = 1e-06
decay_rate = 0.01
clip_fraction = 0.5
lamb_step = 10.0

def param_layout():
    return [('latent', (LAT, D)), ('episode', (EPISODES, D)), ('tok_norm', (2, DIN)), ('lat_norms', (8, D)), ('w_kv', (DIN, 2 * CH)), ('w_q', (D, CH)), ('w_o', (CH, D)), ('w_qkv', (D, 3 * D)), ('w_so', (D, D)), ('w_up', (2, D, FF)), ('w_down', (2, FF, D)), ('hid_bias', (2, FF)), ('out_bias', (4, D))]

def split_flat(flat_vector):
    pieces = {}
    offset = 0
    for tensor_name, tensor_shape in param_layout():
        entries = math.prod(tensor_shape)
        pieces[tensor_name] = flat_vector[offset:offset + entries].reshape(tensor_shape)
        offset += entries
    return pieces

def layer_norm(inputs, norm_gain, norm_bias):
    row_mean = lax.optimization_barrier(jnp.mean(inputs, axis=-1, keepdims=True))
    centered = inputs - row_mean
    row_var = lax.optimization_barrier(jnp.mean(centered * centered, axis=-1, keepdims=True))
    return centered * lax.rsqrt(row_var + norm_eps) * norm_gain + norm_bias

def gelu_exact(inputs):
    return jax.nn.gelu(inputs, approximate=False)

def matmul(left, right):
    return jnp.dot(left, right, precision=lax.Precision.HIGHEST, preferred_element_type=jnp.float32)

def mlp_branch(row_data, norm_gain, norm_bias, w_up, up_bias, w_down, down_bias):
    normed = low(layer_norm(row_data, norm_gain, norm_bias))
    pre_act = low_back(matmul(normed, w_up) + up_bias)
    activation = low(gelu_exact(pre_act))
    return low_back(matmul(activation, w_down) + down_bias)

def self_frame(block):
    heads_view = block.reshape(LAT, 3, HEADS, HEAD_DIM)
    query_part = heads_view[:, 0]
    key_part = heads_view[:, 1]
    value_part = heads_view[:, 2]
    scores = low_back(jnp.einsum('qhd,khd->hqk', query_part, key_part, precision=lax.Precision.HIGHEST) * HEAD_DIM ** (-0.5))
    row_top = lax.optimization_barrier(jnp.max(scores, axis=-1, keepdims=True))
    exp_terms = jnp.exp(scores - row_top)
    attn_prob = low(exp_terms / lax.optimization_barrier(jnp.sum(exp_terms, axis=-1, keepdims=True)))
    mixed = low(low_back(jnp.einsum('hqk,khd->qhd', attn_prob, value_part, precision=lax.Precision.HIGHEST)))
    return mixed.reshape(LAT, D)

def group_forward(weights, token_rows, frame_row, episode_row):
    tok_norm = weights['tok_norm']
    tok_normed = low(layer_norm(token_rows, tok_norm[0], tok_norm[1]))
    key_value = low(low_back(matmul(tok_normed, weights['w_kv'])))
    key_part = key_value[:, :CH]
    value_part = key_value[:, CH:]
    episode_hot = (episode_row[:, None] == jnp.arange(EPISODES, dtype=jnp.int32)[None, :]).astype(jnp.float32)
    initial = weights['latent'][None, :, :] + matmul(episode_hot, weights['episode'])[:, None, :]
    initial = initial.reshape(FRAMES * LAT, D)
    norm_rows = weights['lat_norms']
    biases = weights['out_bias']
    query_in = low(layer_norm(initial, norm_rows[0], norm_rows[1]))
    queries = low(low_back(matmul(query_in, weights['w_q']))).reshape(FRAMES, LAT, CH)

    def cross_frame(inputs):
        query_frame, frame_index = inputs
        scores = low_back(matmul(query_frame, key_part.T) * CH ** (-0.5))
        visible = frame_row[None, :] == frame_index
        masked = jnp.where(visible, scores, masked_fill)
        row_top = lax.optimization_barrier(jnp.max(masked, axis=-1, keepdims=True))
        exp_terms = jnp.exp(masked - row_top)
        attn_prob = low(exp_terms / lax.optimization_barrier(jnp.sum(exp_terms, axis=-1, keepdims=True)))
        return low(low_back(matmul(attn_prob, value_part)))
    attended = lax.map(jax.checkpoint(cross_frame), (queries, jnp.arange(FRAMES, dtype=jnp.int32)))
    hidden_one = initial + low_back(matmul(attended.reshape(FRAMES * LAT, CH), weights['w_o']) + biases[0])
    hidden_two = hidden_one + mlp_branch(hidden_one, norm_rows[2], norm_rows[3], weights['w_up'][0], weights['hid_bias'][0], weights['w_down'][0], biases[1])
    sa_in = low(layer_norm(hidden_two, norm_rows[4], norm_rows[5]))
    qkv = low(low_back(matmul(sa_in, weights['w_qkv']))).reshape(FRAMES, LAT, 3 * D)
    mixed = lax.map(jax.checkpoint(self_frame), qkv).reshape(FRAMES * LAT, D)
    hidden_three = hidden_two + low_back(matmul(mixed, weights['w_so']) + biases[2])
    hidden_four = hidden_three + mlp_branch(hidden_three, norm_rows[6], norm_rows[7], weights['w_up'][1], weights['hid_bias'][1], weights['w_down'][1], biases[3])
    return hidden_four.reshape(FRAMES, LAT, D)

def reference(tokens, frame_ids, episodes, master, moment_one, moment_two, latent_grad):
    layout = param_layout()
    pieces = split_flat(master)

    def forward(pieces_in, token_values):
        weights = {tensor_name: low(tensor) for tensor_name, tensor in pieces_in.items()}

        def one_group(inputs):
            return group_forward(weights, inputs[0], inputs[1], inputs[2])
        return lax.map(jax.checkpoint(one_group), (token_values, frame_ids, episodes))
    latents, pullback = jax.vjp(forward, pieces, tokens.astype(jnp.float32))
    piece_grads, token_grad = pullback(latent_grad.astype(jnp.float32))
    grad_flat = jnp.concatenate([piece_grads[tensor_name].reshape(-1) for tensor_name, tensor_shape in layout])
    bias_grad = piece_grads['hid_bias']
    segment_ids = jnp.concatenate([jnp.full((math.prod(tensor_shape),), position, jnp.int32) for position, (tensor_name, tensor_shape) in enumerate(layout)])
    grad_sq = jnp.sum(grad_flat * grad_flat)
    clip_scale = jnp.minimum(1.0, clip_fraction * math.sqrt(NPARAM) / (jnp.sqrt(grad_sq) + 1e-06))
    clipped = clip_scale * grad_flat
    new_one = beta_one * moment_one + (1.0 - beta_one) * clipped
    new_two = beta_two * moment_two + (1.0 - beta_two) * clipped * clipped
    first_hat = new_one / (1.0 - beta_one ** lamb_step)
    second_hat = new_two / (1.0 - beta_two ** lamb_step)
    lamb_update = first_hat / (jnp.sqrt(second_hat) + adam_eps) + decay_rate * master
    weight_sq = jax.ops.segment_sum(master * master, segment_ids, num_segments=len(layout))
    update_sq = jax.ops.segment_sum(lamb_update * lamb_update, segment_ids, num_segments=len(layout))
    trust = jnp.sqrt(weight_sq) / (jnp.sqrt(update_sq) + 1e-06)
    return (latents.astype(jnp.bfloat16), token_grad.astype(jnp.bfloat16), grad_flat, lamb_update, new_one, new_two, trust, bias_grad)
```

```python
import functools
import math

import jax
import jax.numpy as jnp
from jax import lax
from jax.experimental import pallas as pl
from jax.experimental.pallas import tpu as pltpu
from jax.sharding import PartitionSpec as P

DIN = 256
D = 512
LAT = 512
CH = 64
HEADS = 8
HEAD_DIM = 64
FF = 2048
EPISODES = 11
NPARAM = 5619712
LANES = 128

norm_eps = 1e-05
masked_fill = -1e30
beta_one = 0.9
beta_two = 0.999
adam_eps = 1e-06
decay_rate = 0.01
clip_fraction = 0.5
lamb_step = 10.0

BF = jnp.bfloat16
F32 = jnp.float32
MIB = 1024 * 1024


def param_layout():
    return [
        ("latent", (LAT, D)),
        ("episode", (EPISODES, D)),
        ("tok_norm", (2, DIN)),
        ("lat_norms", (8, D)),
        ("w_kv", (DIN, 2 * CH)),
        ("w_q", (D, CH)),
        ("w_o", (CH, D)),
        ("w_qkv", (D, 3 * D)),
        ("w_so", (D, D)),
        ("w_up", (2, D, FF)),
        ("w_down", (2, FF, D)),
        ("hid_bias", (2, FF)),
        ("out_bias", (4, D)),
    ]


def split_flat(flat_vector):
    pieces = {}
    offset = 0
    for tensor_name, tensor_shape in param_layout():
        entries = math.prod(tensor_shape)
        pieces[tensor_name] = flat_vector[offset : offset + entries].reshape(tensor_shape)
        offset += entries
    return pieces


def layer_norm(inputs, norm_gain, norm_bias):
    row_mean = jnp.mean(inputs, axis=-1, keepdims=True)
    centered = inputs - row_mean
    row_var = jnp.mean(centered * centered, axis=-1, keepdims=True)
    return centered * lax.rsqrt(row_var + norm_eps) * norm_gain + norm_bias


def mm(left, right):
    return jnp.dot(left, right, preferred_element_type=F32)


def mm_t(left, right):
    return lax.dot_general(left, right, (((1,), (1,)), ((), ())), preferred_element_type=F32)


def t_mm(left, right):
    return lax.dot_general(left, right, (((0,), (0,)), ((), ())), preferred_element_type=F32)


def norm_stats(rows):
    mean = jnp.mean(rows, axis=-1, keepdims=True)
    centered = rows - mean
    var = jnp.mean(centered * centered, axis=-1, keepdims=True)
    rstd = lax.rsqrt(var + norm_eps)
    return centered * rstd, rstd


def norm_back(grad, xhat, rstd, gain):
    dxh = grad * gain
    first = jnp.mean(dxh, axis=-1, keepdims=True)
    second = jnp.mean(dxh * xhat, axis=-1, keepdims=True)
    return rstd * (dxh - first - xhat * second)


def col_sum(values):
    return jnp.sum(values, axis=0, keepdims=True)


def gelu_pair(x):
    size = jnp.abs(x)
    t = pl.reciprocal(1.0 + (0.3275911 / math.sqrt(2.0)) * size, approx=True)
    e = jnp.exp(x * x * -0.5)
    poly = 0.5 * 1.061405429
    for coef in (-1.453152027, 1.421413741, -0.284496736, 0.254829592):
        poly = poly * t + 0.5 * coef
    tail = poly * t * e
    cdf = jnp.where(x >= 0.0, 1.0 - tail, tail)
    return x * cdf, cdf + x * (e * (1.0 / math.sqrt(2.0 * math.pi)))


def accumulate(first, ref, value):
    @pl.when(first)
    def _():
        ref[...] = value

    @pl.when(jnp.logical_not(first))
    def _():
        ref[...] += value


def lane_half(shape, half):
    lane = lax.broadcasted_iota(jnp.int32, shape, 1)
    return (lane >= half * 64) & (lane < half * 64 + 64)


def keep_half(values, half):
    return jnp.where(lane_half(values.shape, half), values, jnp.zeros_like(values))


def select_tokens(rank_rows, cap):
    slot = lax.broadcasted_iota(jnp.int32, (cap, LANES), 0)
    parts = []
    for r in range(rank_rows.shape[0]):
        hit = slot == rank_rows[r : r + 1, :]
        parts.append(jnp.where(hit, 1.0, 0.0).astype(BF))
    return jnp.concatenate(parts, axis=1)


def cross_scores(kvf, queries_scaled, count):
    scores = mm_t(kvf, queries_scaled)
    slot = lax.broadcasted_iota(jnp.int32, scores.shape, 0)
    return jnp.where(slot < count, scores, masked_fill)


def cross_fwd_kernel(latent, episode, norms, w_q, w_o, out_bias, kv, rank, count, h1, kvf_out, co_out, lse_out):
    cap = kvf_out.shape[1]
    start = latent[...].astype(F32) + episode[0]
    xhat, unused = norm_stats(start)
    query_in = (xhat * norms[0:1, :] + norms[1:2, :]).astype(BF)
    queries = mm(query_in, w_q[...]).astype(BF) * jnp.asarray(0.125, BF)
    chunk = 8 * LANES
    chunks = kv.shape[0] // chunk

    def step(j, acc):
        sel = select_tokens(rank[0, pl.ds(pl.multiple_of(j * 8, 8), 8), :], cap)
        return acc + mm(sel, kv[pl.ds(pl.multiple_of(j * chunk, chunk), chunk), :])

    kvf = lax.fori_loop(0, chunks, step, jnp.zeros((cap, LANES), F32)).astype(BF)
    scores = cross_scores(kvf, queries, count[0, 0:1, 0:1])
    top = jnp.max(scores, axis=0, keepdims=True)
    terms = jnp.exp(scores - top)
    total = jnp.sum(terms, axis=0, keepdims=True)
    prob = (terms * (1.0 / total)).astype(BF)
    co = t_mm(kvf, prob).T.astype(BF)
    h1[...] = start + mm(co, w_o[...]) + out_bias[0:1, :]
    kvf_out[0] = kvf
    co_out[...] = co
    lse_out[0] = top + jnp.log(total)


def cross_bwd_kernel(
    latent, episode, norms, w_q, w_o, kvf_in, co_in, lse, rank, count, g1,
    dlatent, frame_sum, dnorm, dw_q, dw_o, dbias, dkv_t,
):
    first = pl.program_id(0) == 0
    cap = kvf_in.shape[1]
    start = latent[...].astype(F32) + episode[0]
    xhat, rstd = norm_stats(start)
    query_in = (xhat * norms[0:1, :] + norms[1:2, :]).astype(BF)
    queries = mm(query_in, w_q[...]).astype(BF) * jnp.asarray(0.125, BF)
    kvf = kvf_in[0]
    grad_one = g1[...]
    branch = grad_one.astype(BF)
    grad_co = mm_t(branch, w_o[...]).astype(BF)
    accumulate(first, dw_o, t_mm(co_in[...], branch))
    accumulate(first, dbias, col_sum(branch.astype(F32)))
    scores = cross_scores(kvf, queries, count[0, 0:1, 0:1])
    prob = jnp.exp(scores - lse[0])
    prob_low = prob.astype(BF)
    weighted = prob * mm_t(kvf, grad_co)
    grad_score = (weighted - prob * col_sum(weighted)).astype(BF)
    grad_kv = (mm(grad_score, queries) + mm(prob_low, grad_co)).astype(BF)
    grad_query = (t_mm(kvf, grad_score).T * 0.125).astype(BF)
    accumulate(first, dw_q, t_mm(query_in, grad_query))
    grad_in = mm_t(grad_query, w_q[...])
    grad_start = grad_one + norm_back(grad_in, xhat, rstd, norms[0:1, :])
    accumulate(first, dnorm, jnp.concatenate([col_sum(grad_in * xhat), col_sum(grad_in)], axis=0))
    accumulate(first, dlatent, grad_start)
    frame_sum[0] = col_sum(grad_start)
    grad_kv_t = grad_kv.T
    chunk = 8 * LANES

    @pl.when(first)
    def _():
        dkv_t[...] = jnp.zeros_like(dkv_t)

    def step(j, carry):
        sel = select_tokens(rank[0, pl.ds(pl.multiple_of(j * 8, 8), 8), :], cap)
        dkv_t[:, pl.ds(pl.multiple_of(j * chunk, chunk), chunk)] += mm(grad_kv_t, sel)
        return carry

    lax.fori_loop(0, dkv_t.shape[1] // chunk, step, 0)


FCHUNK = 512


def mlp_one_fwd_kernel(
    h1, norms, hid_bias, out_bias, w_up, w_down, w_qkv, h2, normed_out, act_out, slope_out, sa_out, qkv_out
):
    rows = h1[...]
    xhat, unused = norm_stats(rows)
    normed = (xhat * norms[2:3, :] + norms[3:4, :]).astype(BF)
    normed_out[...] = normed
    total = rows + out_bias[1:2, :]
    for c in range(FF // FCHUNK):
        at = slice(c * FCHUNK, (c + 1) * FCHUNK)
        act, slope = gelu_pair(mm(normed, w_up[:, at]) + hid_bias[0:1, at])
        act = act.astype(BF)
        act_out[:, at] = act
        slope_out[:, at] = slope.astype(BF)
        total = total + mm(act, w_down[at, :])
    h2[...] = total
    xhat, unused = norm_stats(total)
    sa_in = (xhat * norms[4:5, :] + norms[5:6, :]).astype(BF)
    sa_out[...] = sa_in
    for c in range(3):
        at = slice(c * D, (c + 1) * D)
        qkv_out[:, at] = mm(sa_in, w_qkv[:, at]).astype(BF)


def mlp_two_kernel(
    h3, grad, norms, hid_bias, out_bias, w_up, w_down,
    latents, g3, normed_out, act_out, dpre_out, dnorm, dhid, dout, slope_keep,
):
    first = pl.program_id(0) == 0
    rows = h3[...]
    xhat, rstd = norm_stats(rows)
    normed = (xhat * norms[6:7, :] + norms[7:8, :]).astype(BF)
    normed_out[...] = normed
    total = rows + out_bias[3:4, :]
    for c in range(FF // FCHUNK):
        at = slice(c * FCHUNK, (c + 1) * FCHUNK)
        act, slope = gelu_pair(mm(normed, w_up[:, at]) + hid_bias[1:2, at])
        act = act.astype(BF)
        act_out[:, at] = act
        slope_keep[:, at] = slope.astype(BF)
        total = total + mm(act, w_down[at, :])
    latents[...] = total.astype(BF)
    grad_low = grad[...]
    mlp_back(first, grad_low, grad_low.astype(F32), slope_keep, xhat, rstd, norms[6:7, :], w_up, w_down, g3, dpre_out, dnorm, dhid, dout)


def mlp_back(first, grad_low, grad_rows, slope, xhat, rstd, gain, w_up, w_down, grad_out, dpre_out, dnorm, dhid, dout):
    grad_normed = jnp.zeros(grad_rows.shape, F32)
    for c in range(FF // FCHUNK):
        at = slice(c * FCHUNK, (c + 1) * FCHUNK)
        dpre = (mm_t(grad_low, w_down[at, :]) * slope[:, at].astype(F32)).astype(BF)
        dpre_out[:, at] = dpre
        part = col_sum(dpre.astype(F32))

        @pl.when(first)
        def _(at=at, part=part):
            dhid[:, at] = part

        @pl.when(jnp.logical_not(first))
        def _(at=at, part=part):
            dhid[:, at] += part

        grad_normed = grad_normed + mm_t(dpre, w_up[:, at])
    accumulate(first, dnorm, jnp.concatenate([col_sum(grad_normed * xhat), col_sum(grad_normed)], axis=0))
    accumulate(first, dout, col_sum(grad_low.astype(F32)))
    grad_out[...] = grad_rows + norm_back(grad_normed, xhat, rstd, gain)


def mlp_one_bwd_kernel(h1, g2, slope, norms, w_up, w_down, g1, low_out, dpre_out, dnorm, dhid, dout):
    first = pl.program_id(0) == 0
    xhat, rstd = norm_stats(h1[...])
    grad_rows = g2[...]
    grad_low = grad_rows.astype(BF)
    low_out[...] = grad_low
    mlp_back(first, grad_low, grad_rows, slope, xhat, rstd, norms[2:3, :], w_up, w_down, g1, dpre_out, dnorm, dhid, dout)


def self_fwd_kernel(qkv, h2, w_so, out_bias, h3, mixed_out, lse_out):
    scale = jnp.asarray(0.125, BF)
    mixed_rows = []
    for pair in range(HEADS // 2):
        base = pair * LANES
        query_pair = qkv[:, base : base + LANES] * scale
        key_pair = qkv[:, D + base : D + base + LANES]
        value_t = qkv[:, 2 * D + base : 2 * D + base + LANES].T
        for half in range(2):
            scores = mm_t(key_pair, keep_half(query_pair, half))
            top = jnp.max(scores, axis=0, keepdims=True)
            terms = jnp.exp(scores - top)
            total = jnp.sum(terms, axis=0, keepdims=True)
            prob = (terms * (1.0 / total)).astype(BF)
            head = 2 * pair + half
            lse_out[0, head : head + 1, :] = top + jnp.log(total)
            mixed_rows.append(mm(value_t[half * 64 : half * 64 + 64, :], prob))
    mixed = jnp.concatenate(mixed_rows, axis=0).T.astype(BF)
    mixed_out[...] = mixed
    h3[...] = h2[...] + mm(mixed, w_so[...]) + out_bias[2:3, :]


def self_bwd_kernel(qkv, lse, g3, h2, norms, w_so, w_qkv, g2, low_out, dqkv_out, dnorm, dout):
    first = pl.program_id(0) == 0
    scale = jnp.asarray(0.125, BF)
    grad_rows = g3[...]
    grad_low = grad_rows.astype(BF)
    low_out[...] = grad_low
    accumulate(first, dout, col_sum(grad_low.astype(F32)))
    grad_mixed = mm_t(grad_low, w_so[...]).astype(BF)
    for pair in range(HEADS // 2):
        base = pair * LANES
        query_pair = qkv[:, base : base + LANES] * scale
        key_pair = qkv[:, D + base : D + base + LANES]
        value_pair = qkv[:, 2 * D + base : 2 * D + base + LANES]
        grad_pair = grad_mixed[:, base : base + LANES]
        key_t = key_pair.T
        query_t = []
        grad_key = jnp.zeros((LAT, LANES), F32)
        grad_value = jnp.zeros((LAT, LANES), F32)
        for half in range(2):
            head = 2 * pair + half
            query = keep_half(query_pair, half)
            grad_head = keep_half(grad_pair, half)
            prob = jnp.exp(mm_t(key_pair, query) - lse[0, head : head + 1, :])
            grad_value = grad_value + mm(prob.astype(BF), grad_head)
            weighted = prob * mm_t(value_pair, grad_head)
            grad_score = (weighted - prob * col_sum(weighted)).astype(BF)
            grad_key = grad_key + mm(grad_score, query)
            query_t.append(mm(key_t[half * 64 : half * 64 + 64, :], grad_score))
        dqkv_out[:, base : base + LANES] = (jnp.concatenate(query_t, axis=0).T * 0.125).astype(BF)
        dqkv_out[:, D + base : D + base + LANES] = grad_key.astype(BF)
        dqkv_out[:, 2 * D + base : 2 * D + base + LANES] = grad_value.astype(BF)
    grad_in = mm_t(dqkv_out[...], w_qkv[...])
    xhat, rstd = norm_stats(h2[...])
    accumulate(first, dnorm, jnp.concatenate([col_sum(grad_in * xhat), col_sum(grad_in)], axis=0))
    g2[...] = grad_rows + norm_back(grad_in, xhat, rstd, norms[4:5, :])


def segment_hot(starts, ends, base, rows):
    row = lax.broadcasted_iota(jnp.int32, (16, rows), 1) + base
    return jnp.where((row >= starts[:, 0:1]) & (row < ends[:, 0:1]), 1.0, 0.0).astype(BF)


def segment_sums(hot, squares):
    high = squares.astype(BF)
    low = (squares - high.astype(F32)).astype(BF)
    return mm(hot, high) + mm(hot, low)


def grad_stats_kernel(base, starts, ends, summed, master, grad_out, grad_sq, weight_sq):
    i = pl.program_id(0)
    rows = master.shape[0]
    hot = segment_hot(starts, ends, base[0] + i * rows, rows)
    grad = summed[...].astype(F32)
    grad_out[...] = grad
    accumulate(i == 0, grad_sq, col_sum(grad * grad))
    accumulate(i == 0, weight_sq, segment_sums(hot, master[...] * master[...]))


def lamb_kernel(base, clip, starts, ends, grad, master, one, two, update_out, one_out, two_out, update_sq):
    i = pl.program_id(0)
    rows = master.shape[0]
    hot = segment_hot(starts, ends, base[0] + i * rows, rows)
    clipped = clip[0] * grad[...]
    new_one = beta_one * one[...] + (1.0 - beta_one) * clipped
    new_two = beta_two * two[...] + (1.0 - beta_two) * clipped * clipped
    one_out[...] = new_one
    two_out[...] = new_two
    first_hat = new_one * (1.0 / (1.0 - beta_one**lamb_step))
    second_hat = new_two * (1.0 / (1.0 - beta_two**lamb_step))
    update = first_hat / (jnp.sqrt(second_hat) + adam_eps) + decay_rate * master[...]
    update_out[...] = update
    accumulate(i == 0, update_sq, segment_sums(hot, update * update))


def fixed(*shape):
    return pl.BlockSpec(shape, lambda i: (0,) * len(shape), pipeline_mode=pl.Buffered(1))


def kept(*shape):
    return pl.BlockSpec(shape, lambda i: (0,) * len(shape))


def rowed(rows, cols):
    return pl.BlockSpec((rows, cols), lambda i: (i, 0))


def framed(*shape):
    return pl.BlockSpec((1,) + shape, lambda i: (i,) + (0,) * len(shape))


def shaped(shape, dtype=F32):
    return jax.ShapeDtypeStruct(shape, dtype)


def call(kernel, grid, in_specs, outs, args, flops=0, trans=0, scratch=(), limit=56):
    out_specs, out_shapes = zip(*outs)
    moved = sum(math.prod(a.shape) * a.dtype.itemsize for a in args)
    moved += sum(math.prod(s.shape) * s.dtype.itemsize for s in out_shapes)
    return pl.pallas_call(
        kernel,
        grid=(grid,),
        in_specs=in_specs,
        out_specs=list(out_specs),
        out_shape=list(out_shapes),
        scratch_shapes=list(scratch),
        compiler_params=pltpu.CompilerParams(
            dimension_semantics=("arbitrary",), vmem_limit_bytes=limit * MIB
        ),
        cost_estimate=pl.CostEstimate(flops=flops, bytes_accessed=moved, transcendentals=trans),
    )(*args)


def body(tokens, frame_ids, episodes, master, moment_one, moment_two, latent_grad):
    lat_count = lax.axis_size("lat")
    lat_index = lax.axis_index("lat")
    shard_len = master.shape[0]
    frame_total = episodes.shape[1]
    frames = frame_total // lat_count
    rows_total = frames * LAT
    total_keys = frame_ids.shape[1] * lat_count
    cap = total_keys // 8
    token_rows_count = total_keys // LANES

    grad_rows_in = lax.all_to_all(
        latent_grad[0], "lat", split_axis=0, concat_axis=1, tiled=True
    ).reshape(rows_total, D)

    whole_flat = lax.all_gather(master.astype(BF), "lat", axis=0, tiled=True)
    weights = split_flat(whole_flat)
    norms = weights["lat_norms"].astype(F32)
    out_bias = weights["out_bias"].astype(F32)
    hid_bias = weights["hid_bias"].astype(F32)
    tok_norm = weights["tok_norm"].astype(F32)

    frame_tag = lax.all_gather(frame_ids[0].astype(BF), "lat", axis=0, tiled=True).astype(jnp.int32)
    own_frames = lat_index * frames + jnp.arange(frames, dtype=jnp.int32)
    own_hit = frame_tag[None, :] == own_frames[:, None]
    rank = jnp.cumsum(own_hit.astype(jnp.int32), axis=1) - 1
    counts = jnp.broadcast_to(rank[:, -1][:, None, None] + 1, (frames, 8, LANES))
    rank = jnp.where(own_hit, rank, -1).reshape(frames, token_rows_count, LANES)

    token_values = tokens[0].astype(F32)
    tok_full, token_pull = jax.vjp(layer_norm, token_values, tok_norm[0], tok_norm[1])
    tok_normed = tok_full.astype(BF)
    key_value = mm(tok_normed, weights["w_kv"]).astype(BF)
    all_keys = lax.all_gather(key_value, "lat", axis=0, tiled=True)

    episode_index = jnp.arange(EPISODES, dtype=jnp.int32)
    own_episodes = lax.dynamic_slice_in_dim(episodes[0], lat_index * frames, frames, 0)
    episode_match = own_episodes[:, None] == episode_index[None, :]
    episode_rows = mm(episode_match.astype(BF), weights["episode"]).reshape(frames, 1, D)
    w_q = jnp.pad(weights["w_q"], ((0, 0), (0, LANES - CH)))
    w_o = jnp.pad(weights["w_o"], ((LANES - CH, 0), (0, 0)))
    latent = weights["latent"]

    score_flops = rows_total * cap * LANES * 2
    select_flops = frames * cap * total_keys * LANES * 2
    h1, kvf, cross_out, cross_lse = call(
        cross_fwd_kernel,
        frames,
        [
            fixed(LAT, D), framed(1, D), fixed(8, D), fixed(D, LANES), fixed(LANES, D), fixed(4, D),
            fixed(total_keys, LANES), framed(token_rows_count, LANES), framed(8, LANES),
        ],
        [
            (rowed(LAT, D), shaped((rows_total, D))),
            (framed(cap, LANES), shaped((frames, cap, LANES), BF)),
            (rowed(LAT, LANES), shaped((rows_total, LANES), BF)),
            (framed(1, LAT), shaped((frames, 1, LAT))),
        ],
        (latent, episode_rows, norms, w_q, w_o, out_bias, all_keys, rank, counts),
        flops=2 * score_flops + select_flops,
        trans=rows_total * cap,
    )

    block = min(512, rows_total)
    steps = rows_total // block
    mlp_flops = 4 * rows_total * D * FF
    h2, normed_one, act_one, slope_one, sa_in, qkv = call(
        mlp_one_fwd_kernel,
        steps,
        [rowed(block, D), fixed(8, D), fixed(2, FF), fixed(4, D), fixed(D, FF), fixed(FF, D), fixed(D, 3 * D)],
        [
            (rowed(block, D), shaped((rows_total, D))),
            (rowed(block, D), shaped((rows_total, D), BF)),
            (rowed(block, FF), shaped((rows_total, FF), BF)),
            (rowed(block, FF), shaped((rows_total, FF), BF)),
            (rowed(block, D), shaped((rows_total, D), BF)),
            (rowed(block, 3 * D), shaped((rows_total, 3 * D), BF)),
        ],
        (h1, norms, hid_bias, out_bias, weights["w_up"][0], weights["w_down"][0], weights["w_qkv"]),
        flops=mlp_flops + 6 * rows_total * D * D,
        trans=2 * rows_total * FF,
    )

    attn_flops = 4 * rows_total * LAT * D
    h3, mixed, self_lse = call(
        self_fwd_kernel,
        frames,
        [rowed(LAT, 3 * D), rowed(LAT, D), fixed(D, D), fixed(4, D)],
        [
            (rowed(LAT, D), shaped((rows_total, D))),
            (rowed(LAT, D), shaped((rows_total, D), BF)),
            (framed(HEADS, LAT), shaped((frames, HEADS, LAT))),
        ],
        (qkv, h2, weights["w_so"], out_bias),
        flops=4 * attn_flops,
        trans=rows_total * LAT * HEADS,
    )

    latents, g3, normed_two, act_two, dpre_two, dnorm_two, dhid_two, dout_two = call(
        mlp_two_kernel,
        steps,
        [rowed(block, D), rowed(block, D), fixed(8, D), fixed(2, FF), fixed(4, D), fixed(D, FF), fixed(FF, D)],
        [
            (rowed(block, D), shaped((rows_total, D), BF)),
            (rowed(block, D), shaped((rows_total, D))),
            (rowed(block, D), shaped((rows_total, D), BF)),
            (rowed(block, FF), shaped((rows_total, FF), BF)),
            (rowed(block, FF), shaped((rows_total, FF), BF)),
            (kept(2, D), shaped((2, D))),
            (kept(1, FF), shaped((1, FF))),
            (kept(1, D), shaped((1, D))),
        ],
        (h3, grad_rows_in, norms, hid_bias, out_bias, weights["w_up"][1], weights["w_down"][1]),
        flops=2 * mlp_flops,
        trans=2 * rows_total * FF,
        scratch=[pltpu.VMEM((block, FF), BF)],
    )
    latents_out = lax.all_to_all(
        latents.reshape(frames, LAT, D), "lat", split_axis=1, concat_axis=0, tiled=True
    )[None]
    two_down = t_mm(act_two, grad_rows_in)
    two_up = t_mm(normed_two, dpre_two)

    g2, low_three, dqkv, dnorm_sa, dout_so = call(
        self_bwd_kernel,
        frames,
        [
            rowed(LAT, 3 * D), framed(HEADS, LAT), rowed(LAT, D), rowed(LAT, D), fixed(8, D),
            fixed(D, D), fixed(D, 3 * D),
        ],
        [
            (rowed(LAT, D), shaped((rows_total, D))),
            (rowed(LAT, D), shaped((rows_total, D), BF)),
            (rowed(LAT, 3 * D), shaped((rows_total, 3 * D), BF)),
            (kept(2, D), shaped((2, D))),
            (kept(1, D), shaped((1, D))),
        ],
        (qkv, self_lse, g3, h2, norms, weights["w_so"], weights["w_qkv"]),
        flops=10 * attn_flops,
        trans=rows_total * LAT * HEADS,
    )
    grad_so = t_mm(mixed, low_three)
    grad_qkv = t_mm(sa_in, dqkv)

    g1, low_two, dpre_one, dnorm_one, dhid_one, dout_one = call(
        mlp_one_bwd_kernel,
        steps,
        [rowed(block, D), rowed(block, D), rowed(block, FF), fixed(8, D), fixed(D, FF), fixed(FF, D)],
        [
            (rowed(block, D), shaped((rows_total, D))),
            (rowed(block, D), shaped((rows_total, D), BF)),
            (rowed(block, FF), shaped((rows_total, FF), BF)),
            (kept(2, D), shaped((2, D))),
            (kept(1, FF), shaped((1, FF))),
            (kept(1, D), shaped((1, D))),
        ],
        (h1, g2, slope_one, norms, weights["w_up"][0], weights["w_down"][0]),
        flops=mlp_flops,
    )
    one_down = t_mm(act_one, low_two)
    one_up = t_mm(normed_one, dpre_one)

    grad_latent, frame_sums, dnorm_q, dw_q, dw_o, dout_cross, dkv_t = call(
        cross_bwd_kernel,
        frames,
        [
            fixed(LAT, D), framed(1, D), fixed(8, D), fixed(D, LANES), fixed(LANES, D),
            framed(cap, LANES), rowed(LAT, LANES), framed(1, LAT), framed(token_rows_count, LANES),
            framed(8, LANES), rowed(LAT, D),
        ],
        [
            (kept(LAT, D), shaped((LAT, D))),
            (framed(1, D), shaped((frames, 1, D))),
            (kept(2, D), shaped((2, D))),
            (kept(D, LANES), shaped((D, LANES))),
            (kept(LANES, D), shaped((LANES, D))),
            (kept(1, D), shaped((1, D))),
            (kept(LANES, total_keys), shaped((LANES, total_keys))),
        ],
        (latent, episode_rows, norms, w_q, w_o, kvf, cross_out, cross_lse, rank, counts, g1),
        flops=5 * score_flops + select_flops,
        trans=rows_total * cap,
    )
    grad_episode = jnp.sum(episode_match.astype(F32)[:, :, None] * frame_sums, axis=0)

    grad_kv = lax.psum_scatter(dkv_t.T.astype(BF), "lat", scatter_dimension=0, tiled=True)
    grad_w_kv = t_mm(tok_normed, grad_kv)
    grad_tok_normed = mm_t(grad_kv, weights["w_kv"])
    grad_tokens, grad_tok_gain, grad_tok_bias = token_pull(grad_tok_normed)
    token_grad = grad_tokens.astype(BF)[None]

    grads = {
        "latent": grad_latent,
        "episode": grad_episode,
        "tok_norm": jnp.stack([grad_tok_gain, grad_tok_bias]),
        "lat_norms": jnp.concatenate([dnorm_q, dnorm_one, dnorm_sa, dnorm_two]),
        "w_kv": grad_w_kv,
        "w_q": dw_q[:, :CH],
        "w_o": dw_o[LANES - CH :],
        "w_qkv": grad_qkv,
        "w_so": grad_so,
        "w_up": jnp.stack([one_up, two_up]),
        "w_down": jnp.stack([one_down, two_down]),
        "hid_bias": jnp.concatenate([dhid_one, dhid_two]),
        "out_bias": jnp.concatenate([dout_cross, dout_one, dout_so, dout_two]),
    }
    layout = param_layout()
    local_flat = jnp.concatenate([grads[name].astype(BF).reshape(-1) for name, unused in layout])
    summed = lax.psum_scatter(local_flat, "lat", scatter_dimension=0, tiled=True)
    summed = lax.psum(summed, "kf")

    starts, ends, offset, bias_offset = [], [], 0, 0
    for name, shape in layout:
        if name == "hid_bias":
            bias_offset = offset
        starts.append(offset // LANES)
        offset += math.prod(shape)
        ends.append(offset // LANES)
    pad = [0] * (16 - len(layout))
    starts = jnp.broadcast_to(jnp.array(starts + pad, jnp.int32)[:, None], (16, LANES))
    ends = jnp.broadcast_to(jnp.array(ends + pad, jnp.int32)[:, None], (16, LANES))
    shard_rows = shard_len // LANES
    opt_rows = 784 if shard_rows % 784 == 0 else shard_rows
    opt_steps = shard_rows // opt_rows
    base = (lat_index * shard_rows).astype(jnp.int32).reshape(1)
    smem = pl.BlockSpec(memory_space=pltpu.SMEM)
    flat_rows = (shard_rows, LANES)
    master_rows = master.reshape(flat_rows)
    grad_shard, grad_sq, weight_sq = call(
        grad_stats_kernel,
        opt_steps,
        [smem, fixed(16, LANES), fixed(16, LANES), rowed(opt_rows, LANES), rowed(opt_rows, LANES)],
        [
            (rowed(opt_rows, LANES), shaped(flat_rows)),
            (kept(1, LANES), shaped((1, LANES))),
            (kept(16, LANES), shaped((16, LANES))),
        ],
        (base, starts, ends, summed.reshape(flat_rows), master_rows),
    )
    bias_owner, bias_at = divmod(bias_offset, shard_len)
    bias_part = jnp.where(
        lat_index == bias_owner, grad_shard.reshape(-1)[bias_at : bias_at + 2 * FF], 0.0
    )
    total_sq, weight_sq, bias_total = lax.psum(
        (jnp.sum(grad_sq), jnp.sum(weight_sq, axis=1), bias_part), "lat"
    )
    bias_grad = bias_total.reshape(2, FF)
    clip_scale = jnp.minimum(1.0, clip_fraction * math.sqrt(NPARAM) / (jnp.sqrt(total_sq) + 1e-06))
    lamb_update, new_one, new_two, update_sq = call(
        lamb_kernel,
        opt_steps,
        [smem, smem, fixed(16, LANES), fixed(16, LANES)] + [rowed(opt_rows, LANES)] * 4,
        [(rowed(opt_rows, LANES), shaped(flat_rows))] * 3 + [(kept(16, LANES), shaped((16, LANES)))],
        (
            base, clip_scale.reshape(1), starts, ends, grad_shard, master_rows,
            moment_one.reshape(flat_rows), moment_two.reshape(flat_rows),
        ),
    )
    update_sq = lax.psum(jnp.sum(update_sq, axis=1), "lat")
    trust = (jnp.sqrt(weight_sq) / (jnp.sqrt(update_sq) + 1e-06))[: len(layout)]
    return (
        latents_out,
        token_grad,
        grad_shard.reshape(-1),
        lamb_update.reshape(-1),
        new_one.reshape(-1),
        new_two.reshape(-1),
        trust,
        bias_grad,
    )


def solution(mesh):
    return jax.shard_map(
        body,
        mesh=mesh,
        in_specs=(
            P("kf", "lat", None),
            P("kf", "lat"),
            P("kf", None),
            P("lat"),
            P("lat"),
            P("lat"),
            P("kf", None, "lat", None),
        ),
        out_specs=(
            P("kf", None, "lat", None),
            P("kf", "lat", None),
            P("lat"),
            P("lat"),
            P("lat"),
            P("lat"),
            P(),
            P(),
        ),
        check_vma=False,
    )
```

```python
import functools
import math

import jax
import jax.numpy as jnp
from jax import lax
from jax.experimental import pallas as pl
from jax.experimental.pallas import tpu as pltpu
from jax.sharding import PartitionSpec as P

DIN = 256
D = 512
LAT = 512
CH = 64
HEADS = 8
HEAD_DIM = 64
FF = 2048
EPISODES = 11
NPARAM = 5619712
LANES = 128

norm_eps = 1e-05
masked_fill = -1e30
beta_one = 0.9
beta_two = 0.999
adam_eps = 1e-06
decay_rate = 0.01
clip_fraction = 0.5
lamb_step = 10.0

BF = jnp.bfloat16
F32 = jnp.float32
MIB = 1024 * 1024


def param_layout():
    return [
        ("latent", (LAT, D)),
        ("episode", (EPISODES, D)),
        ("tok_norm", (2, DIN)),
        ("lat_norms", (8, D)),
        ("w_kv", (DIN, 2 * CH)),
        ("w_q", (D, CH)),
        ("w_o", (CH, D)),
        ("w_qkv", (D, 3 * D)),
        ("w_so", (D, D)),
        ("w_up", (2, D, FF)),
        ("w_down", (2, FF, D)),
        ("hid_bias", (2, FF)),
        ("out_bias", (4, D)),
    ]


def split_flat(flat_vector):
    pieces = {}
    offset = 0
    for tensor_name, tensor_shape in param_layout():
        entries = math.prod(tensor_shape)
        pieces[tensor_name] = flat_vector[offset : offset + entries].reshape(tensor_shape)
        offset += entries
    return pieces


def layer_norm(inputs, norm_gain, norm_bias):
    row_mean = jnp.mean(inputs, axis=-1, keepdims=True)
    centered = inputs - row_mean
    row_var = jnp.mean(centered * centered, axis=-1, keepdims=True)
    return centered * lax.rsqrt(row_var + norm_eps) * norm_gain + norm_bias


def mm(left, right):
    return jnp.dot(left, right, preferred_element_type=F32)


def mm_t(left, right):
    return lax.dot_general(left, right, (((1,), (1,)), ((), ())), preferred_element_type=F32)


def t_mm(left, right):
    return lax.dot_general(left, right, (((0,), (0,)), ((), ())), preferred_element_type=F32)


def norm_stats(rows):
    mean = jnp.mean(rows, axis=-1, keepdims=True)
    centered = rows - mean
    var = jnp.mean(centered * centered, axis=-1, keepdims=True)
    rstd = lax.rsqrt(var + norm_eps)
    return centered * rstd, rstd


def norm_back(grad, xhat, rstd, gain):
    dxh = grad * gain
    first = jnp.mean(dxh, axis=-1, keepdims=True)
    second = jnp.mean(dxh * xhat, axis=-1, keepdims=True)
    return rstd * (dxh - first - xhat * second)


def col_sum(values):
    return jnp.sum(values, axis=0, keepdims=True)


def gelu_pair(x):
    size = jnp.abs(x)
    t = pl.reciprocal(1.0 + (0.3275911 / math.sqrt(2.0)) * size, approx=True)
    e = jnp.exp(x * x * -0.5)
    poly = 0.5 * 1.061405429
    for coef in (-1.453152027, 1.421413741, -0.284496736, 0.254829592):
        poly = poly * t + 0.5 * coef
    tail = poly * t * e
    cdf = jnp.where(x >= 0.0, 1.0 - tail, tail)
    return x * cdf, cdf + x * (e * (1.0 / math.sqrt(2.0 * math.pi)))


def accumulate(first, ref, value):
    @pl.when(first)
    def _():
        ref[...] = value

    @pl.when(jnp.logical_not(first))
    def _():
        ref[...] += value


def lane_half(shape, half):
    lane = lax.broadcasted_iota(jnp.int32, shape, 1)
    return (lane >= half * 64) & (lane < half * 64 + 64)


def keep_half(values, half):
    return jnp.where(lane_half(values.shape, half), values, jnp.zeros_like(values))


def select_tokens(rank_rows, cap):
    slot = lax.broadcasted_iota(jnp.int32, (cap, LANES), 0)
    parts = []
    for r in range(rank_rows.shape[0]):
        hit = slot == rank_rows[r : r + 1, :]
        parts.append(jnp.where(hit, 1.0, 0.0).astype(BF))
    return jnp.concatenate(parts, axis=1)


def cross_scores(kvf, queries_scaled, count):
    scores = mm_t(kvf, queries_scaled)
    slot = lax.broadcasted_iota(jnp.int32, scores.shape, 0)
    return jnp.where(slot < count, scores, masked_fill)


def cross_fwd_kernel(latent, episode, norms, w_q, w_o, out_bias, kv, rank, count, h1, kvf_out, co_out, lse_out):
    cap = kvf_out.shape[1]
    start = latent[...].astype(F32) + episode[0]
    xhat, unused = norm_stats(start)
    query_in = (xhat * norms[0:1, :] + norms[1:2, :]).astype(BF)
    queries = mm(query_in, w_q[...]).astype(BF) * jnp.asarray(0.125, BF)
    chunk = 8 * LANES
    chunks = kv.shape[0] // chunk

    def step(j, acc):
        sel = select_tokens(rank[0, pl.ds(pl.multiple_of(j * 8, 8), 8), :], cap)
        return acc + mm(sel, kv[pl.ds(pl.multiple_of(j * chunk, chunk), chunk), :])

    kvf = lax.fori_loop(0, chunks, step, jnp.zeros((cap, LANES), F32)).astype(BF)
    scores = cross_scores(kvf, queries, count[0, 0:1, 0:1])
    top = jnp.max(scores, axis=0, keepdims=True)
    terms = jnp.exp(scores - top)
    total = jnp.sum(terms, axis=0, keepdims=True)
    prob = (terms * (1.0 / total)).astype(BF)
    co = t_mm(kvf, prob).T.astype(BF)
    h1[...] = start + mm(co, w_o[...]) + out_bias[0:1, :]
    kvf_out[0] = kvf
    co_out[...] = co
    lse_out[0] = top + jnp.log(total)


def cross_bwd_kernel(
    latent, episode, norms, w_q, w_o, kvf_in, co_in, lse, rank, count, g1,
    dlatent, frame_sum, dnorm, dw_q, dw_o, dbias, dkv_t,
):
    first = pl.program_id(0) == 0
    cap = kvf_in.shape[1]
    start = latent[...].astype(F32) + episode[0]
    xhat, rstd = norm_stats(start)
    query_in = (xhat * norms[0:1, :] + norms[1:2, :]).astype(BF)
    queries = mm(query_in, w_q[...]).astype(BF) * jnp.asarray(0.125, BF)
    kvf = kvf_in[0]
    grad_one = g1[...]
    branch = grad_one.astype(BF)
    grad_co = mm_t(branch, w_o[...]).astype(BF)
    accumulate(first, dw_o, t_mm(co_in[...], branch))
    accumulate(first, dbias, col_sum(branch.astype(F32)))
    scores = cross_scores(kvf, queries, count[0, 0:1, 0:1])
    prob = jnp.exp(scores - lse[0])
    prob_low = prob.astype(BF)
    weighted = prob * mm_t(kvf, grad_co)
    grad_score = (weighted - prob * col_sum(weighted)).astype(BF)
    grad_kv = (mm(grad_score, queries) + mm(prob_low, grad_co)).astype(BF)
    grad_query = (t_mm(kvf, grad_score).T * 0.125).astype(BF)
    accumulate(first, dw_q, t_mm(query_in, grad_query))
    grad_in = mm_t(grad_query, w_q[...])
    grad_start = grad_one + norm_back(grad_in, xhat, rstd, norms[0:1, :])
    accumulate(first, dnorm, jnp.concatenate([col_sum(grad_in * xhat), col_sum(grad_in)], axis=0))
    accumulate(first, dlatent, grad_start)
    frame_sum[0] = col_sum(grad_start)
    grad_kv_t = grad_kv.T
    chunk = 8 * LANES

    @pl.when(first)
    def _():
        dkv_t[...] = jnp.zeros_like(dkv_t)

    def step(j, carry):
        sel = select_tokens(rank[0, pl.ds(pl.multiple_of(j * 8, 8), 8), :], cap)
        dkv_t[:, pl.ds(pl.multiple_of(j * chunk, chunk), chunk)] += mm(grad_kv_t, sel)
        return carry

    lax.fori_loop(0, dkv_t.shape[1] // chunk, step, 0)


FCHUNK = 512


def mlp_one_fwd_kernel(
    h1, norms, hid_bias, out_bias, w_up, w_down, w_qkv, h2, normed_out, act_out, slope_out, sa_out, qkv_out
):
    rows = h1[...]
    xhat, unused = norm_stats(rows)
    normed = (xhat * norms[2:3, :] + norms[3:4, :]).astype(BF)
    normed_out[...] = normed
    total = rows + out_bias[1:2, :]
    for c in range(FF // FCHUNK):
        at = slice(c * FCHUNK, (c + 1) * FCHUNK)
        act, slope = gelu_pair(mm(normed, w_up[:, at]) + hid_bias[0:1, at])
        act = act.astype(BF)
        act_out[:, at] = act
        slope_out[:, at] = slope.astype(BF)
        total = total + mm(act, w_down[at, :])
    h2[...] = total
    xhat, unused = norm_stats(total)
    sa_in = (xhat * norms[4:5, :] + norms[5:6, :]).astype(BF)
    sa_out[...] = sa_in
    for c in range(3):
        at = slice(c * D, (c + 1) * D)
        qkv_out[:, at] = mm(sa_in, w_qkv[:, at]).astype(BF)


def mlp_two_kernel(
    h3, grad, norms, hid_bias, out_bias, w_up, w_down,
    latents, g3, normed_out, act_out, dpre_out, dnorm, dhid, dout, slope_keep,
):
    first = pl.program_id(0) == 0
    rows = h3[...]
    xhat, rstd = norm_stats(rows)
    normed = (xhat * norms[6:7, :] + norms[7:8, :]).astype(BF)
    normed_out[...] = normed
    total = rows + out_bias[3:4, :]
    for c in range(FF // FCHUNK):
        at = slice(c * FCHUNK, (c + 1) * FCHUNK)
        act, slope = gelu_pair(mm(normed, w_up[:, at]) + hid_bias[1:2, at])
        act = act.astype(BF)
        act_out[:, at] = act
        slope_keep[:, at] = slope.astype(BF)
        total = total + mm(act, w_down[at, :])
    latents[...] = total.astype(BF)
    grad_low = grad[...]
    mlp_back(first, grad_low, grad_low.astype(F32), slope_keep, xhat, rstd, norms[6:7, :], w_up, w_down, g3, dpre_out, dnorm, dhid, dout)


def mlp_back(first, grad_low, grad_rows, slope, xhat, rstd, gain, w_up, w_down, grad_out, dpre_out, dnorm, dhid, dout):
    grad_normed = jnp.zeros(grad_rows.shape, F32)
    for c in range(FF // FCHUNK):
        at = slice(c * FCHUNK, (c + 1) * FCHUNK)
        dpre = (mm_t(grad_low, w_down[at, :]) * slope[:, at].astype(F32)).astype(BF)
        dpre_out[:, at] = dpre
        part = col_sum(dpre.astype(F32))

        @pl.when(first)
        def _(at=at, part=part):
            dhid[:, at] = part

        @pl.when(jnp.logical_not(first))
        def _(at=at, part=part):
            dhid[:, at] += part

        grad_normed = grad_normed + mm_t(dpre, w_up[:, at])
    accumulate(first, dnorm, jnp.concatenate([col_sum(grad_normed * xhat), col_sum(grad_normed)], axis=0))
    accumulate(first, dout, col_sum(grad_low.astype(F32)))
    grad_out[...] = grad_rows + norm_back(grad_normed, xhat, rstd, gain)


def mlp_one_bwd_kernel(h1, g2, slope, norms, w_up, w_down, g1, low_out, dpre_out, dnorm, dhid, dout):
    first = pl.program_id(0) == 0
    xhat, rstd = norm_stats(h1[...])
    grad_rows = g2[...]
    grad_low = grad_rows.astype(BF)
    low_out[...] = grad_low
    mlp_back(first, grad_low, grad_rows, slope, xhat, rstd, norms[2:3, :], w_up, w_down, g1, dpre_out, dnorm, dhid, dout)


def self_fwd_kernel(qkv, h2, w_so, out_bias, h3, mixed_out, lse_out):
    scale = jnp.asarray(0.125, BF)
    mixed_rows = []
    for pair in range(HEADS // 2):
        base = pair * LANES
        query_pair = qkv[:, base : base + LANES] * scale
        key_pair = qkv[:, D + base : D + base + LANES]
        value_t = qkv[:, 2 * D + base : 2 * D + base + LANES].T
        for half in range(2):
            scores = mm_t(key_pair, keep_half(query_pair, half))
            top = jnp.max(scores, axis=0, keepdims=True)
            terms = jnp.exp(scores - top)
            total = jnp.sum(terms, axis=0, keepdims=True)
            prob = (terms * (1.0 / total)).astype(BF)
            head = 2 * pair + half
            lse_out[0, head : head + 1, :] = top + jnp.log(total)
            mixed_rows.append(mm(value_t[half * 64 : half * 64 + 64, :], prob))
    mixed = jnp.concatenate(mixed_rows, axis=0).T.astype(BF)
    mixed_out[...] = mixed
    h3[...] = h2[...] + mm(mixed, w_so[...]) + out_bias[2:3, :]


def self_bwd_kernel(qkv, lse, g3, h2, norms, w_so, w_qkv, g2, low_out, dqkv_out, dnorm, dout):
    first = pl.program_id(0) == 0
    scale = jnp.asarray(0.125, BF)
    grad_rows = g3[...]
    grad_low = grad_rows.astype(BF)
    low_out[...] = grad_low
    accumulate(first, dout, col_sum(grad_low.astype(F32)))
    grad_mixed = mm_t(grad_low, w_so[...]).astype(BF)
    for pair in range(HEADS // 2):
        base = pair * LANES
        query_pair = qkv[:, base : base + LANES] * scale
        key_pair = qkv[:, D + base : D + base + LANES]
        value_pair = qkv[:, 2 * D + base : 2 * D + base + LANES]
        grad_pair = grad_mixed[:, base : base + LANES]
        key_t = key_pair.T
        query_t = []
        grad_key = jnp.zeros((LAT, LANES), F32)
        grad_value = jnp.zeros((LAT, LANES), F32)
        for half in range(2):
            head = 2 * pair + half
            query = keep_half(query_pair, half)
            grad_head = keep_half(grad_pair, half)
            prob = jnp.exp(mm_t(key_pair, query) - lse[0, head : head + 1, :])
            grad_value = grad_value + mm(prob.astype(BF), grad_head)
            weighted = prob * mm_t(value_pair, grad_head)
            grad_score = (weighted - prob * col_sum(weighted)).astype(BF)
            grad_key = grad_key + mm(grad_score, query)
            query_t.append(mm(key_t[half * 64 : half * 64 + 64, :], grad_score))
        dqkv_out[:, base : base + LANES] = (jnp.concatenate(query_t, axis=0).T * 0.125).astype(BF)
        dqkv_out[:, D + base : D + base + LANES] = grad_key.astype(BF)
        dqkv_out[:, 2 * D + base : 2 * D + base + LANES] = grad_value.astype(BF)
    grad_in = mm_t(dqkv_out[...], w_qkv[...])
    xhat, rstd = norm_stats(h2[...])
    accumulate(first, dnorm, jnp.concatenate([col_sum(grad_in * xhat), col_sum(grad_in)], axis=0))
    g2[...] = grad_rows + norm_back(grad_in, xhat, rstd, norms[4:5, :])


def segment_hot(starts, ends, base, rows):
    row = lax.broadcasted_iota(jnp.int32, (16, rows), 1) + base
    return jnp.where((row >= starts[:, 0:1]) & (row < ends[:, 0:1]), 1.0, 0.0).astype(BF)


def segment_sums(hot, squares):
    high = squares.astype(BF)
    low = (squares - high.astype(F32)).astype(BF)
    return mm(hot, high) + mm(hot, low)


def grad_stats_kernel(base, starts, ends, summed, master, grad_sq, weight_sq):
    i = pl.program_id(0)
    rows = master.shape[0]
    hot = segment_hot(starts, ends, base[0] + i * rows, rows)
    grad = summed[...].astype(F32)
    accumulate(i == 0, grad_sq, col_sum(grad * grad))
    accumulate(i == 0, weight_sq, segment_sums(hot, master[...] * master[...]))


def lamb_kernel(base, stats, starts, ends, summed, master, one, two, grad_out, update_out, one_out, two_out, update_sq):
    i = pl.program_id(0)
    rows = master.shape[0]
    hot = segment_hot(starts, ends, base[0] + i * rows, rows)
    total_sq = jnp.sum(stats[0:1, :], axis=1, keepdims=True)
    clip = jnp.minimum(1.0, clip_fraction * math.sqrt(NPARAM) / (jnp.sqrt(total_sq) + 1e-06))
    grad = summed[...].astype(F32)
    grad_out[...] = grad
    clipped = clip * grad
    new_one = beta_one * one[...] + (1.0 - beta_one) * clipped
    new_two = beta_two * two[...] + (1.0 - beta_two) * clipped * clipped
    one_out[...] = new_one
    two_out[...] = new_two
    first_hat = new_one * (1.0 / (1.0 - beta_one**lamb_step))
    second_hat = new_two * (1.0 / (1.0 - beta_two**lamb_step))
    update = first_hat / (jnp.sqrt(second_hat) + adam_eps) + decay_rate * master[...]
    update_out[...] = update
    accumulate(i == 0, update_sq, segment_sums(hot, update * update))


BATCH = 256
HALF = 128
QUARTER = 64
MESH = pl.DeviceIdType.MESH


class Place:
    def __init__(self):
        self.z = lax.axis_index("kf")
        self.me = lax.axis_index("lat")
        self.core = lax.rem(self.me, 2)
        self.x = lax.rem(self.me // 2, 2)
        self.y = self.me // 4
        self.z_low = lax.rem(self.z, 2)
        self.z_high = self.z // 2
        self.sibling = (self.z, self.me + 1 - 2 * self.core)
        self.x_side = (self.z, self.me + 2 - 4 * self.x)
        self.y_side = (self.z, self.me + 4 - 8 * self.y)
        self.z_near = (self.z + 1 - 2 * self.z_low, self.me)
        self.z_far = (self.z + 2 - 4 * self.z_high, self.me)

    def z_other(self, step):
        return (lax.rem(self.z + step, 4), self.me)

    def lat_other(self, step):
        return (self.z, lax.rem(self.me + step, 8))


def remote(src, dst, send, recv, device):
    return pltpu.make_async_remote_copy(
        src_ref=src, dst_ref=dst, send_sem=send, recv_sem=recv, device_id=device, device_id_type=MESH
    )


def greet(devices):
    barrier = pltpu.get_barrier_semaphore()
    for device in devices:
        pl.semaphore_signal(barrier, inc=1, device_id=device, device_id_type=MESH)
    pl.semaphore_wait(barrier, len(devices))


def added(left, right):
    return (left.astype(F32) + right.astype(F32)).astype(BF)


class Reduction:
    lags = (0, 1, 3, 5, 7, 9, 11)

    def __init__(self, place, grads, out, bufs, sems):
        self.p = place
        self.grads = grads
        self.out = out
        self.own, self.rc, self.r1, self.r2, self.r3, self.r4, self.res = bufs
        self.own_sem, self.send, self.rc_sem, self.r1_sem, self.r2_sem, self.r3_sem, self.r4_sem, self.res_sem = sems
        self.shard = grads.shape[3]
        self.batches = pl.cdiv(self.shard, BATCH)
        self.back = self.batches * BATCH - self.shard

    @staticmethod
    def scratch(shard):
        n = pl.cdiv(shard, BATCH)
        bufs = [
            pltpu.VMEM((2, 2, 2, BATCH, LANES), BF),
            pltpu.VMEM((n, 2, 2, BATCH, LANES), BF),
            pltpu.VMEM((n, 2, 2, HALF, LANES), BF),
            pltpu.VMEM((n, 2, HALF, LANES), BF),
            pltpu.VMEM((n, HALF, LANES), BF),
            pltpu.VMEM((n, QUARTER, LANES), BF),
            pltpu.VMEM((n, BATCH, LANES), BF),
        ]
        dma = pltpu.SemaphoreType.DMA
        sems = [dma((2,)), dma((10, 4)), dma((n,)), dma((n, 2)), dma((n, 2)), dma((n,)), dma((n,)), dma((n, 3))]
        return bufs + sems

    def row(self, i):
        return pl.multiple_of(i * BATCH - (i // (self.batches - 1)) * self.back, 16)

    def own_copy(self, i):
        slot = lax.rem(i, 2)
        src = self.grads.at[:, :, self.p.core, pl.ds(self.row(i), BATCH), :]
        return pltpu.make_async_copy(src, self.own.at[slot], self.own_sem.at[slot])

    def copies(self, stage, i):
        p, slot = self.p, lax.rem(i, 4)
        if stage == 0:
            src = self.grads.at[:, :, 1 - p.core, pl.ds(self.row(i), BATCH), :]
            return [remote(src, self.rc.at[i], self.send.at[0, slot], self.rc_sem.at[i], p.sibling)]
        if stage == 1:
            to_x = self.rc.at[i, :, 1 - p.x, pl.ds(0, HALF), :]
            to_y = self.rc.at[i, 1 - p.y, :, pl.ds(HALF, HALF), :]
            return [
                remote(to_x, self.r1.at[i, 0], self.send.at[1, slot], self.r1_sem.at[i, 0], p.x_side),
                remote(to_y, self.r1.at[i, 1], self.send.at[2, slot], self.r1_sem.at[i, 1], p.y_side),
            ]
        if stage == 2:
            to_y = self.r1.at[i, 0, 1 - p.y]
            to_x = self.r1.at[i, 1, 1 - p.x]
            return [
                remote(to_y, self.r2.at[i, 0], self.send.at[3, slot], self.r2_sem.at[i, 0], p.y_side),
                remote(to_x, self.r2.at[i, 1], self.send.at[4, slot], self.r2_sem.at[i, 1], p.x_side),
            ]
        if stage == 3:
            src = self.r2.at[i, 1 - p.z_low]
            return [remote(src, self.r3.at[i], self.send.at[5, slot], self.r3_sem.at[i], p.z_near)]
        if stage == 4:
            src = self.r3.at[i, pl.ds(pl.multiple_of((1 - p.z_high) * QUARTER, QUARTER), QUARTER), :]
            return [remote(src, self.r4.at[i], self.send.at[6, slot], self.r4_sem.at[i], p.z_far)]
        mine = self.res.at[i, pl.ds(pl.multiple_of(p.z_low * HALF + p.z_high * QUARTER, QUARTER), QUARTER), :]
        return [
            remote(mine, mine, self.send.at[6 + d, slot], self.res_sem.at[i, d - 1], p.z_other(d))
            for d in (1, 2, 3)
        ]

    def launch(self, stage, i):
        @pl.when(i >= 4)
        def _():
            for copy in self.copies(stage, i - 4):
                copy.wait_send()

        for copy in self.copies(stage, i):
            copy.start()

    def landed(self, stage, i):
        for copy in self.copies(stage, i):
            copy.wait_recv()

    def work(self, stage, i):
        p = self.p
        if stage == 0:
            self.own_copy(i).start()
        elif stage == 1:
            self.landed(0, i)
            self.own_copy(i).wait()
            self.rc[i] = added(self.rc[i], self.own[lax.rem(i, 2)])
        elif stage == 2:
            self.landed(1, i)
            self.r1[i, 0] = added(self.r1[i, 0], self.rc[i, :, p.x, 0:HALF, :])
            self.r1[i, 1] = added(self.r1[i, 1], self.rc[i, p.y, :, HALF:BATCH, :])
        elif stage == 3:
            self.landed(2, i)
            self.r2[i, 0] = added(self.r2[i, 0], self.r1[i, 0, p.y])
            self.r2[i, 1] = added(self.r2[i, 1], self.r1[i, 1, p.x])
        elif stage == 4:
            self.landed(3, i)
            self.r3[i] = added(self.r3[i], self.r2[i, p.z_low])
        elif stage == 5:
            self.landed(4, i)
            part = self.r3[i, pl.ds(pl.multiple_of(p.z_high * QUARTER, QUARTER), QUARTER), :]
            at = pl.multiple_of(p.z_low * HALF + p.z_high * QUARTER, QUARTER)
            self.res[i, pl.ds(at, QUARTER), :] = added(self.r4[i], part)
        else:
            self.landed(5, i)
            self.out[pl.ds(self.row(i), BATCH), :] = self.res[i]
        if stage < 6:
            self.launch(stage, i)

    def tick(self, t):
        for stage, lag in enumerate(self.lags):
            i = t - lag

            @pl.when((i >= 0) & (i < self.batches))
            def _(stage=stage, i=i):
                self.work(stage, i)

    def ticks(self):
        return self.batches + self.lags[-1]

    def finish(self):
        for stage in range(6):
            for back in range(4):
                for copy in self.copies(stage, self.batches - 4 + back):
                    copy.wait_send()

    def partners(self):
        p = self.p
        return [p.sibling, p.x_side, p.y_side] + [p.z_other(d) for d in (1, 2, 3)]


def share_all(place, block, send, recv):
    mine = block.at[place.me]
    copies = [
        remote(mine, mine, send.at[d - 1], recv.at[d - 1], place.lat_other(d)) for d in range(1, 8)
    ]
    for copy in copies:
        copy.start()
    for copy in copies:
        copy.wait()


STAT_ROWS = 56


def reduce_kernel(bias_owner, bias_at, starts, ends, grads, master, summed, stats, *scratch):
    place = Place()
    block, block_send, block_recv = scratch[:3]
    red = Reduction(place, grads, summed, scratch[3:10], scratch[10:])
    greet([place.lat_other(d) for d in range(1, 8)] + [place.z_other(d) for d in (1, 2, 3)])
    lax.fori_loop(0, red.ticks(), lambda t, c: (red.tick(t), c)[1], 0)
    shard = master.shape[0]
    step = 784
    grad_sq = jnp.zeros((1, LANES), F32)
    weight_sq = jnp.zeros((16, LANES), F32)
    for j in range(shard // step):
        at = slice(j * step, (j + 1) * step)
        part = summed[at, :].astype(F32)
        grad_sq = grad_sq + col_sum(part * part)
        hot = segment_hot(starts, ends, place.me * shard + j * step, step)
        part = master[at, :]
        weight_sq = weight_sq + segment_sums(hot, part * part)
    bias = summed[bias_at : bias_at + 2 * FF // LANES, :].astype(F32)
    bias = jnp.where(place.me == bias_owner, bias, 0.0)
    head = jnp.concatenate([grad_sq, jnp.zeros((7, LANES), F32), weight_sq, bias], axis=0)
    block[pl.ds(place.me, 1)] = head[None]
    share_all(place, block, block_send, block_recv)
    total = block[0]
    for s in range(1, 8):
        total = total + block[s]
    stats[...] = total
    red.finish()


def trust_kernel(update_sq, stats, trust, block, send, recv):
    place = Place()
    greet([place.lat_other(d) for d in range(1, 8)])
    block[pl.ds(place.me, 1)] = update_sq[...][None]
    share_all(place, block, send, recv)
    total = block[0]
    for s in range(1, 8):
        total = total + block[s]
    update_norm = jnp.sqrt(jnp.sum(total, axis=1, keepdims=True))
    weight_norm = jnp.sqrt(jnp.sum(stats[8:24, :], axis=1, keepdims=True))
    trust[...] = jnp.broadcast_to(weight_norm / (update_norm + 1e-06), (16, LANES))


def fixed(*shape):
    return pl.BlockSpec(shape, lambda i: (0,) * len(shape), pipeline_mode=pl.Buffered(1))


def kept(*shape):
    return pl.BlockSpec(shape, lambda i: (0,) * len(shape))


def rowed(rows, cols):
    return pl.BlockSpec((rows, cols), lambda i: (i, 0))


def framed(*shape):
    return pl.BlockSpec((1,) + shape, lambda i: (i,) + (0,) * len(shape))


def shaped(shape, dtype=F32):
    return jax.ShapeDtypeStruct(shape, dtype)


def call(kernel, grid, in_specs, outs, args, flops=0, trans=0, scratch=(), limit=56):
    out_specs, out_shapes = zip(*outs)
    moved = sum(math.prod(a.shape) * a.dtype.itemsize for a in args)
    moved += sum(math.prod(s.shape) * s.dtype.itemsize for s in out_shapes)
    return pl.pallas_call(
        kernel,
        grid=(grid,),
        in_specs=in_specs,
        out_specs=list(out_specs),
        out_shape=list(out_shapes),
        scratch_shapes=list(scratch),
        compiler_params=pltpu.CompilerParams(
            dimension_semantics=("arbitrary",), vmem_limit_bytes=limit * MIB
        ),
        cost_estimate=pl.CostEstimate(flops=flops, bytes_accessed=moved, transcendentals=trans),
    )(*args)


def reduce_all(local_flat, master_rows, starts, ends, bias_owner, bias_row):
    shard = master_rows.shape[0]
    vmem = pl.BlockSpec(memory_space=pltpu.VMEM)
    block = [
        pltpu.VMEM((8, STAT_ROWS, LANES), F32),
        pltpu.SemaphoreType.DMA((7,)),
        pltpu.SemaphoreType.DMA((7,)),
    ]
    return pl.pallas_call(
        functools.partial(reduce_kernel, bias_owner, bias_row),
        out_shape=[shaped((shard, LANES), BF), shaped((STAT_ROWS, LANES))],
        in_specs=[vmem, vmem, pl.BlockSpec(memory_space=pl.ANY), vmem],
        out_specs=[vmem, vmem],
        scratch_shapes=block + Reduction.scratch(shard),
        compiler_params=pltpu.CompilerParams(
            collective_id=1, has_side_effects=True, vmem_limit_bytes=48 * MIB
        ),
    )(starts, ends, local_flat.reshape(2, 2, 2, shard, LANES), master_rows)


def body(tokens, frame_ids, episodes, master, moment_one, moment_two, latent_grad):
    lat_count = lax.axis_size("lat")
    lat_index = lax.axis_index("lat")
    shard_len = master.shape[0]
    frame_total = episodes.shape[1]
    frames = frame_total // lat_count
    rows_total = frames * LAT
    total_keys = frame_ids.shape[1] * lat_count
    cap = total_keys // 8
    token_rows_count = total_keys // LANES

    grad_rows_in = lax.all_to_all(
        latent_grad[0], "lat", split_axis=0, concat_axis=1, tiled=True
    ).reshape(rows_total, D)

    whole_flat = lax.all_gather(master.astype(BF), "lat", axis=0, tiled=True)
    weights = split_flat(whole_flat)
    norms = weights["lat_norms"].astype(F32)
    out_bias = weights["out_bias"].astype(F32)
    hid_bias = weights["hid_bias"].astype(F32)
    tok_norm = weights["tok_norm"].astype(F32)

    frame_tag = lax.all_gather(frame_ids[0].astype(BF), "lat", axis=0, tiled=True).astype(jnp.int32)
    own_frames = lat_index * frames + jnp.arange(frames, dtype=jnp.int32)
    own_hit = frame_tag[None, :] == own_frames[:, None]
    rank = jnp.cumsum(own_hit.astype(jnp.int32), axis=1) - 1
    counts = jnp.broadcast_to(rank[:, -1][:, None, None] + 1, (frames, 8, LANES))
    rank = jnp.where(own_hit, rank, -1).reshape(frames, token_rows_count, LANES)

    token_values = tokens[0].astype(F32)
    tok_full, token_pull = jax.vjp(layer_norm, token_values, tok_norm[0], tok_norm[1])
    tok_normed = tok_full.astype(BF)
    key_value = mm(tok_normed, weights["w_kv"]).astype(BF)
    all_keys = lax.all_gather(key_value, "lat", axis=0, tiled=True)

    episode_index = jnp.arange(EPISODES, dtype=jnp.int32)
    own_episodes = lax.dynamic_slice_in_dim(episodes[0], lat_index * frames, frames, 0)
    episode_match = own_episodes[:, None] == episode_index[None, :]
    episode_rows = mm(episode_match.astype(BF), weights["episode"]).reshape(frames, 1, D)
    w_q = jnp.pad(weights["w_q"], ((0, 0), (0, LANES - CH)))
    w_o = jnp.pad(weights["w_o"], ((LANES - CH, 0), (0, 0)))
    latent = weights["latent"]

    score_flops = rows_total * cap * LANES * 2
    select_flops = frames * cap * total_keys * LANES * 2
    h1, kvf, cross_out, cross_lse = call(
        cross_fwd_kernel,
        frames,
        [
            fixed(LAT, D), framed(1, D), fixed(8, D), fixed(D, LANES), fixed(LANES, D), fixed(4, D),
            fixed(total_keys, LANES), framed(token_rows_count, LANES), framed(8, LANES),
        ],
        [
            (rowed(LAT, D), shaped((rows_total, D))),
            (framed(cap, LANES), shaped((frames, cap, LANES), BF)),
            (rowed(LAT, LANES), shaped((rows_total, LANES), BF)),
            (framed(1, LAT), shaped((frames, 1, LAT))),
        ],
        (latent, episode_rows, norms, w_q, w_o, out_bias, all_keys, rank, counts),
        flops=2 * score_flops + select_flops,
        trans=rows_total * cap,
    )

    block = min(512, rows_total)
    steps = rows_total // block
    mlp_flops = 4 * rows_total * D * FF
    h2, normed_one, act_one, slope_one, sa_in, qkv = call(
        mlp_one_fwd_kernel,
        steps,
        [rowed(block, D), fixed(8, D), fixed(2, FF), fixed(4, D), fixed(D, FF), fixed(FF, D), fixed(D, 3 * D)],
        [
            (rowed(block, D), shaped((rows_total, D))),
            (rowed(block, D), shaped((rows_total, D), BF)),
            (rowed(block, FF), shaped((rows_total, FF), BF)),
            (rowed(block, FF), shaped((rows_total, FF), BF)),
            (rowed(block, D), shaped((rows_total, D), BF)),
            (rowed(block, 3 * D), shaped((rows_total, 3 * D), BF)),
        ],
        (h1, norms, hid_bias, out_bias, weights["w_up"][0], weights["w_down"][0], weights["w_qkv"]),
        flops=mlp_flops + 6 * rows_total * D * D,
        trans=2 * rows_total * FF,
    )

    attn_flops = 4 * rows_total * LAT * D
    h3, mixed, self_lse = call(
        self_fwd_kernel,
        frames,
        [rowed(LAT, 3 * D), rowed(LAT, D), fixed(D, D), fixed(4, D)],
        [
            (rowed(LAT, D), shaped((rows_total, D))),
            (rowed(LAT, D), shaped((rows_total, D), BF)),
            (framed(HEADS, LAT), shaped((frames, HEADS, LAT))),
        ],
        (qkv, h2, weights["w_so"], out_bias),
        flops=4 * attn_flops,
        trans=rows_total * LAT * HEADS,
    )

    latents, g3, normed_two, act_two, dpre_two, dnorm_two, dhid_two, dout_two = call(
        mlp_two_kernel,
        steps,
        [rowed(block, D), rowed(block, D), fixed(8, D), fixed(2, FF), fixed(4, D), fixed(D, FF), fixed(FF, D)],
        [
            (rowed(block, D), shaped((rows_total, D), BF)),
            (rowed(block, D), shaped((rows_total, D))),
            (rowed(block, D), shaped((rows_total, D), BF)),
            (rowed(block, FF), shaped((rows_total, FF), BF)),
            (rowed(block, FF), shaped((rows_total, FF), BF)),
            (kept(2, D), shaped((2, D))),
            (kept(1, FF), shaped((1, FF))),
            (kept(1, D), shaped((1, D))),
        ],
        (h3, grad_rows_in, norms, hid_bias, out_bias, weights["w_up"][1], weights["w_down"][1]),
        flops=2 * mlp_flops,
        trans=2 * rows_total * FF,
        scratch=[pltpu.VMEM((block, FF), BF)],
    )
    latents_out = lax.all_to_all(
        latents.reshape(frames, LAT, D), "lat", split_axis=1, concat_axis=0, tiled=True
    )[None]
    two_down = t_mm(act_two, grad_rows_in)
    two_up = t_mm(normed_two, dpre_two)

    g2, low_three, dqkv, dnorm_sa, dout_so = call(
        self_bwd_kernel,
        frames,
        [
            rowed(LAT, 3 * D), framed(HEADS, LAT), rowed(LAT, D), rowed(LAT, D), fixed(8, D),
            fixed(D, D), fixed(D, 3 * D),
        ],
        [
            (rowed(LAT, D), shaped((rows_total, D))),
            (rowed(LAT, D), shaped((rows_total, D), BF)),
            (rowed(LAT, 3 * D), shaped((rows_total, 3 * D), BF)),
            (kept(2, D), shaped((2, D))),
            (kept(1, D), shaped((1, D))),
        ],
        (qkv, self_lse, g3, h2, norms, weights["w_so"], weights["w_qkv"]),
        flops=10 * attn_flops,
        trans=rows_total * LAT * HEADS,
    )
    grad_so = t_mm(mixed, low_three)
    grad_qkv = t_mm(sa_in, dqkv)

    g1, low_two, dpre_one, dnorm_one, dhid_one, dout_one = call(
        mlp_one_bwd_kernel,
        steps,
        [rowed(block, D), rowed(block, D), rowed(block, FF), fixed(8, D), fixed(D, FF), fixed(FF, D)],
        [
            (rowed(block, D), shaped((rows_total, D))),
            (rowed(block, D), shaped((rows_total, D), BF)),
            (rowed(block, FF), shaped((rows_total, FF), BF)),
            (kept(2, D), shaped((2, D))),
            (kept(1, FF), shaped((1, FF))),
            (kept(1, D), shaped((1, D))),
        ],
        (h1, g2, slope_one, norms, weights["w_up"][0], weights["w_down"][0]),
        flops=mlp_flops,
    )
    one_down = t_mm(act_one, low_two)
    one_up = t_mm(normed_one, dpre_one)

    grad_latent, frame_sums, dnorm_q, dw_q, dw_o, dout_cross, dkv_t = call(
        cross_bwd_kernel,
        frames,
        [
            fixed(LAT, D), framed(1, D), fixed(8, D), fixed(D, LANES), fixed(LANES, D),
            framed(cap, LANES), rowed(LAT, LANES), framed(1, LAT), framed(token_rows_count, LANES),
            framed(8, LANES), rowed(LAT, D),
        ],
        [
            (kept(LAT, D), shaped((LAT, D))),
            (framed(1, D), shaped((frames, 1, D))),
            (kept(2, D), shaped((2, D))),
            (kept(D, LANES), shaped((D, LANES))),
            (kept(LANES, D), shaped((LANES, D))),
            (kept(1, D), shaped((1, D))),
            (kept(LANES, total_keys), shaped((LANES, total_keys))),
        ],
        (latent, episode_rows, norms, w_q, w_o, kvf, cross_out, cross_lse, rank, counts, g1),
        flops=5 * score_flops + select_flops,
        trans=rows_total * cap,
    )
    grad_episode = jnp.sum(episode_match.astype(F32)[:, :, None] * frame_sums, axis=0)

    grad_kv = lax.psum_scatter(dkv_t.T.astype(BF), "lat", scatter_dimension=0, tiled=True)
    grad_w_kv = t_mm(tok_normed, grad_kv)
    grad_tok_normed = mm_t(grad_kv, weights["w_kv"])
    grad_tokens, grad_tok_gain, grad_tok_bias = token_pull(grad_tok_normed)
    token_grad = grad_tokens.astype(BF)[None]

    grads = {
        "latent": grad_latent,
        "episode": grad_episode,
        "tok_norm": jnp.stack([grad_tok_gain, grad_tok_bias]),
        "lat_norms": jnp.concatenate([dnorm_q, dnorm_one, dnorm_sa, dnorm_two]),
        "w_kv": grad_w_kv,
        "w_q": dw_q[:, :CH],
        "w_o": dw_o[LANES - CH :],
        "w_qkv": grad_qkv,
        "w_so": grad_so,
        "w_up": jnp.stack([one_up, two_up]),
        "w_down": jnp.stack([one_down, two_down]),
        "hid_bias": jnp.concatenate([dhid_one, dhid_two]),
        "out_bias": jnp.concatenate([dout_cross, dout_one, dout_so, dout_two]),
    }
    layout = param_layout()
    local_flat = jnp.concatenate([grads[name].astype(BF).reshape(-1) for name, unused in layout])
    starts, ends, offset, bias_offset = [], [], 0, 0
    for name, shape in layout:
        if name == "hid_bias":
            bias_offset = offset
        starts.append(offset // LANES)
        offset += math.prod(shape)
        ends.append(offset // LANES)
    pad = [0] * (16 - len(layout))
    starts = jnp.broadcast_to(jnp.array(starts + pad, jnp.int32)[:, None], (16, LANES))
    ends = jnp.broadcast_to(jnp.array(ends + pad, jnp.int32)[:, None], (16, LANES))
    shard_rows = shard_len // LANES
    opt_rows = 784 if shard_rows % 784 == 0 else shard_rows
    opt_steps = shard_rows // opt_rows
    base = (lat_index * shard_rows).astype(jnp.int32).reshape(1)
    smem = pl.BlockSpec(memory_space=pltpu.SMEM)
    flat_rows = (shard_rows, LANES)
    master_rows = master.reshape(flat_rows)
    bias_owner, bias_at = divmod(bias_offset, shard_len)
    reach = lat_count == 8 and lax.axis_size("kf") == 4
    if reach:
        summed, stats = reduce_all(local_flat, master_rows, starts, ends, bias_owner, bias_at // LANES)
    else:
        summed = lax.psum_scatter(local_flat, "lat", scatter_dimension=0, tiled=True)
        summed = lax.psum(summed, "kf").reshape(flat_rows)
        grad_sq, weight_sq = call(
            grad_stats_kernel,
            opt_steps,
            [smem, fixed(16, LANES), fixed(16, LANES), rowed(opt_rows, LANES), rowed(opt_rows, LANES)],
            [(kept(1, LANES), shaped((1, LANES))), (kept(16, LANES), shaped((16, LANES)))],
            (base, starts, ends, summed, master_rows),
        )
        bias_rows = summed[bias_at // LANES : bias_at // LANES + 2 * FF // LANES].astype(F32)
        bias_rows = jnp.where(lat_index == bias_owner, bias_rows, 0.0)
        stats = lax.psum(
            jnp.concatenate([grad_sq, jnp.zeros((7, LANES), F32), weight_sq, bias_rows]), "lat"
        )
    bias_grad = stats[24:STAT_ROWS].reshape(2, FF)
    grad_shard, lamb_update, new_one, new_two, update_sq = call(
        lamb_kernel,
        opt_steps,
        [smem, fixed(STAT_ROWS, LANES), fixed(16, LANES), fixed(16, LANES)] + [rowed(opt_rows, LANES)] * 4,
        [(rowed(opt_rows, LANES), shaped(flat_rows))] * 4 + [(kept(16, LANES), shaped((16, LANES)))],
        (
            base, stats, starts, ends, summed, master_rows,
            moment_one.reshape(flat_rows), moment_two.reshape(flat_rows),
        ),
    )
    if reach:
        vmem = pl.BlockSpec(memory_space=pltpu.VMEM)
        trust = pl.pallas_call(
            trust_kernel,
            out_shape=shaped((16, LANES)),
            in_specs=[vmem, vmem],
            out_specs=vmem,
            scratch_shapes=[
                pltpu.VMEM((8, 16, LANES), F32),
                pltpu.SemaphoreType.DMA((7,)),
                pltpu.SemaphoreType.DMA((7,)),
            ],
            compiler_params=pltpu.CompilerParams(collective_id=2, has_side_effects=True),
        )(update_sq, stats)[: len(layout), 0]
    else:
        update_sq = lax.psum(jnp.sum(update_sq, axis=1), "lat")
        weight_sq = jnp.sum(stats[8:24], axis=1)
        trust = (jnp.sqrt(weight_sq) / (jnp.sqrt(update_sq) + 1e-06))[: len(layout)]
    return (
        latents_out,
        token_grad,
        grad_shard.reshape(-1),
        lamb_update.reshape(-1),
        new_one.reshape(-1),
        new_two.reshape(-1),
        trust,
        bias_grad,
    )


def solution(mesh):
    return jax.shard_map(
        body,
        mesh=mesh,
        in_specs=(
            P("kf", "lat", None),
            P("kf", "lat"),
            P("kf", None),
            P("lat"),
            P("lat"),
            P("lat"),
            P("kf", None, "lat", None),
        ),
        out_specs=(
            P("kf", None, "lat", None),
            P("kf", "lat", None),
            P("lat"),
            P("lat"),
            P("lat"),
            P("lat"),
            P(),
            P(),
        ),
        check_vma=False,
    )
```

```python
import functools
import math

import jax
import jax.numpy as jnp
from jax import lax
from jax.experimental import pallas as pl
from jax.experimental.pallas import tpu as pltpu
from jax.sharding import PartitionSpec as P

DIN = 256
D = 512
LAT = 512
CH = 64
HEADS = 8
HEAD_DIM = 64
FF = 2048
EPISODES = 11
NPARAM = 5619712
LANES = 128

norm_eps = 1e-05
masked_fill = -1e30
beta_one = 0.9
beta_two = 0.999
adam_eps = 1e-06
decay_rate = 0.01
clip_fraction = 0.5
lamb_step = 10.0

BF = jnp.bfloat16
F32 = jnp.float32
MIB = 1024 * 1024


def param_layout():
    return [
        ("latent", (LAT, D)),
        ("episode", (EPISODES, D)),
        ("tok_norm", (2, DIN)),
        ("lat_norms", (8, D)),
        ("w_kv", (DIN, 2 * CH)),
        ("w_q", (D, CH)),
        ("w_o", (CH, D)),
        ("w_qkv", (D, 3 * D)),
        ("w_so", (D, D)),
        ("w_up", (2, D, FF)),
        ("w_down", (2, FF, D)),
        ("hid_bias", (2, FF)),
        ("out_bias", (4, D)),
    ]


def split_flat(flat_vector):
    pieces = {}
    offset = 0
    for tensor_name, tensor_shape in param_layout():
        entries = math.prod(tensor_shape)
        pieces[tensor_name] = flat_vector[offset : offset + entries].reshape(tensor_shape)
        offset += entries
    return pieces


def layer_norm(inputs, norm_gain, norm_bias):
    row_mean = jnp.mean(inputs, axis=-1, keepdims=True)
    centered = inputs - row_mean
    row_var = jnp.mean(centered * centered, axis=-1, keepdims=True)
    return centered * lax.rsqrt(row_var + norm_eps) * norm_gain + norm_bias


def mm(left, right):
    return jnp.dot(left, right, preferred_element_type=F32)


def mm_t(left, right):
    return lax.dot_general(left, right, (((1,), (1,)), ((), ())), preferred_element_type=F32)


def t_mm(left, right):
    return lax.dot_general(left, right, (((0,), (0,)), ((), ())), preferred_element_type=F32)


def norm_stats(rows):
    mean = jnp.mean(rows, axis=-1, keepdims=True)
    centered = rows - mean
    var = jnp.mean(centered * centered, axis=-1, keepdims=True)
    rstd = lax.rsqrt(var + norm_eps)
    return centered * rstd, rstd


def norm_back(grad, xhat, rstd, gain):
    dxh = grad * gain
    first = jnp.mean(dxh, axis=-1, keepdims=True)
    second = jnp.mean(dxh * xhat, axis=-1, keepdims=True)
    return rstd * (dxh - first - xhat * second)


def col_sum(values):
    return jnp.sum(values, axis=0, keepdims=True)


def gelu_pair(x):
    size = jnp.abs(x)
    t = pl.reciprocal(1.0 + (0.3275911 / math.sqrt(2.0)) * size, approx=True)
    e = jnp.exp(x * x * -0.5)
    poly = 0.5 * 1.061405429
    for coef in (-1.453152027, 1.421413741, -0.284496736, 0.254829592):
        poly = poly * t + 0.5 * coef
    tail = poly * t * e
    cdf = jnp.where(x >= 0.0, 1.0 - tail, tail)
    return x * cdf, cdf + x * (e * (1.0 / math.sqrt(2.0 * math.pi)))


def accumulate(first, ref, value):
    @pl.when(first)
    def _():
        ref[...] = value

    @pl.when(jnp.logical_not(first))
    def _():
        ref[...] += value


def lane_half(shape, half):
    lane = lax.broadcasted_iota(jnp.int32, shape, 1)
    return (lane >= half * 64) & (lane < half * 64 + 64)


def keep_half(values, half):
    return jnp.where(lane_half(values.shape, half), values, jnp.zeros_like(values))


def select_tokens(rank_rows, cap):
    slot = lax.broadcasted_iota(jnp.int32, (cap, LANES), 0)
    parts = []
    for r in range(rank_rows.shape[0]):
        hit = slot == rank_rows[r : r + 1, :]
        parts.append(jnp.where(hit, 1.0, 0.0).astype(BF))
    return jnp.concatenate(parts, axis=1)


def cross_scores(kvf, queries_scaled, count):
    scores = mm_t(kvf, queries_scaled)
    slot = lax.broadcasted_iota(jnp.int32, scores.shape, 0)
    return jnp.where(slot < count, scores, masked_fill)


def cross_attend(start, norms, w_q, kvf, count):
    xhat, unused = norm_stats(start)
    query_in = (xhat * norms[0:1, :] + norms[1:2, :]).astype(BF)
    queries = mm(query_in, w_q[...]).astype(BF) * jnp.asarray(0.125, BF)
    scores = cross_scores(kvf, queries, count)
    top = jnp.max(scores, axis=0, keepdims=True)
    terms = jnp.exp(scores - top)
    total = jnp.sum(terms, axis=0, keepdims=True)
    prob = (terms * (1.0 / total)).astype(BF)
    return t_mm(kvf, prob).T.astype(BF), top + jnp.log(total)


def cross_fwd_kernel(latent, episode, norms, w_q, w_o, out_bias, kv, rank, count, h1, kvf_out, co_out, lse_out):
    cap = kvf_out.shape[1]
    start = latent[...].astype(F32) + episode[0]
    chunk = 8 * LANES
    chunks = kv.shape[0] // chunk

    def step(j, acc):
        sel = select_tokens(rank[0, pl.ds(pl.multiple_of(j * 8, 8), 8), :], cap)
        return acc + mm(sel, kv[pl.ds(pl.multiple_of(j * chunk, chunk), chunk), :])

    kvf = lax.fori_loop(0, chunks, step, jnp.zeros((cap, LANES), F32)).astype(BF)
    co, lse = cross_attend(start, norms, w_q, kvf, count[0, 0:1, 0:1])
    h1[...] = start + mm(co, w_o[...]) + out_bias[0:1, :]
    kvf_out[0] = kvf
    co_out[...] = co
    lse_out[0] = lse


def cross_bwd_kernel(
    latent, episode, norms, w_q, w_o, kvf_in, co_in, lse, rank, count, g1,
    dlatent, frame_sum, dnorm, dw_q, dw_o, dbias, dkv_t,
):
    first = pl.program_id(0) == 0
    cap = kvf_in.shape[1]
    start = latent[...].astype(F32) + episode[0]
    xhat, rstd = norm_stats(start)
    query_in = (xhat * norms[0:1, :] + norms[1:2, :]).astype(BF)
    queries = mm(query_in, w_q[...]).astype(BF) * jnp.asarray(0.125, BF)
    kvf = kvf_in[0]
    grad_one = g1[...]
    branch = grad_one.astype(BF)
    grad_co = mm_t(branch, w_o[...]).astype(BF)
    accumulate(first, dw_o, t_mm(co_in[...], branch))
    accumulate(first, dbias, col_sum(branch.astype(F32)))
    scores = cross_scores(kvf, queries, count[0, 0:1, 0:1])
    prob = jnp.exp(scores - lse[0])
    prob_low = prob.astype(BF)
    weighted = prob * mm_t(kvf, grad_co)
    grad_score = (weighted - prob * col_sum(weighted)).astype(BF)
    grad_kv = (mm(grad_score, queries) + mm(prob_low, grad_co)).astype(BF)
    grad_query = (t_mm(kvf, grad_score).T * 0.125).astype(BF)
    accumulate(first, dw_q, t_mm(query_in, grad_query))
    grad_in = mm_t(grad_query, w_q[...])
    grad_start = grad_one + norm_back(grad_in, xhat, rstd, norms[0:1, :])
    accumulate(first, dnorm, jnp.concatenate([col_sum(grad_in * xhat), col_sum(grad_in)], axis=0))
    accumulate(first, dlatent, grad_start)
    frame_sum[0] = col_sum(grad_start)
    grad_kv_t = grad_kv.T
    chunk = 8 * LANES

    @pl.when(first)
    def _():
        dkv_t[...] = jnp.zeros_like(dkv_t)

    def step(j, carry):
        sel = select_tokens(rank[0, pl.ds(pl.multiple_of(j * 8, 8), 8), :], cap)
        dkv_t[:, pl.ds(pl.multiple_of(j * chunk, chunk), chunk)] += mm(grad_kv_t, sel)
        return carry

    lax.fori_loop(0, dkv_t.shape[1] // chunk, step, 0)


FCHUNK = 512


def mlp_one_fwd_kernel(
    h1, norms, hid_bias, out_bias, w_up, w_down, w_qkv, h2, normed_out, act_out, slope_out, sa_out, qkv_out
):
    rows = h1[...]
    xhat, unused = norm_stats(rows)
    normed = (xhat * norms[2:3, :] + norms[3:4, :]).astype(BF)
    normed_out[...] = normed
    total = rows + out_bias[1:2, :]
    for c in range(FF // FCHUNK):
        at = slice(c * FCHUNK, (c + 1) * FCHUNK)
        act, slope = gelu_pair(mm(normed, w_up[:, at]) + hid_bias[0:1, at])
        act = act.astype(BF)
        act_out[:, at] = act
        slope_out[:, at] = slope.astype(BF)
        total = total + mm(act, w_down[at, :])
    h2[...] = total
    xhat, unused = norm_stats(total)
    sa_in = (xhat * norms[4:5, :] + norms[5:6, :]).astype(BF)
    sa_out[...] = sa_in
    for c in range(3):
        at = slice(c * D, (c + 1) * D)
        qkv_out[:, at] = mm(sa_in, w_qkv[:, at]).astype(BF)


def mlp_two_kernel(
    h3, grad, norms, hid_bias, out_bias, w_up, w_down,
    latents, g3, normed_out, act_out, dpre_out, dnorm, dhid, dout, slope_keep,
):
    first = pl.program_id(0) == 0
    rows = h3[...]
    xhat, rstd = norm_stats(rows)
    normed = (xhat * norms[6:7, :] + norms[7:8, :]).astype(BF)
    normed_out[...] = normed
    total = rows + out_bias[3:4, :]
    for c in range(FF // FCHUNK):
        at = slice(c * FCHUNK, (c + 1) * FCHUNK)
        act, slope = gelu_pair(mm(normed, w_up[:, at]) + hid_bias[1:2, at])
        act = act.astype(BF)
        act_out[:, at] = act
        slope_keep[:, at] = slope.astype(BF)
        total = total + mm(act, w_down[at, :])
    latents[...] = total.astype(BF)
    grad_low = grad[...]
    mlp_back(first, grad_low, grad_low.astype(F32), slope_keep, xhat, rstd, norms[6:7, :], w_up, w_down, g3, dpre_out, dnorm, dhid, dout)


def mlp_back(first, grad_low, grad_rows, slope, xhat, rstd, gain, w_up, w_down, grad_out, dpre_out, dnorm, dhid, dout):
    grad_normed = jnp.zeros(grad_rows.shape, F32)
    for c in range(FF // FCHUNK):
        at = slice(c * FCHUNK, (c + 1) * FCHUNK)
        dpre = (mm_t(grad_low, w_down[at, :]) * slope[:, at].astype(F32)).astype(BF)
        dpre_out[:, at] = dpre
        part = col_sum(dpre.astype(F32))

        @pl.when(first)
        def _(at=at, part=part):
            dhid[:, at] = part

        @pl.when(jnp.logical_not(first))
        def _(at=at, part=part):
            dhid[:, at] += part

        grad_normed = grad_normed + mm_t(dpre, w_up[:, at])
    accumulate(first, dnorm, jnp.concatenate([col_sum(grad_normed * xhat), col_sum(grad_normed)], axis=0))
    accumulate(first, dout, col_sum(grad_low.astype(F32)))
    grad_out[...] = grad_rows + norm_back(grad_normed, xhat, rstd, gain)


def mlp_one_bwd_kernel(h1, g2, slope, norms, w_up, w_down, g1, low_out, dpre_out, dnorm, dhid, dout):
    first = pl.program_id(0) == 0
    xhat, rstd = norm_stats(h1[...])
    grad_rows = g2[...]
    grad_low = grad_rows.astype(BF)
    low_out[...] = grad_low
    mlp_back(first, grad_low, grad_rows, slope, xhat, rstd, norms[2:3, :], w_up, w_down, g1, dpre_out, dnorm, dhid, dout)


def self_fwd_kernel(qkv, h2, w_so, out_bias, h3, mixed_out, lse_out):
    scale = jnp.asarray(0.125, BF)
    mixed_rows = []
    for pair in range(HEADS // 2):
        base = pair * LANES
        query_pair = qkv[:, base : base + LANES] * scale
        key_pair = qkv[:, D + base : D + base + LANES]
        value_t = qkv[:, 2 * D + base : 2 * D + base + LANES].T
        for half in range(2):
            scores = mm_t(key_pair, keep_half(query_pair, half))
            top = jnp.max(scores, axis=0, keepdims=True)
            terms = jnp.exp(scores - top)
            total = jnp.sum(terms, axis=0, keepdims=True)
            prob = (terms * (1.0 / total)).astype(BF)
            head = 2 * pair + half
            lse_out[0, head : head + 1, :] = top + jnp.log(total)
            mixed_rows.append(mm(value_t[half * 64 : half * 64 + 64, :], prob))
    mixed = jnp.concatenate(mixed_rows, axis=0).T.astype(BF)
    mixed_out[...] = mixed
    h3[...] = h2[...] + mm(mixed, w_so[...]) + out_bias[2:3, :]


def self_bwd_kernel(qkv, lse, g3, h2, norms, w_so, w_qkv, g2, low_out, dqkv_out, dnorm, dout):
    first = pl.program_id(0) == 0
    scale = jnp.asarray(0.125, BF)
    grad_rows = g3[...]
    grad_low = grad_rows.astype(BF)
    low_out[...] = grad_low
    accumulate(first, dout, col_sum(grad_low.astype(F32)))
    grad_mixed = mm_t(grad_low, w_so[...]).astype(BF)
    for pair in range(HEADS // 2):
        base = pair * LANES
        query_pair = qkv[:, base : base + LANES] * scale
        key_pair = qkv[:, D + base : D + base + LANES]
        value_pair = qkv[:, 2 * D + base : 2 * D + base + LANES]
        grad_pair = grad_mixed[:, base : base + LANES]
        key_t = key_pair.T
        query_t = []
        grad_key = jnp.zeros((LAT, LANES), F32)
        grad_value = jnp.zeros((LAT, LANES), F32)
        for half in range(2):
            head = 2 * pair + half
            query = keep_half(query_pair, half)
            grad_head = keep_half(grad_pair, half)
            prob = jnp.exp(mm_t(key_pair, query) - lse[0, head : head + 1, :])
            grad_value = grad_value + mm(prob.astype(BF), grad_head)
            weighted = prob * mm_t(value_pair, grad_head)
            grad_score = (weighted - prob * col_sum(weighted)).astype(BF)
            grad_key = grad_key + mm(grad_score, query)
            query_t.append(mm(key_t[half * 64 : half * 64 + 64, :], grad_score))
        dqkv_out[:, base : base + LANES] = (jnp.concatenate(query_t, axis=0).T * 0.125).astype(BF)
        dqkv_out[:, D + base : D + base + LANES] = grad_key.astype(BF)
        dqkv_out[:, 2 * D + base : 2 * D + base + LANES] = grad_value.astype(BF)
    grad_in = mm_t(dqkv_out[...], w_qkv[...])
    xhat, rstd = norm_stats(h2[...])
    accumulate(first, dnorm, jnp.concatenate([col_sum(grad_in * xhat), col_sum(grad_in)], axis=0))
    g2[...] = grad_rows + norm_back(grad_in, xhat, rstd, norms[4:5, :])


def segment_hot(starts, ends, base, rows):
    row = lax.broadcasted_iota(jnp.int32, (16, rows), 1) + base
    return jnp.where((row >= starts[:, 0:1]) & (row < ends[:, 0:1]), 1.0, 0.0).astype(BF)


def segment_sums(hot, squares):
    high = squares.astype(BF)
    low = (squares - high.astype(F32)).astype(BF)
    return mm(hot, high) + mm(hot, low)


def grad_stats_kernel(base, starts, ends, summed, master, grad_sq, weight_sq):
    i = pl.program_id(0)
    rows = master.shape[0]
    hot = segment_hot(starts, ends, base[0] + i * rows, rows)
    grad = summed[...].astype(F32)
    accumulate(i == 0, grad_sq, col_sum(grad * grad))
    accumulate(i == 0, weight_sq, segment_sums(hot, master[...] * master[...]))


def lamb_kernel(base, stats, starts, ends, summed, master, one, two, grad_out, update_out, one_out, two_out, update_sq):
    i = pl.program_id(0)
    rows = master.shape[0]
    hot = segment_hot(starts, ends, base[0] + i * rows, rows)
    total_sq = jnp.sum(stats[0:1, :], axis=1, keepdims=True)
    clip = jnp.minimum(1.0, clip_fraction * math.sqrt(NPARAM) / (jnp.sqrt(total_sq) + 1e-06))
    grad = summed[...].astype(F32)
    grad_out[...] = grad
    clipped = clip * grad
    new_one = beta_one * one[...] + (1.0 - beta_one) * clipped
    new_two = beta_two * two[...] + (1.0 - beta_two) * clipped * clipped
    one_out[...] = new_one
    two_out[...] = new_two
    first_hat = new_one * (1.0 / (1.0 - beta_one**lamb_step))
    second_hat = new_two * (1.0 / (1.0 - beta_two**lamb_step))
    update = first_hat / (jnp.sqrt(second_hat) + adam_eps) + decay_rate * master[...]
    update_out[...] = update
    accumulate(i == 0, update_sq, segment_sums(hot, update * update))


BATCH = 256
HALF = 128
QUARTER = 64
MESH = pl.DeviceIdType.MESH


class Place:
    def __init__(self):
        self.z = lax.axis_index("kf")
        self.me = lax.axis_index("lat")
        self.core = lax.rem(self.me, 2)
        self.x = lax.rem(self.me // 2, 2)
        self.y = self.me // 4
        self.z_low = lax.rem(self.z, 2)
        self.z_high = self.z // 2
        self.sibling = (self.z, self.me + 1 - 2 * self.core)
        self.x_side = (self.z, self.me + 2 - 4 * self.x)
        self.y_side = (self.z, self.me + 4 - 8 * self.y)
        self.z_near = (self.z + 1 - 2 * self.z_low, self.me)
        self.z_far = (self.z + 2 - 4 * self.z_high, self.me)

    def z_other(self, step):
        return (lax.rem(self.z + step, 4), self.me)

    def lat_other(self, step):
        return (self.z, lax.rem(self.me + step, 8))


def remote(src, dst, send, recv, device):
    return pltpu.make_async_remote_copy(
        src_ref=src, dst_ref=dst, send_sem=send, recv_sem=recv, device_id=device, device_id_type=MESH
    )


def greet(devices):
    barrier = pltpu.get_barrier_semaphore()
    for device in devices:
        pl.semaphore_signal(barrier, inc=1, device_id=device, device_id_type=MESH)
    pl.semaphore_wait(barrier, len(devices))


def added(left, right):
    return (left.astype(F32) + right.astype(F32)).astype(BF)


class Reduction:
    lags = (0, 1, 3, 5, 7, 9, 11)

    def __init__(self, place, grads, out, bufs, sems):
        self.p = place
        self.grads = grads
        self.out = out
        self.own, self.rc, self.r1, self.r2, self.r3, self.r4, self.res = bufs
        self.own_sem, self.send, self.rc_sem, self.r1_sem, self.r2_sem, self.r3_sem, self.r4_sem, self.res_sem = sems
        self.shard = grads.shape[3]
        self.batches = pl.cdiv(self.shard, BATCH)
        self.back = self.batches * BATCH - self.shard

    @staticmethod
    def scratch(shard):
        n = pl.cdiv(shard, BATCH)
        bufs = [
            pltpu.VMEM((2, 2, 2, BATCH, LANES), BF),
            pltpu.VMEM((n, 2, 2, BATCH, LANES), BF),
            pltpu.VMEM((n, 2, 2, HALF, LANES), BF),
            pltpu.VMEM((n, 2, HALF, LANES), BF),
            pltpu.VMEM((n, HALF, LANES), BF),
            pltpu.VMEM((n, QUARTER, LANES), BF),
            pltpu.VMEM((n, BATCH, LANES), BF),
        ]
        dma = pltpu.SemaphoreType.DMA
        sems = [dma((2,)), dma((10, 4)), dma((n,)), dma((n, 2)), dma((n, 2)), dma((n,)), dma((n,)), dma((n, 3))]
        return bufs + sems

    def row(self, i):
        return pl.multiple_of(i * BATCH - (i // (self.batches - 1)) * self.back, 16)

    def own_copy(self, i):
        slot = lax.rem(i, 2)
        src = self.grads.at[:, :, self.p.core, pl.ds(self.row(i), BATCH), :]
        return pltpu.make_async_copy(src, self.own.at[slot], self.own_sem.at[slot])

    def copies(self, stage, i):
        p, slot = self.p, lax.rem(i, 4)
        if stage == 0:
            src = self.grads.at[:, :, 1 - p.core, pl.ds(self.row(i), BATCH), :]
            return [remote(src, self.rc.at[i], self.send.at[0, slot], self.rc_sem.at[i], p.sibling)]
        if stage == 1:
            to_x = self.rc.at[i, :, 1 - p.x, pl.ds(0, HALF), :]
            to_y = self.rc.at[i, 1 - p.y, :, pl.ds(HALF, HALF), :]
            return [
                remote(to_x, self.r1.at[i, 0], self.send.at[1, slot], self.r1_sem.at[i, 0], p.x_side),
                remote(to_y, self.r1.at[i, 1], self.send.at[2, slot], self.r1_sem.at[i, 1], p.y_side),
            ]
        if stage == 2:
            to_y = self.r1.at[i, 0, 1 - p.y]
            to_x = self.r1.at[i, 1, 1 - p.x]
            return [
                remote(to_y, self.r2.at[i, 0], self.send.at[3, slot], self.r2_sem.at[i, 0], p.y_side),
                remote(to_x, self.r2.at[i, 1], self.send.at[4, slot], self.r2_sem.at[i, 1], p.x_side),
            ]
        if stage == 3:
            src = self.r2.at[i, 1 - p.z_low]
            return [remote(src, self.r3.at[i], self.send.at[5, slot], self.r3_sem.at[i], p.z_near)]
        if stage == 4:
            src = self.r3.at[i, pl.ds(pl.multiple_of((1 - p.z_high) * QUARTER, QUARTER), QUARTER), :]
            return [remote(src, self.r4.at[i], self.send.at[6, slot], self.r4_sem.at[i], p.z_far)]
        mine = self.res.at[i, pl.ds(pl.multiple_of(p.z_low * HALF + p.z_high * QUARTER, QUARTER), QUARTER), :]
        return [
            remote(mine, mine, self.send.at[6 + d, slot], self.res_sem.at[i, d - 1], p.z_other(d))
            for d in (1, 2, 3)
        ]

    def launch(self, stage, i):
        @pl.when(i >= 4)
        def _():
            for copy in self.copies(stage, i - 4):
                copy.wait_send()

        for copy in self.copies(stage, i):
            copy.start()

    def landed(self, stage, i):
        for copy in self.copies(stage, i):
            copy.wait_recv()

    def work(self, stage, i):
        p = self.p
        if stage == 0:
            self.own_copy(i).start()
        elif stage == 1:
            self.landed(0, i)
            self.own_copy(i).wait()
            self.rc[i] = added(self.rc[i], self.own[lax.rem(i, 2)])
        elif stage == 2:
            self.landed(1, i)
            self.r1[i, 0] = added(self.r1[i, 0], self.rc[i, :, p.x, 0:HALF, :])
            self.r1[i, 1] = added(self.r1[i, 1], self.rc[i, p.y, :, HALF:BATCH, :])
        elif stage == 3:
            self.landed(2, i)
            self.r2[i, 0] = added(self.r2[i, 0], self.r1[i, 0, p.y])
            self.r2[i, 1] = added(self.r2[i, 1], self.r1[i, 1, p.x])
        elif stage == 4:
            self.landed(3, i)
            self.r3[i] = added(self.r3[i], self.r2[i, p.z_low])
        elif stage == 5:
            self.landed(4, i)
            part = self.r3[i, pl.ds(pl.multiple_of(p.z_high * QUARTER, QUARTER), QUARTER), :]
            at = pl.multiple_of(p.z_low * HALF + p.z_high * QUARTER, QUARTER)
            self.res[i, pl.ds(at, QUARTER), :] = added(self.r4[i], part)
        else:
            self.landed(5, i)
            self.out[pl.ds(self.row(i), BATCH), :] = self.res[i]
        if stage < 6:
            self.launch(stage, i)

    def tick(self, t):
        for stage, lag in enumerate(self.lags):
            i = t - lag

            @pl.when((i >= 0) & (i < self.batches))
            def _(stage=stage, i=i):
                self.work(stage, i)

    def ticks(self):
        return self.batches + self.lags[-1]

    def finish(self):
        for stage in range(6):
            for back in range(4):
                for copy in self.copies(stage, self.batches - 4 + back):
                    copy.wait_send()

    def partners(self):
        p = self.p
        return [p.sibling, p.x_side, p.y_side] + [p.z_other(d) for d in (1, 2, 3)]


def share_all(place, block, send, recv):
    mine = block.at[place.me]
    copies = [
        remote(mine, mine, send.at[d - 1], recv.at[d - 1], place.lat_other(d)) for d in range(1, 8)
    ]
    for copy in copies:
        copy.start()
    for copy in copies:
        copy.wait()


STAT_ROWS = 56


def reduce_kernel(bias_owner, bias_at, starts, ends, grads, master, summed, stats, *scratch):
    place = Place()
    block, block_send, block_recv = scratch[:3]
    red = Reduction(place, grads, summed, scratch[3:10], scratch[10:])
    greet([place.lat_other(d) for d in range(1, 8)] + [place.z_other(d) for d in (1, 2, 3)])
    lax.fori_loop(0, red.ticks(), lambda t, c: (red.tick(t), c)[1], 0)
    shard = master.shape[0]
    step = 784
    grad_sq = jnp.zeros((1, LANES), F32)
    weight_sq = jnp.zeros((16, LANES), F32)
    for j in range(shard // step):
        at = slice(j * step, (j + 1) * step)
        part = summed[at, :].astype(F32)
        grad_sq = grad_sq + col_sum(part * part)
        hot = segment_hot(starts, ends, place.me * shard + j * step, step)
        part = master[at, :]
        weight_sq = weight_sq + segment_sums(hot, part * part)
    bias = summed[bias_at : bias_at + 2 * FF // LANES, :].astype(F32)
    bias = jnp.where(place.me == bias_owner, bias, 0.0)
    head = jnp.concatenate([grad_sq, jnp.zeros((7, LANES), F32), weight_sq, bias], axis=0)
    block[pl.ds(place.me, 1)] = head[None]
    share_all(place, block, block_send, block_recv)
    total = block[0]
    for s in range(1, 8):
        total = total + block[s]
    stats[...] = total
    red.finish()


def trust_kernel(update_sq, stats, trust, block, send, recv):
    place = Place()
    greet([place.lat_other(d) for d in range(1, 8)])
    block[pl.ds(place.me, 1)] = update_sq[...][None]
    share_all(place, block, send, recv)
    total = block[0]
    for s in range(1, 8):
        total = total + block[s]
    update_norm = jnp.sqrt(jnp.sum(total, axis=1, keepdims=True))
    weight_norm = jnp.sqrt(jnp.sum(stats[8:24, :], axis=1, keepdims=True))
    trust[...] = jnp.broadcast_to(weight_norm / (update_norm + 1e-06), (16, LANES))


def relayout(whole, row, stage, dst, rows, cols):
    wide = cols // LANES
    block = min(rows, 2048 // wide // 128 * 128)

    def step(i, carry):
        at = pl.multiple_of(row + i * (block * wide), 16)
        stage[0 : block * wide, :] = whole[pl.ds(at, block * wide), :].astype(F32)
        for j in range(wide):
            part = stage[pl.ds(j, block, stride=wide), :]
            dst[pl.ds(pl.multiple_of(i * block, 16), block), j * LANES : (j + 1) * LANES] = part.astype(BF)
        return carry

    lax.fori_loop(0, rows // block, step, 0)


def small_matrix(whole, row, stage, rows, cols):
    wide = cols // LANES
    stage[0 : rows * wide, :] = whole[row : row + rows * wide, :].astype(F32)
    return jnp.concatenate([stage[pl.ds(j, rows, stride=wide), :] for j in range(wide)], axis=1)


class Gather:
    def __init__(self, place, whole, shard, chunks, send, recv):
        self.p, self.whole, self.shard, self.chunks, self.send, self.recv = place, whole, shard, chunks, send, recv
        p = place
        x_index, y_index = p.x_side[1], p.y_side[1]
        low = p.z_low
        self.first = x_index + low * (y_index - x_index)
        self.second = y_index + low * (x_index - y_index)
        self.diagonal = x_index + 4 - 8 * p.y

    def copy(self, kind, k):
        p = self.p
        block = (p.me, p.me, self.first, self.first, self.first, self.diagonal, self.second)[kind]
        target = (
            (p.z, self.first), p.sibling, (p.z, self.second), p.z_near, p.sibling, p.sibling, p.sibling
        )[kind]
        row, count = self.chunks[k]
        ref = self.whole.at[pl.ds(pl.multiple_of(block * self.shard + row, 16), count), :]
        return remote(ref, ref, self.send.at[kind, k], self.recv.at[kind, k], target)

    def tick(self, t):
        n = len(self.chunks)
        if t < n:
            self.copy(0, t).start()
            self.copy(1, t).start()
        if 0 <= t - 2 < n:
            self.copy(0, t - 2).wait_recv()
            for kind in (2, 3, 4):
                self.copy(kind, t - 2).start()
        if 0 <= t - 4 < n:
            self.copy(2, t - 4).wait_recv()
            self.copy(5, t - 4).start()
            self.copy(3, t - 4).wait_recv()
            self.copy(6, t - 4).start()
        if 0 <= t - 5 < n:
            for kind in (1, 4, 5, 6):
                self.copy(kind, t - 5).wait_recv()

    def ticks(self):
        return len(self.chunks) + 5

    def finish(self):
        for k in range(len(self.chunks)):
            for kind in range(7):
                self.copy(kind, k).wait_send()


class KeyExchange:
    def __init__(self, place, keys, send, recv):
        self.p, self.keys, self.send, self.recv = place, keys, send, recv
        self.x_index, self.y_index = place.x_side[1], place.y_side[1]
        self.diagonal = self.x_index + 4 - 8 * place.y

    def copy(self, kind):
        p = self.p
        half = self.keys.shape[1] // 2
        low, high, full = pl.ds(0, half), pl.ds(half, half), pl.ds(0, 2 * half)
        block, rows, target = (
            (p.me, full, p.x_side), (p.me, full, p.y_side), (p.me, full, p.sibling),
            (self.x_index, low, p.y_side), (self.y_index, high, p.x_side),
            (self.x_index, full, p.sibling), (self.y_index, full, p.sibling), (self.diagonal, full, p.sibling),
        )[kind]
        ref = self.keys.at[block, rows, :]
        return remote(ref, ref, self.send.at[kind], self.recv.at[kind], target)

    def step(self, s):
        if s == 0:
            waits, starts = (), (0, 1, 2)
        elif s == 1:
            waits, starts = (0, 1), (3, 4, 5, 6)
        elif s == 2:
            waits, starts = (3, 4), (7,)
        else:
            waits, starts = (2, 5, 6, 7), ()
        for kind in waits:
            self.copy(kind).wait_recv()
        for kind in starts:
            self.copy(kind).start()

    def finish(self):
        for kind in range(8):
            self.copy(kind).wait_send()


def flat_rows_of():
    rows, at = {}, 0
    for name, shape in param_layout():
        rows[name] = at // LANES
        at += math.prod(shape)
    return rows


def gather_chunks(shard):
    at = flat_rows_of()
    tail = at["hid_bias"] % shard // 16 * 16
    chunks = [(at["episode"], at["w_o"] - at["episode"]), (tail, shard - tail), (at["w_o"], at["w_qkv"] - at["w_o"])]
    for low, high in ((0, at["episode"]), (at["w_qkv"], tail)):
        while low < high:
            count = min(512, high - low)
            chunks.append((low, count))
            low += count
    return chunks


def begin_kernel(
    chunks, master, tokens, ids, hot,
    up_one, down_one, qkv_w, so_w, up_two, down_two,
    latent, norms, hid_bias, out_bias, w_q, w_o, w_kv, tok_norm, tok_normed, episode, rank, counts,
    kvf_out, co_out, lse_out, h1,
    whole, stage, all_ids, keys, m_up_one, m_down_one, m_qkv, m_so, m_up_two, m_down_two,
    send, recv, key_send, key_recv, id_send, id_recv, out_sem,
):
    place = Place()
    shard = master.shape[0]
    frames, cap = kvf_out.shape[0], kvf_out.shape[1]
    gather = Gather(place, whole, shard, chunks, send, recv)
    exchange = KeyExchange(place, keys, key_send, key_recv)
    at = flat_rows_of()
    greet([place.lat_other(d) for d in range(1, 8)] + [place.z_near])
    all_ids[pl.ds(place.me, 1)] = ids[...][None]
    id_copies = [
        remote(all_ids.at[place.me], all_ids.at[place.me], id_send.at[d - 1], id_recv.at[d - 1], place.lat_other(d))
        for d in range(1, 8)
    ]
    for copy in id_copies:
        copy.start()
    own_at = place.me * shard
    for row, count in chunks:
        whole[pl.ds(pl.multiple_of(own_at + row, 16), count), :] = master[row : row + count, :].astype(BF)
    for t in range(4):
        gather.tick(t)

    for copy in id_copies:
        copy.wait_recv()
    tags = jnp.concatenate([all_ids[s] for s in range(8)], axis=0)
    low = lax.broadcasted_iota(jnp.int32, (LANES, LANES), 0)
    high = lax.broadcasted_iota(jnp.int32, (LANES, LANES), 1)
    upto = jnp.where(low <= high, 1.0, 0.0).astype(BF)
    n = tags.shape[0]
    below = jnp.where(
        lax.broadcasted_iota(jnp.int32, (n, n), 1) < lax.broadcasted_iota(jnp.int32, (n, n), 0), 1.0, 0.0
    ).astype(BF)
    for f in range(frames):
        hit = tags == place.me * frames + f
        hit_low = jnp.where(hit, 1.0, 0.0).astype(BF)
        inside = mm(hit_low, upto)
        row_total = jnp.broadcast_to(inside[:, LANES - 1 : LANES], (n, LANES))
        before = mm(below, row_total.astype(BF))
        place_in = (inside + before).astype(jnp.int32) - 1
        rank[f] = jnp.where(hit, place_in, -1)
        total = jnp.sum(row_total[:, 0:1], axis=0, keepdims=True).astype(jnp.int32)
        counts[f] = jnp.broadcast_to(total, (8, LANES))
    for t in range(4, 7):
        gather.tick(t)

    pair = whole[at["tok_norm"] // 16 * 16 : at["lat_norms"], :].astype(F32)
    pair = pair[at["tok_norm"] % 16 : at["tok_norm"] % 16 + 4, :]
    tok_norm[...] = jnp.concatenate(
        [
            jnp.concatenate([pair[0:1], pair[1:2]], axis=1),
            jnp.concatenate([pair[2:3], pair[3:4]], axis=1),
        ],
        axis=0,
    )
    w_kv[...] = whole[at["w_kv"] : at["w_kv"] + DIN, :]
    xhat, unused = norm_stats(tokens[...].astype(F32))
    normed = (xhat * tok_norm[0:1, :] + tok_norm[1:2, :]).astype(BF)
    tok_normed[...] = normed
    keys[pl.ds(place.me, 1)] = mm(normed, w_kv[...]).astype(BF)[None]
    exchange.step(0)
    norms[...] = small_matrix(whole, at["lat_norms"], stage, 8, D)
    hid_bias[...] = small_matrix(whole, at["hid_bias"], stage, 2, FF)
    out_bias[...] = small_matrix(whole, at["out_bias"], stage, 4, D)
    episode_rows = mm(hot[...], small_matrix(whole, at["episode"], stage, 16, D).astype(BF))
    gather.tick(7)
    exchange.step(1)
    packed = whole[at["w_q"] : at["w_q"] + D // 2, :].astype(F32)
    stage[pl.ds(0, D // 2, stride=2), :] = packed
    stage[pl.ds(1, D // 2, stride=2), :] = pltpu.roll(packed, CH, 1)
    w_q[...] = keep_half(stage[0:D, :], 0).astype(BF)
    w_o[0:CH, :] = jnp.zeros((CH, D), BF)
    w_o[CH : 2 * CH, :] = small_matrix(whole, at["w_o"], stage, CH, D).astype(BF)
    gather.tick(8)
    exchange.step(2)
    for t in range(9, 12):
        gather.tick(t)
    exchange.step(3)
    relayout(whole, 0, stage, latent, LAT, D)

    tick = 12
    chunk = 8 * LANES
    for f in range(frames):
        start = latent[...].astype(F32) + episode_rows[f : f + 1, :]
        episode[f] = episode_rows[f : f + 1, :]
        kvf = jnp.zeros((cap, LANES), F32)
        for j in range(n // 8):
            sel = select_tokens(rank[f, 8 * j : 8 * j + 8, :], cap)
            rows = keys[2 * j : 2 * j + 2].reshape(chunk, LANES)
            kvf = kvf + mm(sel, rows)
        kvf = kvf.astype(BF)
        if tick < gather.ticks():
            gather.tick(tick)
            tick += 1
        co, lse = cross_attend(start, norms, w_q, kvf, counts[f, 0:1, 0:1])
        rows = slice(f * LAT, (f + 1) * LAT)
        h1[rows, :] = start + mm(co, w_o[...]) + out_bias[0:1, :]
        kvf_out[f] = kvf
        co_out[rows, :] = co
        lse_out[f] = lse
        if tick < gather.ticks():
            gather.tick(tick)
            tick += 1
    while tick < gather.ticks():
        gather.tick(tick)
        tick += 1

    big = (
        (up_one, m_up_one, at["w_up"], D, FF),
        (down_one, m_down_one, at["w_down"], FF, D),
        (qkv_w, m_qkv, at["w_qkv"], D, 3 * D),
        (so_w, m_so, at["w_so"], D, D),
        (up_two, m_up_two, at["w_up"] + D * FF // LANES, D, FF),
        (down_two, m_down_two, at["w_down"] + D * FF // LANES, FF, D),
    )
    outs = []
    for j, (out, held, row, rows, cols) in enumerate(big):
        relayout(whole, row, stage, held, rows, cols)
        outs.append(pltpu.make_async_copy(held, out, out_sem.at[j]))
        outs[-1].start()
    for copy in outs:
        copy.wait()
    for copy in id_copies:
        copy.wait_send()
    exchange.finish()
    gather.finish()


def begin_all(master_rows, token_rows, ids, hot, frames, cap):
    shard = master_rows.shape[0]
    tokens = token_rows.shape[0]
    total = 8 * tokens
    chunks = gather_chunks(shard)
    vmem = pl.BlockSpec(memory_space=pltpu.VMEM)
    anywhere = pl.BlockSpec(memory_space=pl.ANY)
    matrices = [(D, FF), (FF, D), (D, 3 * D), (D, D), (D, FF), (FF, D)]
    dma = pltpu.SemaphoreType.DMA
    return pl.pallas_call(
        functools.partial(begin_kernel, chunks),
        out_shape=[shaped(m, BF) for m in matrices]
        + [
            shaped((LAT, D), BF),
            shaped((8, D)),
            shaped((2, FF)),
            shaped((4, D)),
            shaped((D, LANES), BF),
            shaped((LANES, D), BF),
            shaped((DIN, LANES), BF),
            shaped((2, DIN)),
            shaped((tokens, DIN), BF),
            shaped((frames, 1, D)),
            shaped((frames, total // LANES, LANES), jnp.int32),
            shaped((frames, 8, LANES), jnp.int32),
            shaped((frames, cap, LANES), BF),
            shaped((frames * LAT, LANES), BF),
            shaped((frames, 1, LAT)),
            shaped((frames * LAT, D)),
        ],
        in_specs=[vmem] * 4,
        out_specs=[anywhere] * 6 + [vmem] * 16,
        scratch_shapes=[
            pltpu.VMEM((8 * shard, LANES), BF),
            pltpu.VMEM((2048, LANES), F32),
            pltpu.VMEM((8, tokens // LANES, LANES), jnp.int32),
            pltpu.VMEM((8, tokens, LANES), BF),
        ]
        + [pltpu.VMEM(m, BF) for m in matrices]
        + [
            dma((7, len(chunks))), dma((7, len(chunks))), dma((8,)), dma((8,)), dma((7,)), dma((7,)), dma((6,)),
        ],
        compiler_params=pltpu.CompilerParams(
            collective_id=3, has_side_effects=True, vmem_limit_bytes=56 * MIB
        ),
    )(master_rows, token_rows, ids, hot)


def fixed(*shape):
    return pl.BlockSpec(shape, lambda i: (0,) * len(shape), pipeline_mode=pl.Buffered(1))


def kept(*shape):
    return pl.BlockSpec(shape, lambda i: (0,) * len(shape))


def rowed(rows, cols):
    return pl.BlockSpec((rows, cols), lambda i: (i, 0))


def framed(*shape):
    return pl.BlockSpec((1,) + shape, lambda i: (i,) + (0,) * len(shape))


def shaped(shape, dtype=F32):
    return jax.ShapeDtypeStruct(shape, dtype)


def call(kernel, grid, in_specs, outs, args, flops=0, trans=0, scratch=(), limit=56):
    out_specs, out_shapes = zip(*outs)
    moved = sum(math.prod(a.shape) * a.dtype.itemsize for a in args)
    moved += sum(math.prod(s.shape) * s.dtype.itemsize for s in out_shapes)
    return pl.pallas_call(
        kernel,
        grid=(grid,),
        in_specs=in_specs,
        out_specs=list(out_specs),
        out_shape=list(out_shapes),
        scratch_shapes=list(scratch),
        compiler_params=pltpu.CompilerParams(
            dimension_semantics=("arbitrary",), vmem_limit_bytes=limit * MIB
        ),
        cost_estimate=pl.CostEstimate(flops=flops, bytes_accessed=moved, transcendentals=trans),
    )(*args)


def reduce_all(local_flat, master_rows, starts, ends, bias_owner, bias_row):
    shard = master_rows.shape[0]
    vmem = pl.BlockSpec(memory_space=pltpu.VMEM)
    block = [
        pltpu.VMEM((8, STAT_ROWS, LANES), F32),
        pltpu.SemaphoreType.DMA((7,)),
        pltpu.SemaphoreType.DMA((7,)),
    ]
    return pl.pallas_call(
        functools.partial(reduce_kernel, bias_owner, bias_row),
        out_shape=[shaped((shard, LANES), BF), shaped((STAT_ROWS, LANES))],
        in_specs=[vmem, vmem, pl.BlockSpec(memory_space=pl.ANY), vmem],
        out_specs=[vmem, vmem],
        scratch_shapes=block + Reduction.scratch(shard),
        compiler_params=pltpu.CompilerParams(
            collective_id=1, has_side_effects=True, vmem_limit_bytes=48 * MIB
        ),
    )(starts, ends, local_flat.reshape(2, 2, 2, shard, LANES), master_rows)


def body(tokens, frame_ids, episodes, master, moment_one, moment_two, latent_grad):
    lat_count = lax.axis_size("lat")
    lat_index = lax.axis_index("lat")
    shard_len = master.shape[0]
    frame_total = episodes.shape[1]
    frames = frame_total // lat_count
    rows_total = frames * LAT
    total_keys = frame_ids.shape[1] * lat_count
    cap = total_keys // 8
    token_rows_count = total_keys // LANES

    reach = lat_count == 8 and lax.axis_size("kf") == 4
    shard_rows = shard_len // LANES
    master_rows = master.reshape(shard_rows, LANES)
    episode_index = jnp.arange(EPISODES, dtype=jnp.int32)
    own_episodes = lax.dynamic_slice_in_dim(episodes[0], lat_index * frames, frames, 0)
    episode_match = own_episodes[:, None] == episode_index[None, :]
    score_flops = rows_total * cap * LANES * 2
    select_flops = frames * cap * total_keys * LANES * 2
    if reach:
        hot = jnp.pad(episode_match.astype(BF), ((0, 16 - frames), (0, 16 - EPISODES)))
        (
            up_one, down_one, w_qkv, w_so, up_two, down_two,
            latent, norms, hid_bias, out_bias, w_q, w_o, w_kv, tok_norm, tok_normed, episode_rows, rank, counts,
            kvf, cross_out, cross_lse, h1,
        ) = begin_all(master_rows, tokens[0], frame_ids.reshape(-1, LANES), hot, frames, cap)
        latent_grad, h1 = lax.optimization_barrier((latent_grad, h1))
    else:
        weights = split_flat(lax.all_gather(master.astype(BF), "lat", axis=0, tiled=True))
        norms = weights["lat_norms"].astype(F32)
        out_bias = weights["out_bias"].astype(F32)
        hid_bias = weights["hid_bias"].astype(F32)
        tok_norm = weights["tok_norm"].astype(F32)
        w_kv, w_qkv, w_so, latent = (weights[name] for name in ("w_kv", "w_qkv", "w_so", "latent"))
        up_one, up_two = weights["w_up"]
        down_one, down_two = weights["w_down"]
        frame_tag = lax.all_gather(frame_ids[0].astype(BF), "lat", axis=0, tiled=True).astype(jnp.int32)
        own_frames = lat_index * frames + jnp.arange(frames, dtype=jnp.int32)
        own_hit = frame_tag[None, :] == own_frames[:, None]
        rank = jnp.cumsum(own_hit.astype(jnp.int32), axis=1) - 1
        counts = jnp.broadcast_to(rank[:, -1][:, None, None] + 1, (frames, 8, LANES))
        rank = jnp.where(own_hit, rank, -1).reshape(frames, token_rows_count, LANES)
        tok_normed = layer_norm(tokens[0].astype(F32), tok_norm[0], tok_norm[1]).astype(BF)
        key_value = mm(tok_normed, w_kv).astype(BF)
        all_keys = lax.all_gather(key_value, "lat", axis=0, tiled=True)
        episode_rows = mm(episode_match.astype(BF), weights["episode"]).reshape(frames, 1, D)
        w_q = jnp.pad(weights["w_q"], ((0, 0), (0, LANES - CH)))
        w_o = jnp.pad(weights["w_o"], ((LANES - CH, 0), (0, 0)))
        h1, kvf, cross_out, cross_lse = call(
            cross_fwd_kernel,
            frames,
            [
                fixed(LAT, D), framed(1, D), fixed(8, D), fixed(D, LANES), fixed(LANES, D), fixed(4, D),
                fixed(total_keys, LANES), framed(token_rows_count, LANES), framed(8, LANES),
            ],
            [
                (rowed(LAT, D), shaped((rows_total, D))),
                (framed(cap, LANES), shaped((frames, cap, LANES), BF)),
                (rowed(LAT, LANES), shaped((rows_total, LANES), BF)),
                (framed(1, LAT), shaped((frames, 1, LAT))),
            ],
            (latent, episode_rows, norms, w_q, w_o, out_bias, all_keys, rank, counts),
            flops=2 * score_flops + select_flops,
            trans=rows_total * cap,
        )
    grad_rows_in = lax.all_to_all(
        latent_grad[0], "lat", split_axis=0, concat_axis=1, tiled=True
    ).reshape(rows_total, D)

    block = min(512, rows_total)
    steps = rows_total // block
    mlp_flops = 4 * rows_total * D * FF
    h2, normed_one, act_one, slope_one, sa_in, qkv = call(
        mlp_one_fwd_kernel,
        steps,
        [rowed(block, D), fixed(8, D), fixed(2, FF), fixed(4, D), fixed(D, FF), fixed(FF, D), fixed(D, 3 * D)],
        [
            (rowed(block, D), shaped((rows_total, D))),
            (rowed(block, D), shaped((rows_total, D), BF)),
            (rowed(block, FF), shaped((rows_total, FF), BF)),
            (rowed(block, FF), shaped((rows_total, FF), BF)),
            (rowed(block, D), shaped((rows_total, D), BF)),
            (rowed(block, 3 * D), shaped((rows_total, 3 * D), BF)),
        ],
        (h1, norms, hid_bias, out_bias, up_one, down_one, w_qkv),
        flops=mlp_flops + 6 * rows_total * D * D,
        trans=2 * rows_total * FF,
    )

    attn_flops = 4 * rows_total * LAT * D
    h3, mixed, self_lse = call(
        self_fwd_kernel,
        frames,
        [rowed(LAT, 3 * D), rowed(LAT, D), fixed(D, D), fixed(4, D)],
        [
            (rowed(LAT, D), shaped((rows_total, D))),
            (rowed(LAT, D), shaped((rows_total, D), BF)),
            (framed(HEADS, LAT), shaped((frames, HEADS, LAT))),
        ],
        (qkv, h2, w_so, out_bias),
        flops=4 * attn_flops,
        trans=rows_total * LAT * HEADS,
    )

    latents, g3, normed_two, act_two, dpre_two, dnorm_two, dhid_two, dout_two = call(
        mlp_two_kernel,
        steps,
        [rowed(block, D), rowed(block, D), fixed(8, D), fixed(2, FF), fixed(4, D), fixed(D, FF), fixed(FF, D)],
        [
            (rowed(block, D), shaped((rows_total, D), BF)),
            (rowed(block, D), shaped((rows_total, D))),
            (rowed(block, D), shaped((rows_total, D), BF)),
            (rowed(block, FF), shaped((rows_total, FF), BF)),
            (rowed(block, FF), shaped((rows_total, FF), BF)),
            (kept(2, D), shaped((2, D))),
            (kept(1, FF), shaped((1, FF))),
            (kept(1, D), shaped((1, D))),
        ],
        (h3, grad_rows_in, norms, hid_bias, out_bias, up_two, down_two),
        flops=2 * mlp_flops,
        trans=2 * rows_total * FF,
        scratch=[pltpu.VMEM((block, FF), BF)],
    )
    latents_out = lax.all_to_all(
        latents.reshape(frames, LAT, D), "lat", split_axis=1, concat_axis=0, tiled=True
    )[None]
    two_down = t_mm(act_two, grad_rows_in)
    two_up = t_mm(normed_two, dpre_two)

    g2, low_three, dqkv, dnorm_sa, dout_so = call(
        self_bwd_kernel,
        frames,
        [
            rowed(LAT, 3 * D), framed(HEADS, LAT), rowed(LAT, D), rowed(LAT, D), fixed(8, D),
            fixed(D, D), fixed(D, 3 * D),
        ],
        [
            (rowed(LAT, D), shaped((rows_total, D))),
            (rowed(LAT, D), shaped((rows_total, D), BF)),
            (rowed(LAT, 3 * D), shaped((rows_total, 3 * D), BF)),
            (kept(2, D), shaped((2, D))),
            (kept(1, D), shaped((1, D))),
        ],
        (qkv, self_lse, g3, h2, norms, w_so, w_qkv),
        flops=10 * attn_flops,
        trans=rows_total * LAT * HEADS,
    )
    grad_so = t_mm(mixed, low_three)
    grad_qkv = t_mm(sa_in, dqkv)

    g1, low_two, dpre_one, dnorm_one, dhid_one, dout_one = call(
        mlp_one_bwd_kernel,
        steps,
        [rowed(block, D), rowed(block, D), rowed(block, FF), fixed(8, D), fixed(D, FF), fixed(FF, D)],
        [
            (rowed(block, D), shaped((rows_total, D))),
            (rowed(block, D), shaped((rows_total, D), BF)),
            (rowed(block, FF), shaped((rows_total, FF), BF)),
            (kept(2, D), shaped((2, D))),
            (kept(1, FF), shaped((1, FF))),
            (kept(1, D), shaped((1, D))),
        ],
        (h1, g2, slope_one, norms, up_one, down_one),
        flops=mlp_flops,
    )
    one_down = t_mm(act_one, low_two)
    one_up = t_mm(normed_one, dpre_one)

    grad_latent, frame_sums, dnorm_q, dw_q, dw_o, dout_cross, dkv_t = call(
        cross_bwd_kernel,
        frames,
        [
            fixed(LAT, D), framed(1, D), fixed(8, D), fixed(D, LANES), fixed(LANES, D),
            framed(cap, LANES), rowed(LAT, LANES), framed(1, LAT), framed(token_rows_count, LANES),
            framed(8, LANES), rowed(LAT, D),
        ],
        [
            (kept(LAT, D), shaped((LAT, D))),
            (framed(1, D), shaped((frames, 1, D))),
            (kept(2, D), shaped((2, D))),
            (kept(D, LANES), shaped((D, LANES))),
            (kept(LANES, D), shaped((LANES, D))),
            (kept(1, D), shaped((1, D))),
            (kept(LANES, total_keys), shaped((LANES, total_keys))),
        ],
        (latent, episode_rows, norms, w_q, w_o, kvf, cross_out, cross_lse, rank, counts, g1),
        flops=5 * score_flops + select_flops,
        trans=rows_total * cap,
    )
    grad_episode = jnp.sum(episode_match.astype(F32)[:, :, None] * frame_sums, axis=0)

    grad_kv = lax.psum_scatter(dkv_t.T.astype(BF), "lat", scatter_dimension=0, tiled=True)
    grad_w_kv = t_mm(tok_normed, grad_kv)
    grad_tok_normed = mm_t(grad_kv, w_kv)
    unused, token_pull = jax.vjp(layer_norm, tokens[0].astype(F32), tok_norm[0], tok_norm[1])
    grad_tokens, grad_tok_gain, grad_tok_bias = token_pull(grad_tok_normed)
    token_grad = grad_tokens.astype(BF)[None]

    grads = {
        "latent": grad_latent,
        "episode": grad_episode,
        "tok_norm": jnp.stack([grad_tok_gain, grad_tok_bias]),
        "lat_norms": jnp.concatenate([dnorm_q, dnorm_one, dnorm_sa, dnorm_two]),
        "w_kv": grad_w_kv,
        "w_q": dw_q[:, :CH],
        "w_o": dw_o[LANES - CH :],
        "w_qkv": grad_qkv,
        "w_so": grad_so,
        "w_up": jnp.stack([one_up, two_up]),
        "w_down": jnp.stack([one_down, two_down]),
        "hid_bias": jnp.concatenate([dhid_one, dhid_two]),
        "out_bias": jnp.concatenate([dout_cross, dout_one, dout_so, dout_two]),
    }
    layout = param_layout()
    local_flat = jnp.concatenate([grads[name].astype(BF).reshape(-1) for name, unused in layout])
    starts, ends, offset, bias_offset = [], [], 0, 0
    for name, shape in layout:
        if name == "hid_bias":
            bias_offset = offset
        starts.append(offset // LANES)
        offset += math.prod(shape)
        ends.append(offset // LANES)
    pad = [0] * (16 - len(layout))
    starts = jnp.broadcast_to(jnp.array(starts + pad, jnp.int32)[:, None], (16, LANES))
    ends = jnp.broadcast_to(jnp.array(ends + pad, jnp.int32)[:, None], (16, LANES))
    opt_rows = 784 if shard_rows % 784 == 0 else shard_rows
    opt_steps = shard_rows // opt_rows
    base = (lat_index * shard_rows).astype(jnp.int32).reshape(1)
    smem = pl.BlockSpec(memory_space=pltpu.SMEM)
    flat_rows = (shard_rows, LANES)
    bias_owner, bias_at = divmod(bias_offset, shard_len)
    if reach:
        summed, stats = reduce_all(local_flat, master_rows, starts, ends, bias_owner, bias_at // LANES)
    else:
        summed = lax.psum_scatter(local_flat, "lat", scatter_dimension=0, tiled=True)
        summed = lax.psum(summed, "kf").reshape(flat_rows)
        grad_sq, weight_sq = call(
            grad_stats_kernel,
            opt_steps,
            [smem, fixed(16, LANES), fixed(16, LANES), rowed(opt_rows, LANES), rowed(opt_rows, LANES)],
            [(kept(1, LANES), shaped((1, LANES))), (kept(16, LANES), shaped((16, LANES)))],
            (base, starts, ends, summed, master_rows),
        )
        bias_rows = summed[bias_at // LANES : bias_at // LANES + 2 * FF // LANES].astype(F32)
        bias_rows = jnp.where(lat_index == bias_owner, bias_rows, 0.0)
        stats = lax.psum(
            jnp.concatenate([grad_sq, jnp.zeros((7, LANES), F32), weight_sq, bias_rows]), "lat"
        )
    bias_grad = stats[24:STAT_ROWS].reshape(2, FF)
    grad_shard, lamb_update, new_one, new_two, update_sq = call(
        lamb_kernel,
        opt_steps,
        [smem, fixed(STAT_ROWS, LANES), fixed(16, LANES), fixed(16, LANES)] + [rowed(opt_rows, LANES)] * 4,
        [(rowed(opt_rows, LANES), shaped(flat_rows))] * 4 + [(kept(16, LANES), shaped((16, LANES)))],
        (
            base, stats, starts, ends, summed, master_rows,
            moment_one.reshape(flat_rows), moment_two.reshape(flat_rows),
        ),
    )
    if reach:
        vmem = pl.BlockSpec(memory_space=pltpu.VMEM)
        trust = pl.pallas_call(
            trust_kernel,
            out_shape=shaped((16, LANES)),
            in_specs=[vmem, vmem],
            out_specs=vmem,
            scratch_shapes=[
                pltpu.VMEM((8, 16, LANES), F32),
                pltpu.SemaphoreType.DMA((7,)),
                pltpu.SemaphoreType.DMA((7,)),
            ],
            compiler_params=pltpu.CompilerParams(collective_id=2, has_side_effects=True),
        )(update_sq, stats)[: len(layout), 0]
    else:
        update_sq = lax.psum(jnp.sum(update_sq, axis=1), "lat")
        weight_sq = jnp.sum(stats[8:24], axis=1)
        trust = (jnp.sqrt(weight_sq) / (jnp.sqrt(update_sq) + 1e-06))[: len(layout)]
    return (
        latents_out,
        token_grad,
        grad_shard.reshape(-1),
        lamb_update.reshape(-1),
        new_one.reshape(-1),
        new_two.reshape(-1),
        trust,
        bias_grad,
    )


def solution(mesh):
    return jax.shard_map(
        body,
        mesh=mesh,
        in_specs=(
            P("kf", "lat", None),
            P("kf", "lat"),
            P("kf", None),
            P("lat"),
            P("lat"),
            P("lat"),
            P("kf", None, "lat", None),
        ),
        out_specs=(
            P("kf", None, "lat", None),
            P("kf", "lat", None),
            P("lat"),
            P("lat"),
            P("lat"),
            P("lat"),
            P(),
            P(),
        ),
        check_vma=False,
    )
```

```python
import functools
import math

import jax
import jax.numpy as jnp
from jax import lax
from jax.experimental import pallas as pl
from jax.experimental.pallas import tpu as pltpu
from jax.sharding import PartitionSpec as P

DIN = 256
D = 512
LAT = 512
CH = 64
HEADS = 8
HEAD_DIM = 64
FF = 2048
EPISODES = 11
NPARAM = 5619712
LANES = 128

norm_eps = 1e-05
masked_fill = -1e30
beta_one = 0.9
beta_two = 0.999
adam_eps = 1e-06
decay_rate = 0.01
clip_fraction = 0.5
lamb_step = 10.0

BF = jnp.bfloat16
F32 = jnp.float32
MIB = 1024 * 1024


def param_layout():
    return [
        ("latent", (LAT, D)),
        ("episode", (EPISODES, D)),
        ("tok_norm", (2, DIN)),
        ("lat_norms", (8, D)),
        ("w_kv", (DIN, 2 * CH)),
        ("w_q", (D, CH)),
        ("w_o", (CH, D)),
        ("w_qkv", (D, 3 * D)),
        ("w_so", (D, D)),
        ("w_up", (2, D, FF)),
        ("w_down", (2, FF, D)),
        ("hid_bias", (2, FF)),
        ("out_bias", (4, D)),
    ]


def split_flat(flat_vector):
    pieces = {}
    offset = 0
    for tensor_name, tensor_shape in param_layout():
        entries = math.prod(tensor_shape)
        pieces[tensor_name] = flat_vector[offset : offset + entries].reshape(tensor_shape)
        offset += entries
    return pieces


def layer_norm(inputs, norm_gain, norm_bias):
    row_mean = jnp.mean(inputs, axis=-1, keepdims=True)
    centered = inputs - row_mean
    row_var = jnp.mean(centered * centered, axis=-1, keepdims=True)
    return centered * lax.rsqrt(row_var + norm_eps) * norm_gain + norm_bias


def mm(left, right):
    return jnp.dot(left, right, preferred_element_type=F32)


def mm_t(left, right):
    return lax.dot_general(left, right, (((1,), (1,)), ((), ())), preferred_element_type=F32)


def t_mm(left, right):
    return lax.dot_general(left, right, (((0,), (0,)), ((), ())), preferred_element_type=F32)


def norm_stats(rows):
    mean = jnp.mean(rows, axis=-1, keepdims=True)
    centered = rows - mean
    var = jnp.mean(centered * centered, axis=-1, keepdims=True)
    rstd = lax.rsqrt(var + norm_eps)
    return centered * rstd, rstd


def norm_back(grad, xhat, rstd, gain):
    dxh = grad * gain
    first = jnp.mean(dxh, axis=-1, keepdims=True)
    second = jnp.mean(dxh * xhat, axis=-1, keepdims=True)
    return rstd * (dxh - first - xhat * second)


def col_sum(values):
    return jnp.sum(values, axis=0, keepdims=True)


def gelu_pair(x):
    size = jnp.abs(x)
    t = pl.reciprocal(1.0 + (0.3275911 / math.sqrt(2.0)) * size, approx=True)
    e = jnp.exp(x * x * -0.5)
    poly = 0.5 * 1.061405429
    for coef in (-1.453152027, 1.421413741, -0.284496736, 0.254829592):
        poly = poly * t + 0.5 * coef
    tail = poly * t * e
    cdf = jnp.where(x >= 0.0, 1.0 - tail, tail)
    return x * cdf, cdf + x * (e * (1.0 / math.sqrt(2.0 * math.pi)))


def accumulate(first, ref, value):
    @pl.when(first)
    def _():
        ref[...] = value

    @pl.when(jnp.logical_not(first))
    def _():
        ref[...] += value


def lane_half(shape, half):
    lane = lax.broadcasted_iota(jnp.int32, shape, 1)
    return (lane >= half * 64) & (lane < half * 64 + 64)


def keep_half(values, half):
    return jnp.where(lane_half(values.shape, half), values, jnp.zeros_like(values))


def select_tokens(rank_rows, cap):
    slot = lax.broadcasted_iota(jnp.int32, (cap, LANES), 0)
    parts = []
    for r in range(rank_rows.shape[0]):
        hit = slot == rank_rows[r : r + 1, :]
        parts.append(jnp.where(hit, 1.0, 0.0).astype(BF))
    return jnp.concatenate(parts, axis=1)


def cross_scores(kvf, queries_scaled, count):
    scores = mm_t(kvf, queries_scaled)
    slot = lax.broadcasted_iota(jnp.int32, scores.shape, 0)
    return jnp.where(slot < count, scores, masked_fill)


def cross_attend(start, norms, w_q, kvf, count):
    xhat, unused = norm_stats(start)
    query_in = (xhat * norms[0:1, :] + norms[1:2, :]).astype(BF)
    queries = mm(query_in, w_q[...]).astype(BF) * jnp.asarray(0.125, BF)
    scores = cross_scores(kvf, queries, count)
    top = jnp.max(scores, axis=0, keepdims=True)
    terms = jnp.exp(scores - top)
    total = jnp.sum(terms, axis=0, keepdims=True)
    prob = (terms * (1.0 / total)).astype(BF)
    return t_mm(kvf, prob).T.astype(BF), top + jnp.log(total)


def cross_fwd_kernel(latent, episode, norms, w_q, w_o, out_bias, kv, rank, count, h1, kvf_out, co_out, lse_out):
    cap = kvf_out.shape[1]
    start = latent[...].astype(F32) + episode[0]
    chunk = 8 * LANES
    chunks = kv.shape[0] // chunk

    def step(j, acc):
        sel = select_tokens(rank[0, pl.ds(pl.multiple_of(j * 8, 8), 8), :], cap)
        return acc + mm(sel, kv[pl.ds(pl.multiple_of(j * chunk, chunk), chunk), :])

    kvf = lax.fori_loop(0, chunks, step, jnp.zeros((cap, LANES), F32)).astype(BF)
    co, lse = cross_attend(start, norms, w_q, kvf, count[0, 0:1, 0:1])
    h1[...] = start + mm(co, w_o[...]) + out_bias[0:1, :]
    kvf_out[0] = kvf
    co_out[...] = co
    lse_out[0] = lse


def segment_hot(starts, ends, base, rows):
    row = lax.broadcasted_iota(jnp.int32, (16, rows), 1) + base
    return jnp.where((row >= starts[:, 0:1]) & (row < ends[:, 0:1]), 1.0, 0.0).astype(BF)


def segment_sums(hot, squares):
    high = squares.astype(BF)
    low = (squares - high.astype(F32)).astype(BF)
    return mm(hot, high) + mm(hot, low)


def grad_stats_kernel(base, starts, ends, summed, master, grad_sq, weight_sq):
    i = pl.program_id(0)
    rows = master.shape[0]
    hot = segment_hot(starts, ends, base[0] + i * rows, rows)
    grad = summed[...].astype(F32)
    accumulate(i == 0, grad_sq, col_sum(grad * grad))
    accumulate(i == 0, weight_sq, segment_sums(hot, master[...] * master[...]))


def lamb_kernel(base, stats, starts, ends, summed, master, one, two, grad_out, update_out, one_out, two_out, update_sq):
    i = pl.program_id(0)
    rows = master.shape[0]
    hot = segment_hot(starts, ends, base[0] + i * rows, rows)
    total_sq = jnp.sum(stats[0:1, :], axis=1, keepdims=True)
    clip = jnp.minimum(1.0, clip_fraction * math.sqrt(NPARAM) / (jnp.sqrt(total_sq) + 1e-06))
    grad = summed[...].astype(F32)
    grad_out[...] = grad
    clipped = clip * grad
    new_one = beta_one * one[...] + (1.0 - beta_one) * clipped
    new_two = beta_two * two[...] + (1.0 - beta_two) * clipped * clipped
    one_out[...] = new_one
    two_out[...] = new_two
    first_hat = new_one * (1.0 / (1.0 - beta_one**lamb_step))
    second_hat = new_two * (1.0 / (1.0 - beta_two**lamb_step))
    update = first_hat / (jnp.sqrt(second_hat) + adam_eps) + decay_rate * master[...]
    update_out[...] = update
    accumulate(i == 0, update_sq, segment_sums(hot, update * update))


BATCH = 256
HALF = 128
QUARTER = 64
MESH = pl.DeviceIdType.MESH


class Place:
    def __init__(self):
        self.z = lax.axis_index("kf")
        self.me = lax.axis_index("lat")
        self.core = lax.rem(self.me, 2)
        self.x = lax.rem(self.me // 2, 2)
        self.y = self.me // 4
        self.z_low = lax.rem(self.z, 2)
        self.z_high = self.z // 2
        self.sibling = (self.z, self.me + 1 - 2 * self.core)
        self.x_side = (self.z, self.me + 2 - 4 * self.x)
        self.y_side = (self.z, self.me + 4 - 8 * self.y)
        self.z_near = (self.z + 1 - 2 * self.z_low, self.me)
        self.z_far = (self.z + 2 - 4 * self.z_high, self.me)

    def z_other(self, step):
        return (lax.rem(self.z + step, 4), self.me)

    def lat_other(self, step):
        return (self.z, lax.rem(self.me + step, 8))


def remote(src, dst, send, recv, device):
    return pltpu.make_async_remote_copy(
        src_ref=src, dst_ref=dst, send_sem=send, recv_sem=recv, device_id=device, device_id_type=MESH
    )


def greet(devices):
    barrier = pltpu.get_barrier_semaphore()
    for device in devices:
        pl.semaphore_signal(barrier, inc=1, device_id=device, device_id_type=MESH)
    pl.semaphore_wait(barrier, len(devices))


def added(left, right):
    return (left.astype(F32) + right.astype(F32)).astype(BF)


class Reduction:
    lags = (0, 1, 3, 5, 7, 9, 11)

    def __init__(self, place, grads, out, bufs, sems):
        self.p = place
        self.grads = grads
        self.out = out
        self.own, self.rc, self.r1, self.r2, self.r3, self.r4, self.res = bufs
        self.own_sem, self.send, self.rc_sem, self.r1_sem, self.r2_sem, self.r3_sem, self.r4_sem, self.res_sem = sems
        self.shard = grads.shape[3]
        self.batches = pl.cdiv(self.shard, BATCH)
        self.back = self.batches * BATCH - self.shard

    @staticmethod
    def scratch(shard):
        n = pl.cdiv(shard, BATCH)
        bufs = [
            pltpu.VMEM((2, 2, 2, BATCH, LANES), BF),
            pltpu.VMEM((n, 2, 2, BATCH, LANES), BF),
            pltpu.VMEM((n, 2, 2, HALF, LANES), BF),
            pltpu.VMEM((n, 2, HALF, LANES), BF),
            pltpu.VMEM((n, HALF, LANES), BF),
            pltpu.VMEM((n, QUARTER, LANES), BF),
            pltpu.VMEM((n, BATCH, LANES), BF),
        ]
        dma = pltpu.SemaphoreType.DMA
        sems = [dma((2,)), dma((10, 4)), dma((n,)), dma((n, 2)), dma((n, 2)), dma((n,)), dma((n,)), dma((n, 3))]
        return bufs + sems

    def row(self, i):
        return pl.multiple_of(i * BATCH - (i // (self.batches - 1)) * self.back, 16)

    def own_copy(self, i):
        slot = lax.rem(i, 2)
        src = self.grads.at[:, :, self.p.core, pl.ds(self.row(i), BATCH), :]
        return pltpu.make_async_copy(src, self.own.at[slot], self.own_sem.at[slot])

    def copies(self, stage, i):
        p, slot = self.p, lax.rem(i, 4)
        if stage == 0:
            src = self.grads.at[:, :, 1 - p.core, pl.ds(self.row(i), BATCH), :]
            return [remote(src, self.rc.at[i], self.send.at[0, slot], self.rc_sem.at[i], p.sibling)]
        if stage == 1:
            to_x = self.rc.at[i, :, 1 - p.x, pl.ds(0, HALF), :]
            to_y = self.rc.at[i, 1 - p.y, :, pl.ds(HALF, HALF), :]
            return [
                remote(to_x, self.r1.at[i, 0], self.send.at[1, slot], self.r1_sem.at[i, 0], p.x_side),
                remote(to_y, self.r1.at[i, 1], self.send.at[2, slot], self.r1_sem.at[i, 1], p.y_side),
            ]
        if stage == 2:
            to_y = self.r1.at[i, 0, 1 - p.y]
            to_x = self.r1.at[i, 1, 1 - p.x]
            return [
                remote(to_y, self.r2.at[i, 0], self.send.at[3, slot], self.r2_sem.at[i, 0], p.y_side),
                remote(to_x, self.r2.at[i, 1], self.send.at[4, slot], self.r2_sem.at[i, 1], p.x_side),
            ]
        if stage == 3:
            src = self.r2.at[i, 1 - p.z_low]
            return [remote(src, self.r3.at[i], self.send.at[5, slot], self.r3_sem.at[i], p.z_near)]
        if stage == 4:
            src = self.r3.at[i, pl.ds(pl.multiple_of((1 - p.z_high) * QUARTER, QUARTER), QUARTER), :]
            return [remote(src, self.r4.at[i], self.send.at[6, slot], self.r4_sem.at[i], p.z_far)]
        mine = self.res.at[i, pl.ds(pl.multiple_of(p.z_low * HALF + p.z_high * QUARTER, QUARTER), QUARTER), :]
        return [
            remote(mine, mine, self.send.at[6 + d, slot], self.res_sem.at[i, d - 1], p.z_other(d))
            for d in (1, 2, 3)
        ]

    def launch(self, stage, i):
        @pl.when(i >= 4)
        def _():
            for copy in self.copies(stage, i - 4):
                copy.wait_send()

        for copy in self.copies(stage, i):
            copy.start()

    def landed(self, stage, i):
        for copy in self.copies(stage, i):
            copy.wait_recv()

    def work(self, stage, i):
        p = self.p
        if stage == 0:
            self.own_copy(i).start()
        elif stage == 1:
            self.landed(0, i)
            self.own_copy(i).wait()
            self.rc[i] = added(self.rc[i], self.own[lax.rem(i, 2)])
        elif stage == 2:
            self.landed(1, i)
            self.r1[i, 0] = added(self.r1[i, 0], self.rc[i, :, p.x, 0:HALF, :])
            self.r1[i, 1] = added(self.r1[i, 1], self.rc[i, p.y, :, HALF:BATCH, :])
        elif stage == 3:
            self.landed(2, i)
            self.r2[i, 0] = added(self.r2[i, 0], self.r1[i, 0, p.y])
            self.r2[i, 1] = added(self.r2[i, 1], self.r1[i, 1, p.x])
        elif stage == 4:
            self.landed(3, i)
            self.r3[i] = added(self.r3[i], self.r2[i, p.z_low])
        elif stage == 5:
            self.landed(4, i)
            part = self.r3[i, pl.ds(pl.multiple_of(p.z_high * QUARTER, QUARTER), QUARTER), :]
            at = pl.multiple_of(p.z_low * HALF + p.z_high * QUARTER, QUARTER)
            self.res[i, pl.ds(at, QUARTER), :] = added(self.r4[i], part)
        else:
            self.landed(5, i)
            self.out[pl.ds(self.row(i), BATCH), :] = self.res[i]
        if stage < 6:
            self.launch(stage, i)

    def tick(self, t):
        for stage, lag in enumerate(self.lags):
            i = t - lag

            @pl.when((i >= 0) & (i < self.batches))
            def _(stage=stage, i=i):
                self.work(stage, i)

    def ticks(self):
        return self.batches + self.lags[-1]

    def finish(self):
        for stage in range(6):
            for back in range(4):
                for copy in self.copies(stage, self.batches - 4 + back):
                    copy.wait_send()

    def partners(self):
        p = self.p
        return [p.sibling, p.x_side, p.y_side] + [p.z_other(d) for d in (1, 2, 3)]


def share_all(place, block, send, recv):
    mine = block.at[place.me]
    copies = [
        remote(mine, mine, send.at[d - 1], recv.at[d - 1], place.lat_other(d)) for d in range(1, 8)
    ]
    for copy in copies:
        copy.start()
    for copy in copies:
        copy.wait()


STAT_ROWS = 56


def reduce_kernel(bias_owner, bias_at, starts, ends, grads, master, summed, stats, *scratch):
    place = Place()
    block, block_send, block_recv = scratch[:3]
    red = Reduction(place, grads, summed, scratch[3:10], scratch[10:])
    greet([place.lat_other(d) for d in range(1, 8)] + [place.z_other(d) for d in (1, 2, 3)])
    lax.fori_loop(0, red.ticks(), lambda t, c: (red.tick(t), c)[1], 0)
    shard = master.shape[0]
    step = 784
    grad_sq = jnp.zeros((1, LANES), F32)
    weight_sq = jnp.zeros((16, LANES), F32)
    for j in range(shard // step):
        at = slice(j * step, (j + 1) * step)
        part = summed[at, :].astype(F32)
        grad_sq = grad_sq + col_sum(part * part)
        hot = segment_hot(starts, ends, place.me * shard + j * step, step)
        part = master[at, :]
        weight_sq = weight_sq + segment_sums(hot, part * part)
    bias = summed[bias_at : bias_at + 2 * FF // LANES, :].astype(F32)
    bias = jnp.where(place.me == bias_owner, bias, 0.0)
    head = jnp.concatenate([grad_sq, jnp.zeros((7, LANES), F32), weight_sq, bias], axis=0)
    block[pl.ds(place.me, 1)] = head[None]
    share_all(place, block, block_send, block_recv)
    total = block[0]
    for s in range(1, 8):
        total = total + block[s]
    stats[...] = total
    red.finish()


def trust_kernel(update_sq, stats, trust, block, send, recv):
    place = Place()
    greet([place.lat_other(d) for d in range(1, 8)])
    block[pl.ds(place.me, 1)] = update_sq[...][None]
    share_all(place, block, send, recv)
    total = block[0]
    for s in range(1, 8):
        total = total + block[s]
    update_norm = jnp.sqrt(jnp.sum(total, axis=1, keepdims=True))
    weight_norm = jnp.sqrt(jnp.sum(stats[8:24, :], axis=1, keepdims=True))
    trust[...] = jnp.broadcast_to(weight_norm / (update_norm + 1e-06), (16, LANES))


def relayout(whole, row, stage, dst, rows, cols):
    wide = cols // LANES
    block = min(rows, 2048 // wide // 128 * 128)

    def step(i, carry):
        at = pl.multiple_of(row + i * (block * wide), 16)
        stage[0 : block * wide, :] = whole[pl.ds(at, block * wide), :].astype(F32)
        for j in range(wide):
            part = stage[pl.ds(j, block, stride=wide), :]
            dst[pl.ds(pl.multiple_of(i * block, 16), block), j * LANES : (j + 1) * LANES] = part.astype(BF)
        return carry

    lax.fori_loop(0, rows // block, step, 0)


def small_matrix(whole, row, stage, rows, cols):
    wide = cols // LANES
    stage[0 : rows * wide, :] = whole[row : row + rows * wide, :].astype(F32)
    return jnp.concatenate([stage[pl.ds(j, rows, stride=wide), :] for j in range(wide)], axis=1)


class Gather:
    def __init__(self, place, whole, shard, chunks, send, recv):
        self.p, self.whole, self.shard, self.chunks, self.send, self.recv = place, whole, shard, chunks, send, recv
        p = place
        x_index, y_index = p.x_side[1], p.y_side[1]
        low = p.z_low
        self.first = x_index + low * (y_index - x_index)
        self.second = y_index + low * (x_index - y_index)
        self.diagonal = x_index + 4 - 8 * p.y

    def copy(self, kind, k):
        p = self.p
        block = (p.me, p.me, self.first, self.first, self.first, self.diagonal, self.second)[kind]
        target = (
            (p.z, self.first), p.sibling, (p.z, self.second), p.z_near, p.sibling, p.sibling, p.sibling
        )[kind]
        row, count = self.chunks[k]
        ref = self.whole.at[pl.ds(pl.multiple_of(block * self.shard + row, 16), count), :]
        return remote(ref, ref, self.send.at[kind, k], self.recv.at[kind, k], target)

    def tick(self, t):
        n = len(self.chunks)
        if t < n:
            self.copy(0, t).start()
            self.copy(1, t).start()
        if 0 <= t - 2 < n:
            self.copy(0, t - 2).wait_recv()
            for kind in (2, 3, 4):
                self.copy(kind, t - 2).start()
        if 0 <= t - 4 < n:
            self.copy(2, t - 4).wait_recv()
            self.copy(5, t - 4).start()
            self.copy(3, t - 4).wait_recv()
            self.copy(6, t - 4).start()
        if 0 <= t - 5 < n:
            for kind in (1, 4, 5, 6):
                self.copy(kind, t - 5).wait_recv()

    def ticks(self):
        return len(self.chunks) + 5

    def finish(self):
        for k in range(len(self.chunks)):
            for kind in range(7):
                self.copy(kind, k).wait_send()


class KeyExchange:
    def __init__(self, place, keys, send, recv):
        self.p, self.keys, self.send, self.recv = place, keys, send, recv
        self.x_index, self.y_index = place.x_side[1], place.y_side[1]
        self.diagonal = self.x_index + 4 - 8 * place.y

    def copy(self, kind):
        p = self.p
        half = self.keys.shape[1] // 2
        low, high, full = pl.ds(0, half), pl.ds(half, half), pl.ds(0, 2 * half)
        block, rows, target = (
            (p.me, full, p.x_side), (p.me, full, p.y_side), (p.me, full, p.sibling),
            (self.x_index, low, p.y_side), (self.y_index, high, p.x_side),
            (self.x_index, full, p.sibling), (self.y_index, full, p.sibling), (self.diagonal, full, p.sibling),
        )[kind]
        ref = self.keys.at[block, rows, :]
        return remote(ref, ref, self.send.at[kind], self.recv.at[kind], target)

    def step(self, s):
        if s == 0:
            waits, starts = (), (0, 1, 2)
        elif s == 1:
            waits, starts = (0, 1), (3, 4, 5, 6)
        elif s == 2:
            waits, starts = (3, 4), (7,)
        else:
            waits, starts = (2, 5, 6, 7), ()
        for kind in waits:
            self.copy(kind).wait_recv()
        for kind in starts:
            self.copy(kind).start()

    def finish(self):
        for kind in range(8):
            self.copy(kind).wait_send()


def flat_rows_of():
    rows, at = {}, 0
    for name, shape in param_layout():
        rows[name] = at // LANES
        at += math.prod(shape)
    return rows


def gather_chunks(shard):
    at = flat_rows_of()
    tail = at["hid_bias"] % shard // 16 * 16
    chunks = [(at["episode"], at["w_o"] - at["episode"]), (tail, shard - tail), (at["w_o"], at["w_qkv"] - at["w_o"])]
    for low, high in ((0, at["episode"]), (at["w_qkv"], tail)):
        while low < high:
            count = min(512, high - low)
            chunks.append((low, count))
            low += count
    return chunks


def begin_kernel(
    chunks, master, tokens, ids, hot,
    up_one, down_one, qkv_w, so_w, up_two, down_two,
    latent, norms, hid_bias, out_bias, w_q, w_o, w_kv, tok_norm, tok_normed, episode, rank, counts,
    kvf_out, co_out, lse_out, h1,
    whole, stage, all_ids, keys, m_up_one, m_down_one, m_qkv, m_so, m_up_two, m_down_two,
    send, recv, key_send, key_recv, id_send, id_recv, out_sem,
):
    place = Place()
    shard = master.shape[0]
    frames, cap = kvf_out.shape[0], kvf_out.shape[1]
    gather = Gather(place, whole, shard, chunks, send, recv)
    exchange = KeyExchange(place, keys, key_send, key_recv)
    at = flat_rows_of()
    greet([place.lat_other(d) for d in range(1, 8)] + [place.z_near])
    all_ids[pl.ds(place.me, 1)] = ids[...][None]
    id_copies = [
        remote(all_ids.at[place.me], all_ids.at[place.me], id_send.at[d - 1], id_recv.at[d - 1], place.lat_other(d))
        for d in range(1, 8)
    ]
    for copy in id_copies:
        copy.start()
    own_at = place.me * shard
    for row, count in chunks:
        whole[pl.ds(pl.multiple_of(own_at + row, 16), count), :] = master[row : row + count, :].astype(BF)
    for t in range(4):
        gather.tick(t)

    for copy in id_copies:
        copy.wait_recv()
    tags = jnp.concatenate([all_ids[s] for s in range(8)], axis=0)
    low = lax.broadcasted_iota(jnp.int32, (LANES, LANES), 0)
    high = lax.broadcasted_iota(jnp.int32, (LANES, LANES), 1)
    upto = jnp.where(low <= high, 1.0, 0.0).astype(BF)
    n = tags.shape[0]
    below = jnp.where(
        lax.broadcasted_iota(jnp.int32, (n, n), 1) < lax.broadcasted_iota(jnp.int32, (n, n), 0), 1.0, 0.0
    ).astype(BF)
    for f in range(frames):
        hit = tags == place.me * frames + f
        hit_low = jnp.where(hit, 1.0, 0.0).astype(BF)
        inside = mm(hit_low, upto)
        row_total = jnp.broadcast_to(inside[:, LANES - 1 : LANES], (n, LANES))
        before = mm(below, row_total.astype(BF))
        place_in = (inside + before).astype(jnp.int32) - 1
        rank[f] = jnp.where(hit, place_in, -1)
        total = jnp.sum(row_total[:, 0:1], axis=0, keepdims=True).astype(jnp.int32)
        counts[f] = jnp.broadcast_to(total, (8, LANES))
    for t in range(4, 7):
        gather.tick(t)

    pair = whole[at["tok_norm"] // 16 * 16 : at["lat_norms"], :].astype(F32)
    pair = pair[at["tok_norm"] % 16 : at["tok_norm"] % 16 + 4, :]
    tok_norm[...] = jnp.concatenate(
        [
            jnp.concatenate([pair[0:1], pair[1:2]], axis=1),
            jnp.concatenate([pair[2:3], pair[3:4]], axis=1),
        ],
        axis=0,
    )
    w_kv[...] = whole[at["w_kv"] : at["w_kv"] + DIN, :]
    xhat, unused = norm_stats(tokens[...].astype(F32))
    normed = (xhat * tok_norm[0:1, :] + tok_norm[1:2, :]).astype(BF)
    tok_normed[...] = normed
    keys[pl.ds(place.me, 1)] = mm(normed, w_kv[...]).astype(BF)[None]
    exchange.step(0)
    norms[...] = small_matrix(whole, at["lat_norms"], stage, 8, D)
    hid_bias[...] = small_matrix(whole, at["hid_bias"], stage, 2, FF)
    out_bias[...] = small_matrix(whole, at["out_bias"], stage, 4, D)
    episode_rows = mm(hot[...], small_matrix(whole, at["episode"], stage, 16, D).astype(BF))
    gather.tick(7)
    exchange.step(1)
    packed = whole[at["w_q"] : at["w_q"] + D // 2, :].astype(F32)
    stage[pl.ds(0, D // 2, stride=2), :] = packed
    stage[pl.ds(1, D // 2, stride=2), :] = pltpu.roll(packed, CH, 1)
    w_q[...] = keep_half(stage[0:D, :], 0).astype(BF)
    w_o[0:CH, :] = jnp.zeros((CH, D), BF)
    w_o[CH : 2 * CH, :] = small_matrix(whole, at["w_o"], stage, CH, D).astype(BF)
    gather.tick(8)
    exchange.step(2)
    for t in range(9, 12):
        gather.tick(t)
    exchange.step(3)
    relayout(whole, 0, stage, latent, LAT, D)

    tick = 12
    chunk = 8 * LANES
    for f in range(frames):
        start = latent[...].astype(F32) + episode_rows[f : f + 1, :]
        episode[f] = episode_rows[f : f + 1, :]
        kvf = jnp.zeros((cap, LANES), F32)
        for j in range(n // 8):
            sel = select_tokens(rank[f, 8 * j : 8 * j + 8, :], cap)
            rows = keys[2 * j : 2 * j + 2].reshape(chunk, LANES)
            kvf = kvf + mm(sel, rows)
        kvf = kvf.astype(BF)
        if tick < gather.ticks():
            gather.tick(tick)
            tick += 1
        co, lse = cross_attend(start, norms, w_q, kvf, counts[f, 0:1, 0:1])
        rows = slice(f * LAT, (f + 1) * LAT)
        h1[rows, :] = start + mm(co, w_o[...]) + out_bias[0:1, :]
        kvf_out[f] = kvf
        co_out[rows, :] = co
        lse_out[f] = lse
        if tick < gather.ticks():
            gather.tick(tick)
            tick += 1
    while tick < gather.ticks():
        gather.tick(tick)
        tick += 1

    big = (
        (up_one, m_up_one, at["w_up"], D, FF),
        (down_one, m_down_one, at["w_down"], FF, D),
        (qkv_w, m_qkv, at["w_qkv"], D, 3 * D),
        (so_w, m_so, at["w_so"], D, D),
        (up_two, m_up_two, at["w_up"] + D * FF // LANES, D, FF),
        (down_two, m_down_two, at["w_down"] + D * FF // LANES, FF, D),
    )
    outs = []
    for j, (out, held, row, rows, cols) in enumerate(big):
        relayout(whole, row, stage, held, rows, cols)
        outs.append(pltpu.make_async_copy(held, out, out_sem.at[j]))
        outs[-1].start()
    for copy in outs:
        copy.wait()
    for copy in id_copies:
        copy.wait_send()
    exchange.finish()
    gather.finish()


def begin_all(master_rows, token_rows, ids, hot, frames, cap):
    shard = master_rows.shape[0]
    tokens = token_rows.shape[0]
    total = 8 * tokens
    chunks = gather_chunks(shard)
    vmem = pl.BlockSpec(memory_space=pltpu.VMEM)
    anywhere = pl.BlockSpec(memory_space=pl.ANY)
    matrices = [(D, FF), (FF, D), (D, 3 * D), (D, D), (D, FF), (FF, D)]
    dma = pltpu.SemaphoreType.DMA
    return pl.pallas_call(
        functools.partial(begin_kernel, chunks),
        out_shape=[shaped(m, BF) for m in matrices]
        + [
            shaped((LAT, D), BF),
            shaped((8, D)),
            shaped((2, FF)),
            shaped((4, D)),
            shaped((D, LANES), BF),
            shaped((LANES, D), BF),
            shaped((DIN, LANES), BF),
            shaped((2, DIN)),
            shaped((tokens, DIN), BF),
            shaped((frames, 1, D)),
            shaped((frames, total // LANES, LANES), jnp.int32),
            shaped((frames, 8, LANES), jnp.int32),
            shaped((frames, cap, LANES), BF),
            shaped((frames * LAT, LANES), BF),
            shaped((frames, 1, LAT)),
            shaped((frames * LAT, D)),
        ],
        in_specs=[vmem] * 4,
        out_specs=[anywhere] * 6 + [vmem] * 16,
        scratch_shapes=[
            pltpu.VMEM((8 * shard, LANES), BF),
            pltpu.VMEM((2048, LANES), F32),
            pltpu.VMEM((8, tokens // LANES, LANES), jnp.int32),
            pltpu.VMEM((8, tokens, LANES), BF),
        ]
        + [pltpu.VMEM(m, BF) for m in matrices]
        + [
            dma((7, len(chunks))), dma((7, len(chunks))), dma((8,)), dma((8,)), dma((7,)), dma((7,)), dma((6,)),
        ],
        compiler_params=pltpu.CompilerParams(
            collective_id=3, has_side_effects=True, vmem_limit_bytes=56 * MIB
        ),
    )(master_rows, token_rows, ids, hot)


FCHUNK = 512


def add_flat(acc, row, part):
    wide = part.shape[1] // LANES
    for j in range(wide):
        at = pl.ds(row + j, part.shape[0], stride=wide)
        acc[at, :] = acc[at, :] + part[:, j * LANES : (j + 1) * LANES]


def to_flat(stage, matrix):
    rows, wide = matrix.shape[0], matrix.shape[1] // LANES
    for j in range(wide):
        stage[pl.ds(j, rows, stride=wide), :] = matrix[:, j * LANES : (j + 1) * LANES]
    return stage[0 : rows * wide, :]


def feed_forward(rows, gain, bias, up_bias, down_bias, w_up, w_down, act_ref, slope_ref):
    xhat, rstd = norm_stats(rows)
    normed = (xhat * gain + bias).astype(BF)
    total = rows + down_bias
    for c in range(FF // FCHUNK):
        at = slice(c * FCHUNK, (c + 1) * FCHUNK)
        act, slope = gelu_pair(mm(normed, w_up[:, at]) + up_bias[:, at])
        act = act.astype(BF)
        act_ref[:, at] = act
        slope_ref[:, at] = slope.astype(BF)
        total = total + mm(act, w_down[at, :])
    return total, normed, xhat, rstd


def feed_back(grad_low, grad_rows, normed, xhat, rstd, gain, act, slope, w_up, w_down, acc_up, acc_down, dhid, dnorm, dout):
    grad_normed = jnp.zeros(grad_rows.shape, F32)
    normed_t = normed.T
    for c in range(FF // FCHUNK):
        at = slice(c * FCHUNK, (c + 1) * FCHUNK)
        dpre = (mm_t(grad_low, w_down[at, :]) * slope[:, at].astype(F32)).astype(BF)
        dhid[:, at] += col_sum(dpre.astype(F32))
        grad_normed = grad_normed + mm_t(dpre, w_up[:, at])
        part = mm(normed_t, dpre)
        for j in range(FCHUNK // LANES):
            rows = pl.ds(c * (FCHUNK // LANES) + j, D, stride=FF // LANES)
            acc_up[rows, :] = acc_up[rows, :] + part[:, j * LANES : (j + 1) * LANES]
        add_flat(acc_down, c * FCHUNK * (D // LANES), mm(act[:, at].T, grad_low))
    dnorm[...] += jnp.concatenate([col_sum(grad_normed * xhat), col_sum(grad_normed)], axis=0)
    dout[...] += col_sum(grad_low.astype(F32))
    return grad_rows + norm_back(grad_normed, xhat, rstd, gain)


def clear(first, refs):
    @pl.when(first)
    def _():
        for ref in refs:
            ref[...] = jnp.zeros_like(ref)


def write_flat(flat, low, pieces, sems):
    copies = []
    for j, (acc, row) in enumerate(pieces):
        count = acc.shape[0]
        slot = j % 2
        if j >= 2:
            copies[j - 2].wait()
        low[slot, 0:count, :] = acc[...].astype(BF)
        copies.append(
            pltpu.make_async_copy(low.at[slot, pl.ds(0, count), :], flat.at[pl.ds(row, count), :], sems.at[slot])
        )
        copies[-1].start()
    for copy in copies[-2:]:
        copy.wait()


def forward_kernel(
    h1, grad, norms, hid_bias, out_bias, up_one, down_one, w_qkv, w_so, up_two, down_two,
    h2_out, qkv, lse_out, mixed_out, act_one, slope_one, latents, g3, dhid, dnorm, dout, flat,
    act_two, slope_two, acc_up, acc_down, low, sems,
):
    step = pl.program_id(0)
    clear(step == 0, (acc_up, acc_down, dhid, dnorm, dout))
    h2, unused, unused, unused = feed_forward(
        h1[...], norms[2:3, :], norms[3:4, :], hid_bias[0:1, :], out_bias[1:2, :], up_one, down_one, act_one, slope_one
    )
    h2_out[...] = h2
    xhat, unused = norm_stats(h2)
    sa_in = (xhat * norms[4:5, :] + norms[5:6, :]).astype(BF)
    for c in range(3):
        at = slice(c * D, (c + 1) * D)
        qkv[:, at] = mm(sa_in, w_qkv[:, at]).astype(BF)

    scale = jnp.asarray(0.125, BF)
    mixed_rows = []
    for pair in range(HEADS // 2):
        base = pair * LANES
        query_pair = qkv[:, base : base + LANES] * scale
        key_pair = qkv[:, D + base : D + base + LANES]
        value_t = qkv[:, 2 * D + base : 2 * D + base + LANES].T
        for half in range(2):
            scores = mm_t(key_pair, keep_half(query_pair, half))
            top = jnp.max(scores, axis=0, keepdims=True)
            terms = jnp.exp(scores - top)
            total = jnp.sum(terms, axis=0, keepdims=True)
            prob = (terms * (1.0 / total)).astype(BF)
            head = 2 * pair + half
            lse_out[0, head : head + 1, :] = top + jnp.log(total)
            mixed_rows.append(mm(value_t[half * 64 : half * 64 + 64, :], prob))
    mixed = jnp.concatenate(mixed_rows, axis=0).T.astype(BF)
    mixed_out[...] = mixed
    h3 = h2 + mm(mixed, w_so[...]) + out_bias[2:3, :]

    total, normed, xhat, rstd = feed_forward(
        h3, norms[6:7, :], norms[7:8, :], hid_bias[1:2, :], out_bias[3:4, :], up_two, down_two, act_two, slope_two
    )
    latents[...] = total.astype(BF)
    grad_low = grad[...]
    g3[...] = feed_back(
        grad_low, grad_low.astype(F32), normed, xhat, rstd, norms[6:7, :], act_two, slope_two, up_two, down_two,
        acc_up, acc_down, dhid, dnorm, dout,
    )

    @pl.when(step == pl.num_programs(0) - 1)
    def _():
        at = flat_rows_of()
        half = D * FF // LANES
        write_flat(flat, low, [(acc_up, at["w_up"] + half), (acc_down, at["w_down"] + half)], sems)


def backward_kernel(
    qkv, lse, mixed, g3, h2, h1, act_one, slope_one, kvf_in, co_in, cross_lse, rank, count, episode, hot,
    latent, norms, w_so, w_qkv, up_one, down_one, w_q, w_o, dhid_two, dnorm_two, dout_two, flat_in,
    dkv_t, flat,
    dqkv, acc_up, acc_down, acc_qkv, acc_so, acc_latent, acc_q, acc_o, acc_episode,
    dhid, dnorm_sa, dnorm_one, dnorm_cross, dout_so, dout_one, dout_cross, stage, low, sems,
):
    step = pl.program_id(0)
    clear(
        step == 0,
        (
            acc_up, acc_down, acc_qkv, acc_so, acc_latent, acc_q, acc_o, acc_episode, dhid, dnorm_sa, dnorm_one,
            dnorm_cross, dout_so, dout_one, dout_cross, dkv_t,
        ),
    )
    scale = jnp.asarray(0.125, BF)
    grad_three = g3[...]
    grad_low = grad_three.astype(BF)
    dout_so[...] += col_sum(grad_low.astype(F32))
    add_flat(acc_so, 0, t_mm(mixed[...], grad_low))
    grad_mixed = mm_t(grad_low, w_so[...]).astype(BF)
    for pair in range(HEADS // 2):
        base = pair * LANES
        query_pair = qkv[:, base : base + LANES] * scale
        key_pair = qkv[:, D + base : D + base + LANES]
        value_pair = qkv[:, 2 * D + base : 2 * D + base + LANES]
        grad_pair = grad_mixed[:, base : base + LANES]
        key_t = key_pair.T
        query_t = []
        grad_key = jnp.zeros((LAT, LANES), F32)
        grad_value = jnp.zeros((LAT, LANES), F32)
        for half in range(2):
            head = 2 * pair + half
            query = keep_half(query_pair, half)
            grad_head = keep_half(grad_pair, half)
            prob = jnp.exp(mm_t(key_pair, query) - lse[0, head : head + 1, :])
            grad_value = grad_value + mm(prob.astype(BF), grad_head)
            weighted = prob * mm_t(value_pair, grad_head)
            grad_score = (weighted - prob * col_sum(weighted)).astype(BF)
            grad_key = grad_key + mm(grad_score, query)
            query_t.append(mm(key_t[half * 64 : half * 64 + 64, :], grad_score))
        dqkv[:, base : base + LANES] = (jnp.concatenate(query_t, axis=0).T * 0.125).astype(BF)
        dqkv[:, D + base : D + base + LANES] = grad_key.astype(BF)
        dqkv[:, 2 * D + base : 2 * D + base + LANES] = grad_value.astype(BF)
    grad_in = mm_t(dqkv[...], w_qkv[...])
    xhat, rstd = norm_stats(h2[...])
    sa_t = (xhat * norms[4:5, :] + norms[5:6, :]).astype(BF).T
    for c in range(3):
        part = mm(sa_t, dqkv[:, c * D : (c + 1) * D])
        for j in range(D // LANES):
            rows = pl.ds(c * (D // LANES) + j, D, stride=3 * D // LANES)
            acc_qkv[rows, :] = acc_qkv[rows, :] + part[:, j * LANES : (j + 1) * LANES]
    dnorm_sa[...] += jnp.concatenate([col_sum(grad_in * xhat), col_sum(grad_in)], axis=0)
    grad_two = grad_three + norm_back(grad_in, xhat, rstd, norms[4:5, :])

    xhat, rstd = norm_stats(h1[...])
    normed = (xhat * norms[2:3, :] + norms[3:4, :]).astype(BF)
    grad_one = feed_back(
        grad_two.astype(BF), grad_two, normed, xhat, rstd, norms[2:3, :], act_one, slope_one, up_one, down_one,
        acc_up, acc_down, dhid, dnorm_one, dout_one,
    )

    cap = kvf_in.shape[1]
    start = latent[...].astype(F32) + episode[0]
    xhat, rstd = norm_stats(start)
    query_in = (xhat * norms[0:1, :] + norms[1:2, :]).astype(BF)
    queries = mm(query_in, w_q[...]).astype(BF) * scale
    kvf = kvf_in[0]
    branch = grad_one.astype(BF)
    grad_co = mm_t(branch, w_o[...]).astype(BF)
    acc_o[...] += t_mm(co_in[...], branch)
    dout_cross[...] += col_sum(branch.astype(F32))
    scores = cross_scores(kvf, queries, count[0, 0:1, 0:1])
    prob = jnp.exp(scores - cross_lse[0])
    weighted = prob * mm_t(kvf, grad_co)
    grad_score = (weighted - prob * col_sum(weighted)).astype(BF)
    grad_kv = (mm(grad_score, queries) + mm(prob.astype(BF), grad_co)).astype(BF)
    grad_query = (t_mm(kvf, grad_score).T * 0.125).astype(BF)
    acc_q[...] += t_mm(query_in, grad_query)
    grad_in = mm_t(grad_query, w_q[...])
    grad_start = grad_one + norm_back(grad_in, xhat, rstd, norms[0:1, :])
    dnorm_cross[...] += jnp.concatenate([col_sum(grad_in * xhat), col_sum(grad_in)], axis=0)
    add_flat(acc_latent, 0, grad_start)
    acc_episode[...] += hot[0, :, 0:1] * col_sum(grad_start)
    grad_kv_t = grad_kv.T
    chunk = 8 * LANES

    def scatter(j, carry):
        sel = select_tokens(rank[0, pl.ds(pl.multiple_of(j * 8, 8), 8), :], cap)
        dkv_t[:, pl.ds(pl.multiple_of(j * chunk, chunk), chunk)] += mm(grad_kv_t, sel)
        return carry

    lax.fori_loop(0, dkv_t.shape[1] // chunk, scatter, 0)

    @pl.when(step == pl.num_programs(0) - 1)
    def _():
        at = flat_rows_of()
        write_flat(
            flat, low,
            [
                (acc_up, at["w_up"]), (acc_down, at["w_down"]), (acc_qkv, at["w_qkv"]), (acc_so, at["w_so"]),
                (acc_latent, 0),
            ],
            sems,
        )
        small = at["w_qkv"] - at["w_q"]
        first = at["w_q"] - at["episode"]
        head = at["lat_norms"] - at["episode"]
        low[0, 0:first, :] = jnp.zeros((first, LANES), BF)
        norm_grads = jnp.concatenate([dnorm_cross[...], dnorm_one[...], dnorm_sa[...], dnorm_two[...]], axis=0)
        rows = jnp.concatenate([to_flat(stage, acc_episode[...])[0 : EPISODES * (D // LANES), :], jnp.zeros((head - EPISODES * (D // LANES), LANES), F32)], axis=0)
        rows = jnp.concatenate([rows, to_flat(stage, norm_grads)], axis=0)
        low[0, 0 : rows.shape[0], :] = rows.astype(BF)
        stage[0:D, :] = acc_q[...]
        even = stage[pl.ds(0, D // 2, stride=2), :]
        odd = pltpu.roll(stage[pl.ds(1, D // 2, stride=2), :], CH, 1)
        low[0, first : first + D // 2, :] = jnp.where(lane_half(even.shape, 0), even, odd).astype(BF)
        low[0, first + D // 2 : first + small, :] = to_flat(stage, acc_o[CH : 2 * CH, :]).astype(BF)
        hid = to_flat(stage, jnp.concatenate([dhid[...], dhid_two[...]], axis=0))
        low[1, 0 : hid.shape[0], :] = hid.astype(BF)
        outs = jnp.concatenate([dout_cross[...], dout_one[...], dout_so[...], dout_two[...]], axis=0)
        out_rows = 4 * D // LANES
        low[1, hid.shape[0] : hid.shape[0] + out_rows, :] = to_flat(stage, outs).astype(BF)
        total = hid.shape[0] + out_rows
        copies = [
            pltpu.make_async_copy(
                low.at[0, pl.ds(0, first + small), :], flat.at[pl.ds(at["episode"], first + small), :], sems.at[0]
            ),
            pltpu.make_async_copy(
                low.at[1, pl.ds(0, total), :], flat.at[pl.ds(at["hid_bias"], total), :], sems.at[1]
            ),
        ]
        for copy in copies:
            copy.start()
        for copy in copies:
            copy.wait()


def fixed(*shape):
    return pl.BlockSpec(shape, lambda i: (0,) * len(shape), pipeline_mode=pl.Buffered(1))


def kept(*shape):
    return pl.BlockSpec(shape, lambda i: (0,) * len(shape))


def rowed(rows, cols):
    return pl.BlockSpec((rows, cols), lambda i: (i, 0))


def framed(*shape):
    return pl.BlockSpec((1,) + shape, lambda i: (i,) + (0,) * len(shape))


def shaped(shape, dtype=F32):
    return jax.ShapeDtypeStruct(shape, dtype)


def call(kernel, grid, in_specs, outs, args, flops=0, trans=0, scratch=(), limit=56, aliases=None):
    out_specs, out_shapes = zip(*outs)
    moved = sum(math.prod(a.shape) * a.dtype.itemsize for a in args)
    moved += sum(math.prod(s.shape) * s.dtype.itemsize for s in out_shapes)
    return pl.pallas_call(
        kernel,
        grid=(grid,),
        in_specs=in_specs,
        out_specs=list(out_specs),
        out_shape=list(out_shapes),
        scratch_shapes=list(scratch),
        input_output_aliases=aliases or {},
        compiler_params=pltpu.CompilerParams(
            dimension_semantics=("arbitrary",), vmem_limit_bytes=limit * MIB
        ),
        cost_estimate=pl.CostEstimate(flops=flops, bytes_accessed=moved, transcendentals=trans),
    )(*args)


def reduce_all(local_flat, master_rows, starts, ends, bias_owner, bias_row):
    shard = master_rows.shape[0]
    vmem = pl.BlockSpec(memory_space=pltpu.VMEM)
    block = [
        pltpu.VMEM((8, STAT_ROWS, LANES), F32),
        pltpu.SemaphoreType.DMA((7,)),
        pltpu.SemaphoreType.DMA((7,)),
    ]
    return pl.pallas_call(
        functools.partial(reduce_kernel, bias_owner, bias_row),
        out_shape=[shaped((shard, LANES), BF), shaped((STAT_ROWS, LANES))],
        in_specs=[vmem, vmem, pl.BlockSpec(memory_space=pl.ANY), vmem],
        out_specs=[vmem, vmem],
        scratch_shapes=block + Reduction.scratch(shard),
        compiler_params=pltpu.CompilerParams(
            collective_id=1, has_side_effects=True, vmem_limit_bytes=48 * MIB
        ),
    )(starts, ends, local_flat.reshape(2, 2, 2, shard, LANES), master_rows)


def body(tokens, frame_ids, episodes, master, moment_one, moment_two, latent_grad):
    lat_count = lax.axis_size("lat")
    lat_index = lax.axis_index("lat")
    shard_len = master.shape[0]
    frame_total = episodes.shape[1]
    frames = frame_total // lat_count
    rows_total = frames * LAT
    total_keys = frame_ids.shape[1] * lat_count
    cap = total_keys // 8
    token_rows_count = total_keys // LANES

    reach = lat_count == 8 and lax.axis_size("kf") == 4
    shard_rows = shard_len // LANES
    master_rows = master.reshape(shard_rows, LANES)
    episode_index = jnp.arange(EPISODES, dtype=jnp.int32)
    own_episodes = lax.dynamic_slice_in_dim(episodes[0], lat_index * frames, frames, 0)
    episode_match = own_episodes[:, None] == episode_index[None, :]
    score_flops = rows_total * cap * LANES * 2
    select_flops = frames * cap * total_keys * LANES * 2
    if reach:
        hot = jnp.pad(episode_match.astype(BF), ((0, 16 - frames), (0, 16 - EPISODES)))
        (
            up_one, down_one, w_qkv, w_so, up_two, down_two,
            latent, norms, hid_bias, out_bias, w_q, w_o, w_kv, tok_norm, tok_normed, episode_rows, rank, counts,
            kvf, cross_out, cross_lse, h1,
        ) = begin_all(master_rows, tokens[0], frame_ids.reshape(-1, LANES), hot, frames, cap)
        latent_grad, h1 = lax.optimization_barrier((latent_grad, h1))
    else:
        weights = split_flat(lax.all_gather(master.astype(BF), "lat", axis=0, tiled=True))
        norms = weights["lat_norms"].astype(F32)
        out_bias = weights["out_bias"].astype(F32)
        hid_bias = weights["hid_bias"].astype(F32)
        tok_norm = weights["tok_norm"].astype(F32)
        w_kv, w_qkv, w_so, latent = (weights[name] for name in ("w_kv", "w_qkv", "w_so", "latent"))
        up_one, up_two = weights["w_up"]
        down_one, down_two = weights["w_down"]
        frame_tag = lax.all_gather(frame_ids[0].astype(BF), "lat", axis=0, tiled=True).astype(jnp.int32)
        own_frames = lat_index * frames + jnp.arange(frames, dtype=jnp.int32)
        own_hit = frame_tag[None, :] == own_frames[:, None]
        rank = jnp.cumsum(own_hit.astype(jnp.int32), axis=1) - 1
        counts = jnp.broadcast_to(rank[:, -1][:, None, None] + 1, (frames, 8, LANES))
        rank = jnp.where(own_hit, rank, -1).reshape(frames, token_rows_count, LANES)
        tok_normed = layer_norm(tokens[0].astype(F32), tok_norm[0], tok_norm[1]).astype(BF)
        key_value = mm(tok_normed, w_kv).astype(BF)
        all_keys = lax.all_gather(key_value, "lat", axis=0, tiled=True)
        episode_rows = mm(episode_match.astype(BF), weights["episode"]).reshape(frames, 1, D)
        w_q = jnp.pad(weights["w_q"], ((0, 0), (0, LANES - CH)))
        w_o = jnp.pad(weights["w_o"], ((LANES - CH, 0), (0, 0)))
        h1, kvf, cross_out, cross_lse = call(
            cross_fwd_kernel,
            frames,
            [
                fixed(LAT, D), framed(1, D), fixed(8, D), fixed(D, LANES), fixed(LANES, D), fixed(4, D),
                fixed(total_keys, LANES), framed(token_rows_count, LANES), framed(8, LANES),
            ],
            [
                (rowed(LAT, D), shaped((rows_total, D))),
                (framed(cap, LANES), shaped((frames, cap, LANES), BF)),
                (rowed(LAT, LANES), shaped((rows_total, LANES), BF)),
                (framed(1, LAT), shaped((frames, 1, LAT))),
            ],
            (latent, episode_rows, norms, w_q, w_o, out_bias, all_keys, rank, counts),
            flops=2 * score_flops + select_flops,
            trans=rows_total * cap,
        )
    grad_rows_in = lax.all_to_all(
        latent_grad[0], "lat", split_axis=0, concat_axis=1, tiled=True
    ).reshape(rows_total, D)

    mlp_flops = 4 * rows_total * D * FF
    attn_flops = 4 * rows_total * LAT * D
    flat_shape = (NPARAM // LANES, LANES)
    anywhere = pl.BlockSpec(memory_space=pl.ANY)
    slab = D * FF // LANES
    h2, qkv, self_lse, mixed, act_one, slope_one, latents, g3, dhid_two, dnorm_two, dout_two, flat = call(
        forward_kernel,
        frames,
        [
            rowed(LAT, D), rowed(LAT, D), fixed(8, D), fixed(2, FF), fixed(4, D), fixed(D, FF), fixed(FF, D),
            fixed(D, 3 * D), fixed(D, D), fixed(D, FF), fixed(FF, D),
        ],
        [
            (rowed(LAT, D), shaped((rows_total, D))),
            (rowed(LAT, 3 * D), shaped((rows_total, 3 * D), BF)),
            (framed(HEADS, LAT), shaped((frames, HEADS, LAT))),
            (rowed(LAT, D), shaped((rows_total, D), BF)),
            (rowed(LAT, FF), shaped((rows_total, FF), BF)),
            (rowed(LAT, FF), shaped((rows_total, FF), BF)),
            (rowed(LAT, D), shaped((rows_total, D), BF)),
            (rowed(LAT, D), shaped((rows_total, D))),
            (kept(1, FF), shaped((1, FF))),
            (kept(2, D), shaped((2, D))),
            (kept(1, D), shaped((1, D))),
            (anywhere, shaped(flat_shape, BF)),
        ],
        (h1, grad_rows_in, norms, hid_bias, out_bias, up_one, down_one, w_qkv, w_so, up_two, down_two),
        flops=4 * mlp_flops + 4 * attn_flops,
        trans=4 * rows_total * FF,
        scratch=[
            pltpu.VMEM((LAT, FF), BF), pltpu.VMEM((LAT, FF), BF), pltpu.VMEM((slab, LANES), F32),
            pltpu.VMEM((slab, LANES), F32), pltpu.VMEM((2, slab, LANES), BF), pltpu.SemaphoreType.DMA((2,)),
        ],
        limit=60,
    )
    latents_out = lax.all_to_all(
        latents.reshape(frames, LAT, D), "lat", split_axis=1, concat_axis=0, tiled=True
    )[None]
    hot_lanes = jnp.broadcast_to(
        jnp.pad(episode_match.astype(F32), ((0, 0), (0, 16 - EPISODES)))[:, :, None], (frames, 16, LANES)
    )
    dkv_t, flat = call(
        backward_kernel,
        frames,
        [
            rowed(LAT, 3 * D), framed(HEADS, LAT), rowed(LAT, D), rowed(LAT, D), rowed(LAT, D), rowed(LAT, D),
            rowed(LAT, FF), rowed(LAT, FF), framed(cap, LANES), rowed(LAT, LANES), framed(1, LAT),
            framed(token_rows_count, LANES), framed(8, LANES), framed(1, D), framed(16, LANES),
            fixed(LAT, D), fixed(8, D), fixed(D, D), fixed(D, 3 * D), fixed(D, FF), fixed(FF, D), fixed(D, LANES),
            fixed(LANES, D), fixed(1, FF), fixed(2, D), fixed(1, D), anywhere,
        ],
        [(kept(LANES, total_keys), shaped((LANES, total_keys))), (anywhere, shaped(flat_shape, BF))],
        (
            qkv, self_lse, mixed, g3, h2, h1, act_one, slope_one, kvf, cross_out, cross_lse, rank, counts,
            episode_rows, hot_lanes, latent, norms, w_so, w_qkv, up_one, down_one, w_q, w_o, dhid_two, dnorm_two,
            dout_two, flat,
        ),
        flops=2 * mlp_flops + 10 * attn_flops + 6 * score_flops,
        trans=rows_total * LAT * HEADS,
        scratch=[
            pltpu.VMEM((LAT, 3 * D), BF), pltpu.VMEM((slab, LANES), F32), pltpu.VMEM((slab, LANES), F32),
            pltpu.VMEM((3 * D * D // LANES, LANES), F32), pltpu.VMEM((D * D // LANES, LANES), F32),
            pltpu.VMEM((LAT * D // LANES, LANES), F32), pltpu.VMEM((D, LANES), F32), pltpu.VMEM((LANES, D), F32),
            pltpu.VMEM((16, D), F32), pltpu.VMEM((1, FF), F32), pltpu.VMEM((2, D), F32), pltpu.VMEM((2, D), F32),
            pltpu.VMEM((2, D), F32), pltpu.VMEM((1, D), F32), pltpu.VMEM((1, D), F32), pltpu.VMEM((1, D), F32),
            pltpu.VMEM((512, LANES), F32), pltpu.VMEM((2, slab, LANES), BF), pltpu.SemaphoreType.DMA((2,)),
        ],
        limit=60,
        aliases={26: 1},
    )
    grad_kv = lax.psum_scatter(dkv_t.T.astype(BF), "lat", scatter_dimension=0, tiled=True)
    grad_w_kv = t_mm(tok_normed, grad_kv)
    grad_tok_normed = mm_t(grad_kv, w_kv)
    unused, token_pull = jax.vjp(layer_norm, tokens[0].astype(F32), tok_norm[0], tok_norm[1])
    grad_tokens, grad_tok_gain, grad_tok_bias = token_pull(grad_tok_normed)
    token_grad = grad_tokens.astype(BF)[None]
    flat_at = flat_rows_of()
    tok_norm_grad = jnp.stack([grad_tok_gain, grad_tok_bias]).reshape(-1, LANES).astype(BF)
    flat = lax.dynamic_update_slice(flat, tok_norm_grad, (flat_at["tok_norm"], 0))
    flat = lax.dynamic_update_slice(flat, grad_w_kv.astype(BF), (flat_at["w_kv"], 0))
    local_flat = flat.reshape(-1)
    layout = param_layout()

    starts, ends, offset, bias_offset = [], [], 0, 0
    for name, shape in layout:
        if name == "hid_bias":
            bias_offset = offset
        starts.append(offset // LANES)
        offset += math.prod(shape)
        ends.append(offset // LANES)
    pad = [0] * (16 - len(layout))
    starts = jnp.broadcast_to(jnp.array(starts + pad, jnp.int32)[:, None], (16, LANES))
    ends = jnp.broadcast_to(jnp.array(ends + pad, jnp.int32)[:, None], (16, LANES))
    opt_rows = 784 if shard_rows % 784 == 0 else shard_rows
    opt_steps = shard_rows // opt_rows
    base = (lat_index * shard_rows).astype(jnp.int32).reshape(1)
    smem = pl.BlockSpec(memory_space=pltpu.SMEM)
    flat_rows = (shard_rows, LANES)
    bias_owner, bias_at = divmod(bias_offset, shard_len)
    if reach:
        summed, stats = reduce_all(local_flat, master_rows, starts, ends, bias_owner, bias_at // LANES)
    else:
        summed = lax.psum_scatter(local_flat, "lat", scatter_dimension=0, tiled=True)
        summed = lax.psum(summed, "kf").reshape(flat_rows)
        grad_sq, weight_sq = call(
            grad_stats_kernel,
            opt_steps,
            [smem, fixed(16, LANES), fixed(16, LANES), rowed(opt_rows, LANES), rowed(opt_rows, LANES)],
            [(kept(1, LANES), shaped((1, LANES))), (kept(16, LANES), shaped((16, LANES)))],
            (base, starts, ends, summed, master_rows),
        )
        bias_rows = summed[bias_at // LANES : bias_at // LANES + 2 * FF // LANES].astype(F32)
        bias_rows = jnp.where(lat_index == bias_owner, bias_rows, 0.0)
        stats = lax.psum(
            jnp.concatenate([grad_sq, jnp.zeros((7, LANES), F32), weight_sq, bias_rows]), "lat"
        )
    bias_grad = stats[24:STAT_ROWS].reshape(2, FF)
    grad_shard, lamb_update, new_one, new_two, update_sq = call(
        lamb_kernel,
        opt_steps,
        [smem, fixed(STAT_ROWS, LANES), fixed(16, LANES), fixed(16, LANES)] + [rowed(opt_rows, LANES)] * 4,
        [(rowed(opt_rows, LANES), shaped(flat_rows))] * 4 + [(kept(16, LANES), shaped((16, LANES)))],
        (
            base, stats, starts, ends, summed, master_rows,
            moment_one.reshape(flat_rows), moment_two.reshape(flat_rows),
        ),
    )
    if reach:
        vmem = pl.BlockSpec(memory_space=pltpu.VMEM)
        trust = pl.pallas_call(
            trust_kernel,
            out_shape=shaped((16, LANES)),
            in_specs=[vmem, vmem],
            out_specs=vmem,
            scratch_shapes=[
                pltpu.VMEM((8, 16, LANES), F32),
                pltpu.SemaphoreType.DMA((7,)),
                pltpu.SemaphoreType.DMA((7,)),
            ],
            compiler_params=pltpu.CompilerParams(collective_id=2, has_side_effects=True),
        )(update_sq, stats)[: len(layout), 0]
    else:
        update_sq = lax.psum(jnp.sum(update_sq, axis=1), "lat")
        weight_sq = jnp.sum(stats[8:24], axis=1)
        trust = (jnp.sqrt(weight_sq) / (jnp.sqrt(update_sq) + 1e-06))[: len(layout)]
    return (
        latents_out,
        token_grad,
        grad_shard.reshape(-1),
        lamb_update.reshape(-1),
        new_one.reshape(-1),
        new_two.reshape(-1),
        trust,
        bias_grad,
    )


def solution(mesh):
    return jax.shard_map(
        body,
        mesh=mesh,
        in_specs=(
            P("kf", "lat", None),
            P("kf", "lat"),
            P("kf", None),
            P("lat"),
            P("lat"),
            P("lat"),
            P("kf", None, "lat", None),
        ),
        out_specs=(
            P("kf", None, "lat", None),
            P("kf", "lat", None),
            P("lat"),
            P("lat"),
            P("lat"),
            P("lat"),
            P(),
            P(),
        ),
        check_vma=False,
    )
```

```python
import functools
import math

import jax
import jax.numpy as jnp
from jax import lax
from jax.experimental import pallas as pl
from jax.experimental.pallas import tpu as pltpu
from jax.sharding import PartitionSpec as P

DIN = 256
D = 512
LAT = 512
CH = 64
HEADS = 8
HEAD_DIM = 64
FF = 2048
EPISODES = 11
NPARAM = 5619712
LANES = 128

norm_eps = 1e-05
masked_fill = -1e30
beta_one = 0.9
beta_two = 0.999
adam_eps = 1e-06
decay_rate = 0.01
clip_fraction = 0.5
lamb_step = 10.0

BF = jnp.bfloat16
F32 = jnp.float32
MIB = 1024 * 1024


def param_layout():
    return [
        ("latent", (LAT, D)),
        ("episode", (EPISODES, D)),
        ("tok_norm", (2, DIN)),
        ("lat_norms", (8, D)),
        ("w_kv", (DIN, 2 * CH)),
        ("w_q", (D, CH)),
        ("w_o", (CH, D)),
        ("w_qkv", (D, 3 * D)),
        ("w_so", (D, D)),
        ("w_up", (2, D, FF)),
        ("w_down", (2, FF, D)),
        ("hid_bias", (2, FF)),
        ("out_bias", (4, D)),
    ]


def split_flat(flat_vector):
    pieces = {}
    offset = 0
    for tensor_name, tensor_shape in param_layout():
        entries = math.prod(tensor_shape)
        pieces[tensor_name] = flat_vector[offset : offset + entries].reshape(tensor_shape)
        offset += entries
    return pieces


def layer_norm(inputs, norm_gain, norm_bias):
    row_mean = jnp.mean(inputs, axis=-1, keepdims=True)
    centered = inputs - row_mean
    row_var = jnp.mean(centered * centered, axis=-1, keepdims=True)
    return centered * lax.rsqrt(row_var + norm_eps) * norm_gain + norm_bias


def mm(left, right):
    return jnp.dot(left, right, preferred_element_type=F32)


def mm_t(left, right):
    return lax.dot_general(left, right, (((1,), (1,)), ((), ())), preferred_element_type=F32)


def t_mm(left, right):
    return lax.dot_general(left, right, (((0,), (0,)), ((), ())), preferred_element_type=F32)


def norm_stats(rows):
    mean = jnp.mean(rows, axis=-1, keepdims=True)
    centered = rows - mean
    var = jnp.mean(centered * centered, axis=-1, keepdims=True)
    rstd = lax.rsqrt(var + norm_eps)
    return centered * rstd, rstd


def norm_back(grad, xhat, rstd, gain):
    dxh = grad * gain
    first = jnp.mean(dxh, axis=-1, keepdims=True)
    second = jnp.mean(dxh * xhat, axis=-1, keepdims=True)
    return rstd * (dxh - first - xhat * second)


def col_sum(values):
    return jnp.sum(values, axis=0, keepdims=True)


def gelu_pair(x):
    cdf = 0.5 + 0.5 * lax.erf(x * (1.0 / math.sqrt(2.0)))
    density = jnp.exp(x * x * -0.5) * (1.0 / math.sqrt(2.0 * math.pi))
    return x * cdf, cdf + x * density


def accumulate(first, ref, value):
    @pl.when(first)
    def _():
        ref[...] = value

    @pl.when(jnp.logical_not(first))
    def _():
        ref[...] += value


def lane_half(shape, half):
    lane = lax.broadcasted_iota(jnp.int32, shape, 1)
    return (lane >= half * 64) & (lane < half * 64 + 64)


def keep_half(values, half):
    return jnp.where(lane_half(values.shape, half), values, jnp.zeros_like(values))


def select_tokens(rank_rows, cap):
    slot = lax.broadcasted_iota(jnp.int32, (cap, LANES), 0)
    parts = []
    for r in range(rank_rows.shape[0]):
        hit = slot == rank_rows[r : r + 1, :]
        parts.append(jnp.where(hit, 1.0, 0.0).astype(BF))
    return jnp.concatenate(parts, axis=1)


def cross_scores(kvf, queries_scaled, count):
    scores = mm_t(kvf, queries_scaled)
    slot = lax.broadcasted_iota(jnp.int32, scores.shape, 0)
    return jnp.where(slot < count, scores, masked_fill)


def cross_attend(start, norms, w_q, kvf, count):
    xhat, unused = norm_stats(start)
    query_in = (xhat * norms[0:1, :] + norms[1:2, :]).astype(BF)
    queries = mm(query_in, w_q[...]).astype(BF) * jnp.asarray(0.125, BF)
    scores = cross_scores(kvf, queries, count)
    top = jnp.max(scores, axis=0, keepdims=True)
    terms = jnp.exp(scores - top)
    total = jnp.sum(terms, axis=0, keepdims=True)
    prob = (terms * (1.0 / total)).astype(BF)
    return t_mm(kvf, prob).T.astype(BF), top + jnp.log(total)


def cross_fwd_kernel(latent, episode, norms, w_q, w_o, out_bias, kv, rank, count, h1, kvf_out, co_out, lse_out):
    cap = kvf_out.shape[1]
    start = latent[...].astype(F32) + episode[0]
    chunk = 8 * LANES
    chunks = kv.shape[0] // chunk

    def step(j, acc):
        sel = select_tokens(rank[0, pl.ds(pl.multiple_of(j * 8, 8), 8), :], cap)
        return acc + mm(sel, kv[pl.ds(pl.multiple_of(j * chunk, chunk), chunk), :])

    kvf = lax.fori_loop(0, chunks, step, jnp.zeros((cap, LANES), F32)).astype(BF)
    co, lse = cross_attend(start, norms, w_q, kvf, count[0, 0:1, 0:1])
    h1[...] = start + mm(co, w_o[...]) + out_bias[0:1, :]
    kvf_out[0] = kvf
    co_out[...] = co
    lse_out[0] = lse


def segment_hot(starts, ends, base, rows):
    row = lax.broadcasted_iota(jnp.int32, (16, rows), 1) + base
    return jnp.where((row >= starts[:, 0:1]) & (row < ends[:, 0:1]), 1.0, 0.0).astype(BF)


def segment_sums(hot, squares):
    high = squares.astype(BF)
    low = (squares - high.astype(F32)).astype(BF)
    return mm(hot, high) + mm(hot, low)


def grad_stats_kernel(base, starts, ends, summed, master, grad_sq, weight_sq):
    i = pl.program_id(0)
    rows = master.shape[0]
    hot = segment_hot(starts, ends, base[0] + i * rows, rows)
    grad = summed[...].astype(F32)
    accumulate(i == 0, grad_sq, col_sum(grad * grad))
    accumulate(i == 0, weight_sq, segment_sums(hot, master[...] * master[...]))


def lamb_kernel(base, stats, starts, ends, summed, master, one, two, grad_out, update_out, one_out, two_out, update_sq):
    i = pl.program_id(0)
    rows = master.shape[0]
    hot = segment_hot(starts, ends, base[0] + i * rows, rows)
    total_sq = jnp.sum(stats[0:1, :], axis=1, keepdims=True)
    clip = jnp.minimum(1.0, clip_fraction * math.sqrt(NPARAM) / (jnp.sqrt(total_sq) + 1e-06))
    grad = summed[...].astype(F32)
    grad_out[...] = grad
    clipped = clip * grad
    new_one = beta_one * one[...] + (1.0 - beta_one) * clipped
    new_two = beta_two * two[...] + (1.0 - beta_two) * clipped * clipped
    one_out[...] = new_one
    two_out[...] = new_two
    first_hat = new_one * (1.0 / (1.0 - beta_one**lamb_step))
    second_hat = new_two * (1.0 / (1.0 - beta_two**lamb_step))
    update = first_hat / (jnp.sqrt(second_hat) + adam_eps) + decay_rate * master[...]
    update_out[...] = update
    accumulate(i == 0, update_sq, segment_sums(hot, update * update))


BATCH = 256
HALF = 128
QUARTER = 64
MESH = pl.DeviceIdType.MESH


class Place:
    def __init__(self):
        self.z = lax.axis_index("kf")
        self.me = lax.axis_index("lat")
        self.core = lax.rem(self.me, 2)
        self.x = lax.rem(self.me // 2, 2)
        self.y = self.me // 4
        self.z_low = lax.rem(self.z, 2)
        self.z_high = self.z // 2
        self.sibling = (self.z, self.me + 1 - 2 * self.core)
        self.x_side = (self.z, self.me + 2 - 4 * self.x)
        self.y_side = (self.z, self.me + 4 - 8 * self.y)
        self.z_near = (self.z + 1 - 2 * self.z_low, self.me)
        self.z_far = (self.z + 2 - 4 * self.z_high, self.me)

    def z_other(self, step):
        return (lax.rem(self.z + step, 4), self.me)

    def lat_other(self, step):
        return (self.z, lax.rem(self.me + step, 8))


def remote(src, dst, send, recv, device):
    return pltpu.make_async_remote_copy(
        src_ref=src, dst_ref=dst, send_sem=send, recv_sem=recv, device_id=device, device_id_type=MESH
    )


def greet(devices):
    barrier = pltpu.get_barrier_semaphore()
    for device in devices:
        pl.semaphore_signal(barrier, inc=1, device_id=device, device_id_type=MESH)
    pl.semaphore_wait(barrier, len(devices))


def added(left, right):
    return (left.astype(F32) + right.astype(F32)).astype(BF)


class Reduction:
    lags = (0, 1, 3, 5, 7, 9, 11)
    plane = 2

    def __init__(self, place, shard, grads, out, bufs, sems):
        self.p = place
        self.grads = grads
        self.out = out
        self.own, self.rc, self.r1, self.r2, self.r3, self.r4, self.res = bufs
        self.own_sem, self.send, self.rc_sem, self.r1_sem, self.r2_sem, self.r3_sem, self.r4_sem, self.res_sem = sems
        self.shard = shard
        self.full = pl.cdiv(shard, BATCH)
        self.batches = self.full + self.plane
        self.back = self.full * BATCH - shard

    @staticmethod
    def scratch(shard):
        n = pl.cdiv(shard, BATCH) + Reduction.plane
        bufs = [
            pltpu.VMEM((2, 2, 2, BATCH, LANES), BF),
            pltpu.VMEM((n, 2, 2, BATCH, LANES), BF),
            pltpu.VMEM((n, 2, 2, HALF, LANES), BF),
            pltpu.VMEM((n, 2, HALF, LANES), BF),
            pltpu.VMEM((n, HALF, LANES), BF),
            pltpu.VMEM((n, QUARTER, LANES), BF),
            pltpu.VMEM((n, BATCH, LANES), BF),
        ]
        dma = pltpu.SemaphoreType.DMA
        sems = [dma((2,)), dma((10, 4)), dma((n,)), dma((n, 2)), dma((n, 2)), dma((n,)), dma((n,)), dma((n, 3))]
        return bufs + sems

    def row(self, i):
        p, n, held = i - self.plane, self.full, flat_rows_of()["tok_norm"] // BATCH
        late = p // (n - 4)
        b = (1 - late) * lax.rem(p + held + 4, n) + late * (held + lax.rem(p - (n - 4) + 2, 4))
        main = (i + n) // (n + self.plane)
        row = (1 - main) * (self.shard + i * BATCH) + main * (b * BATCH - (b // (n - 1)) * self.back)
        return pl.multiple_of(row, 16)

    def own_copy(self, i):
        slot = lax.rem(i, 2)
        src = self.grads.at[:, :, self.p.core, pl.ds(self.row(i), BATCH), :]
        return pltpu.make_async_copy(src, self.own.at[slot], self.own_sem.at[slot])

    def copies(self, stage, i):
        p, slot = self.p, lax.rem(i, 4)
        if stage == 0:
            src = self.grads.at[:, :, 1 - p.core, pl.ds(self.row(i), BATCH), :]
            return [remote(src, self.rc.at[i], self.send.at[0, slot], self.rc_sem.at[i], p.sibling)]
        if stage == 1:
            to_x = self.rc.at[i, :, 1 - p.x, pl.ds(0, HALF), :]
            to_y = self.rc.at[i, 1 - p.y, :, pl.ds(HALF, HALF), :]
            return [
                remote(to_x, self.r1.at[i, 0], self.send.at[1, slot], self.r1_sem.at[i, 0], p.x_side),
                remote(to_y, self.r1.at[i, 1], self.send.at[2, slot], self.r1_sem.at[i, 1], p.y_side),
            ]
        if stage == 2:
            to_y = self.r1.at[i, 0, 1 - p.y]
            to_x = self.r1.at[i, 1, 1 - p.x]
            return [
                remote(to_y, self.r2.at[i, 0], self.send.at[3, slot], self.r2_sem.at[i, 0], p.y_side),
                remote(to_x, self.r2.at[i, 1], self.send.at[4, slot], self.r2_sem.at[i, 1], p.x_side),
            ]
        if stage == 3:
            src = self.r2.at[i, 1 - p.z_low]
            return [remote(src, self.r3.at[i], self.send.at[5, slot], self.r3_sem.at[i], p.z_near)]
        if stage == 4:
            src = self.r3.at[i, pl.ds(pl.multiple_of((1 - p.z_high) * QUARTER, QUARTER), QUARTER), :]
            return [remote(src, self.r4.at[i], self.send.at[6, slot], self.r4_sem.at[i], p.z_far)]
        mine = self.res.at[i, pl.ds(pl.multiple_of(p.z_low * HALF + p.z_high * QUARTER, QUARTER), QUARTER), :]
        return [
            remote(mine, mine, self.send.at[6 + d, slot], self.res_sem.at[i, d - 1], p.z_other(d))
            for d in (1, 2, 3)
        ]

    def launch(self, stage, i):
        @pl.when(i >= (4 if stage < 3 else 4 + self.plane))
        def _():
            for copy in self.copies(stage, i - 4):
                copy.wait_send()

        for copy in self.copies(stage, i):
            copy.start()

    def landed(self, stage, i):
        for copy in self.copies(stage, i):
            copy.wait_recv()

    def work(self, stage, i):
        p = self.p
        if stage == 0:
            self.own_copy(i).start()
        elif stage == 1:
            self.landed(0, i)
            self.own_copy(i).wait()
            self.rc[i] = added(self.rc[i], self.own[lax.rem(i, 2)])
        elif stage == 2:
            self.landed(1, i)
            self.r1[i, 0] = added(self.r1[i, 0], self.rc[i, :, p.x, 0:HALF, :])
            self.r1[i, 1] = added(self.r1[i, 1], self.rc[i, p.y, :, HALF:BATCH, :])
        elif stage == 3:
            self.landed(2, i)
            self.r2[i, 0] = added(self.r2[i, 0], self.r1[i, 0, p.y])
            self.r2[i, 1] = added(self.r2[i, 1], self.r1[i, 1, p.x])
        elif stage == 4:
            self.landed(3, i)
            self.r3[i] = added(self.r3[i], self.r2[i, p.z_low])
        elif stage == 5:
            self.landed(4, i)
            part = self.r3[i, pl.ds(pl.multiple_of(p.z_high * QUARTER, QUARTER), QUARTER), :]
            at = pl.multiple_of(p.z_low * HALF + p.z_high * QUARTER, QUARTER)
            self.res[i, pl.ds(at, QUARTER), :] = added(self.r4[i], part)
        else:
            self.landed(5, i)
            self.out[pl.ds(self.row(i), BATCH), :] = self.res[i]
        if stage == 3:
            pl.when(i >= self.plane)(lambda: self.launch(stage, i))
        elif stage < 6:
            self.launch(stage, i)

    def tick(self, t):
        for stage, lag in enumerate(self.lags):
            i = t - lag

            @pl.when((i >= (0 if stage < 4 else self.plane)) & (i < self.batches))
            def _(stage=stage, i=i):
                self.work(stage, i)

    def ticks(self):
        return self.batches + self.lags[-1]

    def finish(self):
        for stage in range(6):
            for back in range(4):
                for copy in self.copies(stage, self.batches - 4 + back):
                    copy.wait_send()

    def partners(self):
        p = self.p
        return [p.sibling, p.x_side, p.y_side] + [p.z_other(d) for d in (1, 2, 3)]


def share_all(place, block, send, recv):
    mine = block.at[place.me]
    copies = [
        remote(mine, mine, send.at[d - 1], recv.at[d - 1], place.lat_other(d)) for d in range(1, 8)
    ]
    for copy in copies:
        copy.start()
    for copy in copies:
        copy.wait()


STAT_ROWS = 56


def token_backward(grad_kv, tokens, tok_normed, w_kv, tok_norm, token_grad, kv_grad, edge):
    kv_grad[...] = t_mm(tok_normed[...], grad_kv).astype(BF)
    grad = mm_t(grad_kv, w_kv[...])
    xhat, rstd = norm_stats(tokens[...].astype(F32))
    token_grad[...] = norm_back(grad, xhat, rstd, tok_norm[0:1, :]).astype(BF)
    gain, bias = col_sum(grad * xhat), col_sum(grad)
    parts = [half[:, j * LANES : (j + 1) * LANES] for half in (gain, bias) for j in range(DIN // LANES)]
    keep = edge.shape[0] - len(parts)
    edge[...] = jnp.concatenate([edge[...].astype(F32)[0:keep, :]] + parts, axis=0).astype(BF)


def reduce_kernel(
    bias_owner, bias_at, starts, ends, unused_flat, master, tokens, tok_normed, w_kv, tok_norm,
    summed, stats, token_grad, grads, *scratch,
):
    place = Place()
    block, block_send, block_recv, edge, kv_grad, edge_sem = scratch[:6]
    shard = master.shape[0]
    red = Reduction(place, shard, grads, summed, scratch[6:13], scratch[13:])
    greet([place.lat_other(d) for d in range(1, 8)] + [place.z_other(d) for d in (1, 2, 3)])
    at = flat_rows_of()
    edge_rows = grads.at[0, 0, 0, pl.ds(at["tok_norm"] // 16 * 16, 16), :]
    fetch = pltpu.make_async_copy(edge_rows, edge, edge_sem.at[0])
    fetch.start()
    ready = red.lags[3] + red.plane
    lax.fori_loop(0, ready, lambda t, c: (red.tick(t), c)[1], 0)
    fetch.wait()
    grad_kv = jnp.concatenate([red.r2[i, h] for i in range(red.plane) for h in range(2)], axis=0)
    token_backward(grad_kv, tokens, tok_normed, w_kv, tok_norm, token_grad, kv_grad, edge)
    writes = [
        pltpu.make_async_copy(edge, edge_rows, edge_sem.at[0]),
        pltpu.make_async_copy(kv_grad, grads.at[0, 0, 0, pl.ds(at["w_kv"], DIN), :], edge_sem.at[1]),
    ]
    for copy in writes:
        copy.start()
    for copy in writes:
        copy.wait()
    lax.fori_loop(ready, red.ticks(), lambda t, c: (red.tick(t), c)[1], 0)
    step = 784
    grad_sq = jnp.zeros((1, LANES), F32)
    weight_sq = jnp.zeros((16, LANES), F32)
    for j in range(shard // step):
        at = slice(j * step, (j + 1) * step)
        part = summed[at, :].astype(F32)
        grad_sq = grad_sq + col_sum(part * part)
        hot = segment_hot(starts, ends, place.me * shard + j * step, step)
        part = master[at, :]
        weight_sq = weight_sq + segment_sums(hot, part * part)
    bias = summed[bias_at : bias_at + 2 * FF // LANES, :].astype(F32)
    bias = jnp.where(place.me == bias_owner, bias, 0.0)
    head = jnp.concatenate([grad_sq, jnp.zeros((7, LANES), F32), weight_sq, bias], axis=0)
    block[pl.ds(place.me, 1)] = head[None]
    share_all(place, block, block_send, block_recv)
    total = block[0]
    for s in range(1, 8):
        total = total + block[s]
    stats[...] = total
    red.finish()


def trust_kernel(update_sq, stats, trust, block, send, recv):
    place = Place()
    greet([place.lat_other(d) for d in range(1, 8)])
    block[pl.ds(place.me, 1)] = update_sq[...][None]
    share_all(place, block, send, recv)
    total = block[0]
    for s in range(1, 8):
        total = total + block[s]
    update_norm = jnp.sqrt(jnp.sum(total, axis=1, keepdims=True))
    weight_norm = jnp.sqrt(jnp.sum(stats[8:24, :], axis=1, keepdims=True))
    trust[...] = jnp.broadcast_to(weight_norm / (update_norm + 1e-06), (16, LANES))


def relayout(whole, row, stage, dst, rows, cols):
    wide = cols // LANES
    block = min(rows, 2048 // wide // 128 * 128)

    def step(i, carry):
        at = pl.multiple_of(row + i * (block * wide), 16)
        stage[0 : block * wide, :] = whole[pl.ds(at, block * wide), :].astype(F32)
        for j in range(wide):
            part = stage[pl.ds(j, block, stride=wide), :]
            dst[pl.ds(pl.multiple_of(i * block, 16), block), j * LANES : (j + 1) * LANES] = part.astype(BF)
        return carry

    lax.fori_loop(0, rows // block, step, 0)


def small_matrix(whole, row, stage, rows, cols):
    wide = cols // LANES
    stage[0 : rows * wide, :] = whole[row : row + rows * wide, :].astype(F32)
    return jnp.concatenate([stage[pl.ds(j, rows, stride=wide), :] for j in range(wide)], axis=1)


class Gather:
    def __init__(self, place, whole, shard, chunks, send, recv):
        self.p, self.whole, self.shard, self.chunks, self.send, self.recv = place, whole, shard, chunks, send, recv
        p = place
        x_index, y_index = p.x_side[1], p.y_side[1]
        low = p.z_low
        self.first = x_index + low * (y_index - x_index)
        self.second = y_index + low * (x_index - y_index)
        self.diagonal = x_index + 4 - 8 * p.y

    def copy(self, kind, k):
        p = self.p
        block = (p.me, p.me, self.first, self.first, self.first, self.diagonal, self.second)[kind]
        target = (
            (p.z, self.first), p.sibling, (p.z, self.second), p.z_near, p.sibling, p.sibling, p.sibling
        )[kind]
        row, count = self.chunks[k]
        ref = self.whole.at[pl.ds(pl.multiple_of(block * self.shard + row, 16), count), :]
        return remote(ref, ref, self.send.at[kind, k], self.recv.at[kind, k], target)

    def tick(self, t):
        n = len(self.chunks)
        if t < n:
            self.copy(0, t).start()
            self.copy(1, t).start()
        if 0 <= t - 2 < n:
            self.copy(0, t - 2).wait_recv()
            for kind in (2, 3, 4):
                self.copy(kind, t - 2).start()
        if 0 <= t - 4 < n:
            self.copy(2, t - 4).wait_recv()
            self.copy(5, t - 4).start()
            self.copy(3, t - 4).wait_recv()
            self.copy(6, t - 4).start()
        if 0 <= t - 5 < n:
            for kind in (1, 4, 5, 6):
                self.copy(kind, t - 5).wait_recv()

    def ticks(self):
        return len(self.chunks) + 5

    def finish(self):
        for k in range(len(self.chunks)):
            for kind in range(7):
                self.copy(kind, k).wait_send()


class KeyExchange:
    def __init__(self, place, keys, send, recv):
        self.p, self.keys, self.send, self.recv = place, keys, send, recv
        self.x_index, self.y_index = place.x_side[1], place.y_side[1]
        self.diagonal = self.x_index + 4 - 8 * place.y

    def copy(self, kind):
        p = self.p
        half = self.keys.shape[1] // 2
        low, high, full = pl.ds(0, half), pl.ds(half, half), pl.ds(0, 2 * half)
        block, rows, target = (
            (p.me, full, p.x_side), (p.me, full, p.y_side), (p.me, full, p.sibling),
            (self.x_index, low, p.y_side), (self.y_index, high, p.x_side),
            (self.x_index, full, p.sibling), (self.y_index, full, p.sibling), (self.diagonal, full, p.sibling),
        )[kind]
        ref = self.keys.at[block, rows, :]
        return remote(ref, ref, self.send.at[kind], self.recv.at[kind], target)

    def step(self, s):
        if s == 0:
            waits, starts = (), (0, 1, 2)
        elif s == 1:
            waits, starts = (0, 1), (3, 4, 5, 6)
        elif s == 2:
            waits, starts = (3, 4), (7,)
        else:
            waits, starts = (2, 5, 6, 7), ()
        for kind in waits:
            self.copy(kind).wait_recv()
        for kind in starts:
            self.copy(kind).start()

    def finish(self):
        for kind in range(8):
            self.copy(kind).wait_send()


def flat_rows_of():
    rows, at = {}, 0
    for name, shape in param_layout():
        rows[name] = at // LANES
        at += math.prod(shape)
    return rows


def gather_chunks(shard):
    at = flat_rows_of()
    tail = at["hid_bias"] % shard // 16 * 16
    chunks = [(at["episode"], at["w_o"] - at["episode"]), (tail, shard - tail), (at["w_o"], at["w_qkv"] - at["w_o"])]
    for low, high in ((0, at["episode"]), (at["w_qkv"], tail)):
        while low < high:
            count = min(512, high - low)
            chunks.append((low, count))
            low += count
    return chunks


def begin_kernel(
    chunks, master, tokens, ids, hot,
    up_one, down_one, qkv_w, so_w, up_two, down_two,
    latent, norms, hid_bias, out_bias, w_q, w_o, w_kv, tok_norm, tok_normed, episode, rank, counts,
    kvf_out, co_out, lse_out, h1,
    whole, stage, all_ids, keys, m_up_one, m_down_one, m_qkv, m_so, m_up_two, m_down_two,
    episodes_held, send, recv, key_send, key_recv, id_send, id_recv, out_sem,
):
    place = Place()
    shard = master.shape[0]
    frames, cap = kvf_out.shape[0], kvf_out.shape[1]
    gather = Gather(place, whole, shard, chunks, send, recv)
    exchange = KeyExchange(place, keys, key_send, key_recv)
    at = flat_rows_of()
    greet([place.lat_other(d) for d in range(1, 8)] + [place.z_near])
    all_ids[pl.ds(place.me, 1)] = ids[...][None]
    id_copies = [
        remote(all_ids.at[place.me], all_ids.at[place.me], id_send.at[d - 1], id_recv.at[d - 1], place.lat_other(d))
        for d in range(1, 8)
    ]
    for copy in id_copies:
        copy.start()
    own_at = place.me * shard
    for row, count in chunks:
        whole[pl.ds(pl.multiple_of(own_at + row, 16), count), :] = master[row : row + count, :].astype(BF)
    for t in range(4):
        gather.tick(t)

    for copy in id_copies:
        copy.wait_recv()
    tags = jnp.concatenate([all_ids[s] for s in range(8)], axis=0)
    low = lax.broadcasted_iota(jnp.int32, (LANES, LANES), 0)
    high = lax.broadcasted_iota(jnp.int32, (LANES, LANES), 1)
    upto = jnp.where(low <= high, 1.0, 0.0).astype(BF)
    n = tags.shape[0]
    below = jnp.where(
        lax.broadcasted_iota(jnp.int32, (n, n), 1) < lax.broadcasted_iota(jnp.int32, (n, n), 0), 1.0, 0.0
    ).astype(BF)
    for f in range(frames):
        hit = tags == place.me * frames + f
        hit_low = jnp.where(hit, 1.0, 0.0).astype(BF)
        inside = mm(hit_low, upto)
        row_total = jnp.broadcast_to(inside[:, LANES - 1 : LANES], (n, LANES))
        before = mm(below, row_total.astype(BF))
        place_in = (inside + before).astype(jnp.int32) - 1
        rank[f] = jnp.where(hit, place_in, -1)
        total = jnp.sum(row_total[:, 0:1], axis=0, keepdims=True).astype(jnp.int32)
        counts[f] = jnp.broadcast_to(total, (8, LANES))
    for t in range(4, 7):
        gather.tick(t)

    pair = whole[at["tok_norm"] // 16 * 16 : at["lat_norms"], :].astype(F32)
    pair = pair[at["tok_norm"] % 16 : at["tok_norm"] % 16 + 4, :]
    tok_norm[...] = jnp.concatenate(
        [
            jnp.concatenate([pair[0:1], pair[1:2]], axis=1),
            jnp.concatenate([pair[2:3], pair[3:4]], axis=1),
        ],
        axis=0,
    )
    w_kv[...] = whole[at["w_kv"] : at["w_kv"] + DIN, :]
    xhat, unused = norm_stats(tokens[...].astype(F32))
    normed = (xhat * tok_norm[0:1, :] + tok_norm[1:2, :]).astype(BF)
    tok_normed[...] = normed
    keys[pl.ds(place.me, 1)] = mm(normed, w_kv[...]).astype(BF)[None]
    exchange.step(0)
    norms[...] = small_matrix(whole, at["lat_norms"], stage, 8, D)
    hid_bias[...] = small_matrix(whole, at["hid_bias"], stage, 2, FF)
    out_bias[...] = small_matrix(whole, at["out_bias"], stage, 4, D)
    episode_rows = mm(hot[...], small_matrix(whole, at["episode"], stage, 16, D).astype(BF))
    gather.tick(7)
    exchange.step(1)
    packed = whole[at["w_q"] : at["w_q"] + D // 2, :].astype(F32)
    stage[pl.ds(0, D // 2, stride=2), :] = packed
    stage[pl.ds(1, D // 2, stride=2), :] = pltpu.roll(packed, CH, 1)
    w_q[...] = keep_half(stage[0:D, :], 0).astype(BF)
    w_o[0:CH, :] = jnp.zeros((CH, D), BF)
    w_o[CH : 2 * CH, :] = small_matrix(whole, at["w_o"], stage, CH, D).astype(BF)
    gather.tick(8)
    exchange.step(2)
    for t in range(9, 12):
        gather.tick(t)
    exchange.step(3)
    relayout(whole, 0, stage, latent, LAT, D)

    chunk = 8 * LANES
    episodes_held[...] = episode_rows[0:8, :]

    def attend(f, carry):
        for tick in range(12, gather.ticks()):

            @pl.when(f == (tick - 12) * frames // (gather.ticks() - 12))
            def _(tick=tick):
                gather.tick(tick)

        row = episodes_held[pl.ds(f, 1), :]
        start = latent[...].astype(F32) + row
        episode[pl.ds(f, 1)] = row[None]

        def pick(j, acc):
            sel = select_tokens(rank[f, pl.ds(pl.multiple_of(8 * j, 8), 8), :], cap)
            return acc + mm(sel, keys[pl.ds(2 * j, 2)].reshape(chunk, LANES))

        kvf = lax.fori_loop(0, n // 8, pick, jnp.zeros((cap, LANES), F32)).astype(BF)
        co, lse = cross_attend(start, norms, w_q, kvf, counts[f, 0:1, 0:1])
        rows = pl.ds(pl.multiple_of(f * LAT, LAT), LAT)
        h1[rows, :] = start + mm(co, w_o[...]) + out_bias[0:1, :]
        kvf_out[f] = kvf
        co_out[rows, :] = co
        lse_out[f] = lse
        return carry

    lax.fori_loop(0, frames, attend, 0)

    big = (
        (up_one, m_up_one, at["w_up"], D, FF),
        (down_one, m_down_one, at["w_down"], FF, D),
        (qkv_w, m_qkv, at["w_qkv"], D, 3 * D),
        (so_w, m_so, at["w_so"], D, D),
        (up_two, m_up_two, at["w_up"] + D * FF // LANES, D, FF),
        (down_two, m_down_two, at["w_down"] + D * FF // LANES, FF, D),
    )
    outs = []
    for j, (out, held, row, rows, cols) in enumerate(big):
        relayout(whole, row, stage, held, rows, cols)
        outs.append(pltpu.make_async_copy(held, out, out_sem.at[j]))
        outs[-1].start()
    for copy in outs:
        copy.wait()
    for copy in id_copies:
        copy.wait_send()
    exchange.finish()
    gather.finish()


def begin_all(master_rows, token_rows, ids, hot, frames, cap):
    shard = master_rows.shape[0]
    tokens = token_rows.shape[0]
    total = 8 * tokens
    chunks = gather_chunks(shard)
    vmem = pl.BlockSpec(memory_space=pltpu.VMEM)
    anywhere = pl.BlockSpec(memory_space=pl.ANY)
    matrices = [(D, FF), (FF, D), (D, 3 * D), (D, D), (D, FF), (FF, D)]
    dma = pltpu.SemaphoreType.DMA
    return pl.pallas_call(
        functools.partial(begin_kernel, chunks),
        out_shape=[shaped(m, BF) for m in matrices]
        + [
            shaped((LAT, D), BF),
            shaped((8, D)),
            shaped((2, FF)),
            shaped((4, D)),
            shaped((D, LANES), BF),
            shaped((LANES, D), BF),
            shaped((DIN, LANES), BF),
            shaped((2, DIN)),
            shaped((tokens, DIN), BF),
            shaped((frames, 1, D)),
            shaped((frames, total // LANES, LANES), jnp.int32),
            shaped((frames, 8, LANES), jnp.int32),
            shaped((frames, cap, LANES), BF),
            shaped((frames * LAT, LANES), BF),
            shaped((frames, 1, LAT)),
            shaped((frames * LAT, D)),
        ],
        in_specs=[vmem] * 4,
        out_specs=[anywhere] * 6 + [vmem] * 16,
        scratch_shapes=[
            pltpu.VMEM((8 * shard, LANES), BF),
            pltpu.VMEM((2048, LANES), F32),
            pltpu.VMEM((8, tokens // LANES, LANES), jnp.int32),
            pltpu.VMEM((8, tokens, LANES), BF),
        ]
        + [pltpu.VMEM(m, BF) for m in matrices]
        + [
            pltpu.VMEM((8, D), F32),
            dma((7, len(chunks))), dma((7, len(chunks))), dma((8,)), dma((8,)), dma((7,)), dma((7,)), dma((6,)),
        ],
        compiler_params=pltpu.CompilerParams(
            collective_id=3, has_side_effects=True, vmem_limit_bytes=56 * MIB
        ),
    )(master_rows, token_rows, ids, hot)


FCHUNK = 512


def add_flat(acc, row, part):
    wide = part.shape[1] // LANES
    for j in range(wide):
        at = pl.ds(row + j, part.shape[0], stride=wide)
        acc[at, :] = acc[at, :] + part[:, j * LANES : (j + 1) * LANES]


def to_flat(stage, matrix):
    rows, wide = matrix.shape[0], matrix.shape[1] // LANES
    for j in range(wide):
        stage[pl.ds(j, rows, stride=wide), :] = matrix[:, j * LANES : (j + 1) * LANES]
    return stage[0 : rows * wide, :]


def chunk_of(c, size=FCHUNK):
    return pl.ds(pl.multiple_of(c * size, LANES), size)


def feed_forward(rows, gain, bias, up_bias, down_bias, w_up, w_down, act_ref, slope_ref, normed_ref, total_ref):
    xhat, rstd = norm_stats(rows)
    normed_ref[...] = (xhat * gain + bias).astype(BF)
    total_ref[...] = rows + down_bias

    def step(c, carry):
        at = chunk_of(c)
        act, slope = gelu_pair(mm(normed_ref[...], w_up[:, at]) + up_bias[:, at])
        act = act.astype(BF)
        act_ref[:, at] = act
        slope_ref[:, at] = slope.astype(BF)
        total_ref[...] += mm(act, w_down[at, :])
        return carry

    lax.fori_loop(0, FF // FCHUNK, step, 0)


def feed_back(grad_ref, normed_ref, xhat, rstd, gain, act, slope, w_up, w_down, acc_up, acc_down, dhid, dnorm, dout, work):
    work[...] = jnp.zeros(work.shape, F32)

    def step(c, carry):
        at = chunk_of(c)
        dpre = (mm_t(grad_ref[...], w_down[at, :]) * slope[:, at].astype(F32)).astype(BF)
        dhid[:, at] += col_sum(dpre.astype(F32))
        work[...] += mm_t(dpre, w_up[:, at])
        part = t_mm(normed_ref[...], dpre)
        for j in range(FCHUNK // LANES):
            rows = pl.ds(c * (FCHUNK // LANES) + j, D, stride=FF // LANES)
            acc_up[rows, :] = acc_up[rows, :] + part[:, j * LANES : (j + 1) * LANES]
        add_flat(acc_down, c * FCHUNK * (D // LANES), t_mm(act[:, at], grad_ref[...]))
        return carry

    lax.fori_loop(0, FF // FCHUNK, step, 0)
    grad_normed = work[...]
    dnorm[...] += jnp.concatenate([col_sum(grad_normed * xhat), col_sum(grad_normed)], axis=0)
    dout[...] += col_sum(grad_ref[...].astype(F32))
    return norm_back(grad_normed, xhat, rstd, gain)


def clear(first, refs):
    @pl.when(first)
    def _():
        for ref in refs:
            ref[...] = jnp.zeros_like(ref)


def flat_spans(row, count, shard, extra):
    spans, done = [], 0
    while done < count:
        part = min(count - done, shard - (row + done) % shard)
        spans.append((done, part, row + done + (row + done) // shard * extra))
        done += part
    return spans


def write_flat(flat, low, pieces, sems, shard, extra):
    pending = {}
    for j, (acc, row) in enumerate(pieces):
        count = acc.shape[0]
        slot = j % 2
        for copy in pending.get(slot, []):
            copy.wait()
        low[slot, 0:count, :] = acc[...].astype(BF)
        pending[slot] = [
            pltpu.make_async_copy(low.at[slot, pl.ds(off, part), :], flat.at[pl.ds(at, part), :], sems.at[slot, k])
            for k, (off, part, at) in enumerate(flat_spans(row, count, shard, extra))
        ]
        for copy in pending[slot]:
            copy.start()
    for copies in pending.values():
        for copy in copies:
            copy.wait()


class FrameExchange:
    def __init__(self, place, source, grad, held, result, sems):
        self.p, self.source, self.grad, self.held, self.result = place, source, grad, held, result
        self.in_send, self.in_recv, self.out_send, self.out_recv, self.own_in, self.own_out = sems
        self.frames, self.rows = grad.shape[0], source.shape[1]

    @staticmethod
    def scratch(frames):
        dma = pltpu.SemaphoreType.DMA
        return [dma((frames, 7))] * 4 + [dma((frames,))] * 2

    def block(self, index):
        return pl.ds(pl.multiple_of(index * self.rows, 16), self.rows)

    def arriving(self, f, d):
        target = self.p.lat_other(d)
        src = self.source.at[target[1] * self.frames + f]
        dst = self.grad.at[f, self.block(self.p.me), :]
        return remote(src, dst, self.in_send.at[f, d - 1], self.in_recv.at[f, d - 1], target)

    def own_arriving(self, f):
        src = self.source.at[self.p.me * self.frames + f]
        return pltpu.make_async_copy(src, self.grad.at[f, self.block(self.p.me), :], self.own_in.at[f])

    def leaving(self, f, d):
        target = self.p.lat_other(d)
        src = self.held.at[f, self.block(target[1]), :]
        dst = self.result.at[self.p.me * self.frames + f]
        return remote(src, dst, self.out_send.at[f, d - 1], self.out_recv.at[f, d - 1], target)

    def own_leaving(self, f):
        dst = self.result.at[self.p.me * self.frames + f]
        return pltpu.make_async_copy(self.held.at[f, self.block(self.p.me), :], dst, self.own_out.at[f])

    def begin(self):
        greet([self.p.lat_other(d) for d in range(1, 8)])
        for f in range(self.frames):
            self.own_arriving(f).start()
            for d in range(1, 8):
                self.arriving(f, d).start()

    def await_frame(self, f):
        self.own_arriving(f).wait()
        for d in range(1, 8):
            self.arriving(f, d).wait_recv()

    def send_frame(self, f):
        self.own_leaving(f).start()
        for d in range(1, 8):
            self.leaving(f, d).start()

    def finish(self):
        def step(f, carry):
            self.own_leaving(f).wait()
            for d in range(1, 8):
                self.arriving(f, d).wait_send()
                self.leaving(f, d).wait()
            return carry

        lax.fori_loop(0, self.frames, step, 0)


def forward_kernel(
    reach, shard, extra, h1, grad, norms, hid_bias, out_bias, up_one, down_one, w_qkv, w_so, up_two, down_two,
    h2_out, qkv, lse_out, mixed_out, act_one, slope_one, latents, g3, dhid, dnorm, dout, flat,
    act_two, slope_two, acc_up, acc_down, low, normed, mixed_t, work, sems, *shared,
):
    step = pl.program_id(0)
    if reach:
        place = Place()
        traffic = FrameExchange(place, grad, shared[0], shared[1], latents, shared[2:])
        pl.when(step == 0)(traffic.begin)
        grad = shared[0].at[step]
    clear(step == 0, (acc_up, acc_down, dhid, dnorm, dout))
    feed_forward(
        h1[...], norms[2:3, :], norms[3:4, :], hid_bias.at[0:1], out_bias[1:2, :], up_one, down_one, act_one,
        slope_one, normed, h2_out,
    )
    xhat, unused = norm_stats(h2_out[...])
    normed[...] = (xhat * norms[4:5, :] + norms[5:6, :]).astype(BF)

    def project(c, carry):
        at = chunk_of(c)
        qkv[:, at] = mm(normed[...], w_qkv[:, at]).astype(BF)
        return carry

    lax.fori_loop(0, 3, project, 0)
    scale = jnp.asarray(0.125, BF)

    def attend(pair, carry):
        query_pair = qkv[:, chunk_of(pair, LANES)] * scale
        key_pair = qkv[:, chunk_of(pair + D // LANES, LANES)]
        value_t = qkv[:, chunk_of(pair + 2 * D // LANES, LANES)].T
        for half in range(2):
            scores = mm_t(key_pair, keep_half(query_pair, half))
            top = jnp.max(scores, axis=0, keepdims=True)
            terms = jnp.exp(scores - top)
            total = jnp.sum(terms, axis=0, keepdims=True)
            prob = (terms * (1.0 / total)).astype(BF)
            lse_out[0, pl.ds(2 * pair + half, 1), :] = top + jnp.log(total)
            at = pl.ds(pl.multiple_of(pair * LANES + half * HEAD_DIM, HEAD_DIM), HEAD_DIM)
            mixed_t[at, :] = mm(value_t[half * HEAD_DIM : (half + 1) * HEAD_DIM, :], prob)
        return carry

    lax.fori_loop(0, HEADS // 2, attend, 0)
    mixed = mixed_t[...].T.astype(BF)
    mixed_out[...] = mixed
    h3 = h2_out[...] + mm(mixed, w_so[...]) + out_bias[2:3, :]
    feed_forward(
        h3, norms[6:7, :], norms[7:8, :], hid_bias.at[1:2], out_bias[3:4, :], up_two, down_two, act_two, slope_two,
        normed, work,
    )
    if reach:
        shared[1][step] = work[...].astype(BF)
        traffic.send_frame(step)
        traffic.await_frame(step)
    else:
        latents[...] = work[...].astype(BF)
    xhat, rstd = norm_stats(h3)
    g3[...] = grad[...].astype(F32) + feed_back(
        grad, normed, xhat, rstd, norms[6:7, :], act_two, slope_two, up_two, down_two,
        acc_up, acc_down, dhid, dnorm, dout, work,
    )

    @pl.when(step == pl.num_programs(0) - 1)
    def _():
        at = flat_rows_of()
        half = D * FF // LANES
        write_flat(flat, low, [(acc_up, at["w_up"] + half), (acc_down, at["w_down"] + half)], sems, shard, extra)
        if reach:
            traffic.finish()


def backward_kernel(
    shard, extra, kv_rows, qkv, lse, mixed, g3, h2, h1, act_one, slope_one, kvf_in, co_in, cross_lse, rank, count, episode, hot,
    latent, norms, w_so, w_qkv, up_one, down_one, w_q, w_o, dhid_two, dnorm_two, dout_two, flat_in,
    flat,
    dqkv, acc_up, acc_down, acc_qkv, acc_so, acc_latent, acc_q, acc_o, acc_episode,
    dhid, dnorm_sa, dnorm_one, dnorm_cross, dout_so, dout_one, dout_cross, stage, low, normed, grad_mixed, grad_low,
    work, dkv_t, sems,
):
    step = pl.program_id(0)
    clear(
        step == 0,
        (
            acc_up, acc_down, acc_qkv, acc_so, acc_latent, acc_q, acc_o, acc_episode, dhid, dnorm_sa, dnorm_one,
            dnorm_cross, dout_so, dout_one, dout_cross, dkv_t,
        ),
    )
    scale = jnp.asarray(0.125, BF)
    grad_three = g3[...]
    grad_low[...] = grad_three.astype(BF)
    dout_so[...] += col_sum(grad_low[...].astype(F32))
    add_flat(acc_so, 0, t_mm(mixed[...], grad_low[...]))
    grad_mixed[...] = mm_t(grad_low[...], w_so[...]).astype(BF)

    def attend(pair, carry):
        query_at = chunk_of(pair, LANES)
        key_at = chunk_of(pair + D // LANES, LANES)
        value_at = chunk_of(pair + 2 * D // LANES, LANES)
        query_pair = qkv[:, query_at] * scale
        key_pair = qkv[:, key_at]
        value_pair = qkv[:, value_at]
        grad_pair = grad_mixed[:, query_at]
        key_t = key_pair.T
        query_t = []
        grad_key = jnp.zeros((LAT, LANES), F32)
        grad_value = jnp.zeros((LAT, LANES), F32)
        for half in range(2):
            query = keep_half(query_pair, half)
            grad_head = keep_half(grad_pair, half)
            prob = jnp.exp(mm_t(key_pair, query) - lse[0, pl.ds(2 * pair + half, 1), :])
            grad_value = grad_value + mm(prob.astype(BF), grad_head)
            weighted = prob * mm_t(value_pair, grad_head)
            grad_score = (weighted - prob * col_sum(weighted)).astype(BF)
            grad_key = grad_key + mm(grad_score, query)
            query_t.append(mm(key_t[half * HEAD_DIM : (half + 1) * HEAD_DIM, :], grad_score))
        dqkv[:, query_at] = (jnp.concatenate(query_t, axis=0).T * 0.125).astype(BF)
        dqkv[:, key_at] = grad_key.astype(BF)
        dqkv[:, value_at] = grad_value.astype(BF)
        return carry

    lax.fori_loop(0, HEADS // 2, attend, 0)
    xhat, rstd = norm_stats(h2[...])
    normed[...] = (xhat * norms[4:5, :] + norms[5:6, :]).astype(BF)
    work[...] = jnp.zeros(work.shape, F32)

    def project(c, carry):
        at = chunk_of(c)
        work[...] += mm_t(dqkv[:, at], w_qkv[:, at])
        part = t_mm(normed[...], dqkv[:, at])
        for j in range(D // LANES):
            rows = pl.ds(c * (D // LANES) + j, D, stride=3 * D // LANES)
            acc_qkv[rows, :] = acc_qkv[rows, :] + part[:, j * LANES : (j + 1) * LANES]
        return carry

    lax.fori_loop(0, 3, project, 0)
    grad_in = work[...]
    dnorm_sa[...] += jnp.concatenate([col_sum(grad_in * xhat), col_sum(grad_in)], axis=0)
    grad_two = grad_three + norm_back(grad_in, xhat, rstd, norms[4:5, :])

    xhat, rstd = norm_stats(h1[...])
    normed[...] = (xhat * norms[2:3, :] + norms[3:4, :]).astype(BF)
    grad_low[...] = grad_two.astype(BF)
    grad_one = grad_two + feed_back(
        grad_low, normed, xhat, rstd, norms[2:3, :], act_one, slope_one, up_one, down_one,
        acc_up, acc_down, dhid, dnorm_one, dout_one, work,
    )

    cap = kvf_in.shape[1]
    start = latent[...].astype(F32) + episode[0]
    xhat, rstd = norm_stats(start)
    query_in = (xhat * norms[0:1, :] + norms[1:2, :]).astype(BF)
    queries = mm(query_in, w_q[...]).astype(BF) * scale
    kvf = kvf_in[0]
    branch = grad_one.astype(BF)
    grad_co = mm_t(branch, w_o[...]).astype(BF)
    acc_o[...] += t_mm(co_in[...], branch)
    dout_cross[...] += col_sum(branch.astype(F32))
    scores = cross_scores(kvf, queries, count[0, 0:1, 0:1])
    prob = jnp.exp(scores - cross_lse[0])
    weighted = prob * mm_t(kvf, grad_co)
    grad_score = (weighted - prob * col_sum(weighted)).astype(BF)
    grad_kv = (mm(grad_score, queries) + mm(prob.astype(BF), grad_co)).astype(BF)
    grad_query = (t_mm(kvf, grad_score).T * 0.125).astype(BF)
    acc_q[...] += t_mm(query_in, grad_query)
    grad_in = mm_t(grad_query, w_q[...])
    grad_start = grad_one + norm_back(grad_in, xhat, rstd, norms[0:1, :])
    dnorm_cross[...] += jnp.concatenate([col_sum(grad_in * xhat), col_sum(grad_in)], axis=0)
    add_flat(acc_latent, 0, grad_start)
    acc_episode[...] += hot[0, :, 0:1] * col_sum(grad_start)
    grad_kv_t = grad_kv.T
    chunk = 8 * LANES

    def scatter(j, carry):
        sel = select_tokens(rank[0, pl.ds(pl.multiple_of(j * 8, 8), 8), :], cap)
        at = pl.ds(pl.multiple_of(j * chunk, chunk), chunk)
        dkv_t[:, at] = added(dkv_t[:, at], mm(grad_kv_t, sel))
        return carry

    lax.fori_loop(0, dkv_t.shape[1] // chunk, scatter, 0)

    @pl.when(step == pl.num_programs(0) - 1)
    def _():
        at = flat_rows_of()
        write_flat(
            flat, low,
            [
                (acc_up, at["w_up"]), (acc_down, at["w_down"]), (acc_qkv, at["w_qkv"]), (acc_so, at["w_so"]),
                (acc_latent, 0),
            ],
            sems, shard, extra,
        )
        small = at["w_qkv"] - at["w_q"]
        first = at["w_q"] - at["episode"]
        head = at["lat_norms"] - at["episode"]
        low[0, 0:first, :] = jnp.zeros((first, LANES), BF)
        norm_grads = jnp.concatenate([dnorm_cross[...], dnorm_one[...], dnorm_sa[...], dnorm_two[...]], axis=0)
        rows = jnp.concatenate([to_flat(stage, acc_episode[...])[0 : EPISODES * (D // LANES), :], jnp.zeros((head - EPISODES * (D // LANES), LANES), F32)], axis=0)
        rows = jnp.concatenate([rows, to_flat(stage, norm_grads)], axis=0)
        low[0, 0 : rows.shape[0], :] = rows.astype(BF)
        stage[0:D, :] = acc_q[...]
        even = stage[pl.ds(0, D // 2, stride=2), :]
        odd = pltpu.roll(stage[pl.ds(1, D // 2, stride=2), :], CH, 1)
        low[0, first : first + D // 2, :] = jnp.where(lane_half(even.shape, 0), even, odd).astype(BF)
        low[0, first + D // 2 : first + small, :] = to_flat(stage, acc_o[CH : 2 * CH, :]).astype(BF)
        hid = to_flat(stage, jnp.concatenate([dhid[...], dhid_two[...]], axis=0))
        low[1, 0 : hid.shape[0], :] = hid.astype(BF)
        outs = jnp.concatenate([dout_cross[...], dout_one[...], dout_so[...], dout_two[...]], axis=0)
        out_rows = 4 * D // LANES
        low[1, hid.shape[0] : hid.shape[0] + out_rows, :] = to_flat(stage, outs).astype(BF)
        total = hid.shape[0] + out_rows
        copies = []
        for slot, row, count in ((0, at["episode"], first + small), (1, at["hid_bias"], total)):
            for k, (off, part, to) in enumerate(flat_spans(row, count, shard, extra)):
                copies.append(
                    pltpu.make_async_copy(
                        low.at[slot, pl.ds(off, part), :], flat.at[pl.ds(to, part), :], sems.at[slot, k]
                    )
                )
        for copy in copies:
            copy.start()
        for copy in copies:
            copy.wait()
        tokens = kv_rows[1]
        for group in range(0, dkv_t.shape[1] // tokens, 16):
            copies = []
            for j in range(min(16, dkv_t.shape[1] // tokens - group)):
                rows = pl.ds(j * tokens, tokens)
                low[0, rows, :] = dkv_t[:, (group + j) * tokens : (group + j + 1) * tokens].T
                to = kv_rows[0] + (group + j) * kv_rows[2]
                copies.append(
                    pltpu.make_async_copy(low.at[0, rows, :], flat.at[pl.ds(to, tokens), :], sems.at[0, j])
                )
                copies[-1].start()
            for copy in copies:
                copy.wait()


def fixed(*shape):
    return pl.BlockSpec(shape, lambda i: (0,) * len(shape), pipeline_mode=pl.Buffered(1))


def kept(*shape):
    return pl.BlockSpec(shape, lambda i: (0,) * len(shape))


def rowed(rows, cols):
    return pl.BlockSpec((rows, cols), lambda i: (i, 0))


def framed(*shape):
    return pl.BlockSpec((1,) + shape, lambda i: (i,) + (0,) * len(shape))


def shaped(shape, dtype=F32):
    return jax.ShapeDtypeStruct(shape, dtype)


def call(kernel, grid, in_specs, outs, args, flops=0, trans=0, scratch=(), limit=56, aliases=None, collective=None):
    out_specs, out_shapes = zip(*outs)
    moved = sum(math.prod(a.shape) * a.dtype.itemsize for a in args)
    moved += sum(math.prod(s.shape) * s.dtype.itemsize for s in out_shapes)
    return pl.pallas_call(
        kernel,
        grid=(grid,),
        in_specs=in_specs,
        out_specs=list(out_specs),
        out_shape=list(out_shapes),
        scratch_shapes=list(scratch),
        input_output_aliases=aliases or {},
        compiler_params=pltpu.CompilerParams(
            dimension_semantics=("arbitrary",),
            vmem_limit_bytes=limit * MIB,
            collective_id=collective,
            has_side_effects=collective is not None,
        ),
        cost_estimate=pl.CostEstimate(flops=flops, bytes_accessed=moved, transcendentals=trans),
    )(*args)


def reduce_all(flat, master_rows, starts, ends, bias_owner, bias_row, tokens, tok_normed, w_kv, tok_norm):
    shard = master_rows.shape[0]
    vmem = pl.BlockSpec(memory_space=pltpu.VMEM)
    anywhere = pl.BlockSpec(memory_space=pl.ANY)
    dma = pltpu.SemaphoreType.DMA
    first = [
        pltpu.VMEM((8, STAT_ROWS, LANES), F32), dma((7,)), dma((7,)), pltpu.VMEM((16, LANES), BF),
        pltpu.VMEM((DIN, LANES), BF), dma((2,)),
    ]
    grads = flat.reshape(2, 2, 2, -1, LANES)
    return pl.pallas_call(
        functools.partial(reduce_kernel, bias_owner, bias_row),
        out_shape=[
            shaped((shard, LANES), BF), shaped((STAT_ROWS, LANES)), shaped(tokens.shape, BF),
            shaped(grads.shape, BF),
        ],
        in_specs=[vmem, vmem, anywhere] + [vmem] * 5,
        out_specs=[vmem, vmem, vmem, anywhere],
        scratch_shapes=first + Reduction.scratch(shard),
        input_output_aliases={2: 3},
        compiler_params=pltpu.CompilerParams(
            collective_id=1, has_side_effects=True, vmem_limit_bytes=48 * MIB
        ),
    )(starts, ends, grads, master_rows, tokens, tok_normed, w_kv, tok_norm)


def body(tokens, frame_ids, episodes, master, moment_one, moment_two, latent_grad):
    lat_count = lax.axis_size("lat")
    lat_index = lax.axis_index("lat")
    shard_len = master.shape[0]
    frame_total = episodes.shape[1]
    frames = frame_total // lat_count
    rows_total = frames * LAT
    total_keys = frame_ids.shape[1] * lat_count
    cap = total_keys // 8
    token_rows_count = total_keys // LANES

    reach = lat_count == 8 and lax.axis_size("kf") == 4
    shard_rows = shard_len // LANES
    master_rows = master.reshape(shard_rows, LANES)
    episode_index = jnp.arange(EPISODES, dtype=jnp.int32)
    own_episodes = lax.dynamic_slice_in_dim(episodes[0], lat_index * frames, frames, 0)
    episode_match = own_episodes[:, None] == episode_index[None, :]
    score_flops = rows_total * cap * LANES * 2
    select_flops = frames * cap * total_keys * LANES * 2
    if reach:
        hot = jnp.pad(episode_match.astype(BF), ((0, 16 - frames), (0, 16 - EPISODES)))
        (
            up_one, down_one, w_qkv, w_so, up_two, down_two,
            latent, norms, hid_bias, out_bias, w_q, w_o, w_kv, tok_norm, tok_normed, episode_rows, rank, counts,
            kvf, cross_out, cross_lse, h1,
        ) = begin_all(master_rows, tokens[0], frame_ids.reshape(-1, LANES), hot, frames, cap)
    else:
        weights = split_flat(lax.all_gather(master.astype(BF), "lat", axis=0, tiled=True))
        norms = weights["lat_norms"].astype(F32)
        out_bias = weights["out_bias"].astype(F32)
        hid_bias = weights["hid_bias"].astype(F32)
        tok_norm = weights["tok_norm"].astype(F32)
        w_kv, w_qkv, w_so, latent = (weights[name] for name in ("w_kv", "w_qkv", "w_so", "latent"))
        up_one, up_two = weights["w_up"]
        down_one, down_two = weights["w_down"]
        frame_tag = lax.all_gather(frame_ids[0].astype(BF), "lat", axis=0, tiled=True).astype(jnp.int32)
        own_frames = lat_index * frames + jnp.arange(frames, dtype=jnp.int32)
        own_hit = frame_tag[None, :] == own_frames[:, None]
        rank = jnp.cumsum(own_hit.astype(jnp.int32), axis=1) - 1
        counts = jnp.broadcast_to(rank[:, -1][:, None, None] + 1, (frames, 8, LANES))
        rank = jnp.where(own_hit, rank, -1).reshape(frames, token_rows_count, LANES)
        tok_normed = layer_norm(tokens[0].astype(F32), tok_norm[0], tok_norm[1]).astype(BF)
        key_value = mm(tok_normed, w_kv).astype(BF)
        all_keys = lax.all_gather(key_value, "lat", axis=0, tiled=True)
        episode_rows = mm(episode_match.astype(BF), weights["episode"]).reshape(frames, 1, D)
        w_q = jnp.pad(weights["w_q"], ((0, 0), (0, LANES - CH)))
        w_o = jnp.pad(weights["w_o"], ((LANES - CH, 0), (0, 0)))
        h1, kvf, cross_out, cross_lse = call(
            cross_fwd_kernel,
            frames,
            [
                fixed(LAT, D), framed(1, D), fixed(8, D), fixed(D, LANES), fixed(LANES, D), fixed(4, D),
                fixed(total_keys, LANES), framed(token_rows_count, LANES), framed(8, LANES),
            ],
            [
                (rowed(LAT, D), shaped((rows_total, D))),
                (framed(cap, LANES), shaped((frames, cap, LANES), BF)),
                (rowed(LAT, LANES), shaped((rows_total, LANES), BF)),
                (framed(1, LAT), shaped((frames, 1, LAT))),
            ],
            (latent, episode_rows, norms, w_q, w_o, out_bias, all_keys, rank, counts),
            flops=2 * score_flops + select_flops,
            trans=rows_total * cap,
        )
    mlp_flops = 4 * rows_total * D * FF
    attn_flops = 4 * rows_total * LAT * D
    anywhere = pl.BlockSpec(memory_space=pl.ANY)
    token_count = frame_ids.shape[1]
    if reach:
        flat_shard, extra = shard_rows, token_count
        flat_shape = (lat_count * (shard_rows + extra), LANES)
        kv_rows = (shard_rows, token_count, shard_rows + extra)
        grad_in, grad_spec = latent_grad[0], anywhere
        latents_spec = (anywhere, shaped(latent_grad.shape[1:], BF))
        shared = [pltpu.VMEM((frames, LAT, D), BF)] * 2 + FrameExchange.scratch(frames)
    else:
        flat_shard, extra = NPARAM // LANES, 0
        flat_shape = (flat_shard + total_keys, LANES)
        kv_rows = (flat_shard, 512, 512)
        grad_in = lax.all_to_all(
            latent_grad[0], "lat", split_axis=0, concat_axis=1, tiled=True
        ).reshape(rows_total, D)
        grad_spec = rowed(LAT, D)
        latents_spec = (rowed(LAT, D), shaped((rows_total, D), BF))
        shared = []
    slab = D * FF // LANES
    h2, qkv, self_lse, mixed, act_one, slope_one, latents, g3, dhid_two, dnorm_two, dout_two, flat = call(
        functools.partial(forward_kernel, reach, flat_shard, extra),
        frames,
        [
            rowed(LAT, D), grad_spec, fixed(8, D), fixed(2, FF), fixed(4, D), fixed(D, FF), fixed(FF, D),
            fixed(D, 3 * D), fixed(D, D), fixed(D, FF), fixed(FF, D),
        ],
        [
            (rowed(LAT, D), shaped((rows_total, D))),
            (rowed(LAT, 3 * D), shaped((rows_total, 3 * D), BF)),
            (framed(HEADS, LAT), shaped((frames, HEADS, LAT))),
            (rowed(LAT, D), shaped((rows_total, D), BF)),
            (rowed(LAT, FF), shaped((rows_total, FF), BF)),
            (rowed(LAT, FF), shaped((rows_total, FF), BF)),
            latents_spec,
            (rowed(LAT, D), shaped((rows_total, D))),
            (kept(1, FF), shaped((1, FF))),
            (kept(2, D), shaped((2, D))),
            (kept(1, D), shaped((1, D))),
            (anywhere, shaped(flat_shape, BF)),
        ],
        (h1, grad_in, norms, hid_bias, out_bias, up_one, down_one, w_qkv, w_so, up_two, down_two),
        flops=4 * mlp_flops + 4 * attn_flops,
        trans=4 * rows_total * FF,
        scratch=[
            pltpu.VMEM((LAT, FF), BF), pltpu.VMEM((LAT, FF), BF), pltpu.VMEM((slab, LANES), F32),
            pltpu.VMEM((slab, LANES), F32), pltpu.VMEM((2, slab, LANES), BF), pltpu.VMEM((LAT, D), BF),
            pltpu.VMEM((D, LAT), F32), pltpu.VMEM((LAT, D), F32), pltpu.SemaphoreType.DMA((2, 16)),
        ]
        + shared,
        limit=62,
        collective=4 if reach else None,
    )
    if reach:
        latents_out = latents[None]
    else:
        latents_out = lax.all_to_all(
            latents.reshape(frames, LAT, D), "lat", split_axis=1, concat_axis=0, tiled=True
        )[None]
    hot_lanes = jnp.broadcast_to(
        jnp.pad(episode_match.astype(F32), ((0, 0), (0, 16 - EPISODES)))[:, :, None], (frames, 16, LANES)
    )
    (flat,) = call(
        functools.partial(backward_kernel, flat_shard, extra, kv_rows),
        frames,
        [
            rowed(LAT, 3 * D), framed(HEADS, LAT), rowed(LAT, D), rowed(LAT, D), rowed(LAT, D), rowed(LAT, D),
            rowed(LAT, FF), rowed(LAT, FF), framed(cap, LANES), rowed(LAT, LANES), framed(1, LAT),
            framed(token_rows_count, LANES), framed(8, LANES), framed(1, D), framed(16, LANES),
            fixed(LAT, D), fixed(8, D), fixed(D, D), fixed(D, 3 * D), fixed(D, FF), fixed(FF, D), fixed(D, LANES),
            fixed(LANES, D), fixed(1, FF), fixed(2, D), fixed(1, D), anywhere,
        ],
        [(anywhere, shaped(flat_shape, BF))],
        (
            qkv, self_lse, mixed, g3, h2, h1, act_one, slope_one, kvf, cross_out, cross_lse, rank, counts,
            episode_rows, hot_lanes, latent, norms, w_so, w_qkv, up_one, down_one, w_q, w_o, dhid_two, dnorm_two,
            dout_two, flat,
        ),
        flops=2 * mlp_flops + 10 * attn_flops + 6 * score_flops,
        trans=rows_total * LAT * HEADS,
        scratch=[
            pltpu.VMEM((LAT, 3 * D), BF), pltpu.VMEM((slab, LANES), F32), pltpu.VMEM((slab, LANES), F32),
            pltpu.VMEM((3 * D * D // LANES, LANES), F32), pltpu.VMEM((D * D // LANES, LANES), F32),
            pltpu.VMEM((LAT * D // LANES, LANES), F32), pltpu.VMEM((D, LANES), F32), pltpu.VMEM((LANES, D), F32),
            pltpu.VMEM((16, D), F32), pltpu.VMEM((1, FF), F32), pltpu.VMEM((2, D), F32), pltpu.VMEM((2, D), F32),
            pltpu.VMEM((2, D), F32), pltpu.VMEM((1, D), F32), pltpu.VMEM((1, D), F32), pltpu.VMEM((1, D), F32),
            pltpu.VMEM((512, LANES), F32), pltpu.VMEM((2, slab, LANES), BF), pltpu.VMEM((LAT, D), BF),
            pltpu.VMEM((LAT, D), BF), pltpu.VMEM((LAT, D), BF), pltpu.VMEM((LAT, D), F32),
            pltpu.VMEM((LANES, total_keys), BF), pltpu.SemaphoreType.DMA((2, 16)),
        ],
        limit=60,
        aliases={26: 0},
    )
    layout = param_layout()
    starts, ends, offset, bias_offset = [], [], 0, 0
    for name, shape in layout:
        if name == "hid_bias":
            bias_offset = offset
        starts.append(offset // LANES)
        offset += math.prod(shape)
        ends.append(offset // LANES)
    pad = [0] * (16 - len(layout))
    starts = jnp.broadcast_to(jnp.array(starts + pad, jnp.int32)[:, None], (16, LANES))
    ends = jnp.broadcast_to(jnp.array(ends + pad, jnp.int32)[:, None], (16, LANES))
    opt_rows = 784 if shard_rows % 784 == 0 else shard_rows
    opt_steps = shard_rows // opt_rows
    base = (lat_index * shard_rows).astype(jnp.int32).reshape(1)
    smem = pl.BlockSpec(memory_space=pltpu.SMEM)
    flat_rows = (shard_rows, LANES)
    bias_owner, bias_at = divmod(bias_offset, shard_len)
    if reach:
        summed, stats, token_grad, unused = reduce_all(
            flat, master_rows, starts, ends, bias_owner, bias_at // LANES, tokens[0], tok_normed, w_kv, tok_norm
        )
    else:
        grad_kv = lax.psum_scatter(flat[flat_shard:], "lat", scatter_dimension=0, tiled=True)
        flat = flat[:flat_shard]
        grad_w_kv = t_mm(tok_normed, grad_kv)
        grad_tok_normed = mm_t(grad_kv, w_kv)
        unused, token_pull = jax.vjp(layer_norm, tokens[0].astype(F32), tok_norm[0], tok_norm[1])
        grad_tokens, grad_tok_gain, grad_tok_bias = token_pull(grad_tok_normed)
        token_grad = grad_tokens.astype(BF)
        flat_at = flat_rows_of()
        tok_norm_grad = jnp.stack([grad_tok_gain, grad_tok_bias]).reshape(-1, LANES).astype(BF)
        flat = lax.dynamic_update_slice(flat, tok_norm_grad, (flat_at["tok_norm"], 0))
        flat = lax.dynamic_update_slice(flat, grad_w_kv.astype(BF), (flat_at["w_kv"], 0))
        local_flat = flat.reshape(-1)
        summed = lax.psum_scatter(local_flat, "lat", scatter_dimension=0, tiled=True)
        summed = lax.psum(summed, "kf").reshape(flat_rows)
        grad_sq, weight_sq = call(
            grad_stats_kernel,
            opt_steps,
            [smem, fixed(16, LANES), fixed(16, LANES), rowed(opt_rows, LANES), rowed(opt_rows, LANES)],
            [(kept(1, LANES), shaped((1, LANES))), (kept(16, LANES), shaped((16, LANES)))],
            (base, starts, ends, summed, master_rows),
        )
        bias_rows = summed[bias_at // LANES : bias_at // LANES + 2 * FF // LANES].astype(F32)
        bias_rows = jnp.where(lat_index == bias_owner, bias_rows, 0.0)
        stats = lax.psum(
            jnp.concatenate([grad_sq, jnp.zeros((7, LANES), F32), weight_sq, bias_rows]), "lat"
        )
    bias_grad = stats[24:STAT_ROWS].reshape(2, FF)
    grad_shard, lamb_update, new_one, new_two, update_sq = call(
        lamb_kernel,
        opt_steps,
        [smem, fixed(STAT_ROWS, LANES), fixed(16, LANES), fixed(16, LANES)] + [rowed(opt_rows, LANES)] * 4,
        [(rowed(opt_rows, LANES), shaped(flat_rows))] * 4 + [(kept(16, LANES), shaped((16, LANES)))],
        (
            base, stats, starts, ends, summed, master_rows,
            moment_one.reshape(flat_rows), moment_two.reshape(flat_rows),
        ),
    )
    if reach:
        vmem = pl.BlockSpec(memory_space=pltpu.VMEM)
        trust = pl.pallas_call(
            trust_kernel,
            out_shape=shaped((16, LANES)),
            in_specs=[vmem, vmem],
            out_specs=vmem,
            scratch_shapes=[
                pltpu.VMEM((8, 16, LANES), F32),
                pltpu.SemaphoreType.DMA((7,)),
                pltpu.SemaphoreType.DMA((7,)),
            ],
            compiler_params=pltpu.CompilerParams(collective_id=2, has_side_effects=True),
        )(update_sq, stats)[: len(layout), 0]
    else:
        update_sq = lax.psum(jnp.sum(update_sq, axis=1), "lat")
        weight_sq = jnp.sum(stats[8:24], axis=1)
        trust = (jnp.sqrt(weight_sq) / (jnp.sqrt(update_sq) + 1e-06))[: len(layout)]
    return (
        latents_out,
        token_grad[None],
        grad_shard.reshape(-1),
        lamb_update.reshape(-1),
        new_one.reshape(-1),
        new_two.reshape(-1),
        trust,
        bias_grad,
    )


def solution(mesh):
    return jax.shard_map(
        body,
        mesh=mesh,
        in_specs=(
            P("kf", "lat", None),
            P("kf", "lat"),
            P("kf", None),
            P("lat"),
            P("lat"),
            P("lat"),
            P("kf", None, "lat", None),
        ),
        out_specs=(
            P("kf", None, "lat", None),
            P("kf", "lat", None),
            P("lat"),
            P("lat"),
            P("lat"),
            P("lat"),
            P(),
            P(),
        ),
        check_vma=False,
    )
```

```python
import functools
import math

import jax
import jax.numpy as jnp
from jax import lax
from jax.experimental import pallas as pl
from jax.experimental.pallas import tpu as pltpu
from jax.sharding import PartitionSpec as P

DIN = 256
D = 512
LAT = 512
CH = 64
HEADS = 8
HEAD_DIM = 64
FF = 2048
EPISODES = 11
NPARAM = 5619712
LANES = 128

norm_eps = 1e-05
masked_fill = -1e30
beta_one = 0.9
beta_two = 0.999
adam_eps = 1e-06
decay_rate = 0.01
clip_fraction = 0.5
lamb_step = 10.0

BF = jnp.bfloat16
F32 = jnp.float32
MIB = 1024 * 1024


def param_layout():
    return [
        ("latent", (LAT, D)),
        ("episode", (EPISODES, D)),
        ("tok_norm", (2, DIN)),
        ("lat_norms", (8, D)),
        ("w_kv", (DIN, 2 * CH)),
        ("w_q", (D, CH)),
        ("w_o", (CH, D)),
        ("w_qkv", (D, 3 * D)),
        ("w_so", (D, D)),
        ("w_up", (2, D, FF)),
        ("w_down", (2, FF, D)),
        ("hid_bias", (2, FF)),
        ("out_bias", (4, D)),
    ]


def split_flat(flat_vector):
    pieces = {}
    offset = 0
    for tensor_name, tensor_shape in param_layout():
        entries = math.prod(tensor_shape)
        pieces[tensor_name] = flat_vector[offset : offset + entries].reshape(tensor_shape)
        offset += entries
    return pieces


def layer_norm(inputs, norm_gain, norm_bias):
    row_mean = jnp.mean(inputs, axis=-1, keepdims=True)
    centered = inputs - row_mean
    row_var = jnp.mean(centered * centered, axis=-1, keepdims=True)
    return centered * lax.rsqrt(row_var + norm_eps) * norm_gain + norm_bias


def mm(left, right):
    return jnp.dot(left, right, preferred_element_type=F32)


def mm_t(left, right):
    return lax.dot_general(left, right, (((1,), (1,)), ((), ())), preferred_element_type=F32)


def t_mm(left, right):
    return lax.dot_general(left, right, (((0,), (0,)), ((), ())), preferred_element_type=F32)


def norm_stats(rows):
    mean = jnp.mean(rows, axis=-1, keepdims=True)
    centered = rows - mean
    var = jnp.mean(centered * centered, axis=-1, keepdims=True)
    rstd = lax.rsqrt(var + norm_eps)
    return centered * rstd, rstd


def norm_back(grad, xhat, rstd, gain):
    dxh = grad * gain
    first = jnp.mean(dxh, axis=-1, keepdims=True)
    second = jnp.mean(dxh * xhat, axis=-1, keepdims=True)
    return rstd * (dxh - first - xhat * second)


def col_sum(values):
    return jnp.sum(values, axis=0, keepdims=True)


def gelu_pair(x):
    cdf = 0.5 + 0.5 * lax.erf(x * (1.0 / math.sqrt(2.0)))
    density = jnp.exp(x * x * -0.5) * (1.0 / math.sqrt(2.0 * math.pi))
    return x * cdf, cdf + x * density


def accumulate(first, ref, value):
    @pl.when(first)
    def _():
        ref[...] = value

    @pl.when(jnp.logical_not(first))
    def _():
        ref[...] += value


def lane_half(shape, half):
    lane = lax.broadcasted_iota(jnp.int32, shape, 1)
    return (lane >= half * 64) & (lane < half * 64 + 64)


def keep_half(values, half):
    return jnp.where(lane_half(values.shape, half), values, jnp.zeros_like(values))


def select_tokens(rank_rows, cap):
    slot = lax.broadcasted_iota(jnp.int32, (cap, LANES), 0)
    parts = []
    for r in range(rank_rows.shape[0]):
        hit = slot == rank_rows[r : r + 1, :]
        parts.append(jnp.where(hit, 1.0, 0.0).astype(BF))
    return jnp.concatenate(parts, axis=1)


def cross_scores(kvf, queries_scaled, count):
    scores = mm_t(kvf, queries_scaled)
    slot = lax.broadcasted_iota(jnp.int32, scores.shape, 0)
    return jnp.where(slot < count, scores, masked_fill)


def cross_attend(start, norms, w_q, kvf, count):
    xhat, unused = norm_stats(start)
    query_in = (xhat * norms[0:1, :] + norms[1:2, :]).astype(BF)
    queries = mm(query_in, w_q[...]).astype(BF) * jnp.asarray(0.125, BF)
    scores = cross_scores(kvf, queries, count)
    top = jnp.max(scores, axis=0, keepdims=True)
    terms = jnp.exp(scores - top)
    total = jnp.sum(terms, axis=0, keepdims=True)
    prob = (terms * (1.0 / total)).astype(BF)
    return t_mm(kvf, prob).T.astype(BF), top + jnp.log(total)


def cross_fwd_kernel(latent, episode, norms, w_q, w_o, out_bias, kv, rank, count, h1, kvf_out, co_out, lse_out):
    cap = kvf_out.shape[1]
    start = latent[...].astype(F32) + episode[0]
    chunk = 8 * LANES
    chunks = kv.shape[0] // chunk

    def step(j, acc):
        sel = select_tokens(rank[0, pl.ds(pl.multiple_of(j * 8, 8), 8), :], cap)
        return acc + mm(sel, kv[pl.ds(pl.multiple_of(j * chunk, chunk), chunk), :])

    kvf = lax.fori_loop(0, chunks, step, jnp.zeros((cap, LANES), F32)).astype(BF)
    co, lse = cross_attend(start, norms, w_q, kvf, count[0, 0:1, 0:1])
    h1[...] = start + mm(co, w_o[...]) + out_bias[0:1, :]
    kvf_out[0] = kvf
    co_out[...] = co
    lse_out[0] = lse


def segment_hot(starts, ends, base, rows):
    row = lax.broadcasted_iota(jnp.int32, (16, rows), 1) + base
    return jnp.where((row >= starts[:, 0:1]) & (row < ends[:, 0:1]), 1.0, 0.0).astype(BF)


def segment_sums(hot, squares):
    high = squares.astype(BF)
    low = (squares - high.astype(F32)).astype(BF)
    return mm(hot, high) + mm(hot, low)


def grad_stats_kernel(base, starts, ends, summed, master, grad_sq, weight_sq):
    i = pl.program_id(0)
    rows = master.shape[0]
    hot = segment_hot(starts, ends, base[0] + i * rows, rows)
    grad = summed[...].astype(F32)
    accumulate(i == 0, grad_sq, col_sum(grad * grad))
    accumulate(i == 0, weight_sq, segment_sums(hot, master[...] * master[...]))


def lamb_kernel(base, stats, starts, ends, summed, master, one, two, grad_out, update_out, one_out, two_out, update_sq):
    i = pl.program_id(0)
    rows = master.shape[0]
    hot = segment_hot(starts, ends, base[0] + i * rows, rows)
    total_sq = jnp.sum(stats[0:1, :], axis=1, keepdims=True)
    clip = jnp.minimum(1.0, clip_fraction * math.sqrt(NPARAM) / (jnp.sqrt(total_sq) + 1e-06))
    grad = summed[...].astype(F32)
    grad_out[...] = grad
    clipped = clip * grad
    new_one = beta_one * one[...] + (1.0 - beta_one) * clipped
    new_two = beta_two * two[...] + (1.0 - beta_two) * clipped * clipped
    one_out[...] = new_one
    two_out[...] = new_two
    first_hat = new_one * (1.0 / (1.0 - beta_one**lamb_step))
    second_hat = new_two * (1.0 / (1.0 - beta_two**lamb_step))
    update = first_hat / (jnp.sqrt(second_hat) + adam_eps) + decay_rate * master[...]
    update_out[...] = update
    accumulate(i == 0, update_sq, segment_sums(hot, update * update))


BATCH = 256
HALF = 128
QUARTER = 64
MESH = pl.DeviceIdType.MESH


class Place:
    def __init__(self):
        self.z = lax.axis_index("kf")
        self.me = lax.axis_index("lat")
        self.core = lax.rem(self.me, 2)
        self.x = lax.rem(self.me // 2, 2)
        self.y = self.me // 4
        self.z_low = lax.rem(self.z, 2)
        self.z_high = self.z // 2
        self.sibling = (self.z, self.me + 1 - 2 * self.core)
        self.x_side = (self.z, self.me + 2 - 4 * self.x)
        self.y_side = (self.z, self.me + 4 - 8 * self.y)
        self.z_near = (self.z + 1 - 2 * self.z_low, self.me)
        self.z_far = (self.z + 2 - 4 * self.z_high, self.me)

    def z_other(self, step):
        return (lax.rem(self.z + step, 4), self.me)

    def lat_other(self, step):
        return (self.z, lax.rem(self.me + step, 8))


def remote(src, dst, send, recv, device):
    return pltpu.make_async_remote_copy(
        src_ref=src, dst_ref=dst, send_sem=send, recv_sem=recv, device_id=device, device_id_type=MESH
    )


def greet(devices):
    barrier = pltpu.get_barrier_semaphore()
    for device in devices:
        pl.semaphore_signal(barrier, inc=1, device_id=device, device_id_type=MESH)
    pl.semaphore_wait(barrier, len(devices))


def added(left, right):
    return (left.astype(F32) + right.astype(F32)).astype(BF)


class Reduction:
    lags = (0, 1, 3, 5, 7, 9, 11)
    plane = 2

    def __init__(self, place, shard, grads, out, bufs, sems):
        self.p = place
        self.grads = grads
        self.out = out
        self.own, self.rc, self.r1, self.r2, self.r3, self.r4, self.res = bufs
        self.own_sem, self.send, self.rc_sem, self.r1_sem, self.r2_sem, self.r3_sem, self.r4_sem, self.res_sem = sems
        self.shard = shard
        self.full = pl.cdiv(shard, BATCH)
        self.batches = self.full + self.plane
        self.back = self.full * BATCH - shard
        self.held = flat_rows_of()["tok_norm"] // BATCH
        self.early = self.full - 1 - (self.held + 4)

    @staticmethod
    def scratch(shard):
        n = pl.cdiv(shard, BATCH) + Reduction.plane
        bufs = [
            pltpu.VMEM((2, 2, 2, BATCH, LANES), BF),
            pltpu.VMEM((n, 2, 2, BATCH, LANES), BF),
            pltpu.VMEM((n, 2, 2, HALF, LANES), BF),
            pltpu.VMEM((n, 2, HALF, LANES), BF),
            pltpu.VMEM((n, HALF, LANES), BF),
            pltpu.VMEM((n, QUARTER, LANES), BF),
            pltpu.VMEM((n, BATCH, LANES), BF),
        ]
        dma = pltpu.SemaphoreType.DMA
        sems = [dma((2,)), dma((10, 4)), dma((n,)), dma((n, 2)), dma((n, 2)), dma((n,)), dma((n,)), dma((n, 3))]
        return bufs + sems

    def from_on(self, i, first):
        return (i + 64 - first) // 64

    def row(self, i):
        n, held = self.full, self.held
        on = functools.partial(self.from_on, i)
        keys = on(self.early) - on(self.early + 2)
        shift = held + 4 + on(self.early + 2) * (-2) + on(self.early + 3) * (-n)
        shift = shift + on(self.early + 3 + held) * 2 + on(self.early + 5 + held) * (-4)
        b = i + shift
        row = keys * (self.shard + (i - self.early) * BATCH)
        row = row + (1 - keys) * (b * BATCH - (b // (n - 1)) * self.back)
        return pl.multiple_of(row, 16)

    def is_keys(self, i):
        return (i >= self.early) & (i < self.early + self.plane)

    def own_copy(self, i):
        slot = lax.rem(i, 2)
        src = self.grads.at[:, :, self.p.core, pl.ds(self.row(i), BATCH), :]
        return pltpu.make_async_copy(src, self.own.at[slot], self.own_sem.at[slot])

    def copies(self, stage, i):
        p, slot = self.p, lax.rem(i, 4)
        if stage == 0:
            src = self.grads.at[:, :, 1 - p.core, pl.ds(self.row(i), BATCH), :]
            return [remote(src, self.rc.at[i], self.send.at[0, slot], self.rc_sem.at[i], p.sibling)]
        if stage == 1:
            to_x = self.rc.at[i, :, 1 - p.x, pl.ds(0, HALF), :]
            to_y = self.rc.at[i, 1 - p.y, :, pl.ds(HALF, HALF), :]
            return [
                remote(to_x, self.r1.at[i, 0], self.send.at[1, slot], self.r1_sem.at[i, 0], p.x_side),
                remote(to_y, self.r1.at[i, 1], self.send.at[2, slot], self.r1_sem.at[i, 1], p.y_side),
            ]
        if stage == 2:
            to_y = self.r1.at[i, 0, 1 - p.y]
            to_x = self.r1.at[i, 1, 1 - p.x]
            return [
                remote(to_y, self.r2.at[i, 0], self.send.at[3, slot], self.r2_sem.at[i, 0], p.y_side),
                remote(to_x, self.r2.at[i, 1], self.send.at[4, slot], self.r2_sem.at[i, 1], p.x_side),
            ]
        if stage == 3:
            src = self.r2.at[i, 1 - p.z_low]
            return [remote(src, self.r3.at[i], self.send.at[5, slot], self.r3_sem.at[i], p.z_near)]
        if stage == 4:
            src = self.r3.at[i, pl.ds(pl.multiple_of((1 - p.z_high) * QUARTER, QUARTER), QUARTER), :]
            return [remote(src, self.r4.at[i], self.send.at[6, slot], self.r4_sem.at[i], p.z_far)]
        mine = self.res.at[i, pl.ds(pl.multiple_of(p.z_low * HALF + p.z_high * QUARTER, QUARTER), QUARTER), :]
        return [
            remote(mine, mine, self.send.at[6 + d, slot], self.res_sem.at[i, d - 1], p.z_other(d))
            for d in (1, 2, 3)
        ]

    def launch(self, stage, i):
        before = i - 4
        if stage >= 3:
            before = before - 4 * (self.from_on(before, self.early) - self.from_on(before, self.early + self.plane))

        @pl.when(i >= 4)
        def _():
            for copy in self.copies(stage, before):
                copy.wait_send()

        for copy in self.copies(stage, i):
            copy.start()

    def landed(self, stage, i):
        for copy in self.copies(stage, i):
            copy.wait_recv()

    def work(self, stage, i):
        p = self.p
        if stage == 0:
            self.own_copy(i).start()
        elif stage == 1:
            self.landed(0, i)
            self.own_copy(i).wait()
            self.rc[i] = added(self.rc[i], self.own[lax.rem(i, 2)])
        elif stage == 2:
            self.landed(1, i)
            self.r1[i, 0] = added(self.r1[i, 0], self.rc[i, :, p.x, 0:HALF, :])
            self.r1[i, 1] = added(self.r1[i, 1], self.rc[i, p.y, :, HALF:BATCH, :])
        elif stage == 3:
            self.landed(2, i)
            self.r2[i, 0] = added(self.r2[i, 0], self.r1[i, 0, p.y])
            self.r2[i, 1] = added(self.r2[i, 1], self.r1[i, 1, p.x])
        elif stage == 4:
            self.landed(3, i)
            self.r3[i] = added(self.r3[i], self.r2[i, p.z_low])
        elif stage == 5:
            self.landed(4, i)
            part = self.r3[i, pl.ds(pl.multiple_of(p.z_high * QUARTER, QUARTER), QUARTER), :]
            at = pl.multiple_of(p.z_low * HALF + p.z_high * QUARTER, QUARTER)
            self.res[i, pl.ds(at, QUARTER), :] = added(self.r4[i], part)
        else:
            self.landed(5, i)
            self.out[pl.ds(self.row(i), BATCH), :] = self.res[i]
        if stage == 3:
            pl.when(jnp.logical_not(self.is_keys(i)))(lambda: self.launch(stage, i))
        elif stage < 6:
            self.launch(stage, i)

    def tick(self, t):
        for stage, lag in enumerate(self.lags):
            i = t - lag

            inside = (i >= 0) & (i < self.batches)

            @pl.when(inside if stage < 4 else inside & jnp.logical_not(self.is_keys(i)))
            def _(stage=stage, i=i):
                self.work(stage, i)

    def ticks(self):
        return self.batches + self.lags[-1]

    def finish(self):
        for stage in range(6):
            for back in range(4):
                for copy in self.copies(stage, self.batches - 4 + back):
                    copy.wait_send()

    def partners(self):
        p = self.p
        return [p.sibling, p.x_side, p.y_side] + [p.z_other(d) for d in (1, 2, 3)]


def share_all(place, block, send, recv):
    mine = block.at[place.me]
    copies = [
        remote(mine, mine, send.at[d - 1], recv.at[d - 1], place.lat_other(d)) for d in range(1, 8)
    ]
    for copy in copies:
        copy.start()
    for copy in copies:
        copy.wait()


STAT_ROWS = 56


def token_backward(grad_kv, tokens, tok_normed, w_kv, tok_norm, token_grad, kv_grad, edge):
    kv_grad[...] = t_mm(tok_normed[...], grad_kv).astype(BF)
    grad = mm_t(grad_kv, w_kv[...])
    xhat, rstd = norm_stats(tokens[...].astype(F32))
    token_grad[...] = norm_back(grad, xhat, rstd, tok_norm[0:1, :]).astype(BF)
    gain, bias = col_sum(grad * xhat), col_sum(grad)
    parts = [half[:, j * LANES : (j + 1) * LANES] for half in (gain, bias) for j in range(DIN // LANES)]
    keep = edge.shape[0] - len(parts)
    edge[...] = jnp.concatenate([edge[...].astype(F32)[0:keep, :]] + parts, axis=0).astype(BF)


def reduce_kernel(
    bias_owner, bias_at, starts, ends, unused_flat, master, tokens, tok_normed, w_kv, tok_norm,
    g1, kvf, co, lse, rank, count, episode, hot, latent, norms, w_q, w_o,
    dnorm_one, dnorm_sa, dnorm_two, dhid_one, dhid_two, dout_one, dout_so, dout_two,
    summed, stats, token_grad, grads, *scratch,
):
    place = Place()
    block, block_send, block_recv, edge, kv_grad, edge_sem, g1_held, g1_sem, kv_low, kv_sem = scratch[:10]
    accs, (stage, low, latent_low), engine = scratch[10:17], scratch[17:20], scratch[20:]
    acc_latent, acc_q, acc_o, acc_episode, dnorm, dout, dkv_t = accs
    shard, frames = master.shape[0], kvf.shape[0]
    red = Reduction(place, shard, grads, summed, engine[:7], engine[7:])
    frame_copies = [pltpu.make_async_copy(g1.at[f], g1_held.at[f], g1_sem.at[f]) for f in range(frames)]
    for copy in frame_copies:
        copy.start()
    greet([place.lat_other(d) for d in range(1, 8)] + [place.z_other(d) for d in (1, 2, 3)])
    for ref in accs:
        ref[...] = jnp.zeros_like(ref)

    def run(first, last):
        lax.fori_loop(first, last, lambda t, c: (red.tick(t), c)[1], 0)

    def frame(f, carry):
        red.tick(2 * f)
        pltpu.make_async_copy(g1.at[f], g1_held.at[f], g1_sem.at[f]).wait()
        rows = pl.ds(pl.multiple_of(f * LAT, LAT), LAT)
        cross_back_frame(
            g1_held[f], kvf[f], co[rows, :], lse[f], rank.at[f], count[f, 0:1, 0:1], episode[f], hot[f, :, 0:1],
            latent, norms, w_q, w_o, *accs, pause=lambda: red.tick(2 * f + 1),
        )
        return carry

    lax.fori_loop(0, frames, frame, 0)
    run(2 * frames, red.early)
    at = flat_rows_of()
    copies = []

    def put(source, row):
        owner, local = row if isinstance(row, tuple) else divmod(row, shard)
        dst = grads.at[owner // 4, owner // 2 % 2, owner % 2, pl.ds(local, source.shape[0]), :]
        copies.append(pltpu.make_async_copy(source, dst, kv_sem.at[len(copies)]))
        copies[-1].start()

    write_small(
        put, stage, low, latent_low, acc_latent, acc_q, acc_o, acc_episode,
        stacked(dnorm, dnorm_one, dnorm_sa, dnorm_two), stacked(dhid_one, dhid_two),
        stacked(dout, dout_one, dout_so, dout_two),
    )
    edge_row = at["tok_norm"] // 16 * 16
    edge[...] = low[0, edge_row - at["episode"] : edge_row - at["episode"] + 16, :]
    count_kv = tokens.shape[0]
    for j in range(8):
        kv_low[j] = dkv_t[:, j * count_kv : (j + 1) * count_kv].T
        put(kv_low.at[j], (j, shard))
    for copy in copies:
        copy.wait()
    ready = red.early + red.lags[3] + red.plane
    run(red.early, ready)
    grad_kv = jnp.concatenate([red.r2[red.early + i, h] for i in range(red.plane) for h in range(2)], axis=0)
    token_backward(grad_kv, tokens, tok_normed, w_kv, tok_norm, token_grad, kv_grad, edge)
    writes = [
        pltpu.make_async_copy(edge, grads.at[0, 0, 0, pl.ds(edge_row, 16), :], edge_sem.at[0]),
        pltpu.make_async_copy(kv_grad, grads.at[0, 0, 0, pl.ds(at["w_kv"], DIN), :], edge_sem.at[1]),
    ]
    for copy in writes:
        copy.start()
    run(ready, ready + 2)
    for copy in writes:
        copy.wait()
    step = 784
    weight_sq = jnp.zeros((16, LANES), F32)
    for j in range(shard // step):
        hot_rows = segment_hot(starts, ends, place.me * shard + j * step, step)
        part = master[j * step : (j + 1) * step, :]
        weight_sq = weight_sq + segment_sums(hot_rows, part * part)
    run(ready + 2, red.ticks())
    grad_sq = jnp.zeros((1, LANES), F32)
    for j in range(shard // step):
        part = summed[j * step : (j + 1) * step, :].astype(F32)
        grad_sq = grad_sq + col_sum(part * part)
    bias = summed[bias_at : bias_at + 2 * FF // LANES, :].astype(F32)
    bias = jnp.where(place.me == bias_owner, bias, 0.0)
    head = jnp.concatenate([grad_sq, jnp.zeros((7, LANES), F32), weight_sq, bias], axis=0)
    block[pl.ds(place.me, 1)] = head[None]
    share_all(place, block, block_send, block_recv)
    total = block[0]
    for s in range(1, 8):
        total = total + block[s]
    stats[...] = total
    red.finish()


def trust_kernel(update_sq, stats, trust, block, send, recv):
    place = Place()
    greet([place.lat_other(d) for d in range(1, 8)])
    block[pl.ds(place.me, 1)] = update_sq[...][None]
    share_all(place, block, send, recv)
    total = block[0]
    for s in range(1, 8):
        total = total + block[s]
    update_norm = jnp.sqrt(jnp.sum(total, axis=1, keepdims=True))
    weight_norm = jnp.sqrt(jnp.sum(stats[8:24, :], axis=1, keepdims=True))
    trust[...] = jnp.broadcast_to(weight_norm / (update_norm + 1e-06), (16, LANES))


def relayout(whole, row, stage, dst, rows, cols):
    wide = cols // LANES
    block = min(rows, 2048 // wide // 128 * 128)

    def step(i, carry):
        at = pl.multiple_of(row + i * (block * wide), 16)
        stage[0 : block * wide, :] = whole[pl.ds(at, block * wide), :].astype(F32)
        for j in range(wide):
            part = stage[pl.ds(j, block, stride=wide), :]
            dst[pl.ds(pl.multiple_of(i * block, 16), block), j * LANES : (j + 1) * LANES] = part.astype(BF)
        return carry

    lax.fori_loop(0, rows // block, step, 0)


def small_matrix(whole, row, stage, rows, cols):
    wide = cols // LANES
    stage[0 : rows * wide, :] = whole[row : row + rows * wide, :].astype(F32)
    return jnp.concatenate([stage[pl.ds(j, rows, stride=wide), :] for j in range(wide)], axis=1)


class Gather:
    def __init__(self, place, whole, shard, chunks, send, recv):
        self.p, self.whole, self.shard, self.chunks, self.send, self.recv = place, whole, shard, chunks, send, recv
        p = place
        x_index, y_index = p.x_side[1], p.y_side[1]
        low = p.z_low
        self.first = x_index + low * (y_index - x_index)
        self.second = y_index + low * (x_index - y_index)
        self.diagonal = x_index + 4 - 8 * p.y

    def copy(self, kind, k):
        p = self.p
        block = (p.me, p.me, self.first, self.first, self.first, self.diagonal, self.second)[kind]
        target = (
            (p.z, self.first), p.sibling, (p.z, self.second), p.z_near, p.sibling, p.sibling, p.sibling
        )[kind]
        row, count = self.chunks[k]
        ref = self.whole.at[pl.ds(pl.multiple_of(block * self.shard + row, 16), count), :]
        return remote(ref, ref, self.send.at[kind, k], self.recv.at[kind, k], target)

    def tick(self, t):
        n = len(self.chunks)
        if t < n:
            self.copy(0, t).start()
            self.copy(1, t).start()
        if 0 <= t - 2 < n:
            self.copy(0, t - 2).wait_recv()
            for kind in (2, 3, 4):
                self.copy(kind, t - 2).start()
        if 0 <= t - 4 < n:
            self.copy(2, t - 4).wait_recv()
            self.copy(5, t - 4).start()
            self.copy(3, t - 4).wait_recv()
            self.copy(6, t - 4).start()
        if 0 <= t - 5 < n:
            for kind in (1, 4, 5, 6):
                self.copy(kind, t - 5).wait_recv()

    def ticks(self):
        return len(self.chunks) + 5

    def finish(self):
        for k in range(len(self.chunks)):
            for kind in range(7):
                self.copy(kind, k).wait_send()


class KeyExchange:
    def __init__(self, place, keys, send, recv):
        self.p, self.keys, self.send, self.recv = place, keys, send, recv
        self.x_index, self.y_index = place.x_side[1], place.y_side[1]
        self.diagonal = self.x_index + 4 - 8 * place.y

    def copy(self, kind):
        p = self.p
        half = self.keys.shape[1] // 2
        low, high, full = pl.ds(0, half), pl.ds(half, half), pl.ds(0, 2 * half)
        block, rows, target = (
            (p.me, full, p.x_side), (p.me, full, p.y_side), (p.me, full, p.sibling),
            (self.x_index, low, p.y_side), (self.y_index, high, p.x_side),
            (self.x_index, full, p.sibling), (self.y_index, full, p.sibling), (self.diagonal, full, p.sibling),
        )[kind]
        ref = self.keys.at[block, rows, :]
        return remote(ref, ref, self.send.at[kind], self.recv.at[kind], target)

    def step(self, s):
        if s == 0:
            waits, starts = (), (0, 1, 2)
        elif s == 1:
            waits, starts = (0, 1), (3, 4, 5, 6)
        elif s == 2:
            waits, starts = (3, 4), (7,)
        else:
            waits, starts = (2, 5, 6, 7), ()
        for kind in waits:
            self.copy(kind).wait_recv()
        for kind in starts:
            self.copy(kind).start()

    def finish(self):
        for kind in range(8):
            self.copy(kind).wait_send()


def flat_rows_of():
    rows, at = {}, 0
    for name, shape in param_layout():
        rows[name] = at // LANES
        at += math.prod(shape)
    return rows


def gather_chunks(shard):
    at = flat_rows_of()
    tail = at["hid_bias"] % shard // 16 * 16
    chunks = [(at["episode"], at["w_o"] - at["episode"]), (tail, shard - tail), (at["w_o"], at["w_qkv"] - at["w_o"])]
    for low, high in ((0, at["episode"]), (at["w_qkv"], tail)):
        while low < high:
            count = min(512, high - low)
            chunks.append((low, count))
            low += count
    return chunks


def begin_kernel(
    chunks, master, tokens, ids, hot,
    up_one, down_one, qkv_w, so_w, up_two, down_two,
    latent, norms, hid_bias, out_bias, w_q, w_o, w_kv, tok_norm, tok_normed, episode, rank, counts,
    kvf_out, co_out, lse_out, h1,
    whole, stage, all_ids, keys, m_up_one, m_down_one, m_qkv, m_so, m_up_two, m_down_two,
    episodes_held, send, recv, key_send, key_recv, id_send, id_recv, out_sem,
):
    place = Place()
    shard = master.shape[0]
    frames, cap = kvf_out.shape[0], kvf_out.shape[1]
    gather = Gather(place, whole, shard, chunks, send, recv)
    exchange = KeyExchange(place, keys, key_send, key_recv)
    at = flat_rows_of()
    greet([place.lat_other(d) for d in range(1, 8)] + [place.z_near])
    all_ids[pl.ds(place.me, 1)] = ids[...][None]
    id_copies = [
        remote(all_ids.at[place.me], all_ids.at[place.me], id_send.at[d - 1], id_recv.at[d - 1], place.lat_other(d))
        for d in range(1, 8)
    ]
    for copy in id_copies:
        copy.start()
    own_at = place.me * shard
    for row, count in chunks:
        whole[pl.ds(pl.multiple_of(own_at + row, 16), count), :] = master[row : row + count, :].astype(BF)
    for t in range(4):
        gather.tick(t)

    for copy in id_copies:
        copy.wait_recv()
    tags = jnp.concatenate([all_ids[s] for s in range(8)], axis=0)
    low = lax.broadcasted_iota(jnp.int32, (LANES, LANES), 0)
    high = lax.broadcasted_iota(jnp.int32, (LANES, LANES), 1)
    upto = jnp.where(low <= high, 1.0, 0.0).astype(BF)
    n = tags.shape[0]
    below = jnp.where(
        lax.broadcasted_iota(jnp.int32, (n, n), 1) < lax.broadcasted_iota(jnp.int32, (n, n), 0), 1.0, 0.0
    ).astype(BF)
    for f in range(frames):
        hit = tags == place.me * frames + f
        hit_low = jnp.where(hit, 1.0, 0.0).astype(BF)
        inside = mm(hit_low, upto)
        row_total = jnp.broadcast_to(inside[:, LANES - 1 : LANES], (n, LANES))
        before = mm(below, row_total.astype(BF))
        place_in = (inside + before).astype(jnp.int32) - 1
        rank[f] = jnp.where(hit, place_in, -1)
        total = jnp.sum(row_total[:, 0:1], axis=0, keepdims=True).astype(jnp.int32)
        counts[f] = jnp.broadcast_to(total, (8, LANES))
    for t in range(4, 7):
        gather.tick(t)

    pair = whole[at["tok_norm"] // 16 * 16 : at["lat_norms"], :].astype(F32)
    pair = pair[at["tok_norm"] % 16 : at["tok_norm"] % 16 + 4, :]
    tok_norm[...] = jnp.concatenate(
        [
            jnp.concatenate([pair[0:1], pair[1:2]], axis=1),
            jnp.concatenate([pair[2:3], pair[3:4]], axis=1),
        ],
        axis=0,
    )
    w_kv[...] = whole[at["w_kv"] : at["w_kv"] + DIN, :]
    xhat, unused = norm_stats(tokens[...].astype(F32))
    normed = (xhat * tok_norm[0:1, :] + tok_norm[1:2, :]).astype(BF)
    tok_normed[...] = normed
    keys[pl.ds(place.me, 1)] = mm(normed, w_kv[...]).astype(BF)[None]
    exchange.step(0)
    norms[...] = small_matrix(whole, at["lat_norms"], stage, 8, D)
    hid_bias[...] = small_matrix(whole, at["hid_bias"], stage, 2, FF)
    out_bias[...] = small_matrix(whole, at["out_bias"], stage, 4, D)
    episode_rows = mm(hot[...], small_matrix(whole, at["episode"], stage, 16, D).astype(BF))
    gather.tick(7)
    exchange.step(1)
    packed = whole[at["w_q"] : at["w_q"] + D // 2, :].astype(F32)
    stage[pl.ds(0, D // 2, stride=2), :] = packed
    stage[pl.ds(1, D // 2, stride=2), :] = pltpu.roll(packed, CH, 1)
    w_q[...] = keep_half(stage[0:D, :], 0).astype(BF)
    w_o[0:CH, :] = jnp.zeros((CH, D), BF)
    w_o[CH : 2 * CH, :] = small_matrix(whole, at["w_o"], stage, CH, D).astype(BF)
    gather.tick(8)
    exchange.step(2)
    for t in range(9, 12):
        gather.tick(t)
    exchange.step(3)
    relayout(whole, 0, stage, latent, LAT, D)

    chunk = 8 * LANES
    episodes_held[...] = episode_rows[0:8, :]

    def attend(f, carry):
        for tick in range(12, gather.ticks()):

            @pl.when(f == (tick - 12) * frames // (gather.ticks() - 12))
            def _(tick=tick):
                gather.tick(tick)

        row = episodes_held[pl.ds(f, 1), :]
        start = latent[...].astype(F32) + row
        episode[pl.ds(f, 1)] = row[None]

        def pick(j, acc):
            sel = select_tokens(rank[f, pl.ds(pl.multiple_of(8 * j, 8), 8), :], cap)
            return acc + mm(sel, keys[pl.ds(2 * j, 2)].reshape(chunk, LANES))

        kvf = lax.fori_loop(0, n // 8, pick, jnp.zeros((cap, LANES), F32)).astype(BF)
        co, lse = cross_attend(start, norms, w_q, kvf, counts[f, 0:1, 0:1])
        rows = pl.ds(pl.multiple_of(f * LAT, LAT), LAT)
        h1[rows, :] = start + mm(co, w_o[...]) + out_bias[0:1, :]
        kvf_out[f] = kvf
        co_out[rows, :] = co
        lse_out[f] = lse
        return carry

    lax.fori_loop(0, frames, attend, 0)

    big = (
        (up_one, m_up_one, at["w_up"], D, FF),
        (down_one, m_down_one, at["w_down"], FF, D),
        (qkv_w, m_qkv, at["w_qkv"], D, 3 * D),
        (so_w, m_so, at["w_so"], D, D),
        (up_two, m_up_two, at["w_up"] + D * FF // LANES, D, FF),
        (down_two, m_down_two, at["w_down"] + D * FF // LANES, FF, D),
    )
    outs = []
    for j, (out, held, row, rows, cols) in enumerate(big):
        relayout(whole, row, stage, held, rows, cols)
        outs.append(pltpu.make_async_copy(held, out, out_sem.at[j]))
        outs[-1].start()
    for copy in outs:
        copy.wait()
    for copy in id_copies:
        copy.wait_send()
    exchange.finish()
    gather.finish()


def begin_all(master_rows, token_rows, ids, hot, frames, cap):
    shard = master_rows.shape[0]
    tokens = token_rows.shape[0]
    total = 8 * tokens
    chunks = gather_chunks(shard)
    vmem = pl.BlockSpec(memory_space=pltpu.VMEM)
    anywhere = pl.BlockSpec(memory_space=pl.ANY)
    matrices = [(D, FF), (FF, D), (D, 3 * D), (D, D), (D, FF), (FF, D)]
    dma = pltpu.SemaphoreType.DMA
    return pl.pallas_call(
        functools.partial(begin_kernel, chunks),
        out_shape=[shaped(m, BF) for m in matrices]
        + [
            shaped((LAT, D), BF),
            shaped((8, D)),
            shaped((2, FF)),
            shaped((4, D)),
            shaped((D, LANES), BF),
            shaped((LANES, D), BF),
            shaped((DIN, LANES), BF),
            shaped((2, DIN)),
            shaped((tokens, DIN), BF),
            shaped((frames, 1, D)),
            shaped((frames, total // LANES, LANES), jnp.int32),
            shaped((frames, 8, LANES), jnp.int32),
            shaped((frames, cap, LANES), BF),
            shaped((frames * LAT, LANES), BF),
            shaped((frames, 1, LAT)),
            shaped((frames * LAT, D)),
        ],
        in_specs=[vmem] * 4,
        out_specs=[anywhere] * 6 + [vmem] * 16,
        scratch_shapes=[
            pltpu.VMEM((8 * shard, LANES), BF),
            pltpu.VMEM((2048, LANES), F32),
            pltpu.VMEM((8, tokens // LANES, LANES), jnp.int32),
            pltpu.VMEM((8, tokens, LANES), BF),
        ]
        + [pltpu.VMEM(m, BF) for m in matrices]
        + [
            pltpu.VMEM((8, D), F32),
            dma((7, len(chunks))), dma((7, len(chunks))), dma((8,)), dma((8,)), dma((7,)), dma((7,)), dma((6,)),
        ],
        compiler_params=pltpu.CompilerParams(
            collective_id=3, has_side_effects=True, vmem_limit_bytes=56 * MIB
        ),
    )(master_rows, token_rows, ids, hot)


FCHUNK = 512


def to_flat(stage, matrix):
    rows, wide = matrix.shape[0], matrix.shape[1] // LANES
    for j in range(wide):
        stage[pl.ds(j, rows, stride=wide), :] = matrix[:, j * LANES : (j + 1) * LANES]
    return stage[0 : rows * wide, :]


def chunk_of(c, size=FCHUNK):
    return pl.ds(pl.multiple_of(c * size, LANES), size)


def feed_forward(rows, gain, bias, up_bias, down_bias, w_up, w_down, act_ref, slope_ref, normed_ref, total_ref):
    xhat, rstd = norm_stats(rows)
    normed_ref[...] = (xhat * gain + bias).astype(BF)
    total_ref[...] = rows + down_bias

    for c in range(FF // FCHUNK):
        at = slice(c * FCHUNK, (c + 1) * FCHUNK)
        act, slope = gelu_pair(mm(normed_ref[...], w_up[:, at]) + up_bias[:, at])
        act = act.astype(BF)
        act_ref[:, at] = act
        slope_ref[:, at] = slope.astype(BF)
        total_ref[...] += mm(act, w_down[at, :])


def feed_back(grad_ref, normed_ref, xhat, rstd, gain, act, slope, w_up, w_down, acc_up, acc_down, dhid, dnorm, dout, work):
    work[...] = jnp.zeros(work.shape, F32)
    for c in range(FF // FCHUNK):
        at = slice(c * FCHUNK, (c + 1) * FCHUNK)
        dpre = (mm_t(grad_ref[...], w_down[at, :]) * slope[:, at].astype(F32)).astype(BF)
        dhid[:, at] += col_sum(dpre.astype(F32))
        work[...] += mm_t(dpre, w_up[:, at])
        acc_up[:, at] += t_mm(normed_ref[...], dpre)
        acc_down[at, :] += t_mm(act[:, at], grad_ref[...])
    grad_normed = work[...]
    dnorm[...] += jnp.concatenate([col_sum(grad_normed * xhat), col_sum(grad_normed)], axis=0)
    dout[...] += col_sum(grad_ref[...].astype(F32))
    return norm_back(grad_normed, xhat, rstd, gain)


def clear(first, refs):
    @pl.when(first)
    def _():
        for ref in refs:
            ref[...] = jnp.zeros_like(ref)


def flat_spans(row, count, shard, extra):
    spans, done = [], 0
    while done < count:
        part = min(count - done, shard - (row + done) % shard)
        spans.append((done, part, row + done + (row + done) // shard * extra))
        done += part
    return spans


def flatten(acc, stage, low, slot):
    wide = acc.shape[1] // LANES
    block = min(acc.shape[0], 2048 // wide // 128 * 128)
    span = block * wide

    def step(i, carry):
        part = acc[pl.ds(pl.multiple_of(i * block, block), block), :]
        for j in range(wide):
            stage[pl.ds(j, block, stride=wide), :] = part[:, j * LANES : (j + 1) * LANES]
        low[slot, pl.ds(pl.multiple_of(i * span, span), span), :] = stage[0:span, :].astype(BF)
        return carry

    lax.fori_loop(0, acc.shape[0] // block, step, 0)


def write_flat(flat, stage, low, pieces, sems, shard, extra):
    pending = {}
    for j, (acc, row) in enumerate(pieces):
        count = acc.shape[0] * acc.shape[1] // LANES
        slot = j % 2
        for copy in pending.get(slot, []):
            copy.wait()
        flatten(acc, stage, low, slot)
        pending[slot] = [
            pltpu.make_async_copy(low.at[slot, pl.ds(off, part), :], flat.at[pl.ds(at, part), :], sems.at[slot, k])
            for k, (off, part, at) in enumerate(flat_spans(row, count, shard, extra))
        ]
        for copy in pending[slot]:
            copy.start()
    for copies in pending.values():
        for copy in copies:
            copy.wait()


class FrameExchange:
    def __init__(self, place, source, grad, held, result, sems):
        self.p, self.source, self.grad, self.held, self.result = place, source, grad, held, result
        self.in_send, self.in_recv, self.out_send, self.out_recv, self.own_in, self.own_out = sems
        self.frames, self.rows = grad.shape[0], source.shape[1]

    @staticmethod
    def scratch(frames):
        dma = pltpu.SemaphoreType.DMA
        return [dma((frames, 7))] * 4 + [dma((frames,))] * 2

    def block(self, index):
        return pl.ds(pl.multiple_of(index * self.rows, 16), self.rows)

    def arriving(self, f, d):
        target = self.p.lat_other(d)
        src = self.source.at[target[1] * self.frames + f]
        dst = self.grad.at[f, self.block(self.p.me), :]
        return remote(src, dst, self.in_send.at[f, d - 1], self.in_recv.at[f, d - 1], target)

    def own_arriving(self, f):
        src = self.source.at[self.p.me * self.frames + f]
        return pltpu.make_async_copy(src, self.grad.at[f, self.block(self.p.me), :], self.own_in.at[f])

    def leaving(self, f, d):
        target = self.p.lat_other(d)
        src = self.held.at[f, self.block(target[1]), :]
        dst = self.result.at[self.p.me * self.frames + f]
        return remote(src, dst, self.out_send.at[f, d - 1], self.out_recv.at[f, d - 1], target)

    def own_leaving(self, f):
        dst = self.result.at[self.p.me * self.frames + f]
        return pltpu.make_async_copy(self.held.at[f, self.block(self.p.me), :], dst, self.own_out.at[f])

    def begin(self):
        greet([self.p.lat_other(d) for d in range(1, 8)])
        for f in range(self.frames):
            self.own_arriving(f).start()
            for d in range(1, 8):
                self.arriving(f, d).start()

    def await_frame(self, f):
        self.own_arriving(f).wait()
        for d in range(1, 8):
            self.arriving(f, d).wait_recv()

    def send_frame(self, f):
        self.own_leaving(f).start()
        for d in range(1, 8):
            self.leaving(f, d).start()

    def finish(self):
        def step(f, carry):
            self.own_leaving(f).wait()
            for d in range(1, 8):
                self.arriving(f, d).wait_send()
                self.leaving(f, d).wait()
            return carry

        lax.fori_loop(0, self.frames, step, 0)


def forward_kernel(
    reach, shard, extra, h1, grad, norms, hid_bias, out_bias, up_one, down_one, w_qkv, w_so, up_two, down_two,
    h2_out, qkv, lse_out, mixed_out, act_one, slope_one, latents, g3, dhid, dnorm, dout, flat,
    act_two, slope_two, acc_up, acc_down, stage, low, normed, mixed_t, work, sems, *shared,
):
    step = pl.program_id(0)
    if reach:
        place = Place()
        traffic = FrameExchange(place, grad, shared[0], shared[1], latents, shared[2:])
        pl.when(step == 0)(traffic.begin)
        grad = shared[0].at[step]
    clear(step == 0, (acc_up, acc_down, dhid, dnorm, dout))
    feed_forward(
        h1[...], norms[2:3, :], norms[3:4, :], hid_bias.at[0:1], out_bias[1:2, :], up_one, down_one, act_one,
        slope_one, normed, h2_out,
    )
    xhat, unused = norm_stats(h2_out[...])
    normed[...] = (xhat * norms[4:5, :] + norms[5:6, :]).astype(BF)

    def project(c, carry):
        at = chunk_of(c)
        qkv[:, at] = mm(normed[...], w_qkv[:, at]).astype(BF)
        return carry

    lax.fori_loop(0, 3, project, 0)
    scale = jnp.asarray(0.125, BF)

    ones = jnp.ones((16, LAT), BF)

    def attend(pair, carry):
        query_pair = qkv[:, chunk_of(pair, LANES)] * scale
        key_pair = qkv[:, chunk_of(pair + D // LANES, LANES)]
        value_t = qkv[:, chunk_of(pair + 2 * D // LANES, LANES)].T
        for half in range(2):
            scores = mm_t(key_pair, keep_half(query_pair, half))
            top = jnp.max(scores, axis=0, keepdims=True)
            terms = jnp.exp(scores - top).astype(BF)
            values = jnp.concatenate([value_t[half * HEAD_DIM : (half + 1) * HEAD_DIM, :], ones], axis=0)
            product = mm(values, terms)
            total = product[HEAD_DIM : HEAD_DIM + 1, :]
            lse_out[0, pl.ds(2 * pair + half, 1), :] = top + jnp.log(total)
            at = pl.ds(pl.multiple_of(pair * LANES + half * HEAD_DIM, HEAD_DIM), HEAD_DIM)
            mixed_t[at, :] = product[0:HEAD_DIM, :] * (1.0 / total)
        return carry

    lax.fori_loop(0, HEADS // 2, attend, 0)
    mixed = mixed_t[...].T.astype(BF)
    mixed_out[...] = mixed
    h3 = h2_out[...] + mm(mixed, w_so[...]) + out_bias[2:3, :]
    feed_forward(
        h3, norms[6:7, :], norms[7:8, :], hid_bias.at[1:2], out_bias[3:4, :], up_two, down_two, act_two, slope_two,
        normed, work,
    )
    if reach:
        shared[1][step] = work[...].astype(BF)
        traffic.send_frame(step)
        traffic.await_frame(step)
    else:
        latents[...] = work[...].astype(BF)
    xhat, rstd = norm_stats(h3)
    g3[...] = grad[...].astype(F32) + feed_back(
        grad, normed, xhat, rstd, norms[6:7, :], act_two, slope_two, up_two, down_two,
        acc_up, acc_down, dhid, dnorm, dout, work,
    )

    @pl.when(step == pl.num_programs(0) - 1)
    def _():
        at = flat_rows_of()
        half = D * FF // LANES
        write_flat(flat, stage, low, [(acc_up, at["w_up"] + half), (acc_down, at["w_down"] + half)], sems, shard, extra)
        if reach:
            traffic.finish()


def backward_kernel(
    shard, extra, qkv, lse, mixed, g3, h2, h1, act_one, slope_one, norms, w_so, w_qkv, up_one, down_one, flat_in,
    g1, dhid, dnorm_sa, dnorm_one, dout_so, dout_one, flat,
    dqkv, acc_up, acc_down, acc_qkv, acc_so, stage, low, normed, grad_mixed, grad_low, work, sems,
):
    step = pl.program_id(0)
    clear(
        step == 0,
        (acc_up, acc_down, acc_qkv, acc_so, dhid, dnorm_sa, dnorm_one, dout_so, dout_one),
    )
    scale = jnp.asarray(0.125, BF)
    grad_three = g3[...]
    grad_low[...] = grad_three.astype(BF)
    dout_so[...] += col_sum(grad_low[...].astype(F32))
    acc_so[...] += t_mm(mixed[...], grad_low[...])
    grad_mixed[...] = mm_t(grad_low[...], w_so[...]).astype(BF)

    def attend(pair, carry):
        query_at = chunk_of(pair, LANES)
        key_at = chunk_of(pair + D // LANES, LANES)
        value_at = chunk_of(pair + 2 * D // LANES, LANES)
        query_pair = qkv[:, query_at] * scale
        key_pair = qkv[:, key_at]
        value_pair = qkv[:, value_at]
        grad_pair = grad_mixed[:, query_at]
        key_t = key_pair.T
        query_t = []
        grad_key = jnp.zeros((LAT, LANES), F32)
        grad_value = jnp.zeros((LAT, LANES), F32)
        for half in range(2):
            query = keep_half(query_pair, half)
            grad_head = keep_half(grad_pair, half)
            prob = jnp.exp(mm_t(key_pair, query) - lse[0, pl.ds(2 * pair + half, 1), :])
            grad_value = grad_value + mm(prob.astype(BF), grad_head)
            weighted = prob * mm_t(value_pair, grad_head)
            grad_score = (weighted - prob * col_sum(weighted)).astype(BF)
            grad_key = grad_key + mm(grad_score, query)
            query_t.append(mm(key_t[half * HEAD_DIM : (half + 1) * HEAD_DIM, :], grad_score))
        dqkv[:, query_at] = (jnp.concatenate(query_t, axis=0).T * 0.125).astype(BF)
        dqkv[:, key_at] = grad_key.astype(BF)
        dqkv[:, value_at] = grad_value.astype(BF)
        return carry

    lax.fori_loop(0, HEADS // 2, attend, 0)
    xhat, rstd = norm_stats(h2[...])
    normed[...] = (xhat * norms[4:5, :] + norms[5:6, :]).astype(BF)
    work[...] = jnp.zeros(work.shape, F32)

    for c in range(3):
        at = slice(c * D, (c + 1) * D)
        work[...] += mm_t(dqkv[:, at], w_qkv[:, at])
        acc_qkv[:, at] += t_mm(normed[...], dqkv[:, at])
    grad_in = work[...]
    dnorm_sa[...] += jnp.concatenate([col_sum(grad_in * xhat), col_sum(grad_in)], axis=0)
    grad_two = grad_three + norm_back(grad_in, xhat, rstd, norms[4:5, :])

    xhat, rstd = norm_stats(h1[...])
    normed[...] = (xhat * norms[2:3, :] + norms[3:4, :]).astype(BF)
    grad_low[...] = grad_two.astype(BF)
    grad_one = grad_two + feed_back(
        grad_low, normed, xhat, rstd, norms[2:3, :], act_one, slope_one, up_one, down_one,
        acc_up, acc_down, dhid, dnorm_one, dout_one, work,
    )

    g1[...] = grad_one

    @pl.when(step == pl.num_programs(0) - 1)
    def _():
        at = flat_rows_of()
        write_flat(
            flat, stage, low,
            [(acc_up, at["w_up"]), (acc_down, at["w_down"]), (acc_qkv, at["w_qkv"]), (acc_so, at["w_so"])],
            sems, shard, extra,
        )


def cross_back_frame(
    grad_one, kvf, co, lse, rank_ref, count, episode_row, hot_column, latent, norms, w_q, w_o,
    acc_latent, acc_q, acc_o, acc_episode, dnorm, dout, dkv_t, pause=lambda: None,
):
    cap = kvf.shape[0]
    start = latent[...].astype(F32) + episode_row
    xhat, rstd = norm_stats(start)
    query_in = (xhat * norms[0:1, :] + norms[1:2, :]).astype(BF)
    queries = mm(query_in, w_q[...]).astype(BF) * jnp.asarray(0.125, BF)
    branch = grad_one.astype(BF)
    grad_co = mm_t(branch, w_o[...]).astype(BF)
    acc_o[...] += t_mm(co, branch)
    dout[...] += col_sum(branch.astype(F32))
    scores = cross_scores(kvf, queries, count)
    prob = jnp.exp(scores - lse)
    weighted = prob * mm_t(kvf, grad_co)
    grad_score = (weighted - prob * col_sum(weighted)).astype(BF)
    grad_kv = (mm(grad_score, queries) + mm(prob.astype(BF), grad_co)).astype(BF)
    grad_query = (t_mm(kvf, grad_score).T * 0.125).astype(BF)
    pause()
    acc_q[...] += t_mm(query_in, grad_query)
    grad_in = mm_t(grad_query, w_q[...])
    grad_start = grad_one + norm_back(grad_in, xhat, rstd, norms[0:1, :])
    dnorm[...] += jnp.concatenate([col_sum(grad_in * xhat), col_sum(grad_in)], axis=0)
    acc_latent[...] += grad_start
    acc_episode[...] += hot_column * col_sum(grad_start)
    grad_kv_t = grad_kv.T
    chunk = 8 * LANES

    def scatter(j, carry):
        sel = select_tokens(rank_ref[pl.ds(pl.multiple_of(j * 8, 8), 8), :], cap)
        at = pl.ds(pl.multiple_of(j * chunk, chunk), chunk)
        dkv_t[:, at] = added(dkv_t[:, at], mm(grad_kv_t, sel))
        return carry

    lax.fori_loop(0, dkv_t.shape[1] // chunk, scatter, 0)


def write_small(put, stage, low, latent_low, acc_latent, acc_q, acc_o, acc_episode, norm_grads, hid_grads, out_grads):
    at = flat_rows_of()
    flatten(acc_latent, stage, latent_low, 0)
    put(latent_low.at[0], 0)
    head = at["lat_norms"] - at["episode"]
    used = EPISODES * (D // LANES)
    rows = [to_flat(stage, acc_episode[...])[0:used, :], jnp.zeros((head - used, LANES), F32)]
    rows = jnp.concatenate(rows + [to_flat(stage, norm_grads)], axis=0)
    top = rows.shape[0]
    low[0, 0:top, :] = rows.astype(BF)
    put(low.at[0, pl.ds(0, top), :], at["episode"])
    stage[0:D, :] = acc_q[...]
    even = stage[pl.ds(0, D // 2, stride=2), :]
    odd = pltpu.roll(stage[pl.ds(1, D // 2, stride=2), :], CH, 1)
    low[0, top : top + D // 2, :] = jnp.where(lane_half(even.shape, 0), even, odd).astype(BF)
    both = D // 2 + CH * D // LANES
    low[0, top + D // 2 : top + both, :] = to_flat(stage, acc_o[CH : 2 * CH, :]).astype(BF)
    put(low.at[0, pl.ds(top, both), :], at["w_q"])
    hid = to_flat(stage, hid_grads)
    last = top + both
    low[0, last : last + hid.shape[0], :] = hid.astype(BF)
    end = hid.shape[0] + 4 * D // LANES
    low[0, last + hid.shape[0] : last + end, :] = to_flat(stage, out_grads).astype(BF)
    put(low.at[0, pl.ds(last, end), :], at["hid_bias"])


def cross_accumulators(total_keys):
    shapes = [(LAT, D), (D, LANES), (LANES, D), (16, D), (2, D), (1, D)]
    return [pltpu.VMEM(shape, F32) for shape in shapes] + [pltpu.VMEM((LANES, total_keys), BF)]


def small_buffers():
    return [pltpu.VMEM((2048, LANES), F32), pltpu.VMEM((1, 640, LANES), BF), pltpu.VMEM((1, 2048, LANES), BF)]


def stacked(*parts):
    return jnp.concatenate([part[...] for part in parts], axis=0)


def cross_bwd_kernel(
    kv_rows, g1, kvf, co, lse, rank, count, episode, hot, latent, norms, w_q, w_o,
    dnorm_one, dnorm_sa, dnorm_two, dhid_one, dhid_two, dout_one, dout_so, dout_two, flat_in, flat,
    acc_latent, acc_q, acc_o, acc_episode, dnorm, dout, dkv_t, stage, low, latent_low, kv_low, sems,
):
    step = pl.program_id(0)
    accs = (acc_latent, acc_q, acc_o, acc_episode, dnorm, dout, dkv_t)
    clear(step == 0, accs)
    cross_back_frame(
        g1[...], kvf[0], co[...], lse[0], rank.at[0], count[0, 0:1, 0:1], episode[0], hot[0, :, 0:1],
        latent, norms, w_q, w_o, *accs,
    )

    @pl.when(step == pl.num_programs(0) - 1)
    def _():
        copies = []

        def put(source, row):
            copies.append(
                pltpu.make_async_copy(source, flat.at[pl.ds(row, source.shape[0]), :], sems.at[len(copies)])
            )
            copies[-1].start()

        write_small(
            put, stage, low, latent_low, acc_latent, acc_q, acc_o, acc_episode,
            stacked(dnorm, dnorm_one, dnorm_sa, dnorm_two), stacked(dhid_one, dhid_two),
            stacked(dout, dout_one, dout_so, dout_two),
        )
        for copy in copies:
            copy.wait()
        tokens = kv_rows[1]
        for j in range(dkv_t.shape[1] // tokens):
            kv_low[...] = dkv_t[:, j * tokens : (j + 1) * tokens].T
            copy = pltpu.make_async_copy(kv_low, flat.at[pl.ds(kv_rows[0] + j * tokens, tokens), :], sems.at[0])
            copy.start()
            copy.wait()


def fixed(*shape):
    return pl.BlockSpec(shape, lambda i: (0,) * len(shape), pipeline_mode=pl.Buffered(1))


def kept(*shape):
    return pl.BlockSpec(shape, lambda i: (0,) * len(shape))


def rowed(rows, cols):
    return pl.BlockSpec((rows, cols), lambda i: (i, 0))


def framed(*shape):
    return pl.BlockSpec((1,) + shape, lambda i: (i,) + (0,) * len(shape))


def shaped(shape, dtype=F32):
    return jax.ShapeDtypeStruct(shape, dtype)


def call(kernel, grid, in_specs, outs, args, flops=0, trans=0, scratch=(), limit=56, aliases=None, collective=None):
    out_specs, out_shapes = zip(*outs)
    moved = sum(math.prod(a.shape) * a.dtype.itemsize for a in args)
    moved += sum(math.prod(s.shape) * s.dtype.itemsize for s in out_shapes)
    return pl.pallas_call(
        kernel,
        grid=(grid,),
        in_specs=in_specs,
        out_specs=list(out_specs),
        out_shape=list(out_shapes),
        scratch_shapes=list(scratch),
        input_output_aliases=aliases or {},
        compiler_params=pltpu.CompilerParams(
            dimension_semantics=("arbitrary",),
            vmem_limit_bytes=limit * MIB,
            collective_id=collective,
            has_side_effects=collective is not None,
        ),
        cost_estimate=pl.CostEstimate(flops=flops, bytes_accessed=moved, transcendentals=trans),
    )(*args)


def reduce_all(flat, master_rows, starts, ends, bias_owner, bias_row, tokens, tok_normed, w_kv, tok_norm, g1, cross):
    shard = master_rows.shape[0]
    vmem = pl.BlockSpec(memory_space=pltpu.VMEM)
    anywhere = pl.BlockSpec(memory_space=pl.ANY)
    dma = pltpu.SemaphoreType.DMA
    first = [
        pltpu.VMEM((8, STAT_ROWS, LANES), F32), dma((7,)), dma((7,)), pltpu.VMEM((16, LANES), BF),
        pltpu.VMEM((DIN, LANES), BF), dma((2,)), pltpu.VMEM(g1.shape, F32), dma((g1.shape[0],)),
        pltpu.VMEM((8, tokens.shape[0], LANES), BF), dma((16,)),
    ]
    grads = flat.reshape(2, 2, 2, -1, LANES)
    return pl.pallas_call(
        functools.partial(reduce_kernel, bias_owner, bias_row),
        out_shape=[
            shaped((shard, LANES), BF), shaped((STAT_ROWS, LANES)), shaped(tokens.shape, BF),
            shaped(grads.shape, BF),
        ],
        in_specs=[vmem, vmem, anywhere] + [vmem] * 5 + [anywhere] + [vmem] * len(cross),
        out_specs=[vmem, vmem, vmem, anywhere],
        scratch_shapes=first
        + cross_accumulators(8 * tokens.shape[0])
        + small_buffers()
        + Reduction.scratch(shard),
        input_output_aliases={2: 3},
        compiler_params=pltpu.CompilerParams(
            collective_id=1, has_side_effects=True, vmem_limit_bytes=56 * MIB
        ),
    )(starts, ends, grads, master_rows, tokens, tok_normed, w_kv, tok_norm, g1, *cross)


def body(tokens, frame_ids, episodes, master, moment_one, moment_two, latent_grad):
    lat_count = lax.axis_size("lat")
    lat_index = lax.axis_index("lat")
    shard_len = master.shape[0]
    frame_total = episodes.shape[1]
    frames = frame_total // lat_count
    rows_total = frames * LAT
    total_keys = frame_ids.shape[1] * lat_count
    cap = total_keys // 8
    token_rows_count = total_keys // LANES

    reach = lat_count == 8 and lax.axis_size("kf") == 4
    shard_rows = shard_len // LANES
    master_rows = master.reshape(shard_rows, LANES)
    episode_index = jnp.arange(EPISODES, dtype=jnp.int32)
    own_episodes = lax.dynamic_slice_in_dim(episodes[0], lat_index * frames, frames, 0)
    episode_match = own_episodes[:, None] == episode_index[None, :]
    score_flops = rows_total * cap * LANES * 2
    select_flops = frames * cap * total_keys * LANES * 2
    if reach:
        hot = jnp.pad(episode_match.astype(BF), ((0, 16 - frames), (0, 16 - EPISODES)))
        (
            up_one, down_one, w_qkv, w_so, up_two, down_two,
            latent, norms, hid_bias, out_bias, w_q, w_o, w_kv, tok_norm, tok_normed, episode_rows, rank, counts,
            kvf, cross_out, cross_lse, h1,
        ) = begin_all(master_rows, tokens[0], frame_ids.reshape(-1, LANES), hot, frames, cap)
    else:
        weights = split_flat(lax.all_gather(master.astype(BF), "lat", axis=0, tiled=True))
        norms = weights["lat_norms"].astype(F32)
        out_bias = weights["out_bias"].astype(F32)
        hid_bias = weights["hid_bias"].astype(F32)
        tok_norm = weights["tok_norm"].astype(F32)
        w_kv, w_qkv, w_so, latent = (weights[name] for name in ("w_kv", "w_qkv", "w_so", "latent"))
        up_one, up_two = weights["w_up"]
        down_one, down_two = weights["w_down"]
        frame_tag = lax.all_gather(frame_ids[0].astype(BF), "lat", axis=0, tiled=True).astype(jnp.int32)
        own_frames = lat_index * frames + jnp.arange(frames, dtype=jnp.int32)
        own_hit = frame_tag[None, :] == own_frames[:, None]
        rank = jnp.cumsum(own_hit.astype(jnp.int32), axis=1) - 1
        counts = jnp.broadcast_to(rank[:, -1][:, None, None] + 1, (frames, 8, LANES))
        rank = jnp.where(own_hit, rank, -1).reshape(frames, token_rows_count, LANES)
        tok_normed = layer_norm(tokens[0].astype(F32), tok_norm[0], tok_norm[1]).astype(BF)
        key_value = mm(tok_normed, w_kv).astype(BF)
        all_keys = lax.all_gather(key_value, "lat", axis=0, tiled=True)
        episode_rows = mm(episode_match.astype(BF), weights["episode"]).reshape(frames, 1, D)
        w_q = jnp.pad(weights["w_q"], ((0, 0), (0, LANES - CH)))
        w_o = jnp.pad(weights["w_o"], ((LANES - CH, 0), (0, 0)))
        h1, kvf, cross_out, cross_lse = call(
            cross_fwd_kernel,
            frames,
            [
                fixed(LAT, D), framed(1, D), fixed(8, D), fixed(D, LANES), fixed(LANES, D), fixed(4, D),
                fixed(total_keys, LANES), framed(token_rows_count, LANES), framed(8, LANES),
            ],
            [
                (rowed(LAT, D), shaped((rows_total, D))),
                (framed(cap, LANES), shaped((frames, cap, LANES), BF)),
                (rowed(LAT, LANES), shaped((rows_total, LANES), BF)),
                (framed(1, LAT), shaped((frames, 1, LAT))),
            ],
            (latent, episode_rows, norms, w_q, w_o, out_bias, all_keys, rank, counts),
            flops=2 * score_flops + select_flops,
            trans=rows_total * cap,
        )
    mlp_flops = 4 * rows_total * D * FF
    attn_flops = 4 * rows_total * LAT * D
    anywhere = pl.BlockSpec(memory_space=pl.ANY)
    token_count = frame_ids.shape[1]
    if reach:
        flat_shard, extra = shard_rows, token_count
        flat_shape = (lat_count * (shard_rows + extra), LANES)
        kv_rows = (shard_rows, token_count, shard_rows + extra)
        grad_in, grad_spec = latent_grad[0], anywhere
        latents_spec = (anywhere, shaped(latent_grad.shape[1:], BF))
        shared = [pltpu.VMEM((frames, LAT, D), BF)] * 2 + FrameExchange.scratch(frames)
    else:
        flat_shard, extra = NPARAM // LANES, 0
        flat_shape = (flat_shard + total_keys, LANES)
        kv_rows = (flat_shard, 512, 512)
        grad_in = lax.all_to_all(
            latent_grad[0], "lat", split_axis=0, concat_axis=1, tiled=True
        ).reshape(rows_total, D)
        grad_spec = rowed(LAT, D)
        latents_spec = (rowed(LAT, D), shaped((rows_total, D), BF))
        shared = []
    slab = D * FF // LANES
    h2, qkv, self_lse, mixed, act_one, slope_one, latents, g3, dhid_two, dnorm_two, dout_two, flat = call(
        functools.partial(forward_kernel, reach, flat_shard, extra),
        frames,
        [
            rowed(LAT, D), grad_spec, fixed(8, D), fixed(2, FF), fixed(4, D), fixed(D, FF), fixed(FF, D),
            fixed(D, 3 * D), fixed(D, D), fixed(D, FF), fixed(FF, D),
        ],
        [
            (rowed(LAT, D), shaped((rows_total, D))),
            (rowed(LAT, 3 * D), shaped((rows_total, 3 * D), BF)),
            (framed(HEADS, LAT), shaped((frames, HEADS, LAT))),
            (rowed(LAT, D), shaped((rows_total, D), BF)),
            (rowed(LAT, FF), shaped((rows_total, FF), BF)),
            (rowed(LAT, FF), shaped((rows_total, FF), BF)),
            latents_spec,
            (rowed(LAT, D), shaped((rows_total, D))),
            (kept(1, FF), shaped((1, FF))),
            (kept(2, D), shaped((2, D))),
            (kept(1, D), shaped((1, D))),
            (anywhere, shaped(flat_shape, BF)),
        ],
        (h1, grad_in, norms, hid_bias, out_bias, up_one, down_one, w_qkv, w_so, up_two, down_two),
        flops=4 * mlp_flops + 4 * attn_flops,
        trans=4 * rows_total * FF,
        scratch=[
            pltpu.VMEM((LAT, FF), BF), pltpu.VMEM((LAT, FF), BF), pltpu.VMEM((D, FF), F32), pltpu.VMEM((FF, D), F32),
            pltpu.VMEM((2048, LANES), F32), pltpu.VMEM((2, slab, LANES), BF), pltpu.VMEM((LAT, D), BF),
            pltpu.VMEM((D, LAT), F32), pltpu.VMEM((LAT, D), F32), pltpu.SemaphoreType.DMA((2, 16)),
        ]
        + shared,
        limit=62,
        collective=4 if reach else None,
    )
    if reach:
        latents_out = latents[None]
    else:
        latents_out = lax.all_to_all(
            latents.reshape(frames, LAT, D), "lat", split_axis=1, concat_axis=0, tiled=True
        )[None]
    hot_lanes = jnp.broadcast_to(
        jnp.pad(episode_match.astype(F32), ((0, 0), (0, 16 - EPISODES)))[:, :, None], (frames, 16, LANES)
    )
    g1, dhid_one, dnorm_sa, dnorm_one, dout_so, dout_one, flat = call(
        functools.partial(backward_kernel, flat_shard, extra),
        frames,
        [
            rowed(LAT, 3 * D), framed(HEADS, LAT), rowed(LAT, D), rowed(LAT, D), rowed(LAT, D), rowed(LAT, D),
            rowed(LAT, FF), rowed(LAT, FF), fixed(8, D), fixed(D, D), fixed(D, 3 * D), fixed(D, FF), fixed(FF, D),
            anywhere,
        ],
        [
            (rowed(LAT, D), shaped((rows_total, D))),
            (kept(1, FF), shaped((1, FF))),
            (kept(2, D), shaped((2, D))),
            (kept(2, D), shaped((2, D))),
            (kept(1, D), shaped((1, D))),
            (kept(1, D), shaped((1, D))),
            (anywhere, shaped(flat_shape, BF)),
        ],
        (
            qkv, self_lse, mixed, g3, h2, h1, act_one, slope_one, norms, w_so, w_qkv, up_one, down_one, flat,
        ),
        flops=2 * mlp_flops + 10 * attn_flops,
        trans=rows_total * LAT * HEADS,
        scratch=[
            pltpu.VMEM((LAT, 3 * D), BF), pltpu.VMEM((D, FF), F32), pltpu.VMEM((FF, D), F32),
            pltpu.VMEM((D, 3 * D), F32), pltpu.VMEM((D, D), F32),
            pltpu.VMEM((2048, LANES), F32), pltpu.VMEM((2, slab, LANES), BF), pltpu.VMEM((LAT, D), BF),
            pltpu.VMEM((LAT, D), BF), pltpu.VMEM((LAT, D), BF), pltpu.VMEM((LAT, D), F32),
            pltpu.SemaphoreType.DMA((2, 16)),
        ],
        limit=60,
        aliases={13: 6},
    )
    cross = (
        kvf, cross_out, cross_lse, rank, counts, episode_rows, hot_lanes, latent, norms, w_q, w_o,
        dnorm_one, dnorm_sa, dnorm_two, dhid_one, dhid_two, dout_one, dout_so, dout_two,
    )
    layout = param_layout()
    starts, ends, offset, bias_offset = [], [], 0, 0
    for name, shape in layout:
        if name == "hid_bias":
            bias_offset = offset
        starts.append(offset // LANES)
        offset += math.prod(shape)
        ends.append(offset // LANES)
    pad = [0] * (16 - len(layout))
    starts = jnp.broadcast_to(jnp.array(starts + pad, jnp.int32)[:, None], (16, LANES))
    ends = jnp.broadcast_to(jnp.array(ends + pad, jnp.int32)[:, None], (16, LANES))
    opt_rows = shard_rows // 2 if shard_rows % 16 == 0 else shard_rows
    opt_steps = shard_rows // opt_rows
    base = (lat_index * shard_rows).astype(jnp.int32).reshape(1)
    smem = pl.BlockSpec(memory_space=pltpu.SMEM)
    flat_rows = (shard_rows, LANES)
    bias_owner, bias_at = divmod(bias_offset, shard_len)
    if reach:
        summed, stats, token_grad, unused = reduce_all(
            flat, master_rows, starts, ends, bias_owner, bias_at // LANES, tokens[0], tok_normed, w_kv, tok_norm,
            g1.reshape(frames, LAT, D), cross,
        )
    else:
        (flat,) = call(
            functools.partial(cross_bwd_kernel, kv_rows),
            frames,
            [
                rowed(LAT, D), framed(cap, LANES), rowed(LAT, LANES), framed(1, LAT), framed(token_rows_count, LANES),
                framed(8, LANES), framed(1, D), framed(16, LANES), fixed(LAT, D), fixed(8, D), fixed(D, LANES),
                fixed(LANES, D),
            ]
            + [fixed(*part.shape) for part in cross[11:]]
            + [anywhere],
            [(anywhere, shaped(flat_shape, BF))],
            (g1,) + cross + (flat,),
            flops=6 * score_flops,
            trans=rows_total * cap,
            scratch=cross_accumulators(total_keys)
            + small_buffers()
            + [pltpu.VMEM((kv_rows[1], LANES), BF), pltpu.SemaphoreType.DMA((8,))],
            aliases={20: 0},
        )
        grad_kv = lax.psum_scatter(flat[flat_shard:], "lat", scatter_dimension=0, tiled=True)
        flat = flat[:flat_shard]
        grad_w_kv = t_mm(tok_normed, grad_kv)
        grad_tok_normed = mm_t(grad_kv, w_kv)
        unused, token_pull = jax.vjp(layer_norm, tokens[0].astype(F32), tok_norm[0], tok_norm[1])
        grad_tokens, grad_tok_gain, grad_tok_bias = token_pull(grad_tok_normed)
        token_grad = grad_tokens.astype(BF)
        flat_at = flat_rows_of()
        tok_norm_grad = jnp.stack([grad_tok_gain, grad_tok_bias]).reshape(-1, LANES).astype(BF)
        flat = lax.dynamic_update_slice(flat, tok_norm_grad, (flat_at["tok_norm"], 0))
        flat = lax.dynamic_update_slice(flat, grad_w_kv.astype(BF), (flat_at["w_kv"], 0))
        local_flat = flat.reshape(-1)
        summed = lax.psum_scatter(local_flat, "lat", scatter_dimension=0, tiled=True)
        summed = lax.psum(summed, "kf").reshape(flat_rows)
        grad_sq, weight_sq = call(
            grad_stats_kernel,
            opt_steps,
            [smem, fixed(16, LANES), fixed(16, LANES), rowed(opt_rows, LANES), rowed(opt_rows, LANES)],
            [(kept(1, LANES), shaped((1, LANES))), (kept(16, LANES), shaped((16, LANES)))],
            (base, starts, ends, summed, master_rows),
        )
        bias_rows = summed[bias_at // LANES : bias_at // LANES + 2 * FF // LANES].astype(F32)
        bias_rows = jnp.where(lat_index == bias_owner, bias_rows, 0.0)
        stats = lax.psum(
            jnp.concatenate([grad_sq, jnp.zeros((7, LANES), F32), weight_sq, bias_rows]), "lat"
        )
    bias_grad = stats[24:STAT_ROWS].reshape(2, FF)
    grad_shard, lamb_update, new_one, new_two, update_sq = call(
        lamb_kernel,
        opt_steps,
        [smem, fixed(STAT_ROWS, LANES), fixed(16, LANES), fixed(16, LANES)] + [rowed(opt_rows, LANES)] * 4,
        [(rowed(opt_rows, LANES), shaped(flat_rows))] * 4 + [(kept(16, LANES), shaped((16, LANES)))],
        (
            base, stats, starts, ends, summed, master_rows,
            moment_one.reshape(flat_rows), moment_two.reshape(flat_rows),
        ),
    )
    if reach:
        vmem = pl.BlockSpec(memory_space=pltpu.VMEM)
        trust = pl.pallas_call(
            trust_kernel,
            out_shape=shaped((16, LANES)),
            in_specs=[vmem, vmem],
            out_specs=vmem,
            scratch_shapes=[
                pltpu.VMEM((8, 16, LANES), F32),
                pltpu.SemaphoreType.DMA((7,)),
                pltpu.SemaphoreType.DMA((7,)),
            ],
            compiler_params=pltpu.CompilerParams(collective_id=2, has_side_effects=True),
        )(update_sq, stats)[: len(layout), 0]
    else:
        update_sq = lax.psum(jnp.sum(update_sq, axis=1), "lat")
        weight_sq = jnp.sum(stats[8:24], axis=1)
        trust = (jnp.sqrt(weight_sq) / (jnp.sqrt(update_sq) + 1e-06))[: len(layout)]
    return (
        latents_out,
        token_grad[None],
        grad_shard.reshape(-1),
        lamb_update.reshape(-1),
        new_one.reshape(-1),
        new_two.reshape(-1),
        trust,
        bias_grad,
    )


def solution(mesh):
    return jax.shard_map(
        body,
        mesh=mesh,
        in_specs=(
            P("kf", "lat", None),
            P("kf", "lat"),
            P("kf", None),
            P("lat"),
            P("lat"),
            P("lat"),
            P("kf", None, "lat", None),
        ),
        out_specs=(
            P("kf", None, "lat", None),
            P("kf", "lat", None),
            P("lat"),
            P("lat"),
            P("lat"),
            P("lat"),
            P(),
            P(),
        ),
        check_vma=False,
    )
```

```python
import functools
import math

import jax
import jax.numpy as jnp
import numpy as np
from jax import lax
from jax.experimental import pallas as pl
from jax.experimental.pallas import tpu as pltpu
from jax.sharding import PartitionSpec as P

DIN = 256
D = 512
LAT = 512
CH = 64
HEADS = 8
HEAD_DIM = 64
FF = 2048
EPISODES = 11
NPARAM = 5619712
LANES = 128

norm_eps = 1e-05
masked_fill = -1e30
beta_one = 0.9
beta_two = 0.999
adam_eps = 1e-06
decay_rate = 0.01
clip_fraction = 0.5
lamb_step = 10.0

BF = jnp.bfloat16
F32 = jnp.float32
MIB = 1024 * 1024


def param_layout():
    return [
        ("latent", (LAT, D)),
        ("episode", (EPISODES, D)),
        ("tok_norm", (2, DIN)),
        ("lat_norms", (8, D)),
        ("w_kv", (DIN, 2 * CH)),
        ("w_q", (D, CH)),
        ("w_o", (CH, D)),
        ("w_qkv", (D, 3 * D)),
        ("w_so", (D, D)),
        ("w_up", (2, D, FF)),
        ("w_down", (2, FF, D)),
        ("hid_bias", (2, FF)),
        ("out_bias", (4, D)),
    ]


def split_flat(flat_vector):
    pieces = {}
    offset = 0
    for tensor_name, tensor_shape in param_layout():
        entries = math.prod(tensor_shape)
        pieces[tensor_name] = flat_vector[offset : offset + entries].reshape(tensor_shape)
        offset += entries
    return pieces


def layer_norm(inputs, norm_gain, norm_bias):
    row_mean = jnp.mean(inputs, axis=-1, keepdims=True)
    centered = inputs - row_mean
    row_var = jnp.mean(centered * centered, axis=-1, keepdims=True)
    return centered * lax.rsqrt(row_var + norm_eps) * norm_gain + norm_bias


def mm(left, right):
    return jnp.dot(left, right, preferred_element_type=F32)


def mm_t(left, right):
    return lax.dot_general(left, right, (((1,), (1,)), ((), ())), preferred_element_type=F32)


def t_mm(left, right):
    return lax.dot_general(left, right, (((0,), (0,)), ((), ())), preferred_element_type=F32)


def norm_stats(rows):
    mean = jnp.mean(rows, axis=-1, keepdims=True)
    centered = rows - mean
    var = jnp.mean(centered * centered, axis=-1, keepdims=True)
    rstd = lax.rsqrt(var + norm_eps)
    return centered * rstd, rstd


def norm_back(grad, xhat, rstd, gain):
    dxh = grad * gain
    first = jnp.mean(dxh, axis=-1, keepdims=True)
    second = jnp.mean(dxh * xhat, axis=-1, keepdims=True)
    return rstd * (dxh - first - xhat * second)


def col_sum(values):
    return jnp.sum(values, axis=0, keepdims=True)


def gelu_pair(x):
    cdf = 0.5 + 0.5 * lax.erf(x * (1.0 / math.sqrt(2.0)))
    density = jnp.exp(x * x * -0.5) * (1.0 / math.sqrt(2.0 * math.pi))
    return x * cdf, cdf + x * density


def accumulate(first, ref, value):
    @pl.when(first)
    def _():
        ref[...] = value

    @pl.when(jnp.logical_not(first))
    def _():
        ref[...] += value


def lane_half(shape, half):
    lane = lax.broadcasted_iota(jnp.int32, shape, 1)
    return (lane >= half * 64) & (lane < half * 64 + 64)


def keep_half(values, half):
    return jnp.where(lane_half(values.shape, half), values, jnp.zeros_like(values))


def select_tokens(rank_rows, cap):
    slot = lax.broadcasted_iota(jnp.int32, (cap, LANES), 0)
    parts = []
    for r in range(rank_rows.shape[0]):
        hit = slot == rank_rows[r : r + 1, :]
        parts.append(jnp.where(hit, 1.0, 0.0).astype(BF))
    return jnp.concatenate(parts, axis=1)


def cross_scores(kvf, queries_scaled, count):
    scores = mm_t(kvf, queries_scaled)
    slot = lax.broadcasted_iota(jnp.int32, scores.shape, 0)
    return jnp.where(slot < count, scores, masked_fill)


def cross_attend(start, norms, w_q, kvf, count):
    xhat, unused = norm_stats(start)
    query_in = (xhat * norms[0:1, :] + norms[1:2, :]).astype(BF)
    queries = mm(query_in, w_q[...]).astype(BF) * jnp.asarray(0.125, BF)
    scores = cross_scores(kvf, queries, count)
    top = jnp.max(scores, axis=0, keepdims=True)
    terms = jnp.exp(scores - top)
    total = jnp.sum(terms, axis=0, keepdims=True)
    prob = (terms * (1.0 / total)).astype(BF)
    return t_mm(kvf, prob).T.astype(BF), top + jnp.log(total)


def cross_fwd_kernel(latent, episode, norms, w_q, w_o, out_bias, kv, rank, count, h1, kvf_out, co_out, lse_out):
    cap = kvf_out.shape[1]
    start = latent[...].astype(F32) + episode[0]
    chunk = 8 * LANES
    chunks = kv.shape[0] // chunk

    def step(j, acc):
        sel = select_tokens(rank[0, pl.ds(pl.multiple_of(j * 8, 8), 8), :], cap)
        return acc + mm(sel, kv[pl.ds(pl.multiple_of(j * chunk, chunk), chunk), :])

    kvf = lax.fori_loop(0, chunks, step, jnp.zeros((cap, LANES), F32)).astype(BF)
    co, lse = cross_attend(start, norms, w_q, kvf, count[0, 0:1, 0:1])
    h1[...] = start + mm(co, w_o[...]) + out_bias[0:1, :]
    kvf_out[0] = kvf
    co_out[...] = co
    lse_out[0] = lse


def segment_hot(starts, ends, base, rows):
    row = lax.broadcasted_iota(jnp.int32, (16, rows), 1) + base
    return jnp.where((row >= starts[:, 0:1]) & (row < ends[:, 0:1]), 1.0, 0.0).astype(BF)


def segment_sums(hot, squares):
    high = squares.astype(BF)
    low = (squares - high.astype(F32)).astype(BF)
    return mm(hot, high) + mm(hot, low)


def grad_stats_kernel(base, starts, ends, summed, master, grad_sq, weight_sq):
    i = pl.program_id(0)
    rows = master.shape[0]
    hot = segment_hot(starts, ends, base[0] + i * rows, rows)
    grad = summed[...].astype(F32)
    accumulate(i == 0, grad_sq, col_sum(grad * grad))
    accumulate(i == 0, weight_sq, segment_sums(hot, master[...] * master[...]))


def lamb_kernel(base, stats, starts, ends, summed, master, one, two, grad_out, update_out, one_out, two_out, update_sq):
    i = pl.program_id(0)
    rows = master.shape[0]
    hot = segment_hot(starts, ends, base[0] + i * rows, rows)
    total_sq = jnp.sum(stats[0:1, :], axis=1, keepdims=True)
    clip = jnp.minimum(1.0, clip_fraction * math.sqrt(NPARAM) / (jnp.sqrt(total_sq) + 1e-06))
    grad = summed[...].astype(F32)
    grad_out[...] = grad
    clipped = clip * grad
    new_one = beta_one * one[...] + (1.0 - beta_one) * clipped
    new_two = beta_two * two[...] + (1.0 - beta_two) * clipped * clipped
    one_out[...] = new_one
    two_out[...] = new_two
    first_hat = new_one * (1.0 / (1.0 - beta_one**lamb_step))
    second_hat = new_two * (1.0 / (1.0 - beta_two**lamb_step))
    update = first_hat / (jnp.sqrt(second_hat) + adam_eps) + decay_rate * master[...]
    update_out[...] = update
    accumulate(i == 0, update_sq, segment_sums(hot, update * update))


BATCH = 256
HALF = 128
QUARTER = 64
MESH = pl.DeviceIdType.MESH


class Place:
    def __init__(self):
        self.z = lax.axis_index("kf")
        self.me = lax.axis_index("lat")
        self.core = lax.rem(self.me, 2)
        self.x = lax.rem(self.me // 2, 2)
        self.y = self.me // 4
        self.z_low = lax.rem(self.z, 2)
        self.z_high = self.z // 2
        self.sibling = (self.z, self.me + 1 - 2 * self.core)
        self.x_side = (self.z, self.me + 2 - 4 * self.x)
        self.y_side = (self.z, self.me + 4 - 8 * self.y)
        self.z_near = (self.z + 1 - 2 * self.z_low, self.me)
        self.z_far = (self.z + 2 - 4 * self.z_high, self.me)

    def z_other(self, step):
        return (lax.rem(self.z + step, 4), self.me)

    def lat_other(self, step):
        return (self.z, lax.rem(self.me + step, 8))


def remote(src, dst, send, recv, device):
    return pltpu.make_async_remote_copy(
        src_ref=src, dst_ref=dst, send_sem=send, recv_sem=recv, device_id=device, device_id_type=MESH
    )


def greet(devices):
    barrier = pltpu.get_barrier_semaphore()
    for device in devices:
        pl.semaphore_signal(barrier, inc=1, device_id=device, device_id_type=MESH)
    pl.semaphore_wait(barrier, len(devices))


def added(left, right):
    return (left.astype(F32) + right.astype(F32)).astype(BF)


class Reduction:
    lags = (0, 1, 3, 5, 7, 9, 11)
    plane = 2

    def __init__(self, place, shard, grads, out, bufs, sems):
        self.p = place
        self.grads = grads
        self.out = out
        self.own, self.rc, self.r1, self.r2, self.r3, self.r4, self.res = bufs
        self.own_sem, self.send, self.rc_sem, self.r1_sem, self.r2_sem, self.r3_sem, self.r4_sem, self.res_sem = sems
        self.shard = shard
        self.full = pl.cdiv(shard, BATCH)
        self.batches = self.full + self.plane
        self.back = self.full * BATCH - shard
        self.held = flat_rows_of()["tok_norm"] // BATCH
        self.early = self.full - 1 - (self.held + 4)

    @staticmethod
    def scratch(shard):
        n = pl.cdiv(shard, BATCH) + Reduction.plane
        bufs = [
            pltpu.VMEM((2, 2, 2, BATCH, LANES), BF),
            pltpu.VMEM((n, 2, 2, BATCH, LANES), BF),
            pltpu.VMEM((n, 2, 2, HALF, LANES), BF),
            pltpu.VMEM((n, 2, HALF, LANES), BF),
            pltpu.VMEM((n, HALF, LANES), BF),
            pltpu.VMEM((n, QUARTER, LANES), BF),
            pltpu.VMEM((n, BATCH, LANES), BF),
        ]
        dma = pltpu.SemaphoreType.DMA
        sems = [dma((2,)), dma((10, 4)), dma((n,)), dma((n, 2)), dma((n, 2)), dma((n,)), dma((n,)), dma((n, 3))]
        return bufs + sems

    def from_on(self, i, first):
        return (i + 64 - first) // 64

    def row(self, i):
        n, held = self.full, self.held
        on = functools.partial(self.from_on, i)
        keys = on(self.early) - on(self.early + 2)
        shift = held + 4 + on(self.early + 2) * (-2) + on(self.early + 3) * (-n)
        shift = shift + on(self.early + 3 + held) * 2 + on(self.early + 5 + held) * (-4)
        b = i + shift
        row = keys * (self.shard + (i - self.early) * BATCH)
        row = row + (1 - keys) * (b * BATCH - (b // (n - 1)) * self.back)
        return pl.multiple_of(row, 16)

    def is_keys(self, i):
        return (i >= self.early) & (i < self.early + self.plane)

    def own_copy(self, i):
        slot = lax.rem(i, 2)
        src = self.grads.at[:, :, self.p.core, pl.ds(self.row(i), BATCH), :]
        return pltpu.make_async_copy(src, self.own.at[slot], self.own_sem.at[slot])

    def copies(self, stage, i):
        p, slot = self.p, lax.rem(i, 4)
        if stage == 0:
            src = self.grads.at[:, :, 1 - p.core, pl.ds(self.row(i), BATCH), :]
            return [remote(src, self.rc.at[i], self.send.at[0, slot], self.rc_sem.at[i], p.sibling)]
        if stage == 1:
            to_x = self.rc.at[i, :, 1 - p.x, pl.ds(0, HALF), :]
            to_y = self.rc.at[i, 1 - p.y, :, pl.ds(HALF, HALF), :]
            return [
                remote(to_x, self.r1.at[i, 0], self.send.at[1, slot], self.r1_sem.at[i, 0], p.x_side),
                remote(to_y, self.r1.at[i, 1], self.send.at[2, slot], self.r1_sem.at[i, 1], p.y_side),
            ]
        if stage == 2:
            to_y = self.r1.at[i, 0, 1 - p.y]
            to_x = self.r1.at[i, 1, 1 - p.x]
            return [
                remote(to_y, self.r2.at[i, 0], self.send.at[3, slot], self.r2_sem.at[i, 0], p.y_side),
                remote(to_x, self.r2.at[i, 1], self.send.at[4, slot], self.r2_sem.at[i, 1], p.x_side),
            ]
        if stage == 3:
            src = self.r2.at[i, 1 - p.z_low]
            return [remote(src, self.r3.at[i], self.send.at[5, slot], self.r3_sem.at[i], p.z_near)]
        if stage == 4:
            src = self.r3.at[i, pl.ds(pl.multiple_of((1 - p.z_high) * QUARTER, QUARTER), QUARTER), :]
            return [remote(src, self.r4.at[i], self.send.at[6, slot], self.r4_sem.at[i], p.z_far)]
        mine = self.res.at[i, pl.ds(pl.multiple_of(p.z_low * HALF + p.z_high * QUARTER, QUARTER), QUARTER), :]
        return [
            remote(mine, mine, self.send.at[6 + d, slot], self.res_sem.at[i, d - 1], p.z_other(d))
            for d in (1, 2, 3)
        ]

    def launch(self, stage, i):
        before = i - 4
        if stage >= 3:
            before = before - 4 * (self.from_on(before, self.early) - self.from_on(before, self.early + self.plane))

        @pl.when(i >= 4)
        def _():
            for copy in self.copies(stage, before):
                copy.wait_send()

        for copy in self.copies(stage, i):
            copy.start()

    def landed(self, stage, i):
        for copy in self.copies(stage, i):
            copy.wait_recv()

    def work(self, stage, i):
        p = self.p
        if stage == 0:
            self.own_copy(i).start()
        elif stage == 1:
            self.landed(0, i)
            self.own_copy(i).wait()
            self.rc[i] = added(self.rc[i], self.own[lax.rem(i, 2)])
        elif stage == 2:
            self.landed(1, i)
            self.r1[i, 0] = added(self.r1[i, 0], self.rc[i, :, p.x, 0:HALF, :])
            self.r1[i, 1] = added(self.r1[i, 1], self.rc[i, p.y, :, HALF:BATCH, :])
        elif stage == 3:
            self.landed(2, i)
            self.r2[i, 0] = added(self.r2[i, 0], self.r1[i, 0, p.y])
            self.r2[i, 1] = added(self.r2[i, 1], self.r1[i, 1, p.x])
        elif stage == 4:
            self.landed(3, i)
            self.r3[i] = added(self.r3[i], self.r2[i, p.z_low])
        elif stage == 5:
            self.landed(4, i)
            part = self.r3[i, pl.ds(pl.multiple_of(p.z_high * QUARTER, QUARTER), QUARTER), :]
            at = pl.multiple_of(p.z_low * HALF + p.z_high * QUARTER, QUARTER)
            self.res[i, pl.ds(at, QUARTER), :] = added(self.r4[i], part)
        else:
            self.landed(5, i)
            self.out[pl.ds(self.row(i), BATCH), :] = self.res[i]
        if stage == 3:
            pl.when(jnp.logical_not(self.is_keys(i)))(lambda: self.launch(stage, i))
        elif stage < 6:
            self.launch(stage, i)

    def tick(self, t):
        for stage, lag in enumerate(self.lags):
            i = t - lag

            inside = (i >= 0) & (i < self.batches)

            @pl.when(inside if stage < 4 else inside & jnp.logical_not(self.is_keys(i)))
            def _(stage=stage, i=i):
                self.work(stage, i)

    def ticks(self):
        return self.batches + self.lags[-1]

    def finish(self):
        for stage in range(6):
            for back in range(4):
                for copy in self.copies(stage, self.batches - 4 + back):
                    copy.wait_send()

    def partners(self):
        p = self.p
        return [p.sibling, p.x_side, p.y_side] + [p.z_other(d) for d in (1, 2, 3)]


def share_all(place, block, send, recv):
    mine = block.at[place.me]
    copies = [
        remote(mine, mine, send.at[d - 1], recv.at[d - 1], place.lat_other(d)) for d in range(1, 8)
    ]
    for copy in copies:
        copy.start()
    for copy in copies:
        copy.wait()


STAT_ROWS = 56


def token_backward(grad_kv, tokens, tok_normed, w_kv, tok_norm, token_grad, kv_grad, edge):
    kv_grad[...] = t_mm(tok_normed[...], grad_kv).astype(BF)
    grad = mm_t(grad_kv, w_kv[...])
    xhat, rstd = norm_stats(tokens[...].astype(F32))
    token_grad[...] = norm_back(grad, xhat, rstd, tok_norm[0:1, :]).astype(BF)
    gain, bias = col_sum(grad * xhat), col_sum(grad)
    parts = [half[:, j * LANES : (j + 1) * LANES] for half in (gain, bias) for j in range(DIN // LANES)]
    keep = edge.shape[0] - len(parts)
    edge[...] = jnp.concatenate([edge[...].astype(F32)[0:keep, :]] + parts, axis=0).astype(BF)


def reduce_kernel(
    bias_owner, bias_at, starts, ends, unused_flat, master, tokens, tok_normed, w_kv, tok_norm,
    g1, kvf, co, lse, rank, count, episode, hot, latent, norms, w_q, w_o,
    dnorm_one, dnorm_sa, dnorm_two, dhid_one, dhid_two, dout_one, dout_so, dout_two,
    summed, stats, token_grad, grads, *scratch,
):
    place = Place()
    block, block_send, block_recv, edge, kv_grad, edge_sem, g1_held, g1_sem, kv_low, kv_sem = scratch[:10]
    accs, (stage, low, latent_low), engine = scratch[10:17], scratch[17:20], scratch[20:]
    acc_latent, acc_q, acc_o, acc_episode, dnorm, dout, dkv_t = accs
    shard, frames = master.shape[0], kvf.shape[0]
    red = Reduction(place, shard, grads, summed, engine[:7], engine[7:])
    frame_copies = [pltpu.make_async_copy(g1.at[f], g1_held.at[f], g1_sem.at[f]) for f in range(frames)]
    for copy in frame_copies:
        copy.start()
    greet([place.lat_other(d) for d in range(1, 8)] + [place.z_other(d) for d in (1, 2, 3)])
    for ref in accs:
        ref[...] = jnp.zeros_like(ref)

    def run(first, last):
        lax.fori_loop(first, last, lambda t, c: (red.tick(t), c)[1], 0)

    def frame(f, carry):
        red.tick(2 * f)
        pltpu.make_async_copy(g1.at[f], g1_held.at[f], g1_sem.at[f]).wait()
        rows = pl.ds(pl.multiple_of(f * LAT, LAT), LAT)
        cross_back_frame(
            g1_held[f], kvf[f], co[rows, :], lse[f], rank.at[f], count[f, 0:1, 0:1], episode[f], hot[f, :, 0:1],
            latent, norms, w_q, w_o, *accs, pause=lambda: red.tick(2 * f + 1),
        )
        return carry

    lax.fori_loop(0, frames, frame, 0)
    run(2 * frames, red.early)
    at = flat_rows_of()
    copies = []

    def put(source, row):
        owner, local = row if isinstance(row, tuple) else divmod(row, shard)
        dst = grads.at[owner // 4, owner // 2 % 2, owner % 2, pl.ds(local, source.shape[0]), :]
        copies.append(pltpu.make_async_copy(source, dst, kv_sem.at[len(copies)]))
        copies[-1].start()

    write_small(
        put, stage, low, latent_low, acc_latent, acc_q, acc_o, acc_episode,
        stacked(dnorm, dnorm_one, dnorm_sa, dnorm_two), stacked(dhid_one, dhid_two),
        stacked(dout, dout_one, dout_so, dout_two),
    )
    edge_row = at["tok_norm"] // 16 * 16
    edge[...] = low[0, edge_row - at["episode"] : edge_row - at["episode"] + 16, :]
    count_kv = tokens.shape[0]
    for j in range(8):
        kv_low[j] = dkv_t[:, j * count_kv : (j + 1) * count_kv].T
        put(kv_low.at[j], (j, shard))
    for copy in copies:
        copy.wait()
    ready = red.early + red.lags[3] + red.plane
    run(red.early, ready)
    grad_kv = jnp.concatenate([red.r2[red.early + i, h] for i in range(red.plane) for h in range(2)], axis=0)
    token_backward(grad_kv, tokens, tok_normed, w_kv, tok_norm, token_grad, kv_grad, edge)
    writes = [
        pltpu.make_async_copy(edge, grads.at[0, 0, 0, pl.ds(edge_row, 16), :], edge_sem.at[0]),
        pltpu.make_async_copy(kv_grad, grads.at[0, 0, 0, pl.ds(at["w_kv"], DIN), :], edge_sem.at[1]),
    ]
    for copy in writes:
        copy.start()
    run(ready, ready + 2)
    for copy in writes:
        copy.wait()
    step = 784
    weight_sq = jnp.zeros((16, LANES), F32)
    for j in range(shard // step):
        hot_rows = segment_hot(starts, ends, place.me * shard + j * step, step)
        part = master[j * step : (j + 1) * step, :]
        weight_sq = weight_sq + segment_sums(hot_rows, part * part)
    run(ready + 2, red.ticks())
    grad_sq = jnp.zeros((1, LANES), F32)
    for j in range(shard // step):
        part = summed[j * step : (j + 1) * step, :].astype(F32)
        grad_sq = grad_sq + col_sum(part * part)
    bias = summed[bias_at : bias_at + 2 * FF // LANES, :].astype(F32)
    bias = jnp.where(place.me == bias_owner, bias, 0.0)
    head = jnp.concatenate([grad_sq, jnp.zeros((7, LANES), F32), weight_sq, bias], axis=0)
    block[pl.ds(place.me, 1)] = head[None]
    share_all(place, block, block_send, block_recv)
    total = block[0]
    for s in range(1, 8):
        total = total + block[s]
    stats[...] = total
    red.finish()


def trust_kernel(update_sq, stats, trust, block, send, recv):
    place = Place()
    greet([place.lat_other(d) for d in range(1, 8)])
    block[pl.ds(place.me, 1)] = update_sq[...][None]
    share_all(place, block, send, recv)
    total = block[0]
    for s in range(1, 8):
        total = total + block[s]
    update_norm = jnp.sqrt(jnp.sum(total, axis=1, keepdims=True))
    weight_norm = jnp.sqrt(jnp.sum(stats[8:24, :], axis=1, keepdims=True))
    trust[...] = jnp.broadcast_to(weight_norm / (update_norm + 1e-06), (16, LANES))


def relayout(whole, row, stage, dst, rows, cols):
    wide = cols // LANES
    block = min(rows, 2048 // wide // 128 * 128)

    def step(i, carry):
        at = pl.multiple_of(row + i * (block * wide), 16)
        stage[0 : block * wide, :] = whole[pl.ds(at, block * wide), :].astype(F32)
        for j in range(wide):
            part = stage[pl.ds(j, block, stride=wide), :]
            dst[pl.ds(pl.multiple_of(i * block, 16), block), j * LANES : (j + 1) * LANES] = part.astype(BF)
        return carry

    lax.fori_loop(0, rows // block, step, 0)


def small_matrix(whole, row, stage, rows, cols):
    wide = cols // LANES
    stage[0 : rows * wide, :] = whole[row : row + rows * wide, :].astype(F32)
    return jnp.concatenate([stage[pl.ds(j, rows, stride=wide), :] for j in range(wide)], axis=1)


class Gather:
    def __init__(self, place, whole, shard, chunks, send, recv):
        self.p, self.whole, self.shard, self.chunks, self.send, self.recv = place, whole, shard, chunks, send, recv
        p = place
        x_index, y_index = p.x_side[1], p.y_side[1]
        low = p.z_low
        self.first = x_index + low * (y_index - x_index)
        self.second = y_index + low * (x_index - y_index)
        self.diagonal = x_index + 4 - 8 * p.y

    def copy(self, kind, k):
        p = self.p
        block = (p.me, p.me, self.first, self.first, self.first, self.diagonal, self.second)[kind]
        target = (
            (p.z, self.first), p.sibling, (p.z, self.second), p.z_near, p.sibling, p.sibling, p.sibling
        )[kind]
        row, count = self.chunks[k]
        ref = self.whole.at[pl.ds(pl.multiple_of(block * self.shard + row, 16), count), :]
        return remote(ref, ref, self.send.at[kind, k], self.recv.at[kind, k], target)

    def play(self, *events):
        for event in events:
            kind, k = event[0], int(event[1:])
            if kind == "a":
                self.copy(0, k).start()
                self.copy(1, k).start()
            elif kind == "b":
                self.copy(0, k).wait_recv()
                for way in (2, 3, 4):
                    self.copy(way, k).start()
            elif kind == "c":
                for arrived, onward in ((2, 5), (3, 6)):
                    self.copy(arrived, k).wait_recv()
                    self.copy(onward, k).start()
            else:
                for way in (1, 4, 5, 6):
                    self.copy(way, k).wait_recv()

    def finish(self):
        for k in range(len(self.chunks)):
            for kind in range(7):
                self.copy(kind, k).wait_send()


class KeyExchange:
    def __init__(self, place, keys, send, recv):
        self.p, self.keys, self.send, self.recv = place, keys, send, recv
        self.x_index, self.y_index = place.x_side[1], place.y_side[1]
        self.diagonal = self.x_index + 4 - 8 * place.y

    def copy(self, kind):
        p = self.p
        half = self.keys.shape[1] // 2
        low, high, full = pl.ds(0, half), pl.ds(half, half), pl.ds(0, 2 * half)
        block, rows, target = (
            (p.me, full, p.x_side), (p.me, full, p.y_side), (p.me, full, p.sibling),
            (self.x_index, low, p.y_side), (self.y_index, high, p.x_side),
            (self.x_index, full, p.sibling), (self.y_index, full, p.sibling), (self.diagonal, full, p.sibling),
        )[kind]
        ref = self.keys.at[block, rows, :]
        return remote(ref, ref, self.send.at[kind], self.recv.at[kind], target)

    def step(self, s):
        if s == 0:
            waits, starts = (), (0, 1, 2)
        elif s == 1:
            waits, starts = (0, 1), (3, 4, 5, 6)
        elif s == 2:
            waits, starts = (3, 4), (7,)
        else:
            waits, starts = (2, 5, 6, 7), ()
        for kind in waits:
            self.copy(kind).wait_recv()
        for kind in starts:
            self.copy(kind).start()

    def finish(self):
        for kind in range(8):
            self.copy(kind).wait_send()


def flat_rows_of():
    rows, at = {}, 0
    for name, shape in param_layout():
        rows[name] = at // LANES
        at += math.prod(shape)
    return rows


def gather_chunks(shard):
    at = flat_rows_of()
    tail = at["hid_bias"] % shard // 16 * 16
    chunks = [(at["episode"], at["w_o"] - at["episode"]), (tail, shard - tail), (at["w_o"], at["w_qkv"] - at["w_o"])]
    for low, high in ((0, at["episode"]), (at["w_qkv"], tail)):
        while low < high:
            count = min(512, high - low)
            chunks.append((low, count))
            low += count
    return chunks


def begin_kernel(
    chunks, master, tokens, ids, hot,
    up_one, down_one, qkv_w, so_w, up_two, down_two,
    latent, norms, hid_bias, out_bias, w_q, w_o, w_kv, tok_norm, tok_normed, episode, rank, counts,
    kvf_out, co_out, lse_out, h1,
    whole, stage, all_ids, keys, m_up_one, m_down_one, m_qkv, m_so, m_up_two, m_down_two,
    episodes_held, h1_held, h1_sem, send, recv, key_send, key_recv, id_send, id_recv, out_sem,
):
    place = Place()
    shard = master.shape[0]
    frames, cap = kvf_out.shape[0], kvf_out.shape[1]
    gather = Gather(place, whole, shard, chunks, send, recv)
    exchange = KeyExchange(place, keys, key_send, key_recv)
    at = flat_rows_of()
    greet([place.lat_other(d) for d in range(1, 8)] + [place.z_near])
    all_ids[pl.ds(place.me, 1)] = ids[...][None]
    id_copies = [
        remote(all_ids.at[place.me], all_ids.at[place.me], id_send.at[d - 1], id_recv.at[d - 1], place.lat_other(d))
        for d in range(1, 8)
    ]
    for copy in id_copies:
        copy.start()
    own_at = place.me * shard
    for row, count in chunks:
        whole[pl.ds(pl.multiple_of(own_at + row, 16), count), :] = master[row : row + count, :].astype(BF)
    gather.play("a0", "a1", "a2", "a3", "a4")

    for copy in id_copies:
        copy.wait_recv()
    tags = jnp.concatenate([all_ids[s] for s in range(8)], axis=0)
    low = lax.broadcasted_iota(jnp.int32, (LANES, LANES), 0)
    high = lax.broadcasted_iota(jnp.int32, (LANES, LANES), 1)
    upto = jnp.where(low <= high, 1.0, 0.0).astype(BF)
    n = tags.shape[0]
    below = jnp.where(
        lax.broadcasted_iota(jnp.int32, (n, n), 1) < lax.broadcasted_iota(jnp.int32, (n, n), 0), 1.0, 0.0
    ).astype(BF)
    for f in range(frames):
        hit = tags == place.me * frames + f
        hit_low = jnp.where(hit, 1.0, 0.0).astype(BF)
        inside = mm(hit_low, upto)
        row_total = jnp.broadcast_to(inside[:, LANES - 1 : LANES], (n, LANES))
        before = mm(below, row_total.astype(BF))
        place_in = (inside + before).astype(jnp.int32) - 1
        rank[f] = jnp.where(hit, place_in, -1)
        total = jnp.sum(row_total[:, 0:1], axis=0, keepdims=True).astype(jnp.int32)
        counts[f] = jnp.broadcast_to(total, (8, LANES))
    gather.play("b0", "b1", "a5", "b2", "c0", "c1", "a6", "d0", "d1")

    pair = whole[at["tok_norm"] // 16 * 16 : at["lat_norms"], :].astype(F32)
    pair = pair[at["tok_norm"] % 16 : at["tok_norm"] % 16 + 4, :]
    tok_norm[...] = jnp.concatenate(
        [
            jnp.concatenate([pair[0:1], pair[1:2]], axis=1),
            jnp.concatenate([pair[2:3], pair[3:4]], axis=1),
        ],
        axis=0,
    )
    w_kv[...] = whole[at["w_kv"] : at["w_kv"] + DIN, :]
    xhat, unused = norm_stats(tokens[...].astype(F32))
    normed = (xhat * tok_norm[0:1, :] + tok_norm[1:2, :]).astype(BF)
    tok_normed[...] = normed
    keys[pl.ds(place.me, 1)] = mm(normed, w_kv[...]).astype(BF)[None]
    exchange.step(0)
    gather.play("a7", "a8", "b3", "c2")
    norms[...] = small_matrix(whole, at["lat_norms"], stage, 8, D)
    hid_bias[...] = small_matrix(whole, at["hid_bias"], stage, 2, FF)
    out_bias[...] = small_matrix(whole, at["out_bias"], stage, 4, D)
    episode_rows = mm(hot[...], small_matrix(whole, at["episode"], stage, 16, D).astype(BF))
    gather.play("b4", "c3", "d2", "b5", "c4", "d3", "b6")
    exchange.step(1)
    gather.play("a9", "a10", "c5", "d4", "c6", "d5")
    packed = whole[at["w_q"] : at["w_q"] + D // 2, :].astype(F32)
    stage[pl.ds(0, D // 2, stride=2), :] = packed
    stage[pl.ds(1, D // 2, stride=2), :] = pltpu.roll(packed, CH, 1)
    w_q[...] = keep_half(stage[0:D, :], 0).astype(BF)
    w_o[0:CH, :] = jnp.zeros((CH, D), BF)
    w_o[CH : 2 * CH, :] = small_matrix(whole, at["w_o"], stage, CH, D).astype(BF)
    exchange.step(2)
    gather.play("a11", "b7", "d6")
    exchange.step(3)
    relayout(whole, 0, stage, latent, LAT, D)

    chunk = 8 * LANES
    episodes_held[...] = episode_rows[0:8, :]
    before = [("b8",), ("b9", "d7"), ("b10", "d8"), ("b11", "d9")]
    midway = [("c7",), ("c8",), ("c9",), ("c10",)]

    def play(frame, parts):
        for step, events in enumerate(parts):
            pl.when(frame == step)(functools.partial(gather.play, *events))

    def attend(f, carry):
        play(f, before)
        row = episodes_held[pl.ds(f, 1), :]
        start = latent[...].astype(F32) + row
        episode[pl.ds(f, 1)] = row[None]

        def pick(j, acc):
            sel = select_tokens(rank[f, pl.ds(pl.multiple_of(8 * j, 8), 8), :], cap)
            return acc + mm(sel, keys[pl.ds(2 * j, 2)].reshape(chunk, LANES))

        kvf = lax.fori_loop(0, n // 8, pick, jnp.zeros((cap, LANES), F32)).astype(BF)
        play(f, midway)
        co, lse = cross_attend(start, norms, w_q, kvf, counts[f, 0:1, 0:1])
        rows = pl.ds(pl.multiple_of(f * LAT, LAT), LAT)
        h1_held[f] = start + mm(co, w_o[...]) + out_bias[0:1, :]
        pltpu.make_async_copy(h1_held.at[f], h1.at[rows, :], h1_sem.at[f]).start()
        kvf_out[f] = kvf
        co_out[rows, :] = co
        lse_out[f] = lse
        return carry

    lax.fori_loop(0, frames, attend, 0)
    gather.play("c11", "d10", "d11")

    big = (
        (up_one, m_up_one, at["w_up"], D, FF),
        (down_one, m_down_one, at["w_down"], FF, D),
        (qkv_w, m_qkv, at["w_qkv"], D, 3 * D),
        (so_w, m_so, at["w_so"], D, D),
        (up_two, m_up_two, at["w_up"] + D * FF // LANES, D, FF),
        (down_two, m_down_two, at["w_down"] + D * FF // LANES, FF, D),
    )
    outs = []
    for j, (out, held, row, rows, cols) in enumerate(big):
        relayout(whole, row, stage, held, rows, cols)
        outs.append(pltpu.make_async_copy(held, out, out_sem.at[j]))
        outs[-1].start()
    for copy in outs:
        copy.wait()
    for f in range(frames):
        pltpu.make_async_copy(h1_held.at[f], h1.at[f * LAT : (f + 1) * LAT, :], h1_sem.at[f]).wait()
    for copy in id_copies:
        copy.wait_send()
    exchange.finish()
    gather.finish()


def begin_all(master_rows, token_rows, ids, hot, frames, cap):
    shard = master_rows.shape[0]
    tokens = token_rows.shape[0]
    total = 8 * tokens
    chunks = gather_chunks(shard)
    vmem = pl.BlockSpec(memory_space=pltpu.VMEM)
    anywhere = pl.BlockSpec(memory_space=pl.ANY)
    matrices = [(D, FF), (FF, D), (D, 3 * D), (D, D), (D, FF), (FF, D)]
    dma = pltpu.SemaphoreType.DMA
    return pl.pallas_call(
        functools.partial(begin_kernel, chunks),
        out_shape=[shaped(m, BF) for m in matrices]
        + [
            shaped((LAT, D), BF),
            shaped((8, D)),
            shaped((2, FF)),
            shaped((4, D)),
            shaped((D, LANES), BF),
            shaped((LANES, D), BF),
            shaped((DIN, LANES), BF),
            shaped((2, DIN)),
            shaped((tokens, DIN), BF),
            shaped((frames, 1, D)),
            shaped((frames, total // LANES, LANES), jnp.int32),
            shaped((frames, 8, LANES), jnp.int32),
            shaped((frames, cap, LANES), BF),
            shaped((frames * LAT, LANES), BF),
            shaped((frames, 1, LAT)),
            shaped((frames * LAT, D)),
        ],
        in_specs=[vmem] * 4,
        out_specs=[anywhere] * 6 + [vmem] * 15 + [anywhere],
        scratch_shapes=[
            pltpu.VMEM((8 * shard, LANES), BF),
            pltpu.VMEM((2048, LANES), F32),
            pltpu.VMEM((8, tokens // LANES, LANES), jnp.int32),
            pltpu.VMEM((8, tokens, LANES), BF),
        ]
        + [pltpu.VMEM(m, BF) for m in matrices]
        + [
            pltpu.VMEM((8, D), F32),
            pltpu.VMEM((frames, LAT, D), F32),
            dma((frames,)),
            dma((7, len(chunks))), dma((7, len(chunks))), dma((8,)), dma((8,)), dma((7,)), dma((7,)), dma((6,)),
        ],
        compiler_params=pltpu.CompilerParams(
            collective_id=3, has_side_effects=True, vmem_limit_bytes=56 * MIB
        ),
    )(master_rows, token_rows, ids, hot)


FCHUNK = 512


def to_flat(stage, matrix):
    rows, wide = matrix.shape[0], matrix.shape[1] // LANES
    for j in range(wide):
        stage[pl.ds(j, rows, stride=wide), :] = matrix[:, j * LANES : (j + 1) * LANES]
    return stage[0 : rows * wide, :]


def chunk_of(c, size=FCHUNK):
    return pl.ds(pl.multiple_of(c * size, LANES), size)


def feed_forward(rows, gain, bias, up_bias, down_bias, w_up, w_down, act_ref, slope_ref, normed_ref, total_ref):
    xhat, rstd = norm_stats(rows)
    normed_ref[...] = (xhat * gain + bias).astype(BF)
    total_ref[...] = rows + down_bias

    for c in range(2):
        at = slice(c * FF // 2, (c + 1) * FF // 2)
        act, slope = gelu_pair(mm(normed_ref[...], w_up[:, at]) + up_bias[:, at])
        act = act.astype(BF)
        act_ref[:, at] = act
        slope_ref[:, at] = slope.astype(BF)
        total_ref[...] += mm(act, w_down[at, :])


def feed_back(grad_ref, normed_ref, xhat, rstd, gain, act, slope, w_up, w_down, acc_up, acc_down, dhid, dnorm, dout, work):
    work[...] = jnp.zeros(work.shape, F32)
    for c in range(FF // FCHUNK):
        at = slice(c * FCHUNK, (c + 1) * FCHUNK)
        dpre = (mm_t(grad_ref[...], w_down[at, :]) * slope[:, at].astype(F32)).astype(BF)
        dhid[:, at] += col_sum(dpre.astype(F32))
        work[...] += mm_t(dpre, w_up[:, at])
        acc_up[:, at] += t_mm(normed_ref[...], dpre)
        acc_down[at, :] += t_mm(act[:, at], grad_ref[...])
    grad_normed = work[...]
    dnorm[...] += jnp.concatenate([col_sum(grad_normed * xhat), col_sum(grad_normed)], axis=0)
    dout[...] += col_sum(grad_ref[...].astype(F32))
    return norm_back(grad_normed, xhat, rstd, gain)


def clear(first, refs):
    @pl.when(first)
    def _():
        for ref in refs:
            ref[...] = jnp.zeros_like(ref)


def flat_spans(row, count, shard, extra):
    spans, done = [], 0
    while done < count:
        part = min(count - done, shard - (row + done) % shard)
        spans.append((done, part, row + done + (row + done) // shard * extra))
        done += part
    return spans


def flatten(acc, stage, low, slot):
    wide = acc.shape[1] // LANES
    block = min(acc.shape[0], 2048 // wide // 128 * 128)
    span = block * wide

    def step(i, carry):
        part = acc[pl.ds(pl.multiple_of(i * block, block), block), :]
        for j in range(wide):
            stage[pl.ds(j, block, stride=wide), :] = part[:, j * LANES : (j + 1) * LANES]
        low[slot, pl.ds(pl.multiple_of(i * span, span), span), :] = stage[0:span, :].astype(BF)
        return carry

    lax.fori_loop(0, acc.shape[0] // block, step, 0)


def write_flat(flat, stage, low, pieces, sems, shard, extra):
    pending = {}
    for j, (acc, row) in enumerate(pieces):
        count = acc.shape[0] * acc.shape[1] // LANES
        slot = j % 2
        for copy in pending.get(slot, []):
            copy.wait()
        flatten(acc, stage, low, slot)
        pending[slot] = [
            pltpu.make_async_copy(low.at[slot, pl.ds(off, part), :], flat.at[pl.ds(at, part), :], sems.at[slot, k])
            for k, (off, part, at) in enumerate(flat_spans(row, count, shard, extra))
        ]
        for copy in pending[slot]:
            copy.start()
    for copies in pending.values():
        for copy in copies:
            copy.wait()


class FrameExchange:
    def __init__(self, place, source, grad, held, result, sems):
        self.p, self.source, self.grad, self.held, self.result = place, source, grad, held, result
        self.in_send, self.in_recv, self.out_send, self.out_recv, self.own_in, self.own_out = sems
        self.frames, self.rows = grad.shape[0], source.shape[1]

    @staticmethod
    def scratch(frames):
        dma = pltpu.SemaphoreType.DMA
        return [dma((frames, 7))] * 4 + [dma((frames,))] * 2

    def block(self, index):
        return pl.ds(pl.multiple_of(index * self.rows, 16), self.rows)

    def arriving(self, f, d):
        target = self.p.lat_other(d)
        src = self.source.at[target[1] * self.frames + f]
        dst = self.grad.at[f, self.block(self.p.me), :]
        return remote(src, dst, self.in_send.at[f, d - 1], self.in_recv.at[f, d - 1], target)

    def own_arriving(self, f):
        src = self.source.at[self.p.me * self.frames + f]
        return pltpu.make_async_copy(src, self.grad.at[f, self.block(self.p.me), :], self.own_in.at[f])

    def leaving(self, f, d):
        target = self.p.lat_other(d)
        src = self.held.at[f, self.block(target[1]), :]
        dst = self.result.at[self.p.me * self.frames + f]
        return remote(src, dst, self.out_send.at[f, d - 1], self.out_recv.at[f, d - 1], target)

    def own_leaving(self, f):
        dst = self.result.at[self.p.me * self.frames + f]
        return pltpu.make_async_copy(self.held.at[f, self.block(self.p.me), :], dst, self.own_out.at[f])

    def begin(self):
        greet([self.p.lat_other(d) for d in range(1, 8)])
        for f in range(self.frames):
            self.own_arriving(f).start()
            for d in range(1, 8):
                self.arriving(f, d).start()

    def await_frame(self, f):
        self.own_arriving(f).wait()
        for d in range(1, 8):
            self.arriving(f, d).wait_recv()

    def send_frame(self, f):
        self.own_leaving(f).start()
        for d in range(1, 8):
            self.leaving(f, d).start()

    def finish(self):
        def step(f, carry):
            self.own_leaving(f).wait()
            for d in range(1, 8):
                self.arriving(f, d).wait_send()
                self.leaving(f, d).wait()
            return carry

        lax.fori_loop(0, self.frames, step, 0)


class Late:
    def __init__(self, step, sources, refs, sems):
        self.first = step == 0
        self.copies = [
            pltpu.make_async_copy(src, ref, sems.at[k]) for k, (src, ref) in enumerate(zip(sources, refs))
        ]

        @pl.when(self.first)
        def _():
            for copy in self.copies:
                copy.start()

    def need(self, *which):
        @pl.when(self.first)
        def _():
            for k in which:
                self.copies[k].wait()


def forward_kernel(
    reach, shard, extra, h1, grad, norms, hid_bias, out_bias, up_one, down_one, *rest,
):
    forward_body(reach, shard, extra, h1, grad, norms, hid_bias, out_bias, up_one, down_one, rest[:4], *rest[4:])


def forward_body(
    reach, shard, extra, h1, grad, norms, hid_bias, out_bias, up_one, down_one, late_sources,
    h2_out, qkv, lse_out, mixed_out, act_one, slope_one, latents, g3, dhid, dnorm, dout, flat,
    act_two, slope_two, acc_up, acc_down, stage, low, normed, mixed_t, work, sems,
    w_qkv, w_so, up_two, down_two, late_sems, *shared,
):
    step = pl.program_id(0)
    late = Late(step, late_sources, (w_qkv, w_so, up_two, down_two), late_sems)
    if reach:
        place = Place()
        traffic = FrameExchange(place, grad, shared[0], shared[1], latents, shared[2:])
        pl.when(step == 0)(traffic.begin)
        grad = shared[0].at[step]
    clear(step == 0, (acc_up, acc_down, dhid, dnorm, dout))
    feed_forward(
        h1[...], norms[2:3, :], norms[3:4, :], hid_bias.at[0:1], out_bias[1:2, :], up_one, down_one, act_one,
        slope_one, normed, h2_out,
    )
    xhat, unused = norm_stats(h2_out[...])
    normed[...] = (xhat * norms[4:5, :] + norms[5:6, :]).astype(BF)

    late.need(0)

    def project(c, carry):
        at = chunk_of(c)
        qkv[:, at] = mm(normed[...], w_qkv[:, at]).astype(BF)
        return carry

    lax.fori_loop(0, 3, project, 0)
    scale = jnp.asarray(0.125, BF)

    ones = jnp.ones((16, LAT), BF)

    for pair in range(HEADS // 2):
        base = pair * LANES
        query_pair = qkv[:, base : base + LANES] * scale
        key_pair = qkv[:, D + base : D + base + LANES]
        value_t = qkv[:, 2 * D + base : 2 * D + base + LANES].T
        for half in range(2):
            scores = mm_t(key_pair, keep_half(query_pair, half))
            top = jnp.max(scores, axis=0, keepdims=True)
            terms = jnp.exp(scores - top).astype(BF)
            values = jnp.concatenate([value_t[half * HEAD_DIM : (half + 1) * HEAD_DIM, :], ones], axis=0)
            product = mm(values, terms)
            total = product[HEAD_DIM : HEAD_DIM + 1, :]
            head = 2 * pair + half
            lse_out[0, head : head + 1, :] = top + jnp.log(total)
            mixed_t[head * HEAD_DIM : (head + 1) * HEAD_DIM, :] = product[0:HEAD_DIM, :] * (1.0 / total)
    late.need(1, 2, 3)
    mixed = mixed_t[...].T.astype(BF)
    mixed_out[...] = mixed
    h3 = h2_out[...] + mm(mixed, w_so[...]) + out_bias[2:3, :]
    feed_forward(
        h3, norms[6:7, :], norms[7:8, :], hid_bias.at[1:2], out_bias[3:4, :], up_two, down_two, act_two, slope_two,
        normed, work,
    )
    if reach:
        shared[1][step] = work[...].astype(BF)
        traffic.send_frame(step)
        traffic.await_frame(step)
    else:
        latents[...] = work[...].astype(BF)
    xhat, rstd = norm_stats(h3)
    g3[...] = grad[...].astype(F32) + feed_back(
        grad, normed, xhat, rstd, norms[6:7, :], act_two, slope_two, up_two, down_two,
        acc_up, acc_down, dhid, dnorm, dout, work,
    )

    @pl.when(step == pl.num_programs(0) - 1)
    def _():
        at = flat_rows_of()
        half = D * FF // LANES
        write_flat(flat, stage, low, [(acc_up, at["w_up"] + half), (acc_down, at["w_down"] + half)], sems, shard, extra)
        if reach:
            traffic.finish()


def backward_kernel(
    shard, extra, qkv, lse, mixed, g3, h2, h1, act_one, slope_one, norms, w_so, src_qkv, src_up, src_down, flat_in,
    g1, dhid, dnorm_sa, dnorm_one, dout_so, dout_one, flat,
    dqkv, acc_up, acc_down, acc_qkv, acc_so, stage, low, normed, grad_mixed, grad_low, work, sems,
    w_qkv, up_one, down_one, late_sems,
):
    step = pl.program_id(0)
    late = Late(step, (src_qkv, src_up, src_down), (w_qkv, up_one, down_one), late_sems)
    clear(
        step == 0,
        (acc_up, acc_down, acc_qkv, acc_so, dhid, dnorm_sa, dnorm_one, dout_so, dout_one),
    )
    scale = jnp.asarray(0.125, BF)
    grad_three = g3[...]
    grad_low[...] = grad_three.astype(BF)
    dout_so[...] += col_sum(grad_low[...].astype(F32))
    acc_so[...] += t_mm(mixed[...], grad_low[...])
    grad_mixed[...] = mm_t(grad_low[...], w_so[...]).astype(BF)

    def attend(pair, carry):
        query_at = chunk_of(pair, LANES)
        key_at = chunk_of(pair + D // LANES, LANES)
        value_at = chunk_of(pair + 2 * D // LANES, LANES)
        query_pair = qkv[:, query_at] * scale
        key_pair = qkv[:, key_at]
        value_pair = qkv[:, value_at]
        grad_pair = grad_mixed[:, query_at]
        key_t = key_pair.T
        query_t = []
        grad_key = jnp.zeros((LAT, LANES), F32)
        grad_value = jnp.zeros((LAT, LANES), F32)
        for half in range(2):
            query = keep_half(query_pair, half)
            grad_head = keep_half(grad_pair, half)
            prob = jnp.exp(mm_t(key_pair, query) - lse[0, pl.ds(2 * pair + half, 1), :])
            grad_value = grad_value + mm(prob.astype(BF), grad_head)
            weighted = prob * mm_t(value_pair, grad_head)
            grad_score = (weighted - prob * col_sum(weighted)).astype(BF)
            grad_key = grad_key + mm(grad_score, query)
            query_t.append(mm(key_t[half * HEAD_DIM : (half + 1) * HEAD_DIM, :], grad_score))
        dqkv[:, query_at] = (jnp.concatenate(query_t, axis=0).T * 0.125).astype(BF)
        dqkv[:, key_at] = grad_key.astype(BF)
        dqkv[:, value_at] = grad_value.astype(BF)
        return carry

    lax.fori_loop(0, HEADS // 2, attend, 0)
    late.need(0, 1, 2)
    xhat, rstd = norm_stats(h2[...])
    normed[...] = (xhat * norms[4:5, :] + norms[5:6, :]).astype(BF)
    work[...] = jnp.zeros(work.shape, F32)

    for c in range(3):
        at = slice(c * D, (c + 1) * D)
        work[...] += mm_t(dqkv[:, at], w_qkv[:, at])
        acc_qkv[:, at] += t_mm(normed[...], dqkv[:, at])
    grad_in = work[...]
    dnorm_sa[...] += jnp.concatenate([col_sum(grad_in * xhat), col_sum(grad_in)], axis=0)
    grad_two = grad_three + norm_back(grad_in, xhat, rstd, norms[4:5, :])

    xhat, rstd = norm_stats(h1[...])
    normed[...] = (xhat * norms[2:3, :] + norms[3:4, :]).astype(BF)
    grad_low[...] = grad_two.astype(BF)
    grad_one = grad_two + feed_back(
        grad_low, normed, xhat, rstd, norms[2:3, :], act_one, slope_one, up_one, down_one,
        acc_up, acc_down, dhid, dnorm_one, dout_one, work,
    )

    g1[...] = grad_one

    @pl.when(step == pl.num_programs(0) - 1)
    def _():
        at = flat_rows_of()
        write_flat(
            flat, stage, low,
            [(acc_up, at["w_up"]), (acc_down, at["w_down"]), (acc_qkv, at["w_qkv"]), (acc_so, at["w_so"])],
            sems, shard, extra,
        )


def cross_back_frame(
    grad_one, kvf, co, lse, rank_ref, count, episode_row, hot_column, latent, norms, w_q, w_o,
    acc_latent, acc_q, acc_o, acc_episode, dnorm, dout, dkv_t, pause=lambda: None,
):
    cap = kvf.shape[0]
    start = latent[...].astype(F32) + episode_row
    xhat, rstd = norm_stats(start)
    query_in = (xhat * norms[0:1, :] + norms[1:2, :]).astype(BF)
    queries = mm(query_in, w_q[...]).astype(BF) * jnp.asarray(0.125, BF)
    branch = grad_one.astype(BF)
    grad_co = mm_t(branch, w_o[...]).astype(BF)
    acc_o[...] += t_mm(co, branch)
    dout[...] += col_sum(branch.astype(F32))
    scores = cross_scores(kvf, queries, count)
    prob = jnp.exp(scores - lse)
    weighted = prob * mm_t(kvf, grad_co)
    grad_score = (weighted - prob * col_sum(weighted)).astype(BF)
    grad_kv = (mm(grad_score, queries) + mm(prob.astype(BF), grad_co)).astype(BF)
    grad_query = (t_mm(kvf, grad_score).T * 0.125).astype(BF)
    pause()
    acc_q[...] += t_mm(query_in, grad_query)
    grad_in = mm_t(grad_query, w_q[...])
    grad_start = grad_one + norm_back(grad_in, xhat, rstd, norms[0:1, :])
    dnorm[...] += jnp.concatenate([col_sum(grad_in * xhat), col_sum(grad_in)], axis=0)
    acc_latent[...] += grad_start
    acc_episode[...] += hot_column * col_sum(grad_start)
    grad_kv_t = grad_kv.T
    chunk = 8 * LANES

    def scatter(j, carry):
        sel = select_tokens(rank_ref[pl.ds(pl.multiple_of(j * 8, 8), 8), :], cap)
        at = pl.ds(pl.multiple_of(j * chunk, chunk), chunk)
        dkv_t[:, at] = added(dkv_t[:, at], mm(grad_kv_t, sel))
        return carry

    lax.fori_loop(0, dkv_t.shape[1] // chunk, scatter, 0)


def write_small(put, stage, low, latent_low, acc_latent, acc_q, acc_o, acc_episode, norm_grads, hid_grads, out_grads):
    at = flat_rows_of()
    flatten(acc_latent, stage, latent_low, 0)
    put(latent_low.at[0], 0)
    head = at["lat_norms"] - at["episode"]
    used = EPISODES * (D // LANES)
    rows = [to_flat(stage, acc_episode[...])[0:used, :], jnp.zeros((head - used, LANES), F32)]
    rows = jnp.concatenate(rows + [to_flat(stage, norm_grads)], axis=0)
    top = rows.shape[0]
    low[0, 0:top, :] = rows.astype(BF)
    put(low.at[0, pl.ds(0, top), :], at["episode"])
    stage[0:D, :] = acc_q[...]
    even = stage[pl.ds(0, D // 2, stride=2), :]
    odd = pltpu.roll(stage[pl.ds(1, D // 2, stride=2), :], CH, 1)
    low[0, top : top + D // 2, :] = jnp.where(lane_half(even.shape, 0), even, odd).astype(BF)
    both = D // 2 + CH * D // LANES
    low[0, top + D // 2 : top + both, :] = to_flat(stage, acc_o[CH : 2 * CH, :]).astype(BF)
    put(low.at[0, pl.ds(top, both), :], at["w_q"])
    hid = to_flat(stage, hid_grads)
    last = top + both
    low[0, last : last + hid.shape[0], :] = hid.astype(BF)
    end = hid.shape[0] + 4 * D // LANES
    low[0, last + hid.shape[0] : last + end, :] = to_flat(stage, out_grads).astype(BF)
    put(low.at[0, pl.ds(last, end), :], at["hid_bias"])


def cross_accumulators(total_keys):
    shapes = [(LAT, D), (D, LANES), (LANES, D), (16, D), (2, D), (1, D)]
    return [pltpu.VMEM(shape, F32) for shape in shapes] + [pltpu.VMEM((LANES, total_keys), BF)]


def small_buffers():
    return [pltpu.VMEM((2048, LANES), F32), pltpu.VMEM((1, 640, LANES), BF), pltpu.VMEM((1, 2048, LANES), BF)]


def stacked(*parts):
    return jnp.concatenate([part[...] for part in parts], axis=0)


def cross_bwd_kernel(
    kv_rows, g1, kvf, co, lse, rank, count, episode, hot, latent, norms, w_q, w_o,
    dnorm_one, dnorm_sa, dnorm_two, dhid_one, dhid_two, dout_one, dout_so, dout_two, flat_in, flat,
    acc_latent, acc_q, acc_o, acc_episode, dnorm, dout, dkv_t, stage, low, latent_low, kv_low, sems,
):
    step = pl.program_id(0)
    accs = (acc_latent, acc_q, acc_o, acc_episode, dnorm, dout, dkv_t)
    clear(step == 0, accs)
    cross_back_frame(
        g1[...], kvf[0], co[...], lse[0], rank.at[0], count[0, 0:1, 0:1], episode[0], hot[0, :, 0:1],
        latent, norms, w_q, w_o, *accs,
    )

    @pl.when(step == pl.num_programs(0) - 1)
    def _():
        copies = []

        def put(source, row):
            copies.append(
                pltpu.make_async_copy(source, flat.at[pl.ds(row, source.shape[0]), :], sems.at[len(copies)])
            )
            copies[-1].start()

        write_small(
            put, stage, low, latent_low, acc_latent, acc_q, acc_o, acc_episode,
            stacked(dnorm, dnorm_one, dnorm_sa, dnorm_two), stacked(dhid_one, dhid_two),
            stacked(dout, dout_one, dout_so, dout_two),
        )
        for copy in copies:
            copy.wait()
        tokens = kv_rows[1]
        for j in range(dkv_t.shape[1] // tokens):
            kv_low[...] = dkv_t[:, j * tokens : (j + 1) * tokens].T
            copy = pltpu.make_async_copy(kv_low, flat.at[pl.ds(kv_rows[0] + j * tokens, tokens), :], sems.at[0])
            copy.start()
            copy.wait()


def fixed(*shape):
    return pl.BlockSpec(shape, lambda i: (0,) * len(shape), pipeline_mode=pl.Buffered(1))


def kept(*shape):
    return pl.BlockSpec(shape, lambda i: (0,) * len(shape))


def rowed(rows, cols):
    return pl.BlockSpec((rows, cols), lambda i: (i, 0))


def framed(*shape):
    return pl.BlockSpec((1,) + shape, lambda i: (i,) + (0,) * len(shape))


def shaped(shape, dtype=F32):
    return jax.ShapeDtypeStruct(shape, dtype)


def call(kernel, grid, in_specs, outs, args, flops=0, trans=0, scratch=(), limit=56, aliases=None, collective=None):
    out_specs, out_shapes = zip(*outs)
    moved = sum(math.prod(a.shape) * a.dtype.itemsize for a in args)
    moved += sum(math.prod(s.shape) * s.dtype.itemsize for s in out_shapes)
    return pl.pallas_call(
        kernel,
        grid=(grid,),
        in_specs=in_specs,
        out_specs=list(out_specs),
        out_shape=list(out_shapes),
        scratch_shapes=list(scratch),
        input_output_aliases=aliases or {},
        compiler_params=pltpu.CompilerParams(
            dimension_semantics=("arbitrary",),
            vmem_limit_bytes=limit * MIB,
            collective_id=collective,
            has_side_effects=collective is not None,
        ),
        cost_estimate=pl.CostEstimate(flops=flops, bytes_accessed=moved, transcendentals=trans),
    )(*args)


def reduce_all(flat, master_rows, starts, ends, bias_owner, bias_row, tokens, tok_normed, w_kv, tok_norm, g1, cross):
    shard = master_rows.shape[0]
    vmem = pl.BlockSpec(memory_space=pltpu.VMEM)
    anywhere = pl.BlockSpec(memory_space=pl.ANY)
    dma = pltpu.SemaphoreType.DMA
    first = [
        pltpu.VMEM((8, STAT_ROWS, LANES), F32), dma((7,)), dma((7,)), pltpu.VMEM((16, LANES), BF),
        pltpu.VMEM((DIN, LANES), BF), dma((2,)), pltpu.VMEM(g1.shape, F32), dma((g1.shape[0],)),
        pltpu.VMEM((8, tokens.shape[0], LANES), BF), dma((16,)),
    ]
    grads = flat.reshape(2, 2, 2, -1, LANES)
    return pl.pallas_call(
        functools.partial(reduce_kernel, bias_owner, bias_row),
        out_shape=[
            shaped((shard, LANES), BF), shaped((STAT_ROWS, LANES)), shaped(tokens.shape, BF),
            shaped(grads.shape, BF),
        ],
        in_specs=[vmem, vmem, anywhere] + [vmem] * 5 + [anywhere] + [vmem] * len(cross),
        out_specs=[vmem, vmem, vmem, anywhere],
        scratch_shapes=first
        + cross_accumulators(8 * tokens.shape[0])
        + small_buffers()
        + Reduction.scratch(shard),
        input_output_aliases={2: 3},
        compiler_params=pltpu.CompilerParams(
            collective_id=1, has_side_effects=True, vmem_limit_bytes=56 * MIB
        ),
    )(starts, ends, grads, master_rows, tokens, tok_normed, w_kv, tok_norm, g1, *cross)


def body(tokens, frame_ids, episodes, master, moment_one, moment_two, latent_grad):
    lat_count = lax.axis_size("lat")
    lat_index = lax.axis_index("lat")
    shard_len = master.shape[0]
    frame_total = episodes.shape[1]
    frames = frame_total // lat_count
    rows_total = frames * LAT
    total_keys = frame_ids.shape[1] * lat_count
    cap = total_keys // 8
    token_rows_count = total_keys // LANES

    reach = lat_count == 8 and lax.axis_size("kf") == 4
    shard_rows = shard_len // LANES
    master_rows = master.reshape(shard_rows, LANES)
    episode_index = jnp.arange(EPISODES, dtype=jnp.int32)
    own_episodes = lax.dynamic_slice_in_dim(episodes[0], lat_index * frames, frames, 0)
    episode_match = own_episodes[:, None] == episode_index[None, :]
    score_flops = rows_total * cap * LANES * 2
    select_flops = frames * cap * total_keys * LANES * 2
    if reach:
        hot = jnp.pad(episode_match.astype(BF), ((0, 16 - frames), (0, 16 - EPISODES)))
        (
            up_one, down_one, w_qkv, w_so, up_two, down_two,
            latent, norms, hid_bias, out_bias, w_q, w_o, w_kv, tok_norm, tok_normed, episode_rows, rank, counts,
            kvf, cross_out, cross_lse, h1,
        ) = begin_all(master_rows, tokens[0], frame_ids.reshape(-1, LANES), hot, frames, cap)
    else:
        weights = split_flat(lax.all_gather(master.astype(BF), "lat", axis=0, tiled=True))
        norms = weights["lat_norms"].astype(F32)
        out_bias = weights["out_bias"].astype(F32)
        hid_bias = weights["hid_bias"].astype(F32)
        tok_norm = weights["tok_norm"].astype(F32)
        w_kv, w_qkv, w_so, latent = (weights[name] for name in ("w_kv", "w_qkv", "w_so", "latent"))
        up_one, up_two = weights["w_up"]
        down_one, down_two = weights["w_down"]
        frame_tag = lax.all_gather(frame_ids[0].astype(BF), "lat", axis=0, tiled=True).astype(jnp.int32)
        own_frames = lat_index * frames + jnp.arange(frames, dtype=jnp.int32)
        own_hit = frame_tag[None, :] == own_frames[:, None]
        rank = jnp.cumsum(own_hit.astype(jnp.int32), axis=1) - 1
        counts = jnp.broadcast_to(rank[:, -1][:, None, None] + 1, (frames, 8, LANES))
        rank = jnp.where(own_hit, rank, -1).reshape(frames, token_rows_count, LANES)
        tok_normed = layer_norm(tokens[0].astype(F32), tok_norm[0], tok_norm[1]).astype(BF)
        key_value = mm(tok_normed, w_kv).astype(BF)
        all_keys = lax.all_gather(key_value, "lat", axis=0, tiled=True)
        episode_rows = mm(episode_match.astype(BF), weights["episode"]).reshape(frames, 1, D)
        w_q = jnp.pad(weights["w_q"], ((0, 0), (0, LANES - CH)))
        w_o = jnp.pad(weights["w_o"], ((LANES - CH, 0), (0, 0)))
        h1, kvf, cross_out, cross_lse = call(
            cross_fwd_kernel,
            frames,
            [
                fixed(LAT, D), framed(1, D), fixed(8, D), fixed(D, LANES), fixed(LANES, D), fixed(4, D),
                fixed(total_keys, LANES), framed(token_rows_count, LANES), framed(8, LANES),
            ],
            [
                (rowed(LAT, D), shaped((rows_total, D))),
                (framed(cap, LANES), shaped((frames, cap, LANES), BF)),
                (rowed(LAT, LANES), shaped((rows_total, LANES), BF)),
                (framed(1, LAT), shaped((frames, 1, LAT))),
            ],
            (latent, episode_rows, norms, w_q, w_o, out_bias, all_keys, rank, counts),
            flops=2 * score_flops + select_flops,
            trans=rows_total * cap,
        )
    mlp_flops = 4 * rows_total * D * FF
    attn_flops = 4 * rows_total * LAT * D
    anywhere = pl.BlockSpec(memory_space=pl.ANY)
    token_count = frame_ids.shape[1]
    if reach:
        flat_shard, extra = shard_rows, token_count
        flat_shape = (lat_count * (shard_rows + extra), LANES)
        kv_rows = (shard_rows, token_count, shard_rows + extra)
        grad_in, grad_spec = latent_grad[0], anywhere
        latents_spec = (anywhere, shaped(latent_grad.shape[1:], BF))
        shared = [pltpu.VMEM((frames, LAT, D), BF)] * 2 + FrameExchange.scratch(frames)
    else:
        flat_shard, extra = NPARAM // LANES, 0
        flat_shape = (flat_shard + total_keys, LANES)
        kv_rows = (flat_shard, 512, 512)
        grad_in = lax.all_to_all(
            latent_grad[0], "lat", split_axis=0, concat_axis=1, tiled=True
        ).reshape(rows_total, D)
        grad_spec = rowed(LAT, D)
        latents_spec = (rowed(LAT, D), shaped((rows_total, D), BF))
        shared = []
    slab = D * FF // LANES
    h2, qkv, self_lse, mixed, act_one, slope_one, latents, g3, dhid_two, dnorm_two, dout_two, flat = call(
        functools.partial(forward_kernel, reach, flat_shard, extra),
        frames,
        [
            rowed(LAT, D), grad_spec, fixed(8, D), fixed(2, FF), fixed(4, D), fixed(D, FF), fixed(FF, D),
        ]
        + [anywhere] * 4,
        [
            (rowed(LAT, D), shaped((rows_total, D))),
            (rowed(LAT, 3 * D), shaped((rows_total, 3 * D), BF)),
            (framed(HEADS, LAT), shaped((frames, HEADS, LAT))),
            (rowed(LAT, D), shaped((rows_total, D), BF)),
            (rowed(LAT, FF), shaped((rows_total, FF), BF)),
            (rowed(LAT, FF), shaped((rows_total, FF), BF)),
            latents_spec,
            (rowed(LAT, D), shaped((rows_total, D))),
            (kept(1, FF), shaped((1, FF))),
            (kept(2, D), shaped((2, D))),
            (kept(1, D), shaped((1, D))),
            (anywhere, shaped(flat_shape, BF)),
        ],
        (h1, grad_in, norms, hid_bias, out_bias, up_one, down_one, w_qkv, w_so, up_two, down_two),
        flops=4 * mlp_flops + 4 * attn_flops,
        trans=4 * rows_total * FF,
        scratch=[
            pltpu.VMEM((LAT, FF), BF), pltpu.VMEM((LAT, FF), BF), pltpu.VMEM((D, FF), F32), pltpu.VMEM((FF, D), F32),
            pltpu.VMEM((2048, LANES), F32), pltpu.VMEM((2, slab, LANES), BF), pltpu.VMEM((LAT, D), BF),
            pltpu.VMEM((D, LAT), F32), pltpu.VMEM((LAT, D), F32), pltpu.SemaphoreType.DMA((2, 16)),
            pltpu.VMEM((D, 3 * D), BF), pltpu.VMEM((D, D), BF), pltpu.VMEM((D, FF), BF), pltpu.VMEM((FF, D), BF),
            pltpu.SemaphoreType.DMA((4,)),
        ]
        + shared,
        limit=62,
        collective=4 if reach else None,
    )
    if reach:
        latents_out = latents[None]
    else:
        latents_out = lax.all_to_all(
            latents.reshape(frames, LAT, D), "lat", split_axis=1, concat_axis=0, tiled=True
        )[None]
    hot_lanes = jnp.broadcast_to(
        jnp.pad(episode_match.astype(F32), ((0, 0), (0, 16 - EPISODES)))[:, :, None], (frames, 16, LANES)
    )
    g1, dhid_one, dnorm_sa, dnorm_one, dout_so, dout_one, flat = call(
        functools.partial(backward_kernel, flat_shard, extra),
        frames,
        [
            rowed(LAT, 3 * D), framed(HEADS, LAT), rowed(LAT, D), rowed(LAT, D), rowed(LAT, D), rowed(LAT, D),
            rowed(LAT, FF), rowed(LAT, FF), fixed(8, D), fixed(D, D),
        ]
        + [anywhere] * 4,
        [
            (rowed(LAT, D), shaped((rows_total, D))),
            (kept(1, FF), shaped((1, FF))),
            (kept(2, D), shaped((2, D))),
            (kept(2, D), shaped((2, D))),
            (kept(1, D), shaped((1, D))),
            (kept(1, D), shaped((1, D))),
            (anywhere, shaped(flat_shape, BF)),
        ],
        (
            qkv, self_lse, mixed, g3, h2, h1, act_one, slope_one, norms, w_so, w_qkv, up_one, down_one, flat,
        ),
        flops=2 * mlp_flops + 10 * attn_flops,
        trans=rows_total * LAT * HEADS,
        scratch=[
            pltpu.VMEM((LAT, 3 * D), BF), pltpu.VMEM((D, FF), F32), pltpu.VMEM((FF, D), F32),
            pltpu.VMEM((D, 3 * D), F32), pltpu.VMEM((D, D), F32),
            pltpu.VMEM((2048, LANES), F32), pltpu.VMEM((2, slab, LANES), BF), pltpu.VMEM((LAT, D), BF),
            pltpu.VMEM((LAT, D), BF), pltpu.VMEM((LAT, D), BF), pltpu.VMEM((LAT, D), F32),
            pltpu.SemaphoreType.DMA((2, 16)),
            pltpu.VMEM((D, 3 * D), BF), pltpu.VMEM((D, FF), BF), pltpu.VMEM((FF, D), BF),
            pltpu.SemaphoreType.DMA((3,)),
        ],
        limit=60,
        aliases={13: 6},
    )
    cross = (
        kvf, cross_out, cross_lse, rank, counts, episode_rows, hot_lanes, latent, norms, w_q, w_o,
        dnorm_one, dnorm_sa, dnorm_two, dhid_one, dhid_two, dout_one, dout_so, dout_two,
    )
    layout = param_layout()
    starts, ends, offset, bias_offset = [], [], 0, 0
    for name, shape in layout:
        if name == "hid_bias":
            bias_offset = offset
        starts.append(offset // LANES)
        offset += math.prod(shape)
        ends.append(offset // LANES)
    pad = [0] * (16 - len(layout))
    starts, ends = (np.tile(np.array(v + pad, np.int32)[:, None], (1, LANES)) for v in (starts, ends))
    opt_rows = shard_rows // 2 if shard_rows % 16 == 0 else shard_rows
    opt_steps = shard_rows // opt_rows
    base = (lat_index * shard_rows).astype(jnp.int32).reshape(1)
    smem = pl.BlockSpec(memory_space=pltpu.SMEM)
    flat_rows = (shard_rows, LANES)
    bias_owner, bias_at = divmod(bias_offset, shard_len)
    if reach:
        summed, stats, token_grad, unused = reduce_all(
            flat, master_rows, starts, ends, bias_owner, bias_at // LANES, tokens[0], tok_normed, w_kv, tok_norm,
            g1.reshape(frames, LAT, D), cross,
        )
    else:
        (flat,) = call(
            functools.partial(cross_bwd_kernel, kv_rows),
            frames,
            [
                rowed(LAT, D), framed(cap, LANES), rowed(LAT, LANES), framed(1, LAT), framed(token_rows_count, LANES),
                framed(8, LANES), framed(1, D), framed(16, LANES), fixed(LAT, D), fixed(8, D), fixed(D, LANES),
                fixed(LANES, D),
            ]
            + [fixed(*part.shape) for part in cross[11:]]
            + [anywhere],
            [(anywhere, shaped(flat_shape, BF))],
            (g1,) + cross + (flat,),
            flops=6 * score_flops,
            trans=rows_total * cap,
            scratch=cross_accumulators(total_keys)
            + small_buffers()
            + [pltpu.VMEM((kv_rows[1], LANES), BF), pltpu.SemaphoreType.DMA((8,))],
            aliases={20: 0},
        )
        grad_kv = lax.psum_scatter(flat[flat_shard:], "lat", scatter_dimension=0, tiled=True)
        flat = flat[:flat_shard]
        grad_w_kv = t_mm(tok_normed, grad_kv)
        grad_tok_normed = mm_t(grad_kv, w_kv)
        unused, token_pull = jax.vjp(layer_norm, tokens[0].astype(F32), tok_norm[0], tok_norm[1])
        grad_tokens, grad_tok_gain, grad_tok_bias = token_pull(grad_tok_normed)
        token_grad = grad_tokens.astype(BF)
        flat_at = flat_rows_of()
        tok_norm_grad = jnp.stack([grad_tok_gain, grad_tok_bias]).reshape(-1, LANES).astype(BF)
        flat = lax.dynamic_update_slice(flat, tok_norm_grad, (flat_at["tok_norm"], 0))
        flat = lax.dynamic_update_slice(flat, grad_w_kv.astype(BF), (flat_at["w_kv"], 0))
        local_flat = flat.reshape(-1)
        summed = lax.psum_scatter(local_flat, "lat", scatter_dimension=0, tiled=True)
        summed = lax.psum(summed, "kf").reshape(flat_rows)
        grad_sq, weight_sq = call(
            grad_stats_kernel,
            opt_steps,
            [smem, fixed(16, LANES), fixed(16, LANES), rowed(opt_rows, LANES), rowed(opt_rows, LANES)],
            [(kept(1, LANES), shaped((1, LANES))), (kept(16, LANES), shaped((16, LANES)))],
            (base, starts, ends, summed, master_rows),
        )
        bias_rows = summed[bias_at // LANES : bias_at // LANES + 2 * FF // LANES].astype(F32)
        bias_rows = jnp.where(lat_index == bias_owner, bias_rows, 0.0)
        stats = lax.psum(
            jnp.concatenate([grad_sq, jnp.zeros((7, LANES), F32), weight_sq, bias_rows]), "lat"
        )
    bias_grad = stats[24:STAT_ROWS].reshape(2, FF)
    grad_shard, lamb_update, new_one, new_two, update_sq = call(
        lamb_kernel,
        opt_steps,
        [smem, fixed(STAT_ROWS, LANES), fixed(16, LANES), fixed(16, LANES)] + [rowed(opt_rows, LANES)] * 4,
        [(rowed(opt_rows, LANES), shaped(flat_rows))] * 4 + [(kept(16, LANES), shaped((16, LANES)))],
        (
            base, stats, starts, ends, summed, master_rows,
            moment_one.reshape(flat_rows), moment_two.reshape(flat_rows),
        ),
    )
    if reach:
        vmem = pl.BlockSpec(memory_space=pltpu.VMEM)
        trust = pl.pallas_call(
            trust_kernel,
            out_shape=shaped((16, LANES)),
            in_specs=[vmem, vmem],
            out_specs=vmem,
            scratch_shapes=[
                pltpu.VMEM((8, 16, LANES), F32),
                pltpu.SemaphoreType.DMA((7,)),
                pltpu.SemaphoreType.DMA((7,)),
            ],
            compiler_params=pltpu.CompilerParams(collective_id=2, has_side_effects=True),
        )(update_sq, stats)[: len(layout), 0]
    else:
        update_sq = lax.psum(jnp.sum(update_sq, axis=1), "lat")
        weight_sq = jnp.sum(stats[8:24], axis=1)
        trust = (jnp.sqrt(weight_sq) / (jnp.sqrt(update_sq) + 1e-06))[: len(layout)]
    return (
        latents_out,
        token_grad[None],
        grad_shard.reshape(-1),
        lamb_update.reshape(-1),
        new_one.reshape(-1),
        new_two.reshape(-1),
        trust,
        bias_grad,
    )


def solution(mesh):
    return jax.shard_map(
        body,
        mesh=mesh,
        in_specs=(
            P("kf", "lat", None),
            P("kf", "lat"),
            P("kf", None),
            P("lat"),
            P("lat"),
            P("lat"),
            P("kf", None, "lat", None),
        ),
        out_specs=(
            P("kf", None, "lat", None),
            P("kf", "lat", None),
            P("lat"),
            P("lat"),
            P("lat"),
            P("lat"),
            P(),
            P(),
        ),
        check_vma=False,
    )
```

```python
import functools
import math

import jax
import jax.numpy as jnp
import numpy as np
from jax import lax
from jax.experimental import pallas as pl
from jax.experimental.pallas import tpu as pltpu
from jax.sharding import PartitionSpec as P

DIN = 256
D = 512
LAT = 512
CH = 64
HEADS = 8
HEAD_DIM = 64
FF = 2048
FRAMES = 32
EPISODES = 11
NPARAM = 5619712
LANES = 128

norm_eps = 1e-05
masked_fill = -1e30
beta_one = 0.9
beta_two = 0.999
adam_eps = 1e-06
decay_rate = 0.01
clip_fraction = 0.5
lamb_step = 10.0

BF = jnp.bfloat16
F32 = jnp.float32
MIB = 1024 * 1024


def param_layout():
    return [
        ("latent", (LAT, D)),
        ("episode", (EPISODES, D)),
        ("tok_norm", (2, DIN)),
        ("lat_norms", (8, D)),
        ("w_kv", (DIN, 2 * CH)),
        ("w_q", (D, CH)),
        ("w_o", (CH, D)),
        ("w_qkv", (D, 3 * D)),
        ("w_so", (D, D)),
        ("w_up", (2, D, FF)),
        ("w_down", (2, FF, D)),
        ("hid_bias", (2, FF)),
        ("out_bias", (4, D)),
    ]


def split_flat(flat_vector):
    pieces = {}
    offset = 0
    for tensor_name, tensor_shape in param_layout():
        entries = math.prod(tensor_shape)
        pieces[tensor_name] = flat_vector[offset : offset + entries].reshape(tensor_shape)
        offset += entries
    return pieces


def layer_norm(inputs, norm_gain, norm_bias):
    row_mean = jnp.mean(inputs, axis=-1, keepdims=True)
    centered = inputs - row_mean
    row_var = jnp.mean(centered * centered, axis=-1, keepdims=True)
    return centered * lax.rsqrt(row_var + norm_eps) * norm_gain + norm_bias


def mm(left, right):
    return jnp.dot(left, right, preferred_element_type=F32)


def mm_t(left, right):
    return lax.dot_general(left, right, (((1,), (1,)), ((), ())), preferred_element_type=F32)


def t_mm(left, right):
    return lax.dot_general(left, right, (((0,), (0,)), ((), ())), preferred_element_type=F32)


def norm_stats(rows):
    mean = jnp.mean(rows, axis=-1, keepdims=True)
    centered = rows - mean
    var = jnp.mean(centered * centered, axis=-1, keepdims=True)
    rstd = lax.rsqrt(var + norm_eps)
    return centered * rstd, rstd


def norm_back(grad, xhat, rstd, gain):
    dxh = grad * gain
    first = jnp.mean(dxh, axis=-1, keepdims=True)
    second = jnp.mean(dxh * xhat, axis=-1, keepdims=True)
    return rstd * (dxh - first - xhat * second)


def col_sum(values):
    return jnp.sum(values, axis=0, keepdims=True)


def gelu_pair(x):
    cdf = 0.5 + 0.5 * lax.erf(x * (1.0 / math.sqrt(2.0)))
    density = jnp.exp(x * x * -0.5) * (1.0 / math.sqrt(2.0 * math.pi))
    return x * cdf, cdf + x * density


def accumulate(first, ref, value):
    @pl.when(first)
    def _():
        ref[...] = value

    @pl.when(jnp.logical_not(first))
    def _():
        ref[...] += value


def lane_half(shape, half):
    lane = lax.broadcasted_iota(jnp.int32, shape, 1)
    return (lane >= half * 64) & (lane < half * 64 + 64)


def keep_half(values, half):
    return jnp.where(lane_half(values.shape, half), values, jnp.zeros_like(values))


def select_tokens(rank_rows, cap):
    slot = lax.broadcasted_iota(jnp.int32, (cap, LANES), 0)
    parts = []
    for r in range(rank_rows.shape[0]):
        hit = slot == rank_rows[r : r + 1, :]
        parts.append(jnp.where(hit, 1.0, 0.0).astype(BF))
    return jnp.concatenate(parts, axis=1)


def cross_scores(kvf, queries_scaled, count):
    scores = mm_t(kvf, queries_scaled)
    slot = lax.broadcasted_iota(jnp.int32, scores.shape, 0)
    return jnp.where(slot < count, scores, masked_fill)


def cross_attend(start, norms, w_q, kvf, count):
    xhat, unused = norm_stats(start)
    query_in = (xhat * norms[0:1, :] + norms[1:2, :]).astype(BF)
    queries = mm(query_in, w_q[...]).astype(BF) * jnp.asarray(0.125, BF)
    scores = cross_scores(kvf, queries, count)
    top = jnp.max(scores, axis=0, keepdims=True)
    terms = jnp.exp(scores - top)
    total = jnp.sum(terms, axis=0, keepdims=True)
    prob = (terms * (1.0 / total)).astype(BF)
    return t_mm(kvf, prob).T.astype(BF), top + jnp.log(total)


def cross_fwd_kernel(latent, episode, norms, w_q, w_o, out_bias, kv, rank, count, h1, kvf_out, co_out, lse_out):
    cap = kvf_out.shape[1]
    start = latent[...].astype(F32) + episode[0]
    chunk = 8 * LANES
    chunks = kv.shape[0] // chunk

    def step(j, acc):
        sel = select_tokens(rank[0, pl.ds(pl.multiple_of(j * 8, 8), 8), :], cap)
        return acc + mm(sel, kv[pl.ds(pl.multiple_of(j * chunk, chunk), chunk), :])

    kvf = lax.fori_loop(0, chunks, step, jnp.zeros((cap, LANES), F32)).astype(BF)
    co, lse = cross_attend(start, norms, w_q, kvf, count[0, 0:1, 0:1])
    h1[...] = start + mm(co, w_o[...]) + out_bias[0:1, :]
    kvf_out[0] = kvf
    co_out[...] = co
    lse_out[0] = lse


def segment_hot(starts, ends, base, rows):
    row = lax.broadcasted_iota(jnp.int32, (16, rows), 1) + base
    return jnp.where((row >= starts[:, 0:1]) & (row < ends[:, 0:1]), 1.0, 0.0).astype(BF)


def segment_sums(hot, squares):
    high = squares.astype(BF)
    low = (squares - high.astype(F32)).astype(BF)
    return mm(hot, high) + mm(hot, low)


def lamb_kernel(base, stats, starts, ends, summed, master, one, two, grad_out, update_out, one_out, two_out, norms_sq, bias):
    i = pl.program_id(0)
    rows = master.shape[0]
    hot = segment_hot(starts, ends, base[0] + i * rows, rows)
    total_sq = jnp.sum(stats[0:1, :], axis=1, keepdims=True)
    clip = jnp.minimum(1.0, clip_fraction * math.sqrt(NPARAM) / (jnp.sqrt(total_sq) + 1e-06))
    grad = summed[...].astype(F32)
    grad_out[...] = grad
    clipped = clip * grad
    new_one = beta_one * one[...] + (1.0 - beta_one) * clipped
    new_two = beta_two * two[...] + (1.0 - beta_two) * clipped * clipped
    one_out[...] = new_one
    two_out[...] = new_two
    first_hat = new_one * (1.0 / (1.0 - beta_one**lamb_step))
    second_hat = new_two * (1.0 / (1.0 - beta_two**lamb_step))
    update = first_hat / (jnp.sqrt(second_hat) + adam_eps) + decay_rate * master[...]
    update_out[...] = update
    accumulate(i == 0, norms_sq, segment_sums(hot, jnp.concatenate([update * update, master[...] * master[...]], axis=1)))
    for j in range(2 * FF // LANES):
        r, c = divmod(j, FF // LANES)
        bias[r : r + 1, c * LANES : (c + 1) * LANES] = stats[8 + j : 9 + j, :]


BATCH = 256
HALF = 128
QUARTER = 64
MESH = pl.DeviceIdType.MESH


class Place:
    def __init__(self):
        self.z = lax.axis_index("kf")
        self.me = lax.axis_index("lat")
        self.core = lax.rem(self.me, 2)
        self.x = lax.rem(self.me // 2, 2)
        self.y = self.me // 4
        self.z_low = lax.rem(self.z, 2)
        self.z_high = self.z // 2
        self.sibling = (self.z, self.me + 1 - 2 * self.core)
        self.x_side = (self.z, self.me + 2 - 4 * self.x)
        self.y_side = (self.z, self.me + 4 - 8 * self.y)
        self.z_near = (self.z + 1 - 2 * self.z_low, self.me)
        self.z_far = (self.z + 2 - 4 * self.z_high, self.me)

    def z_other(self, step):
        return (lax.rem(self.z + step, 4), self.me)

    def lat_other(self, step):
        return (self.z, lax.rem(self.me + step, 8))


def remote(src, dst, send, recv, device):
    return pltpu.make_async_remote_copy(
        src_ref=src, dst_ref=dst, send_sem=send, recv_sem=recv, device_id=device, device_id_type=MESH
    )


def greet(devices):
    barrier = pltpu.get_barrier_semaphore()
    for device in devices:
        pl.semaphore_signal(barrier, inc=1, device_id=device, device_id_type=MESH)


def met(devices):
    pl.semaphore_wait(pltpu.get_barrier_semaphore(), len(devices))


def added(left, right):
    return (left.astype(F32) + right.astype(F32)).astype(BF)


class Reduction:
    lags = (0, 1, 3, 5, 7, 9, 11)
    plane = 2

    def __init__(self, place, shard, grads, out, bufs, sems):
        self.p = place
        self.grads = grads
        self.out = out
        self.own, self.rc, self.r1, self.r2, self.r3, self.r4, self.res = bufs
        self.own_sem, self.send, self.rc_sem, self.r1_sem, self.r2_sem, self.r3_sem, self.r4_sem, self.res_sem = sems
        self.shard = shard
        self.full = pl.cdiv(shard, BATCH)
        self.batches = self.full + self.plane
        self.back = self.full * BATCH - shard
        self.held = flat_rows_of()["tok_norm"] // BATCH
        self.early = self.full - 1 - (self.held + 4)

    @staticmethod
    def scratch(shard):
        n = pl.cdiv(shard, BATCH) + Reduction.plane
        bufs = [
            pltpu.VMEM((2, 2, 2, BATCH, LANES), BF),
            pltpu.VMEM((n, 2, 2, BATCH, LANES), BF),
            pltpu.VMEM((n, 2, 2, HALF, LANES), BF),
            pltpu.VMEM((n, 2, HALF, LANES), BF),
            pltpu.VMEM((n, HALF, LANES), BF),
            pltpu.VMEM((n, QUARTER, LANES), BF),
            pltpu.VMEM((n, BATCH, LANES), BF),
        ]
        dma = pltpu.SemaphoreType.DMA
        sems = [dma((2,)), dma((10, 4)), dma((n,)), dma((n, 2)), dma((n, 2)), dma((n,)), dma((n,)), dma((n, 3))]
        return bufs + sems

    def from_on(self, i, first):
        return (i + 64 - first) // 64

    def row(self, i):
        n, held = self.full, self.held
        on = functools.partial(self.from_on, i)
        keys = on(self.early) - on(self.early + 2)
        shift = held + 4 + on(self.early + 2) * (-2) + on(self.early + 3) * (-n)
        shift = shift + on(self.early + 3 + held) * 2 + on(self.early + 5 + held) * (-4)
        b = i + shift
        row = keys * (self.shard + (i - self.early) * BATCH)
        row = row + (1 - keys) * (b * BATCH - (b // (n - 1)) * self.back)
        return pl.multiple_of(row, 16)

    def is_keys(self, i):
        return (i >= self.early) & (i < self.early + self.plane)

    def own_copy(self, i):
        slot = lax.rem(i, 2)
        src = self.grads.at[:, :, self.p.core, pl.ds(self.row(i), BATCH), :]
        return pltpu.make_async_copy(src, self.own.at[slot], self.own_sem.at[slot])

    def copies(self, stage, i):
        p, slot = self.p, lax.rem(i, 4)
        if stage == 0:
            src = self.grads.at[:, :, 1 - p.core, pl.ds(self.row(i), BATCH), :]
            return [remote(src, self.rc.at[i], self.send.at[0, slot], self.rc_sem.at[i], p.sibling)]
        if stage == 1:
            to_x = self.rc.at[i, :, 1 - p.x, pl.ds(0, HALF), :]
            to_y = self.rc.at[i, 1 - p.y, :, pl.ds(HALF, HALF), :]
            return [
                remote(to_x, self.r1.at[i, 0], self.send.at[1, slot], self.r1_sem.at[i, 0], p.x_side),
                remote(to_y, self.r1.at[i, 1], self.send.at[2, slot], self.r1_sem.at[i, 1], p.y_side),
            ]
        if stage == 2:
            to_y = self.r1.at[i, 0, 1 - p.y]
            to_x = self.r1.at[i, 1, 1 - p.x]
            return [
                remote(to_y, self.r2.at[i, 0], self.send.at[3, slot], self.r2_sem.at[i, 0], p.y_side),
                remote(to_x, self.r2.at[i, 1], self.send.at[4, slot], self.r2_sem.at[i, 1], p.x_side),
            ]
        if stage == 3:
            src = self.r2.at[i, 1 - p.z_low]
            return [remote(src, self.r3.at[i], self.send.at[5, slot], self.r3_sem.at[i], p.z_near)]
        if stage == 4:
            src = self.r3.at[i, pl.ds(pl.multiple_of((1 - p.z_high) * QUARTER, QUARTER), QUARTER), :]
            return [remote(src, self.r4.at[i], self.send.at[6, slot], self.r4_sem.at[i], p.z_far)]
        mine = self.res.at[i, pl.ds(pl.multiple_of(p.z_low * HALF + p.z_high * QUARTER, QUARTER), QUARTER), :]
        return [
            remote(mine, mine, self.send.at[6 + d, slot], self.res_sem.at[i, d - 1], p.z_other(d))
            for d in (1, 2, 3)
        ]

    def launch(self, stage, i):
        before = i - 4
        if stage >= 3:
            before = before - 4 * (self.from_on(before, self.early) - self.from_on(before, self.early + self.plane))

        @pl.when(i >= 4)
        def _():
            for copy in self.copies(stage, before):
                copy.wait_send()

        for copy in self.copies(stage, i):
            copy.start()

    def landed(self, stage, i):
        for copy in self.copies(stage, i):
            copy.wait_recv()

    def work(self, stage, i):
        p = self.p
        if stage == 0:
            self.own_copy(i).start()
        elif stage == 1:
            self.landed(0, i)
            self.own_copy(i).wait()
            self.rc[i] = added(self.rc[i], self.own[lax.rem(i, 2)])
        elif stage == 2:
            self.landed(1, i)
            self.r1[i, 0] = added(self.r1[i, 0], self.rc[i, :, p.x, 0:HALF, :])
            self.r1[i, 1] = added(self.r1[i, 1], self.rc[i, p.y, :, HALF:BATCH, :])
        elif stage == 3:
            self.landed(2, i)
            self.r2[i, 0] = added(self.r2[i, 0], self.r1[i, 0, p.y])
            self.r2[i, 1] = added(self.r2[i, 1], self.r1[i, 1, p.x])
        elif stage == 4:
            self.landed(3, i)
            self.r3[i] = added(self.r3[i], self.r2[i, p.z_low])
        elif stage == 5:
            self.landed(4, i)
            part = self.r3[i, pl.ds(pl.multiple_of(p.z_high * QUARTER, QUARTER), QUARTER), :]
            at = pl.multiple_of(p.z_low * HALF + p.z_high * QUARTER, QUARTER)
            self.res[i, pl.ds(at, QUARTER), :] = added(self.r4[i], part)
        else:
            self.landed(5, i)
            self.out[pl.ds(self.row(i), BATCH), :] = self.res[i]
        if stage == 3:
            pl.when(jnp.logical_not(self.is_keys(i)))(lambda: self.launch(stage, i))
        elif stage < 6:
            self.launch(stage, i)

    def tick(self, t):
        for stage, lag in enumerate(self.lags):
            i = t - lag

            inside = (i >= 0) & (i < self.batches)

            @pl.when(inside if stage < 4 else inside & jnp.logical_not(self.is_keys(i)))
            def _(stage=stage, i=i):
                self.work(stage, i)

    def ticks(self):
        return self.batches + self.lags[-1]

    def finish(self):
        for stage in range(6):
            for back in range(4):
                for copy in self.copies(stage, self.batches - 4 + back):
                    copy.wait_send()

    def partners(self):
        p = self.p
        return [p.sibling, p.x_side, p.y_side] + [p.z_other(d) for d in (1, 2, 3)]


def share_all(place, block, send, recv):
    mine = block.at[place.me]
    copies = [
        remote(mine, mine, send.at[d - 1], recv.at[d - 1], place.lat_other(d)) for d in range(1, 8)
    ]
    for copy in copies:
        copy.start()
    for copy in copies:
        copy.wait()


STAT_ROWS = 40


def token_backward(grad_kv, tokens, tok_normed, w_kv, tok_norm, token_grad, kv_grad, edge):
    kv_grad[...] = t_mm(tok_normed[...], grad_kv).astype(BF)
    grad = mm_t(grad_kv, w_kv[...])
    xhat, rstd = norm_stats(tokens[...].astype(F32))
    token_grad[...] = norm_back(grad, xhat, rstd, tok_norm[0:1, :]).astype(BF)
    gain, bias = col_sum(grad * xhat), col_sum(grad)
    parts = [half[:, j * LANES : (j + 1) * LANES] for half in (gain, bias) for j in range(DIN // LANES)]
    keep = edge.shape[0] - len(parts)
    edge[...] = jnp.concatenate([edge[...].astype(F32)[0:keep, :]] + parts, axis=0).astype(BF)


def reduce_kernel(
    shard, bias_owner, bias_at, unused_flat, tokens, tok_normed, w_kv, tok_norm,
    g1, kvf, co, lse, rank, count, episode, hot, latent, norms, w_q, w_o,
    dnorm_one, dnorm_sa, dnorm_two, dhid_one, dhid_two, dout_one, dout_so, dout_two,
    summed, stats, token_grad, grads, *scratch,
):
    place = Place()
    block, block_send, block_recv, edge, kv_grad, edge_sem, g1_held, g1_sem, kv_low, kv_sem = scratch[:10]
    accs, (stage, low, latent_low), engine = scratch[10:17], scratch[17:20], scratch[20:]
    acc_latent, acc_q, acc_o, acc_episode, dnorm, dout, dkv_t = accs
    frames = kvf.shape[0]
    red = Reduction(place, shard, grads, summed, engine[:7], engine[7:])
    frame_copies = [pltpu.make_async_copy(g1.at[f], g1_held.at[f], g1_sem.at[f]) for f in range(frames)]
    for copy in frame_copies:
        copy.start()
    partners = [place.lat_other(d) for d in range(1, 8)] + [place.z_other(d) for d in (1, 2, 3)]
    greet(partners)
    for ref in accs:
        ref[...] = jnp.zeros_like(ref)
    met(partners)

    def run(first, last):
        lax.fori_loop(first, last, lambda t, c: (red.tick(t), c)[1], 0)

    def frame(f, carry):
        red.tick(2 * f)
        pltpu.make_async_copy(g1.at[f], g1_held.at[f], g1_sem.at[f]).wait()
        rows = pl.ds(pl.multiple_of(f * LAT, LAT), LAT)
        cross_back_frame(
            g1_held[f], kvf[f], co[rows, :], lse[f], rank.at[f], count[f, 0:1, 0:1], episode[f], hot[f, :, 0:1],
            latent, norms, w_q, w_o, *accs, pause=lambda: red.tick(2 * f + 1),
        )
        return carry

    lax.fori_loop(0, frames, frame, 0)
    run(2 * frames, red.early)
    at = flat_rows_of()
    copies = []

    def put(source, row):
        owner, local = row if isinstance(row, tuple) else divmod(row, shard)
        dst = grads.at[owner // 4, owner // 2 % 2, owner % 2, pl.ds(local, source.shape[0]), :]
        copies.append(pltpu.make_async_copy(source, dst, kv_sem.at[len(copies)]))
        copies[-1].start()

    write_small(
        put, stage, low, latent_low, acc_latent, acc_q, acc_o, acc_episode,
        stacked(dnorm, dnorm_one, dnorm_sa, dnorm_two), stacked(dhid_one, dhid_two),
        stacked(dout, dout_one, dout_so, dout_two),
    )
    edge_row = at["tok_norm"] // 16 * 16
    edge[...] = low[0, edge_row - at["episode"] : edge_row - at["episode"] + 16, :]
    count_kv = tokens.shape[0]
    for j in range(8):
        kv_low[j] = dkv_t[:, j * count_kv : (j + 1) * count_kv].T
        put(kv_low.at[j], (j, shard))
    for copy in copies:
        copy.wait()
    ready = red.early + red.lags[3] + red.plane
    run(red.early, ready)
    grad_kv = jnp.concatenate([red.r2[red.early + i, h] for i in range(red.plane) for h in range(2)], axis=0)
    token_backward(grad_kv, tokens, tok_normed, w_kv, tok_norm, token_grad, kv_grad, edge)
    writes = [
        pltpu.make_async_copy(edge, grads.at[0, 0, 0, pl.ds(edge_row, 16), :], edge_sem.at[0]),
        pltpu.make_async_copy(kv_grad, grads.at[0, 0, 0, pl.ds(at["w_kv"], DIN), :], edge_sem.at[1]),
    ]
    for copy in writes:
        copy.start()
    run(ready, ready + 2)
    for copy in writes:
        copy.wait()
    run(ready + 2, red.ticks())
    grad_sq = jnp.zeros((1, LANES), F32)
    step = 784
    for j in range(shard // step):
        part = summed[j * step : (j + 1) * step, :].astype(F32)
        grad_sq = grad_sq + col_sum(part * part)
    bias = summed[bias_at : bias_at + 2 * FF // LANES, :].astype(F32)
    bias = jnp.where(place.me == bias_owner, bias, 0.0)
    head = jnp.concatenate([grad_sq, jnp.zeros((7, LANES), F32), bias], axis=0)
    block[pl.ds(place.me, 1)] = head[None]
    share_all(place, block, block_send, block_recv)
    total = block[0]
    for s in range(1, 8):
        total = total + block[s]
    stats[...] = total
    red.finish()


def trust_kernel(norms_sq, trust, block, send, recv):
    place = Place()
    partners = [place.lat_other(d) for d in range(1, 8)]
    greet(partners)
    block[pl.ds(place.me, 1)] = norms_sq[...][None]
    met(partners)
    share_all(place, block, send, recv)
    total = block[0]
    for s in range(1, 8):
        total = total + block[s]
    update_sq = jnp.sum(total[:, 0:LANES].T, axis=0, keepdims=True)
    weight_sq = jnp.sum(total[:, LANES : 2 * LANES].T, axis=0, keepdims=True)
    ratio = jnp.sqrt(weight_sq) / (jnp.sqrt(update_sq) + 1e-06)
    trust[...] = ratio[:, 0 : trust.shape[1]]


def relayout(whole, row, stage, dst, rows, cols):
    wide = cols // LANES
    block = min(rows, 2048 // wide // 128 * 128)

    def step(i, carry):
        at = pl.multiple_of(row + i * (block * wide), 16)
        stage[0 : block * wide, :] = whole[pl.ds(at, block * wide), :].astype(F32)
        for j in range(wide):
            part = stage[pl.ds(j, block, stride=wide), :]
            dst[pl.ds(pl.multiple_of(i * block, 16), block), j * LANES : (j + 1) * LANES] = part.astype(BF)
        return carry

    lax.fori_loop(0, rows // block, step, 0)


def small_matrix(whole, row, stage, rows, cols):
    wide = cols // LANES
    stage[0 : rows * wide, :] = whole[row : row + rows * wide, :].astype(F32)
    return jnp.concatenate([stage[pl.ds(j, rows, stride=wide), :] for j in range(wide)], axis=1)


class Gather:
    def __init__(self, place, whole, shard, chunks, send, recv):
        self.p, self.whole, self.shard, self.chunks, self.send, self.recv = place, whole, shard, chunks, send, recv
        p = place
        x_index, y_index = p.x_side[1], p.y_side[1]
        low = p.z_low
        self.first = x_index + low * (y_index - x_index)
        self.second = y_index + low * (x_index - y_index)
        self.diagonal = x_index + 4 - 8 * p.y

    def copy(self, kind, k):
        p = self.p
        block = (p.me, p.me, self.first, self.first, self.first, self.diagonal, self.second)[kind]
        target = (
            (p.z, self.first), p.sibling, (p.z, self.second), p.z_near, p.sibling, p.sibling, p.sibling
        )[kind]
        row, count = self.chunks[k]
        ref = self.whole.at[pl.ds(pl.multiple_of(block * self.shard + row, 16), count), :]
        return remote(ref, ref, self.send.at[kind, k], self.recv.at[kind, k], target)

    def play(self, *events):
        for event in events:
            kind, k = event[0], int(event[1:])
            if kind == "a":
                self.copy(0, k).start()
                self.copy(1, k).start()
            elif kind == "b":
                self.copy(0, k).wait_recv()
                for way in (2, 3, 4):
                    self.copy(way, k).start()
            elif kind == "c":
                for arrived, onward in ((2, 5), (3, 6)):
                    self.copy(arrived, k).wait_recv()
                    self.copy(onward, k).start()
            else:
                for way in (1, 4, 5, 6):
                    self.copy(way, k).wait_recv()

    def finish(self):
        for k in range(len(self.chunks)):
            for kind in range(7):
                self.copy(kind, k).wait_send()


class KeyExchange:
    def __init__(self, place, keys, send, recv):
        self.p, self.keys, self.send, self.recv = place, keys, send, recv
        self.x_index, self.y_index = place.x_side[1], place.y_side[1]
        self.diagonal = self.x_index + 4 - 8 * place.y

    def copy(self, kind):
        p = self.p
        half = self.keys.shape[1] // 2
        low, high, full = pl.ds(0, half), pl.ds(half, half), pl.ds(0, 2 * half)
        block, rows, target = (
            (p.me, full, p.x_side), (p.me, full, p.y_side), (p.me, full, p.sibling),
            (self.x_index, low, p.y_side), (self.y_index, high, p.x_side),
            (self.x_index, full, p.sibling), (self.y_index, full, p.sibling), (self.diagonal, full, p.sibling),
        )[kind]
        ref = self.keys.at[block, rows, :]
        return remote(ref, ref, self.send.at[kind], self.recv.at[kind], target)

    def step(self, s):
        if s == 0:
            waits, starts = (), (0, 1, 2)
        elif s == 1:
            waits, starts = (0, 1), (3, 4, 5, 6)
        elif s == 2:
            waits, starts = (3, 4), (7,)
        else:
            waits, starts = (2, 5, 6, 7), ()
        for kind in waits:
            self.copy(kind).wait_recv()
        for kind in starts:
            self.copy(kind).start()

    def finish(self):
        for kind in range(8):
            self.copy(kind).wait_send()


def flat_rows_of():
    rows, at = {}, 0
    for name, shape in param_layout():
        rows[name] = at // LANES
        at += math.prod(shape)
    return rows


def gather_chunks(shard):
    at = flat_rows_of()
    tail = at["hid_bias"] % shard // 16 * 16
    chunks = [(at["episode"], at["w_o"] - at["episode"]), (tail, shard - tail), (at["w_o"], at["w_qkv"] - at["w_o"])]
    for low, high in ((0, at["episode"]), (at["w_qkv"], tail)):
        while low < high:
            count = min(512, high - low)
            chunks.append((low, count))
            low += count
    return chunks


def begin_kernel(
    chunks, master, tokens, ids, episodes,
    up_one, down_one, qkv_w, so_w, up_two, down_two,
    latent, norms, hid_bias, out_bias, w_q, w_o, w_kv, tok_norm, tok_normed, episode, rank, counts,
    kvf_out, co_out, lse_out, hot_lanes, h1,
    whole, stage, all_ids, keys, m_up_one, m_down_one, m_qkv, m_so, m_up_two, m_down_two,
    episodes_held, h1_held, h1_sem, send, recv, key_send, key_recv, id_send, id_recv, out_sem,
):
    place = Place()
    shard = master.shape[0]
    frames, cap = kvf_out.shape[0], kvf_out.shape[1]
    gather = Gather(place, whole, shard, chunks, send, recv)
    exchange = KeyExchange(place, keys, key_send, key_recv)
    at = flat_rows_of()
    partners = [place.lat_other(d) for d in range(1, 8)] + [place.z_near]
    greet(partners)
    all_ids[pl.ds(place.me, 1)] = ids[...][None]
    id_copies = [
        remote(all_ids.at[place.me], all_ids.at[place.me], id_send.at[d - 1], id_recv.at[d - 1], place.lat_other(d))
        for d in range(1, 8)
    ]
    own_at = place.me * shard
    for row, count in chunks:
        whole[pl.ds(pl.multiple_of(own_at + row, 16), count), :] = master[row : row + count, :].astype(BF)
    met(partners)
    for copy in id_copies:
        copy.start()
    gather.play("a0", "a1", "a2", "a3", "a4")

    for copy in id_copies:
        copy.wait_recv()
    tags = jnp.concatenate([all_ids[s] for s in range(8)], axis=0)
    low = lax.broadcasted_iota(jnp.int32, (LANES, LANES), 0)
    high = lax.broadcasted_iota(jnp.int32, (LANES, LANES), 1)
    upto = jnp.where(low <= high, 1.0, 0.0).astype(BF)
    n = tags.shape[0]
    below = jnp.where(
        lax.broadcasted_iota(jnp.int32, (n, n), 1) < lax.broadcasted_iota(jnp.int32, (n, n), 0), 1.0, 0.0
    ).astype(BF)
    for f in range(frames):
        hit = tags == place.me * frames + f
        hit_low = jnp.where(hit, 1.0, 0.0).astype(BF)
        inside = mm(hit_low, upto)
        row_total = jnp.broadcast_to(inside[:, LANES - 1 : LANES], (n, LANES))
        before = mm(below, row_total.astype(BF))
        place_in = (inside + before).astype(jnp.int32) - 1
        rank[f] = jnp.where(hit, place_in, -1)
        total = jnp.sum(row_total[:, 0:1], axis=0, keepdims=True).astype(jnp.int32)
        counts[f] = jnp.broadcast_to(total, (8, LANES))
    gather.play("b0", "b1", "a5", "b2", "c0", "c1", "a6", "d0", "d1")

    pair = whole[at["tok_norm"] // 16 * 16 : at["lat_norms"], :].astype(F32)
    pair = pair[at["tok_norm"] % 16 : at["tok_norm"] % 16 + 4, :]
    tok_norm[...] = jnp.concatenate(
        [
            jnp.concatenate([pair[0:1], pair[1:2]], axis=1),
            jnp.concatenate([pair[2:3], pair[3:4]], axis=1),
        ],
        axis=0,
    )
    w_kv[...] = whole[at["w_kv"] : at["w_kv"] + DIN, :]
    xhat, unused = norm_stats(tokens[...].astype(F32))
    normed = (xhat * tok_norm[0:1, :] + tok_norm[1:2, :]).astype(BF)
    tok_normed[...] = normed
    keys[pl.ds(place.me, 1)] = mm(normed, w_kv[...]).astype(BF)[None]
    exchange.step(0)
    gather.play("a7", "a8", "b3", "c2")
    norms[...] = small_matrix(whole, at["lat_norms"], stage, 8, D)
    hid_bias[...] = small_matrix(whole, at["hid_bias"], stage, 2, FF)
    out_bias[...] = small_matrix(whole, at["out_bias"], stage, 4, D)
    mine = lax.broadcasted_iota(jnp.int32, (16, FRAMES), 0) + place.me * frames
    mine = mine == lax.broadcasted_iota(jnp.int32, (16, FRAMES), 1)
    own = jnp.sum(jnp.where(mine, episodes[...].astype(F32), 0.0), axis=1, keepdims=True)
    hot = jnp.where(lax.broadcasted_iota(jnp.int32, (16, 16), 1).astype(F32) == own, 1.0, 0.0).astype(BF)
    for f in range(frames):
        row = lax.broadcasted_iota(jnp.int32, (16, LANES), 0).astype(F32)
        hot_lanes[f] = jnp.where(row == own[f : f + 1, 0:1], 1.0, 0.0)
    episode_rows = mm(hot, small_matrix(whole, at["episode"], stage, 16, D).astype(BF))
    gather.play("b4", "c3", "d2", "b5", "c4", "d3", "b6")
    exchange.step(1)
    gather.play("a9", "a10", "c5", "d4", "c6", "d5")
    packed = whole[at["w_q"] : at["w_q"] + D // 2, :].astype(F32)
    stage[pl.ds(0, D // 2, stride=2), :] = packed
    stage[pl.ds(1, D // 2, stride=2), :] = pltpu.roll(packed, CH, 1)
    w_q[...] = keep_half(stage[0:D, :], 0).astype(BF)
    w_o[0:CH, :] = jnp.zeros((CH, D), BF)
    w_o[CH : 2 * CH, :] = small_matrix(whole, at["w_o"], stage, CH, D).astype(BF)
    exchange.step(2)
    gather.play("a11", "b7", "d6")
    exchange.step(3)
    relayout(whole, 0, stage, latent, LAT, D)

    chunk = 8 * LANES
    episodes_held[...] = episode_rows[0:8, :]
    before = [("b8",), ("b9", "d7"), ("b10", "d8"), ("b11", "d9")]
    midway = [("c7",), ("c8",), ("c9",), ("c10",)]

    def play(frame, parts):
        for step, events in enumerate(parts):
            pl.when(frame == step)(functools.partial(gather.play, *events))

    def attend(f, carry):
        play(f, before)
        row = episodes_held[pl.ds(f, 1), :]
        start = latent[...].astype(F32) + row
        episode[pl.ds(f, 1)] = row[None]

        def pick(j, acc):
            sel = select_tokens(rank[f, pl.ds(pl.multiple_of(8 * j, 8), 8), :], cap)
            return acc + mm(sel, keys[pl.ds(2 * j, 2)].reshape(chunk, LANES))

        kvf = lax.fori_loop(0, n // 8, pick, jnp.zeros((cap, LANES), F32)).astype(BF)
        play(f, midway)
        co, lse = cross_attend(start, norms, w_q, kvf, counts[f, 0:1, 0:1])
        rows = pl.ds(pl.multiple_of(f * LAT, LAT), LAT)
        h1_held[f] = start + mm(co, w_o[...]) + out_bias[0:1, :]
        pltpu.make_async_copy(h1_held.at[f], h1.at[rows, :], h1_sem.at[f]).start()
        kvf_out[f] = kvf
        co_out[rows, :] = co
        lse_out[f] = lse
        return carry

    lax.fori_loop(0, frames, attend, 0)
    gather.play("c11", "d10", "d11")

    big = (
        (up_one, m_up_one, at["w_up"], D, FF),
        (down_one, m_down_one, at["w_down"], FF, D),
        (qkv_w, m_qkv, at["w_qkv"], D, 3 * D),
        (so_w, m_so, at["w_so"], D, D),
        (up_two, m_up_two, at["w_up"] + D * FF // LANES, D, FF),
        (down_two, m_down_two, at["w_down"] + D * FF // LANES, FF, D),
    )
    outs = []
    for j, (out, held, row, rows, cols) in enumerate(big):
        relayout(whole, row, stage, held, rows, cols)
        outs.append(pltpu.make_async_copy(held, out, out_sem.at[j]))
        outs[-1].start()
    for copy in outs:
        copy.wait()
    for f in range(frames):
        pltpu.make_async_copy(h1_held.at[f], h1.at[f * LAT : (f + 1) * LAT, :], h1_sem.at[f]).wait()
    for copy in id_copies:
        copy.wait_send()
    exchange.finish()
    gather.finish()


def begin_all(master_rows, token_rows, ids, episodes, frames, cap):
    shard = master_rows.shape[0]
    tokens = token_rows.shape[0]
    total = 8 * tokens
    chunks = gather_chunks(shard)
    vmem = pl.BlockSpec(memory_space=pltpu.VMEM)
    anywhere = pl.BlockSpec(memory_space=pl.ANY)
    matrices = [(D, FF), (FF, D), (D, 3 * D), (D, D), (D, FF), (FF, D)]
    dma = pltpu.SemaphoreType.DMA
    return pl.pallas_call(
        functools.partial(begin_kernel, chunks),
        out_shape=[shaped(m, BF) for m in matrices]
        + [
            shaped((LAT, D), BF),
            shaped((8, D)),
            shaped((2, FF)),
            shaped((4, D)),
            shaped((D, LANES), BF),
            shaped((LANES, D), BF),
            shaped((DIN, LANES), BF),
            shaped((2, DIN)),
            shaped((tokens, DIN), BF),
            shaped((frames, 1, D)),
            shaped((frames, total // LANES, LANES), jnp.int32),
            shaped((frames, 8, LANES), jnp.int32),
            shaped((frames, cap, LANES), BF),
            shaped((frames * LAT, LANES), BF),
            shaped((frames, 1, LAT)),
            shaped((frames, 16, LANES)),
            shaped((frames * LAT, D)),
        ],
        in_specs=[vmem] * 4,
        out_specs=[anywhere] * 6 + [vmem] * 16 + [anywhere],
        scratch_shapes=[
            pltpu.VMEM((8 * shard, LANES), BF),
            pltpu.VMEM((2048, LANES), F32),
            pltpu.VMEM((8, tokens // LANES, LANES), jnp.int32),
            pltpu.VMEM((8, tokens, LANES), BF),
        ]
        + [pltpu.VMEM(m, BF) for m in matrices]
        + [
            pltpu.VMEM((8, D), F32),
            pltpu.VMEM((frames, LAT, D), F32),
            dma((frames,)),
            dma((7, len(chunks))), dma((7, len(chunks))), dma((8,)), dma((8,)), dma((7,)), dma((7,)), dma((6,)),
        ],
        compiler_params=pltpu.CompilerParams(
            collective_id=3, has_side_effects=True, vmem_limit_bytes=56 * MIB
        ),
    )(master_rows, token_rows, ids, episodes)


FCHUNK = 512


def to_flat(stage, matrix):
    rows, wide = matrix.shape[0], matrix.shape[1] // LANES
    for j in range(wide):
        stage[pl.ds(j, rows, stride=wide), :] = matrix[:, j * LANES : (j + 1) * LANES]
    return stage[0 : rows * wide, :]


def chunk_of(c, size=FCHUNK):
    return pl.ds(pl.multiple_of(c * size, LANES), size)


def feed_forward(rows, gain, bias, up_bias, down_bias, w_up, w_down, act_ref, slope_ref, normed_ref, total_ref):
    xhat, rstd = norm_stats(rows)
    normed_ref[...] = (xhat * gain + bias).astype(BF)
    total_ref[...] = rows + down_bias

    for c in range(2):
        at = slice(c * FF // 2, (c + 1) * FF // 2)
        act, slope = gelu_pair(mm(normed_ref[...], w_up[:, at]) + up_bias[:, at])
        act = act.astype(BF)
        act_ref[:, at] = act
        slope_ref[:, at] = slope.astype(BF)
        total_ref[...] += mm(act, w_down[at, :])


def feed_back(grad_ref, normed_ref, xhat, rstd, gain, act, slope, w_up, w_down, acc_up, acc_down, dhid, dnorm, dout, work):
    work[...] = jnp.zeros(work.shape, F32)
    for c in range(FF // FCHUNK):
        at = slice(c * FCHUNK, (c + 1) * FCHUNK)
        dpre = (mm_t(grad_ref[...], w_down[at, :]) * slope[:, at].astype(F32)).astype(BF)
        dhid[:, at] += col_sum(dpre.astype(F32))
        work[...] += mm_t(dpre, w_up[:, at])
        acc_up[:, at] += t_mm(normed_ref[...], dpre)
        acc_down[at, :] += t_mm(act[:, at], grad_ref[...])
    grad_normed = work[...]
    dnorm[...] += jnp.concatenate([col_sum(grad_normed * xhat), col_sum(grad_normed)], axis=0)
    dout[...] += col_sum(grad_ref[...].astype(F32))
    return norm_back(grad_normed, xhat, rstd, gain)


def clear(first, refs):
    @pl.when(first)
    def _():
        for ref in refs:
            ref[...] = jnp.zeros_like(ref)


def flat_spans(row, count, shard, extra):
    spans, done = [], 0
    while done < count:
        part = min(count - done, shard - (row + done) % shard)
        spans.append((done, part, row + done + (row + done) // shard * extra))
        done += part
    return spans


def flatten(acc, stage, low, slot):
    wide = acc.shape[1] // LANES
    block = min(acc.shape[0], 2048 // wide // 128 * 128)
    span = block * wide

    def step(i, carry):
        part = acc[pl.ds(pl.multiple_of(i * block, block), block), :]
        for j in range(wide):
            stage[pl.ds(j, block, stride=wide), :] = part[:, j * LANES : (j + 1) * LANES]
        low[slot, pl.ds(pl.multiple_of(i * span, span), span), :] = stage[0:span, :].astype(BF)
        return carry

    lax.fori_loop(0, acc.shape[0] // block, step, 0)


def write_flat(flat, stage, low, pieces, sems, shard, extra):
    pending = {}
    for j, (acc, row) in enumerate(pieces):
        count = acc.shape[0] * acc.shape[1] // LANES
        slot = j % 2
        for copy in pending.get(slot, []):
            copy.wait()
        flatten(acc, stage, low, slot)
        pending[slot] = [
            pltpu.make_async_copy(low.at[slot, pl.ds(off, part), :], flat.at[pl.ds(at, part), :], sems.at[slot, k])
            for k, (off, part, at) in enumerate(flat_spans(row, count, shard, extra))
        ]
        for copy in pending[slot]:
            copy.start()
    for copies in pending.values():
        for copy in copies:
            copy.wait()


class FrameExchange:
    def __init__(self, place, source, grad, held, result, sems):
        self.p, self.source, self.grad, self.held, self.result = place, source, grad, held, result
        self.in_send, self.in_recv, self.out_send, self.out_recv, self.own_in, self.own_out = sems
        self.frames, self.rows = grad.shape[0], source.shape[1]

    @staticmethod
    def scratch(frames):
        dma = pltpu.SemaphoreType.DMA
        return [dma((frames, 7))] * 4 + [dma((frames,))] * 2

    def block(self, index):
        return pl.ds(pl.multiple_of(index * self.rows, 16), self.rows)

    def arriving(self, f, d):
        target = self.p.lat_other(d)
        src = self.source.at[target[1] * self.frames + f]
        dst = self.grad.at[f, self.block(self.p.me), :]
        return remote(src, dst, self.in_send.at[f, d - 1], self.in_recv.at[f, d - 1], target)

    def own_arriving(self, f):
        src = self.source.at[self.p.me * self.frames + f]
        return pltpu.make_async_copy(src, self.grad.at[f, self.block(self.p.me), :], self.own_in.at[f])

    def leaving(self, f, d):
        target = self.p.lat_other(d)
        src = self.held.at[f, self.block(target[1]), :]
        dst = self.result.at[self.p.me * self.frames + f]
        return remote(src, dst, self.out_send.at[f, d - 1], self.out_recv.at[f, d - 1], target)

    def own_leaving(self, f):
        dst = self.result.at[self.p.me * self.frames + f]
        return pltpu.make_async_copy(self.held.at[f, self.block(self.p.me), :], dst, self.own_out.at[f])

    def partners(self):
        return [self.p.lat_other(d) for d in range(1, 8)]

    def begin(self):
        met(self.partners())
        for f in range(self.frames):
            self.own_arriving(f).start()
            for d in range(1, 8):
                self.arriving(f, d).start()

    def await_frame(self, f):
        self.own_arriving(f).wait()
        for d in range(1, 8):
            self.arriving(f, d).wait_recv()

    def send_frame(self, f):
        self.own_leaving(f).start()
        for d in range(1, 8):
            self.leaving(f, d).start()

    def finish(self):
        def step(f, carry):
            self.own_leaving(f).wait()
            for d in range(1, 8):
                self.arriving(f, d).wait_send()
                self.leaving(f, d).wait()
            return carry

        lax.fori_loop(0, self.frames, step, 0)


class Late:
    def __init__(self, step, sources, refs, sems):
        self.first = step == 0
        self.copies = [
            pltpu.make_async_copy(src, ref, sems.at[k]) for k, (src, ref) in enumerate(zip(sources, refs))
        ]

        @pl.when(self.first)
        def _():
            for copy in self.copies:
                copy.start()

    def need(self, *which):
        @pl.when(self.first)
        def _():
            for k in which:
                self.copies[k].wait()


def forward_kernel(
    reach, shard, extra, h1, grad, norms, hid_bias, out_bias, up_one, down_one, *rest,
):
    forward_body(reach, shard, extra, h1, grad, norms, hid_bias, out_bias, up_one, down_one, rest[:4], *rest[4:])


def forward_body(
    reach, shard, extra, h1, grad, norms, hid_bias, out_bias, up_one, down_one, late_sources,
    h2_out, qkv, lse_out, mixed_out, act_one, slope_one, latents, g3, dhid, dnorm, dout, flat,
    act_two, slope_two, acc_up, acc_down, stage, low, normed, mixed_t, work, sems,
    w_qkv, w_so, up_two, down_two, late_sems, *shared,
):
    step = pl.program_id(0)
    late = Late(step, late_sources, (w_qkv, w_so, up_two, down_two), late_sems)
    if reach:
        place = Place()
        traffic = FrameExchange(place, grad, shared[0], shared[1], latents, shared[2:])
        pl.when(step == 0)(lambda: greet(traffic.partners()))
        grad = shared[0].at[step]
    clear(step == 0, (acc_up, acc_down, dhid, dnorm, dout))
    feed_forward(
        h1[...], norms[2:3, :], norms[3:4, :], hid_bias.at[0:1], out_bias[1:2, :], up_one, down_one, act_one,
        slope_one, normed, h2_out,
    )
    xhat, unused = norm_stats(h2_out[...])
    normed[...] = (xhat * norms[4:5, :] + norms[5:6, :]).astype(BF)

    late.need(0)
    if reach:
        pl.when(step == 0)(traffic.begin)

    def project(c, carry):
        at = chunk_of(c)
        qkv[:, at] = mm(normed[...], w_qkv[:, at]).astype(BF)
        return carry

    lax.fori_loop(0, 3, project, 0)
    scale = jnp.asarray(0.125, BF)

    ones = jnp.ones((16, LAT), BF)

    for pair in range(HEADS // 2):
        base = pair * LANES
        query_pair = qkv[:, base : base + LANES] * scale
        key_pair = qkv[:, D + base : D + base + LANES]
        value_t = qkv[:, 2 * D + base : 2 * D + base + LANES].T
        for half in range(2):
            scores = mm_t(key_pair, keep_half(query_pair, half))
            top = jnp.max(scores, axis=0, keepdims=True)
            terms = jnp.exp(scores - top).astype(BF)
            values = jnp.concatenate([value_t[half * HEAD_DIM : (half + 1) * HEAD_DIM, :], ones], axis=0)
            product = mm(values, terms)
            total = product[HEAD_DIM : HEAD_DIM + 1, :]
            head = 2 * pair + half
            lse_out[0, head : head + 1, :] = top + jnp.log(total)
            mixed_t[head * HEAD_DIM : (head + 1) * HEAD_DIM, :] = product[0:HEAD_DIM, :] * (1.0 / total)
    late.need(1, 2, 3)
    mixed = mixed_t[...].T.astype(BF)
    mixed_out[...] = mixed
    h3 = h2_out[...] + mm(mixed, w_so[...]) + out_bias[2:3, :]
    feed_forward(
        h3, norms[6:7, :], norms[7:8, :], hid_bias.at[1:2], out_bias[3:4, :], up_two, down_two, act_two, slope_two,
        normed, work,
    )
    if reach:
        shared[1][step] = work[...].astype(BF)
        traffic.send_frame(step)
        traffic.await_frame(step)
    else:
        latents[...] = work[...].astype(BF)
    xhat, rstd = norm_stats(h3)
    g3[...] = grad[...].astype(F32) + feed_back(
        grad, normed, xhat, rstd, norms[6:7, :], act_two, slope_two, up_two, down_two,
        acc_up, acc_down, dhid, dnorm, dout, work,
    )

    @pl.when(step == pl.num_programs(0) - 1)
    def _():
        at = flat_rows_of()
        half = D * FF // LANES
        write_flat(flat, stage, low, [(acc_up, at["w_up"] + half), (acc_down, at["w_down"] + half)], sems, shard, extra)
        if reach:
            traffic.finish()


def backward_kernel(
    shard, extra, qkv, lse, mixed, g3, h2, h1, act_one, slope_one, norms, w_so, src_qkv, src_up, src_down, flat_in,
    g1, dhid, dnorm_sa, dnorm_one, dout_so, dout_one, flat,
    dqkv, acc_up, acc_down, acc_qkv, acc_so, stage, low, normed, grad_mixed, grad_low, work, sems,
    w_qkv, up_one, down_one, late_sems,
):
    step = pl.program_id(0)
    late = Late(step, (src_qkv, src_up, src_down), (w_qkv, up_one, down_one), late_sems)
    clear(
        step == 0,
        (acc_up, acc_down, acc_qkv, acc_so, dhid, dnorm_sa, dnorm_one, dout_so, dout_one),
    )
    scale = jnp.asarray(0.125, BF)
    grad_three = g3[...]
    grad_low[...] = grad_three.astype(BF)
    dout_so[...] += col_sum(grad_low[...].astype(F32))
    acc_so[...] += t_mm(mixed[...], grad_low[...])
    grad_mixed[...] = mm_t(grad_low[...], w_so[...]).astype(BF)

    def attend(pair, carry):
        query_at = chunk_of(pair, LANES)
        key_at = chunk_of(pair + D // LANES, LANES)
        value_at = chunk_of(pair + 2 * D // LANES, LANES)
        query_pair = qkv[:, query_at] * scale
        key_pair = qkv[:, key_at]
        value_pair = qkv[:, value_at]
        grad_pair = grad_mixed[:, query_at]
        key_t = key_pair.T
        query_t = []
        grad_key = jnp.zeros((LAT, LANES), F32)
        grad_value = jnp.zeros((LAT, LANES), F32)
        for half in range(2):
            query = keep_half(query_pair, half)
            grad_head = keep_half(grad_pair, half)
            prob = jnp.exp(mm_t(key_pair, query) - lse[0, pl.ds(2 * pair + half, 1), :])
            grad_value = grad_value + mm(prob.astype(BF), grad_head)
            weighted = prob * mm_t(value_pair, grad_head)
            grad_score = (weighted - prob * col_sum(weighted)).astype(BF)
            grad_key = grad_key + mm(grad_score, query)
            query_t.append(mm(key_t[half * HEAD_DIM : (half + 1) * HEAD_DIM, :], grad_score))
        dqkv[:, query_at] = (jnp.concatenate(query_t, axis=0).T * 0.125).astype(BF)
        dqkv[:, key_at] = grad_key.astype(BF)
        dqkv[:, value_at] = grad_value.astype(BF)
        return carry

    lax.fori_loop(0, HEADS // 2, attend, 0)
    late.need(0, 1, 2)
    xhat, rstd = norm_stats(h2[...])
    normed[...] = (xhat * norms[4:5, :] + norms[5:6, :]).astype(BF)
    work[...] = jnp.zeros(work.shape, F32)

    for c in range(3):
        at = slice(c * D, (c + 1) * D)
        work[...] += mm_t(dqkv[:, at], w_qkv[:, at])
        acc_qkv[:, at] += t_mm(normed[...], dqkv[:, at])
    grad_in = work[...]
    dnorm_sa[...] += jnp.concatenate([col_sum(grad_in * xhat), col_sum(grad_in)], axis=0)
    grad_two = grad_three + norm_back(grad_in, xhat, rstd, norms[4:5, :])

    xhat, rstd = norm_stats(h1[...])
    normed[...] = (xhat * norms[2:3, :] + norms[3:4, :]).astype(BF)
    grad_low[...] = grad_two.astype(BF)
    grad_one = grad_two + feed_back(
        grad_low, normed, xhat, rstd, norms[2:3, :], act_one, slope_one, up_one, down_one,
        acc_up, acc_down, dhid, dnorm_one, dout_one, work,
    )

    g1[...] = grad_one

    @pl.when(step == pl.num_programs(0) - 1)
    def _():
        at = flat_rows_of()
        write_flat(
            flat, stage, low,
            [(acc_up, at["w_up"]), (acc_down, at["w_down"]), (acc_qkv, at["w_qkv"]), (acc_so, at["w_so"])],
            sems, shard, extra,
        )


def cross_back_frame(
    grad_one, kvf, co, lse, rank_ref, count, episode_row, hot_column, latent, norms, w_q, w_o,
    acc_latent, acc_q, acc_o, acc_episode, dnorm, dout, dkv_t, pause=lambda: None,
):
    cap = kvf.shape[0]
    start = latent[...].astype(F32) + episode_row
    xhat, rstd = norm_stats(start)
    query_in = (xhat * norms[0:1, :] + norms[1:2, :]).astype(BF)
    queries = mm(query_in, w_q[...]).astype(BF) * jnp.asarray(0.125, BF)
    branch = grad_one.astype(BF)
    grad_co = mm_t(branch, w_o[...]).astype(BF)
    acc_o[...] += t_mm(co, branch)
    dout[...] += col_sum(branch.astype(F32))
    scores = cross_scores(kvf, queries, count)
    prob = jnp.exp(scores - lse)
    weighted = prob * mm_t(kvf, grad_co)
    grad_score = (weighted - prob * col_sum(weighted)).astype(BF)
    grad_kv = (mm(grad_score, queries) + mm(prob.astype(BF), grad_co)).astype(BF)
    grad_query = (t_mm(kvf, grad_score).T * 0.125).astype(BF)
    pause()
    acc_q[...] += t_mm(query_in, grad_query)
    grad_in = mm_t(grad_query, w_q[...])
    grad_start = grad_one + norm_back(grad_in, xhat, rstd, norms[0:1, :])
    dnorm[...] += jnp.concatenate([col_sum(grad_in * xhat), col_sum(grad_in)], axis=0)
    acc_latent[...] += grad_start
    acc_episode[...] += hot_column * col_sum(grad_start)
    grad_kv_t = grad_kv.T
    chunk = 8 * LANES

    def scatter(j, carry):
        sel = select_tokens(rank_ref[pl.ds(pl.multiple_of(j * 8, 8), 8), :], cap)
        at = pl.ds(pl.multiple_of(j * chunk, chunk), chunk)
        dkv_t[:, at] = added(dkv_t[:, at], mm(grad_kv_t, sel))
        return carry

    lax.fori_loop(0, dkv_t.shape[1] // chunk, scatter, 0)


def write_small(put, stage, low, latent_low, acc_latent, acc_q, acc_o, acc_episode, norm_grads, hid_grads, out_grads):
    at = flat_rows_of()
    flatten(acc_latent, stage, latent_low, 0)
    put(latent_low.at[0], 0)
    head = at["lat_norms"] - at["episode"]
    used = EPISODES * (D // LANES)
    rows = [to_flat(stage, acc_episode[...])[0:used, :], jnp.zeros((head - used, LANES), F32)]
    rows = jnp.concatenate(rows + [to_flat(stage, norm_grads)], axis=0)
    top = rows.shape[0]
    low[0, 0:top, :] = rows.astype(BF)
    put(low.at[0, pl.ds(0, top), :], at["episode"])
    stage[0:D, :] = acc_q[...]
    even = stage[pl.ds(0, D // 2, stride=2), :]
    odd = pltpu.roll(stage[pl.ds(1, D // 2, stride=2), :], CH, 1)
    low[0, top : top + D // 2, :] = jnp.where(lane_half(even.shape, 0), even, odd).astype(BF)
    both = D // 2 + CH * D // LANES
    low[0, top + D // 2 : top + both, :] = to_flat(stage, acc_o[CH : 2 * CH, :]).astype(BF)
    put(low.at[0, pl.ds(top, both), :], at["w_q"])
    hid = to_flat(stage, hid_grads)
    last = top + both
    low[0, last : last + hid.shape[0], :] = hid.astype(BF)
    end = hid.shape[0] + 4 * D // LANES
    low[0, last + hid.shape[0] : last + end, :] = to_flat(stage, out_grads).astype(BF)
    put(low.at[0, pl.ds(last, end), :], at["hid_bias"])


def cross_accumulators(total_keys):
    shapes = [(LAT, D), (D, LANES), (LANES, D), (16, D), (2, D), (1, D)]
    return [pltpu.VMEM(shape, F32) for shape in shapes] + [pltpu.VMEM((LANES, total_keys), BF)]


def small_buffers():
    return [pltpu.VMEM((2048, LANES), F32), pltpu.VMEM((1, 640, LANES), BF), pltpu.VMEM((1, 2048, LANES), BF)]


def stacked(*parts):
    return jnp.concatenate([part[...] for part in parts], axis=0)


def cross_bwd_kernel(
    kv_rows, g1, kvf, co, lse, rank, count, episode, hot, latent, norms, w_q, w_o,
    dnorm_one, dnorm_sa, dnorm_two, dhid_one, dhid_two, dout_one, dout_so, dout_two, flat_in, flat,
    acc_latent, acc_q, acc_o, acc_episode, dnorm, dout, dkv_t, stage, low, latent_low, kv_low, sems,
):
    step = pl.program_id(0)
    accs = (acc_latent, acc_q, acc_o, acc_episode, dnorm, dout, dkv_t)
    clear(step == 0, accs)
    cross_back_frame(
        g1[...], kvf[0], co[...], lse[0], rank.at[0], count[0, 0:1, 0:1], episode[0], hot[0, :, 0:1],
        latent, norms, w_q, w_o, *accs,
    )

    @pl.when(step == pl.num_programs(0) - 1)
    def _():
        copies = []

        def put(source, row):
            copies.append(
                pltpu.make_async_copy(source, flat.at[pl.ds(row, source.shape[0]), :], sems.at[len(copies)])
            )
            copies[-1].start()

        write_small(
            put, stage, low, latent_low, acc_latent, acc_q, acc_o, acc_episode,
            stacked(dnorm, dnorm_one, dnorm_sa, dnorm_two), stacked(dhid_one, dhid_two),
            stacked(dout, dout_one, dout_so, dout_two),
        )
        for copy in copies:
            copy.wait()
        tokens = kv_rows[1]
        for j in range(dkv_t.shape[1] // tokens):
            kv_low[...] = dkv_t[:, j * tokens : (j + 1) * tokens].T
            copy = pltpu.make_async_copy(kv_low, flat.at[pl.ds(kv_rows[0] + j * tokens, tokens), :], sems.at[0])
            copy.start()
            copy.wait()


def fixed(*shape):
    return pl.BlockSpec(shape, lambda i: (0,) * len(shape), pipeline_mode=pl.Buffered(1))


def kept(*shape):
    return pl.BlockSpec(shape, lambda i: (0,) * len(shape))


def rowed(rows, cols):
    return pl.BlockSpec((rows, cols), lambda i: (i, 0))


def framed(*shape):
    return pl.BlockSpec((1,) + shape, lambda i: (i,) + (0,) * len(shape))


def shaped(shape, dtype=F32):
    return jax.ShapeDtypeStruct(shape, dtype)


def call(kernel, grid, in_specs, outs, args, flops=0, trans=0, scratch=(), limit=56, aliases=None, collective=None):
    out_specs, out_shapes = zip(*outs)
    moved = sum(math.prod(a.shape) * a.dtype.itemsize for a in args)
    moved += sum(math.prod(s.shape) * s.dtype.itemsize for s in out_shapes)
    return pl.pallas_call(
        kernel,
        grid=(grid,),
        in_specs=in_specs,
        out_specs=list(out_specs),
        out_shape=list(out_shapes),
        scratch_shapes=list(scratch),
        input_output_aliases=aliases or {},
        compiler_params=pltpu.CompilerParams(
            dimension_semantics=("arbitrary",),
            vmem_limit_bytes=limit * MIB,
            collective_id=collective,
            has_side_effects=collective is not None,
        ),
        cost_estimate=pl.CostEstimate(flops=flops, bytes_accessed=moved, transcendentals=trans),
    )(*args)


def reduce_all(flat, shard, bias_owner, bias_row, tokens, tok_normed, w_kv, tok_norm, g1, cross):
    vmem = pl.BlockSpec(memory_space=pltpu.VMEM)
    anywhere = pl.BlockSpec(memory_space=pl.ANY)
    dma = pltpu.SemaphoreType.DMA
    first = [
        pltpu.VMEM((8, STAT_ROWS, LANES), F32), dma((7,)), dma((7,)), pltpu.VMEM((16, LANES), BF),
        pltpu.VMEM((DIN, LANES), BF), dma((2,)), pltpu.VMEM(g1.shape, F32), dma((g1.shape[0],)),
        pltpu.VMEM((8, tokens.shape[0], LANES), BF), dma((16,)),
    ]
    grads = flat.reshape(2, 2, 2, -1, LANES)
    return pl.pallas_call(
        functools.partial(reduce_kernel, shard, bias_owner, bias_row),
        out_shape=[
            shaped((shard, LANES), BF), shaped((STAT_ROWS, LANES)), shaped(tokens.shape, BF),
            shaped(grads.shape, BF),
        ],
        in_specs=[anywhere] + [vmem] * 4 + [anywhere] + [vmem] * len(cross),
        out_specs=[vmem, vmem, vmem, anywhere],
        scratch_shapes=first
        + cross_accumulators(8 * tokens.shape[0])
        + small_buffers()
        + Reduction.scratch(shard),
        input_output_aliases={0: 3},
        compiler_params=pltpu.CompilerParams(
            collective_id=1, has_side_effects=True, vmem_limit_bytes=56 * MIB
        ),
    )(grads, tokens, tok_normed, w_kv, tok_norm, g1, *cross)


def body(tokens, frame_ids, episodes, master, moment_one, moment_two, latent_grad):
    lat_count = lax.axis_size("lat")
    lat_index = lax.axis_index("lat")
    shard_len = master.shape[0]
    frame_total = episodes.shape[1]
    frames = frame_total // lat_count
    rows_total = frames * LAT
    total_keys = frame_ids.shape[1] * lat_count
    cap = total_keys // 8
    token_rows_count = total_keys // LANES

    reach = lat_count == 8 and lax.axis_size("kf") == 4
    shard_rows = shard_len // LANES
    master_rows = master.reshape(shard_rows, LANES)
    score_flops = rows_total * cap * LANES * 2
    select_flops = frames * cap * total_keys * LANES * 2
    if reach:
        (
            up_one, down_one, w_qkv, w_so, up_two, down_two,
            latent, norms, hid_bias, out_bias, w_q, w_o, w_kv, tok_norm, tok_normed, episode_rows, rank, counts,
            kvf, cross_out, cross_lse, hot_lanes, h1,
        ) = begin_all(master_rows, tokens[0], frame_ids.reshape(-1, LANES), episodes, frames, cap)
    else:
        own_episodes = lax.dynamic_slice_in_dim(episodes[0], lat_index * frames, frames, 0)
        episode_match = own_episodes[:, None] == jnp.arange(EPISODES, dtype=jnp.int32)[None, :]
        hot_lanes = jnp.broadcast_to(
            jnp.pad(episode_match.astype(F32), ((0, 0), (0, 16 - EPISODES)))[:, :, None], (frames, 16, LANES)
        )
        weights = split_flat(lax.all_gather(master.astype(BF), "lat", axis=0, tiled=True))
        norms = weights["lat_norms"].astype(F32)
        out_bias = weights["out_bias"].astype(F32)
        hid_bias = weights["hid_bias"].astype(F32)
        tok_norm = weights["tok_norm"].astype(F32)
        w_kv, w_qkv, w_so, latent = (weights[name] for name in ("w_kv", "w_qkv", "w_so", "latent"))
        up_one, up_two = weights["w_up"]
        down_one, down_two = weights["w_down"]
        frame_tag = lax.all_gather(frame_ids[0].astype(BF), "lat", axis=0, tiled=True).astype(jnp.int32)
        own_frames = lat_index * frames + jnp.arange(frames, dtype=jnp.int32)
        own_hit = frame_tag[None, :] == own_frames[:, None]
        rank = jnp.cumsum(own_hit.astype(jnp.int32), axis=1) - 1
        counts = jnp.broadcast_to(rank[:, -1][:, None, None] + 1, (frames, 8, LANES))
        rank = jnp.where(own_hit, rank, -1).reshape(frames, token_rows_count, LANES)
        tok_normed = layer_norm(tokens[0].astype(F32), tok_norm[0], tok_norm[1]).astype(BF)
        key_value = mm(tok_normed, w_kv).astype(BF)
        all_keys = lax.all_gather(key_value, "lat", axis=0, tiled=True)
        episode_rows = mm(episode_match.astype(BF), weights["episode"]).reshape(frames, 1, D)
        w_q = jnp.pad(weights["w_q"], ((0, 0), (0, LANES - CH)))
        w_o = jnp.pad(weights["w_o"], ((LANES - CH, 0), (0, 0)))
        h1, kvf, cross_out, cross_lse = call(
            cross_fwd_kernel,
            frames,
            [
                fixed(LAT, D), framed(1, D), fixed(8, D), fixed(D, LANES), fixed(LANES, D), fixed(4, D),
                fixed(total_keys, LANES), framed(token_rows_count, LANES), framed(8, LANES),
            ],
            [
                (rowed(LAT, D), shaped((rows_total, D))),
                (framed(cap, LANES), shaped((frames, cap, LANES), BF)),
                (rowed(LAT, LANES), shaped((rows_total, LANES), BF)),
                (framed(1, LAT), shaped((frames, 1, LAT))),
            ],
            (latent, episode_rows, norms, w_q, w_o, out_bias, all_keys, rank, counts),
            flops=2 * score_flops + select_flops,
            trans=rows_total * cap,
        )
    mlp_flops = 4 * rows_total * D * FF
    attn_flops = 4 * rows_total * LAT * D
    anywhere = pl.BlockSpec(memory_space=pl.ANY)
    token_count = frame_ids.shape[1]
    if reach:
        flat_shard, extra = shard_rows, token_count
        flat_shape = (lat_count * (shard_rows + extra), LANES)
        kv_rows = (shard_rows, token_count, shard_rows + extra)
        grad_in, grad_spec = latent_grad[0], anywhere
        latents_spec = (anywhere, shaped(latent_grad.shape[1:], BF))
        shared = [pltpu.VMEM((frames, LAT, D), BF)] * 2 + FrameExchange.scratch(frames)
    else:
        flat_shard, extra = NPARAM // LANES, 0
        flat_shape = (flat_shard + total_keys, LANES)
        kv_rows = (flat_shard, 512, 512)
        grad_in = lax.all_to_all(
            latent_grad[0], "lat", split_axis=0, concat_axis=1, tiled=True
        ).reshape(rows_total, D)
        grad_spec = rowed(LAT, D)
        latents_spec = (rowed(LAT, D), shaped((rows_total, D), BF))
        shared = []
    slab = D * FF // LANES
    h2, qkv, self_lse, mixed, act_one, slope_one, latents, g3, dhid_two, dnorm_two, dout_two, flat = call(
        functools.partial(forward_kernel, reach, flat_shard, extra),
        frames,
        [
            rowed(LAT, D), grad_spec, fixed(8, D), fixed(2, FF), fixed(4, D), fixed(D, FF), fixed(FF, D),
        ]
        + [anywhere] * 4,
        [
            (rowed(LAT, D), shaped((rows_total, D))),
            (rowed(LAT, 3 * D), shaped((rows_total, 3 * D), BF)),
            (framed(HEADS, LAT), shaped((frames, HEADS, LAT))),
            (rowed(LAT, D), shaped((rows_total, D), BF)),
            (rowed(LAT, FF), shaped((rows_total, FF), BF)),
            (rowed(LAT, FF), shaped((rows_total, FF), BF)),
            latents_spec,
            (rowed(LAT, D), shaped((rows_total, D))),
            (kept(1, FF), shaped((1, FF))),
            (kept(2, D), shaped((2, D))),
            (kept(1, D), shaped((1, D))),
            (anywhere, shaped(flat_shape, BF)),
        ],
        (h1, grad_in, norms, hid_bias, out_bias, up_one, down_one, w_qkv, w_so, up_two, down_two),
        flops=4 * mlp_flops + 4 * attn_flops,
        trans=4 * rows_total * FF,
        scratch=[
            pltpu.VMEM((LAT, FF), BF), pltpu.VMEM((LAT, FF), BF), pltpu.VMEM((D, FF), F32), pltpu.VMEM((FF, D), F32),
            pltpu.VMEM((2048, LANES), F32), pltpu.VMEM((2, slab, LANES), BF), pltpu.VMEM((LAT, D), BF),
            pltpu.VMEM((D, LAT), F32), pltpu.VMEM((LAT, D), F32), pltpu.SemaphoreType.DMA((2, 16)),
            pltpu.VMEM((D, 3 * D), BF), pltpu.VMEM((D, D), BF), pltpu.VMEM((D, FF), BF), pltpu.VMEM((FF, D), BF),
            pltpu.SemaphoreType.DMA((4,)),
        ]
        + shared,
        limit=62,
        collective=4 if reach else None,
    )
    if reach:
        latents_out = latents[None]
    else:
        latents_out = lax.all_to_all(
            latents.reshape(frames, LAT, D), "lat", split_axis=1, concat_axis=0, tiled=True
        )[None]
    g1, dhid_one, dnorm_sa, dnorm_one, dout_so, dout_one, flat = call(
        functools.partial(backward_kernel, flat_shard, extra),
        frames,
        [
            rowed(LAT, 3 * D), framed(HEADS, LAT), rowed(LAT, D), rowed(LAT, D), rowed(LAT, D), rowed(LAT, D),
            rowed(LAT, FF), rowed(LAT, FF), fixed(8, D), fixed(D, D),
        ]
        + [anywhere] * 4,
        [
            (rowed(LAT, D), shaped((rows_total, D))),
            (kept(1, FF), shaped((1, FF))),
            (kept(2, D), shaped((2, D))),
            (kept(2, D), shaped((2, D))),
            (kept(1, D), shaped((1, D))),
            (kept(1, D), shaped((1, D))),
            (anywhere, shaped(flat_shape, BF)),
        ],
        (
            qkv, self_lse, mixed, g3, h2, h1, act_one, slope_one, norms, w_so, w_qkv, up_one, down_one, flat,
        ),
        flops=2 * mlp_flops + 10 * attn_flops,
        trans=rows_total * LAT * HEADS,
        scratch=[
            pltpu.VMEM((LAT, 3 * D), BF), pltpu.VMEM((D, FF), F32), pltpu.VMEM((FF, D), F32),
            pltpu.VMEM((D, 3 * D), F32), pltpu.VMEM((D, D), F32),
            pltpu.VMEM((2048, LANES), F32), pltpu.VMEM((2, slab, LANES), BF), pltpu.VMEM((LAT, D), BF),
            pltpu.VMEM((LAT, D), BF), pltpu.VMEM((LAT, D), BF), pltpu.VMEM((LAT, D), F32),
            pltpu.SemaphoreType.DMA((2, 16)),
            pltpu.VMEM((D, 3 * D), BF), pltpu.VMEM((D, FF), BF), pltpu.VMEM((FF, D), BF),
            pltpu.SemaphoreType.DMA((3,)),
        ],
        limit=60,
        aliases={13: 6},
    )
    cross = (
        kvf, cross_out, cross_lse, rank, counts, episode_rows, hot_lanes, latent, norms, w_q, w_o,
        dnorm_one, dnorm_sa, dnorm_two, dhid_one, dhid_two, dout_one, dout_so, dout_two,
    )
    layout = param_layout()
    starts, ends, offset, bias_offset = [], [], 0, 0
    for name, shape in layout:
        if name == "hid_bias":
            bias_offset = offset
        starts.append(offset // LANES)
        offset += math.prod(shape)
        ends.append(offset // LANES)
    pad = [0] * (16 - len(layout))
    starts, ends = (np.tile(np.array(v + pad, np.int32)[:, None], (1, LANES)) for v in (starts, ends))
    opt_rows = shard_rows // 2 if shard_rows % 16 == 0 else shard_rows
    opt_steps = shard_rows // opt_rows
    base = (lat_index * shard_rows).astype(jnp.int32).reshape(1)
    smem = pl.BlockSpec(memory_space=pltpu.SMEM)
    flat_rows = (shard_rows, LANES)
    bias_owner, bias_at = divmod(bias_offset, shard_len)
    if reach:
        summed, stats, token_grad, unused = reduce_all(
            flat, shard_rows, bias_owner, bias_at // LANES, tokens[0], tok_normed, w_kv, tok_norm,
            g1.reshape(frames, LAT, D), cross,
        )
    else:
        (flat,) = call(
            functools.partial(cross_bwd_kernel, kv_rows),
            frames,
            [
                rowed(LAT, D), framed(cap, LANES), rowed(LAT, LANES), framed(1, LAT), framed(token_rows_count, LANES),
                framed(8, LANES), framed(1, D), framed(16, LANES), fixed(LAT, D), fixed(8, D), fixed(D, LANES),
                fixed(LANES, D),
            ]
            + [fixed(*part.shape) for part in cross[11:]]
            + [anywhere],
            [(anywhere, shaped(flat_shape, BF))],
            (g1,) + cross + (flat,),
            flops=6 * score_flops,
            trans=rows_total * cap,
            scratch=cross_accumulators(total_keys)
            + small_buffers()
            + [pltpu.VMEM((kv_rows[1], LANES), BF), pltpu.SemaphoreType.DMA((8,))],
            aliases={20: 0},
        )
        grad_kv = lax.psum_scatter(flat[flat_shard:], "lat", scatter_dimension=0, tiled=True)
        flat = flat[:flat_shard]
        grad_w_kv = t_mm(tok_normed, grad_kv)
        grad_tok_normed = mm_t(grad_kv, w_kv)
        unused, token_pull = jax.vjp(layer_norm, tokens[0].astype(F32), tok_norm[0], tok_norm[1])
        grad_tokens, grad_tok_gain, grad_tok_bias = token_pull(grad_tok_normed)
        token_grad = grad_tokens.astype(BF)
        flat_at = flat_rows_of()
        tok_norm_grad = jnp.stack([grad_tok_gain, grad_tok_bias]).reshape(-1, LANES).astype(BF)
        flat = lax.dynamic_update_slice(flat, tok_norm_grad, (flat_at["tok_norm"], 0))
        flat = lax.dynamic_update_slice(flat, grad_w_kv.astype(BF), (flat_at["w_kv"], 0))
        local_flat = flat.reshape(-1)
        summed = lax.psum_scatter(local_flat, "lat", scatter_dimension=0, tiled=True)
        summed = lax.psum(summed, "kf").reshape(flat_rows)
        bias_rows = summed[bias_at // LANES : bias_at // LANES + 2 * FF // LANES].astype(F32)
        bias_rows = jnp.where(lat_index == bias_owner, bias_rows, 0.0)
        grad_sq = jnp.sum(jnp.square(summed.astype(F32)), axis=0, keepdims=True)
        stats = lax.psum(jnp.concatenate([grad_sq, jnp.zeros((7, LANES), F32), bias_rows]), "lat")
    grad_shard, lamb_update, new_one, new_two, norms_sq, bias_grad = call(
        lamb_kernel,
        opt_steps,
        [smem, fixed(STAT_ROWS, LANES), fixed(16, LANES), fixed(16, LANES)] + [rowed(opt_rows, LANES)] * 4,
        [(rowed(opt_rows, LANES), shaped(flat_rows))] * 4
        + [(kept(16, 2 * LANES), shaped((16, 2 * LANES))), (kept(2, FF), shaped((2, FF)))],
        (
            base, stats, starts, ends, summed, master_rows,
            moment_one.reshape(flat_rows), moment_two.reshape(flat_rows),
        ),
    )
    if reach:
        vmem = pl.BlockSpec(memory_space=pltpu.VMEM)
        trust = pl.pallas_call(
            trust_kernel,
            out_shape=shaped((1, len(layout))),
            in_specs=[vmem],
            out_specs=vmem,
            scratch_shapes=[
                pltpu.VMEM((8, 16, 2 * LANES), F32),
                pltpu.SemaphoreType.DMA((7,)),
                pltpu.SemaphoreType.DMA((7,)),
            ],
            compiler_params=pltpu.CompilerParams(collective_id=2, has_side_effects=True),
        )(norms_sq).reshape(-1)
    else:
        sums = lax.psum(jnp.sum(norms_sq.reshape(16, 2, LANES), axis=2), "lat")[: len(layout)]
        trust = jnp.sqrt(sums[:, 1]) / (jnp.sqrt(sums[:, 0]) + 1e-06)
    return (
        latents_out,
        token_grad[None],
        grad_shard.reshape(-1),
        lamb_update.reshape(-1),
        new_one.reshape(-1),
        new_two.reshape(-1),
        trust,
        bias_grad,
    )


def solution(mesh):
    return jax.shard_map(
        body,
        mesh=mesh,
        in_specs=(
            P("kf", "lat", None),
            P("kf", "lat"),
            P("kf", None),
            P("lat"),
            P("lat"),
            P("lat"),
            P("kf", None, "lat", None),
        ),
        out_specs=(
            P("kf", None, "lat", None),
            P("kf", "lat", None),
            P("lat"),
            P("lat"),
            P("lat"),
            P("lat"),
            P(),
            P(),
        ),
        check_vma=False,
    )
```

```python
import functools
import math

import jax
import jax.numpy as jnp
import numpy as np
from jax import lax
from jax.experimental import pallas as pl
from jax.experimental.pallas import tpu as pltpu
from jax.sharding import PartitionSpec as P

DIN = 256
D = 512
LAT = 512
CH = 64
HEADS = 8
HEAD_DIM = 64
FF = 2048
FRAMES = 32
EPISODES = 11
NPARAM = 5619712
LANES = 128

norm_eps = 1e-05
masked_fill = -1e30
beta_one = 0.9
beta_two = 0.999
adam_eps = 1e-06
decay_rate = 0.01
clip_fraction = 0.5
lamb_step = 10.0

BF = jnp.bfloat16
F32 = jnp.float32
MIB = 1024 * 1024


def param_layout():
    return [
        ("latent", (LAT, D)),
        ("episode", (EPISODES, D)),
        ("tok_norm", (2, DIN)),
        ("lat_norms", (8, D)),
        ("w_kv", (DIN, 2 * CH)),
        ("w_q", (D, CH)),
        ("w_o", (CH, D)),
        ("w_qkv", (D, 3 * D)),
        ("w_so", (D, D)),
        ("w_up", (2, D, FF)),
        ("w_down", (2, FF, D)),
        ("hid_bias", (2, FF)),
        ("out_bias", (4, D)),
    ]


def split_flat(flat_vector):
    pieces = {}
    offset = 0
    for tensor_name, tensor_shape in param_layout():
        entries = math.prod(tensor_shape)
        pieces[tensor_name] = flat_vector[offset : offset + entries].reshape(tensor_shape)
        offset += entries
    return pieces


def layer_norm(inputs, norm_gain, norm_bias):
    row_mean = jnp.mean(inputs, axis=-1, keepdims=True)
    centered = inputs - row_mean
    row_var = jnp.mean(centered * centered, axis=-1, keepdims=True)
    return centered * lax.rsqrt(row_var + norm_eps) * norm_gain + norm_bias


def mm(left, right):
    return jnp.dot(left, right, preferred_element_type=F32)


def mm_t(left, right):
    return lax.dot_general(left, right, (((1,), (1,)), ((), ())), preferred_element_type=F32)


def t_mm(left, right):
    return lax.dot_general(left, right, (((0,), (0,)), ((), ())), preferred_element_type=F32)


def norm_stats(rows):
    mean = jnp.mean(rows, axis=-1, keepdims=True)
    centered = rows - mean
    var = jnp.mean(centered * centered, axis=-1, keepdims=True)
    rstd = lax.rsqrt(var + norm_eps)
    return centered * rstd, rstd


def norm_back(grad, xhat, rstd, gain):
    dxh = grad * gain
    first = jnp.mean(dxh, axis=-1, keepdims=True)
    second = jnp.mean(dxh * xhat, axis=-1, keepdims=True)
    return rstd * (dxh - first - xhat * second)


def col_sum(values):
    return jnp.sum(values, axis=0, keepdims=True)


def gelu_pair(x):
    cdf = 0.5 + 0.5 * lax.erf(x * (1.0 / math.sqrt(2.0)))
    density = jnp.exp(x * x * -0.5) * (1.0 / math.sqrt(2.0 * math.pi))
    return x * cdf, cdf + x * density


def accumulate(first, ref, value):
    @pl.when(first)
    def _():
        ref[...] = value

    @pl.when(jnp.logical_not(first))
    def _():
        ref[...] += value


def lane_half(shape, half):
    lane = lax.broadcasted_iota(jnp.int32, shape, 1)
    return (lane >= half * HEAD_DIM) & (lane < (half + 1) * HEAD_DIM)


def keep_half(values, half):
    return jnp.where(lane_half(values.shape, half), values, jnp.zeros_like(values))


def by_head(values):
    return jnp.concatenate([keep_half(values, h) for h in range(values.shape[1] // HEAD_DIM)], axis=0)


def select_tokens(rank_rows, cap):
    slot = lax.broadcasted_iota(jnp.int32, (cap, LANES), 0)
    parts = []
    for r in range(rank_rows.shape[0]):
        hit = slot == rank_rows[r : r + 1, :]
        parts.append(jnp.where(hit, 1.0, 0.0).astype(BF))
    return jnp.concatenate(parts, axis=1)


def cross_scores(kvf, queries_scaled, count):
    scores = mm_t(kvf, queries_scaled)
    slot = lax.broadcasted_iota(jnp.int32, scores.shape, 0)
    return jnp.where(slot < count, scores, masked_fill)


def cross_attend(start, norms, w_q, kvf, count):
    xhat, unused = norm_stats(start)
    query_in = (xhat * norms[0:1, :] + norms[1:2, :]).astype(BF)
    queries = mm(query_in, w_q[...]).astype(BF) * jnp.asarray(0.125, BF)
    scores = cross_scores(kvf, queries, count)
    top = jnp.max(scores, axis=0, keepdims=True)
    terms = jnp.exp(scores - top)
    total = jnp.sum(terms, axis=0, keepdims=True)
    prob = (terms * (1.0 / total)).astype(BF)
    return t_mm(kvf, prob).T.astype(BF), top + jnp.log(total)


def cross_fwd_kernel(latent, episode, norms, w_q, w_o, out_bias, kv, rank, count, h1, kvf_out, co_out, lse_out):
    cap = kvf_out.shape[1]
    start = latent[...].astype(F32) + episode[0]
    chunk = 8 * LANES
    chunks = kv.shape[0] // chunk

    def step(j, acc):
        sel = select_tokens(rank[0, pl.ds(pl.multiple_of(j * 8, 8), 8), :], cap)
        return acc + mm(sel, kv[pl.ds(pl.multiple_of(j * chunk, chunk), chunk), :])

    kvf = lax.fori_loop(0, chunks, step, jnp.zeros((cap, LANES), F32)).astype(BF)
    co, lse = cross_attend(start, norms, w_q, kvf, count[0, 0:1, 0:1])
    h1[...] = start + mm(co, w_o[...]) + out_bias[0:1, :]
    kvf_out[0] = kvf
    co_out[...] = co
    lse_out[0] = lse


def segment_hot(starts, ends, base, rows):
    row = lax.broadcasted_iota(jnp.int32, (16, rows), 1) + base
    return jnp.where((row >= starts[:, 0:1]) & (row < ends[:, 0:1]), 1.0, 0.0).astype(BF)


def segment_sums(hot, squares):
    high = squares.astype(BF)
    low = (squares - high.astype(F32)).astype(BF)
    return mm(hot, high) + mm(hot, low)


def lamb_kernel(
    base, stats, starts, ends, summed, master, one, two, token_in,
    grad_out, update_out, one_out, two_out, norms_sq, bias, token_out,
):
    i = pl.program_id(0)
    token_out[...] = token_in[...]
    rows = master.shape[0]
    hot = segment_hot(starts, ends, base[0] + i * rows, rows)
    total_sq = jnp.sum(stats[0:1, :], axis=1, keepdims=True)
    clip = jnp.minimum(1.0, clip_fraction * math.sqrt(NPARAM) / (jnp.sqrt(total_sq) + 1e-06))
    grad = summed[...].astype(F32)
    grad_out[...] = grad
    clipped = clip * grad
    new_one = beta_one * one[...] + (1.0 - beta_one) * clipped
    new_two = beta_two * two[...] + (1.0 - beta_two) * clipped * clipped
    one_out[...] = new_one
    two_out[...] = new_two
    first_hat = new_one * (1.0 / (1.0 - beta_one**lamb_step))
    second_hat = new_two * (1.0 / (1.0 - beta_two**lamb_step))
    update = first_hat / (jnp.sqrt(second_hat) + adam_eps) + decay_rate * master[...]
    update_out[...] = update
    accumulate(i == 0, norms_sq, segment_sums(hot, jnp.concatenate([update * update, master[...] * master[...]], axis=1)))
    for j in range(2 * FF // LANES):
        r, c = divmod(j, FF // LANES)
        bias[r : r + 1, c * LANES : (c + 1) * LANES] = stats[8 + j : 9 + j, :]


BATCH = 256
HALF = 128
QUARTER = 64
MESH = pl.DeviceIdType.MESH


class Place:
    def __init__(self):
        self.z = lax.axis_index("kf")
        self.me = lax.axis_index("lat")
        self.core = lax.rem(self.me, 2)
        self.x = lax.rem(self.me // 2, 2)
        self.y = self.me // 4
        self.z_low = lax.rem(self.z, 2)
        self.z_high = self.z // 2
        self.sibling = (self.z, self.me + 1 - 2 * self.core)
        self.x_side = (self.z, self.me + 2 - 4 * self.x)
        self.y_side = (self.z, self.me + 4 - 8 * self.y)
        self.z_near = (self.z + 1 - 2 * self.z_low, self.me)
        self.z_far = (self.z + 2 - 4 * self.z_high, self.me)

    def z_other(self, step):
        return (lax.rem(self.z + step, 4), self.me)

    def lat_other(self, step):
        return (self.z, lax.rem(self.me + step, 8))


def remote(src, dst, send, recv, device):
    return pltpu.make_async_remote_copy(
        src_ref=src, dst_ref=dst, send_sem=send, recv_sem=recv, device_id=device, device_id_type=MESH
    )


def greet(devices):
    barrier = pltpu.get_barrier_semaphore()
    for device in devices:
        pl.semaphore_signal(barrier, inc=1, device_id=device, device_id_type=MESH)


def met(devices):
    pl.semaphore_wait(pltpu.get_barrier_semaphore(), len(devices))


def added(left, right):
    return (left.astype(F32) + right.astype(F32)).astype(BF)


class Reduction:
    lags = (0, 1, 3, 5, 7, 9, 11)
    plane = 2

    def __init__(self, place, shard, grads, out, bufs, sems):
        self.p = place
        self.grads = grads
        self.out = out
        self.own, self.rc, self.r1, self.r2, self.r3, self.r4, self.res = bufs
        self.own_sem, self.send, self.rc_sem, self.r1_sem, self.r2_sem, self.r3_sem, self.r4_sem, self.res_sem = sems
        self.shard = shard
        self.full = pl.cdiv(shard, BATCH)
        self.batches = self.full + self.plane
        self.back = self.full * BATCH - shard
        self.held = flat_rows_of()["tok_norm"] // BATCH
        self.early = self.full - 1 - (self.held + 4)

    @staticmethod
    def scratch(shard):
        n = pl.cdiv(shard, BATCH) + Reduction.plane
        bufs = [
            pltpu.VMEM((2, 2, 2, BATCH, LANES), BF),
            pltpu.VMEM((n, 2, 2, BATCH, LANES), BF),
            pltpu.VMEM((n, 2, 2, HALF, LANES), BF),
            pltpu.VMEM((n, 2, HALF, LANES), BF),
            pltpu.VMEM((n, HALF, LANES), BF),
            pltpu.VMEM((n, QUARTER, LANES), BF),
            pltpu.VMEM((n, BATCH, LANES), BF),
        ]
        dma = pltpu.SemaphoreType.DMA
        sems = [dma((2,)), dma((10, 4)), dma((n,)), dma((n, 2)), dma((n, 2)), dma((n,)), dma((n,)), dma((n, 3))]
        return bufs + sems

    def from_on(self, i, first):
        return (i + 64 - first) // 64

    def row(self, i):
        n, held = self.full, self.held
        on = functools.partial(self.from_on, i)
        keys = on(self.early) - on(self.early + 2)
        shift = held + 4 + on(self.early + 2) * (-2) + on(self.early + 3) * (-n)
        shift = shift + on(self.early + 3 + held) * 2 + on(self.early + 5 + held) * (-4)
        b = i + shift
        row = keys * (self.shard + (i - self.early) * BATCH)
        row = row + (1 - keys) * (b * BATCH - (b // (n - 1)) * self.back)
        return pl.multiple_of(row, 16)

    def is_keys(self, i):
        return (i >= self.early) & (i < self.early + self.plane)

    def own_copy(self, i):
        slot = lax.rem(i, 2)
        src = self.grads.at[:, :, self.p.core, pl.ds(self.row(i), BATCH), :]
        return pltpu.make_async_copy(src, self.own.at[slot], self.own_sem.at[slot])

    def copies(self, stage, i):
        p, slot = self.p, lax.rem(i, 4)
        if stage == 0:
            src = self.grads.at[:, :, 1 - p.core, pl.ds(self.row(i), BATCH), :]
            return [remote(src, self.rc.at[i], self.send.at[0, slot], self.rc_sem.at[i], p.sibling)]
        if stage == 1:
            to_x = self.rc.at[i, :, 1 - p.x, pl.ds(0, HALF), :]
            to_y = self.rc.at[i, 1 - p.y, :, pl.ds(HALF, HALF), :]
            return [
                remote(to_x, self.r1.at[i, 0], self.send.at[1, slot], self.r1_sem.at[i, 0], p.x_side),
                remote(to_y, self.r1.at[i, 1], self.send.at[2, slot], self.r1_sem.at[i, 1], p.y_side),
            ]
        if stage == 2:
            to_y = self.r1.at[i, 0, 1 - p.y]
            to_x = self.r1.at[i, 1, 1 - p.x]
            return [
                remote(to_y, self.r2.at[i, 0], self.send.at[3, slot], self.r2_sem.at[i, 0], p.y_side),
                remote(to_x, self.r2.at[i, 1], self.send.at[4, slot], self.r2_sem.at[i, 1], p.x_side),
            ]
        if stage == 3:
            src = self.r2.at[i, 1 - p.z_low]
            return [remote(src, self.r3.at[i], self.send.at[5, slot], self.r3_sem.at[i], p.z_near)]
        if stage == 4:
            src = self.r3.at[i, pl.ds(pl.multiple_of((1 - p.z_high) * QUARTER, QUARTER), QUARTER), :]
            return [remote(src, self.r4.at[i], self.send.at[6, slot], self.r4_sem.at[i], p.z_far)]
        mine = self.res.at[i, pl.ds(pl.multiple_of(p.z_low * HALF + p.z_high * QUARTER, QUARTER), QUARTER), :]
        return [
            remote(mine, mine, self.send.at[6 + d, slot], self.res_sem.at[i, d - 1], p.z_other(d))
            for d in (1, 2, 3)
        ]

    def launch(self, stage, i):
        before = i - 4
        if stage >= 3:
            before = before - 4 * (self.from_on(before, self.early) - self.from_on(before, self.early + self.plane))

        @pl.when(i >= 4)
        def _():
            for copy in self.copies(stage, before):
                copy.wait_send()

        for copy in self.copies(stage, i):
            copy.start()

    def landed(self, stage, i):
        for copy in self.copies(stage, i):
            copy.wait_recv()

    def work(self, stage, i):
        p = self.p
        if stage == 0:
            self.own_copy(i).start()
        elif stage == 1:
            self.landed(0, i)
            self.own_copy(i).wait()
            self.rc[i] = added(self.rc[i], self.own[lax.rem(i, 2)])
        elif stage == 2:
            self.landed(1, i)
            self.r1[i, 0] = added(self.r1[i, 0], self.rc[i, :, p.x, 0:HALF, :])
            self.r1[i, 1] = added(self.r1[i, 1], self.rc[i, p.y, :, HALF:BATCH, :])
        elif stage == 3:
            self.landed(2, i)
            self.r2[i, 0] = added(self.r2[i, 0], self.r1[i, 0, p.y])
            self.r2[i, 1] = added(self.r2[i, 1], self.r1[i, 1, p.x])
        elif stage == 4:
            self.landed(3, i)
            self.r3[i] = added(self.r3[i], self.r2[i, p.z_low])
        elif stage == 5:
            self.landed(4, i)
            part = self.r3[i, pl.ds(pl.multiple_of(p.z_high * QUARTER, QUARTER), QUARTER), :]
            at = pl.multiple_of(p.z_low * HALF + p.z_high * QUARTER, QUARTER)
            self.res[i, pl.ds(at, QUARTER), :] = added(self.r4[i], part)
        else:
            self.landed(5, i)
            self.out[pl.ds(self.row(i), BATCH), :] = self.res[i]
        if stage == 3:
            pl.when(jnp.logical_not(self.is_keys(i)))(lambda: self.launch(stage, i))
        elif stage < 6:
            self.launch(stage, i)

    def tick(self, t):
        for stage, lag in enumerate(self.lags):
            i = t - lag

            inside = (i >= 0) & (i < self.batches)

            @pl.when(inside if stage < 4 else inside & jnp.logical_not(self.is_keys(i)))
            def _(stage=stage, i=i):
                self.work(stage, i)

    def ticks(self):
        return self.batches + self.lags[-1]

    def finish(self):
        for stage in range(6):
            for back in range(4):
                for copy in self.copies(stage, self.batches - 4 + back):
                    copy.wait_send()

    def partners(self):
        p = self.p
        return [p.sibling, p.x_side, p.y_side] + [p.z_other(d) for d in (1, 2, 3)]


def share_all(place, block, send, recv):
    mine = block.at[place.me]
    copies = [
        remote(mine, mine, send.at[d - 1], recv.at[d - 1], place.lat_other(d)) for d in range(1, 8)
    ]
    for copy in copies:
        copy.start()
    for copy in copies:
        copy.wait()


STAT_ROWS = 40


def token_backward(grad_kv, tokens, tok_normed, w_kv, tok_norm, token_grad, kv_grad, edge):
    kv_grad[...] = t_mm(tok_normed[...], grad_kv).astype(BF)
    grad = mm_t(grad_kv, w_kv[...])
    xhat, rstd = norm_stats(tokens[...].astype(F32))
    token_grad[...] = norm_back(grad, xhat, rstd, tok_norm[0:1, :]).astype(BF)
    gain, bias = col_sum(grad * xhat), col_sum(grad)
    parts = [half[:, j * LANES : (j + 1) * LANES] for half in (gain, bias) for j in range(DIN // LANES)]
    keep = edge.shape[0] - len(parts)
    edge[...] = jnp.concatenate([edge[...].astype(F32)[0:keep, :]] + parts, axis=0).astype(BF)


def reduce_kernel(
    shard, bias_owner, bias_at, unused_flat, tokens, tok_normed, w_kv, tok_norm,
    g1, kvf, co, lse, rank, count, episode, hot, latent, norms, w_q, w_o,
    dnorm_one, dnorm_sa, dnorm_two, dhid_one, dhid_two, dout_one, dout_so, dout_two,
    summed, stats, token_grad, grads, *scratch,
):
    place = Place()
    block, block_send, block_recv, edge, kv_grad, edge_sem, g1_held, g1_sem, kv_low, kv_sem = scratch[:10]
    accs, (stage, low, latent_low), engine = scratch[10:17], scratch[17:20], scratch[20:]
    acc_latent, acc_q, acc_o, acc_episode, dnorm, dout, dkv_t = accs
    frames = kvf.shape[0]
    red = Reduction(place, shard, grads, summed, engine[:7], engine[7:])
    frame_copies = [pltpu.make_async_copy(g1.at[f], g1_held.at[f], g1_sem.at[f]) for f in range(frames)]
    for copy in frame_copies:
        copy.start()
    partners = [place.lat_other(d) for d in range(1, 8)] + [place.z_other(d) for d in (1, 2, 3)]
    greet(partners)
    for ref in accs:
        ref[...] = jnp.zeros_like(ref)
    met(partners)

    def run(first, last):
        lax.fori_loop(first, last, lambda t, c: (red.tick(t), c)[1], 0)

    def frame(f, carry):
        red.tick(2 * f)
        pltpu.make_async_copy(g1.at[f], g1_held.at[f], g1_sem.at[f]).wait()
        rows = pl.ds(pl.multiple_of(f * LAT, LAT), LAT)
        cross_back_frame(
            g1_held[f], kvf[f], co[rows, :], lse[f], rank.at[f], count[f, 0:1, 0:1], episode[f], hot[f, :, 0:1],
            latent, norms, w_q, w_o, *accs, pause=lambda: red.tick(2 * f + 1),
        )
        return carry

    lax.fori_loop(0, frames, frame, 0)
    run(2 * frames, red.early)
    at = flat_rows_of()
    copies = []

    def put(source, row):
        owner, local = row if isinstance(row, tuple) else divmod(row, shard)
        dst = grads.at[owner // 4, owner // 2 % 2, owner % 2, pl.ds(local, source.shape[0]), :]
        copies.append(pltpu.make_async_copy(source, dst, kv_sem.at[len(copies)]))
        copies[-1].start()

    write_small(
        put, stage, low, latent_low, acc_latent, acc_q, acc_o, acc_episode,
        stacked(dnorm, dnorm_one, dnorm_sa, dnorm_two), stacked(dhid_one, dhid_two),
        stacked(dout, dout_one, dout_so, dout_two),
    )
    edge_row = at["tok_norm"] // 16 * 16
    edge[...] = low[0, edge_row - at["episode"] : edge_row - at["episode"] + 16, :]
    count_kv = tokens.shape[0]
    for j in range(8):
        kv_low[j] = dkv_t[:, j * count_kv : (j + 1) * count_kv].T
        put(kv_low.at[j], (j, shard))
    for copy in copies:
        copy.wait()
    ready = red.early + red.lags[3] + red.plane
    run(red.early, ready)
    grad_kv = jnp.concatenate([red.r2[red.early + i, h] for i in range(red.plane) for h in range(2)], axis=0)
    token_backward(grad_kv, tokens, tok_normed, w_kv, tok_norm, token_grad, kv_grad, edge)
    writes = [
        pltpu.make_async_copy(edge, grads.at[0, 0, 0, pl.ds(edge_row, 16), :], edge_sem.at[0]),
        pltpu.make_async_copy(kv_grad, grads.at[0, 0, 0, pl.ds(at["w_kv"], DIN), :], edge_sem.at[1]),
    ]
    for copy in writes:
        copy.start()
    run(ready, ready + 2)
    for copy in writes:
        copy.wait()
    run(ready + 2, red.ticks())
    grad_sq = jnp.zeros((1, LANES), F32)
    step = 784
    for j in range(shard // step):
        part = summed[j * step : (j + 1) * step, :].astype(F32)
        grad_sq = grad_sq + col_sum(part * part)
    bias = summed[bias_at : bias_at + 2 * FF // LANES, :].astype(F32)
    bias = jnp.where(place.me == bias_owner, bias, 0.0)
    head = jnp.concatenate([grad_sq, jnp.zeros((7, LANES), F32), bias], axis=0)
    block[pl.ds(place.me, 1)] = head[None]
    share_all(place, block, block_send, block_recv)
    total = block[0]
    for s in range(1, 8):
        total = total + block[s]
    stats[...] = total
    red.finish()


def trust_kernel(norms_sq, trust, block, send, recv):
    place = Place()
    partners = [place.lat_other(d) for d in range(1, 8)]
    greet(partners)
    block[pl.ds(place.me, 1)] = norms_sq[...][None]
    met(partners)
    share_all(place, block, send, recv)
    total = block[0]
    for s in range(1, 8):
        total = total + block[s]
    update_sq = jnp.sum(total[:, 0:LANES].T, axis=0, keepdims=True)
    weight_sq = jnp.sum(total[:, LANES : 2 * LANES].T, axis=0, keepdims=True)
    ratio = jnp.sqrt(weight_sq) / (jnp.sqrt(update_sq) + 1e-06)
    trust[...] = ratio[:, 0 : trust.shape[1]]


def relayout(whole, row, stage, dst, rows, cols):
    wide = cols // LANES
    block = min(rows, 2048 // wide // 128 * 128)

    def step(i, carry):
        at = pl.multiple_of(row + i * (block * wide), 16)
        stage[0 : block * wide, :] = whole[pl.ds(at, block * wide), :].astype(F32)
        for j in range(wide):
            part = stage[pl.ds(j, block, stride=wide), :]
            dst[pl.ds(pl.multiple_of(i * block, 16), block), j * LANES : (j + 1) * LANES] = part.astype(BF)
        return carry

    lax.fori_loop(0, rows // block, step, 0)


def small_matrix(whole, row, stage, rows, cols):
    wide = cols // LANES
    stage[0 : rows * wide, :] = whole[row : row + rows * wide, :].astype(F32)
    return jnp.concatenate([stage[pl.ds(j, rows, stride=wide), :] for j in range(wide)], axis=1)


class Gather:
    def __init__(self, place, whole, shard, chunks, send, recv):
        self.p, self.whole, self.shard, self.chunks, self.send, self.recv = place, whole, shard, chunks, send, recv
        p = place
        x_index, y_index = p.x_side[1], p.y_side[1]
        low = p.z_low
        self.first = x_index + low * (y_index - x_index)
        self.second = y_index + low * (x_index - y_index)
        self.diagonal = x_index + 4 - 8 * p.y

    def copy(self, kind, k):
        p = self.p
        block = (p.me, p.me, self.first, self.first, self.first, self.diagonal, self.second)[kind]
        target = (
            (p.z, self.first), p.sibling, (p.z, self.second), p.z_near, p.sibling, p.sibling, p.sibling
        )[kind]
        row, count = self.chunks[k]
        ref = self.whole.at[pl.ds(pl.multiple_of(block * self.shard + row, 16), count), :]
        return remote(ref, ref, self.send.at[kind, k], self.recv.at[kind, k], target)

    def play(self, *events):
        for event in events:
            kind, k = event[0], int(event[1:])
            if kind == "a":
                self.copy(0, k).start()
                self.copy(1, k).start()
            elif kind == "b":
                self.copy(0, k).wait_recv()
                for way in (2, 3, 4):
                    self.copy(way, k).start()
            elif kind == "c":
                for arrived, onward in ((2, 5), (3, 6)):
                    self.copy(arrived, k).wait_recv()
                    self.copy(onward, k).start()
            else:
                for way in (1, 4, 5, 6):
                    self.copy(way, k).wait_recv()

    def finish(self):
        for k in range(len(self.chunks)):
            for kind in range(7):
                self.copy(kind, k).wait_send()


class KeyExchange:
    def __init__(self, place, keys, send, recv):
        self.p, self.keys, self.send, self.recv = place, keys, send, recv
        self.x_index, self.y_index = place.x_side[1], place.y_side[1]
        self.diagonal = self.x_index + 4 - 8 * place.y

    def copy(self, kind):
        p = self.p
        half = self.keys.shape[1] // 2
        low, high, full = pl.ds(0, half), pl.ds(half, half), pl.ds(0, 2 * half)
        block, rows, target = (
            (p.me, full, p.x_side), (p.me, full, p.y_side), (p.me, full, p.sibling),
            (self.x_index, low, p.y_side), (self.y_index, high, p.x_side),
            (self.x_index, full, p.sibling), (self.y_index, full, p.sibling), (self.diagonal, full, p.sibling),
        )[kind]
        ref = self.keys.at[block, rows, :]
        return remote(ref, ref, self.send.at[kind], self.recv.at[kind], target)

    def step(self, s):
        if s == 0:
            waits, starts = (), (0, 1, 2)
        elif s == 1:
            waits, starts = (0, 1), (3, 4, 5, 6)
        elif s == 2:
            waits, starts = (3, 4), (7,)
        else:
            waits, starts = (2, 5, 6, 7), ()
        for kind in waits:
            self.copy(kind).wait_recv()
        for kind in starts:
            self.copy(kind).start()

    def finish(self):
        for kind in range(8):
            self.copy(kind).wait_send()


def flat_rows_of():
    rows, at = {}, 0
    for name, shape in param_layout():
        rows[name] = at // LANES
        at += math.prod(shape)
    return rows


def gather_chunks(shard):
    at = flat_rows_of()
    tail = at["hid_bias"] % shard // 16 * 16
    chunks = [(at["episode"], at["w_o"] - at["episode"]), (tail, shard - tail), (at["w_o"], at["w_qkv"] - at["w_o"])]
    for low, high in ((0, at["episode"]), (at["w_qkv"], tail)):
        while low < high:
            count = min(512, high - low)
            chunks.append((low, count))
            low += count
    return chunks


def begin_kernel(
    chunks, master, tokens, ids, episodes,
    up_one, down_one, qkv_w, so_w, up_two, down_two,
    latent, norms, hid_bias, out_bias, w_q, w_o, w_kv, tok_norm, tok_normed, episode, rank, counts,
    kvf_out, co_out, lse_out, hot_lanes, h1,
    whole, stage, all_ids, keys, m_up_one, m_down_one, m_qkv, m_so, m_up_two, m_down_two,
    episodes_held, h1_held, h1_sem, send, recv, key_send, key_recv, id_send, id_recv, out_sem,
):
    place = Place()
    shard = master.shape[0]
    frames, cap = kvf_out.shape[0], kvf_out.shape[1]
    gather = Gather(place, whole, shard, chunks, send, recv)
    exchange = KeyExchange(place, keys, key_send, key_recv)
    at = flat_rows_of()
    partners = [place.lat_other(d) for d in range(1, 8)] + [place.z_near]
    greet(partners)
    all_ids[pl.ds(place.me, 1)] = ids[...][None]
    id_copies = [
        remote(all_ids.at[place.me], all_ids.at[place.me], id_send.at[d - 1], id_recv.at[d - 1], place.lat_other(d))
        for d in range(1, 8)
    ]
    own_at = place.me * shard
    for row, count in chunks:
        whole[pl.ds(pl.multiple_of(own_at + row, 16), count), :] = master[row : row + count, :].astype(BF)
    met(partners)
    for copy in id_copies:
        copy.start()
    gather.play("a0", "a1", "a2", "a3", "a4")

    for copy in id_copies:
        copy.wait_recv()
    tags = jnp.concatenate([all_ids[s] for s in range(8)], axis=0)
    low = lax.broadcasted_iota(jnp.int32, (LANES, LANES), 0)
    high = lax.broadcasted_iota(jnp.int32, (LANES, LANES), 1)
    upto = jnp.where(low <= high, 1.0, 0.0).astype(BF)
    n = tags.shape[0]
    below = jnp.where(
        lax.broadcasted_iota(jnp.int32, (n, n), 1) < lax.broadcasted_iota(jnp.int32, (n, n), 0), 1.0, 0.0
    ).astype(BF)
    for f in range(frames):
        hit = tags == place.me * frames + f
        hit_low = jnp.where(hit, 1.0, 0.0).astype(BF)
        inside = mm(hit_low, upto)
        row_total = jnp.broadcast_to(inside[:, LANES - 1 : LANES], (n, LANES))
        before = mm(below, row_total.astype(BF))
        place_in = (inside + before).astype(jnp.int32) - 1
        rank[f] = jnp.where(hit, place_in, -1)
        total = jnp.sum(row_total[:, 0:1], axis=0, keepdims=True).astype(jnp.int32)
        counts[f] = jnp.broadcast_to(total, (8, LANES))
    gather.play("b0", "b1", "a5", "b2", "c0", "c1", "a6", "d0", "d1")

    pair = whole[at["tok_norm"] // 16 * 16 : at["lat_norms"], :].astype(F32)
    pair = pair[at["tok_norm"] % 16 : at["tok_norm"] % 16 + 4, :]
    tok_norm[...] = jnp.concatenate(
        [
            jnp.concatenate([pair[0:1], pair[1:2]], axis=1),
            jnp.concatenate([pair[2:3], pair[3:4]], axis=1),
        ],
        axis=0,
    )
    w_kv[...] = whole[at["w_kv"] : at["w_kv"] + DIN, :]
    xhat, unused = norm_stats(tokens[...].astype(F32))
    normed = (xhat * tok_norm[0:1, :] + tok_norm[1:2, :]).astype(BF)
    tok_normed[...] = normed
    keys[pl.ds(place.me, 1)] = mm(normed, w_kv[...]).astype(BF)[None]
    exchange.step(0)
    gather.play("a7", "a8", "b3", "c2")
    norms[...] = small_matrix(whole, at["lat_norms"], stage, 8, D)
    hid_bias[...] = small_matrix(whole, at["hid_bias"], stage, 2, FF)
    out_bias[...] = small_matrix(whole, at["out_bias"], stage, 4, D)
    mine = lax.broadcasted_iota(jnp.int32, (16, FRAMES), 0) + place.me * frames
    mine = mine == lax.broadcasted_iota(jnp.int32, (16, FRAMES), 1)
    own = jnp.sum(jnp.where(mine, episodes[...].astype(F32), 0.0), axis=1, keepdims=True)
    hot = jnp.where(lax.broadcasted_iota(jnp.int32, (16, 16), 1).astype(F32) == own, 1.0, 0.0).astype(BF)
    for f in range(frames):
        row = lax.broadcasted_iota(jnp.int32, (16, LANES), 0).astype(F32)
        hot_lanes[f] = jnp.where(row == own[f : f + 1, 0:1], 1.0, 0.0)
    episode_rows = mm(hot, small_matrix(whole, at["episode"], stage, 16, D).astype(BF))
    gather.play("b4", "c3", "d2", "b5", "c4", "d3", "b6")
    exchange.step(1)
    gather.play("a9", "a10", "c5", "d4", "c6", "d5")
    packed = whole[at["w_q"] : at["w_q"] + D // 2, :].astype(F32)
    stage[pl.ds(0, D // 2, stride=2), :] = packed
    stage[pl.ds(1, D // 2, stride=2), :] = pltpu.roll(packed, CH, 1)
    w_q[...] = keep_half(stage[0:D, :], 0).astype(BF)
    w_o[0:CH, :] = jnp.zeros((CH, D), BF)
    w_o[CH : 2 * CH, :] = small_matrix(whole, at["w_o"], stage, CH, D).astype(BF)
    exchange.step(2)
    gather.play("a11", "b7", "d6")
    exchange.step(3)
    relayout(whole, 0, stage, latent, LAT, D)

    chunk = 8 * LANES
    episodes_held[...] = episode_rows[0:8, :]
    before = [("b8",), ("b9", "d7"), ("b10", "d8"), ("b11", "d9")]
    midway = [("c7",), ("c8",), ("c9",), ("c10",)]

    def play(frame, parts):
        for step, events in enumerate(parts):
            pl.when(frame == step)(functools.partial(gather.play, *events))

    def attend(f, carry):
        play(f, before)
        row = episodes_held[pl.ds(f, 1), :]
        start = latent[...].astype(F32) + row
        episode[pl.ds(f, 1)] = row[None]

        def pick(j, acc):
            sel = select_tokens(rank[f, pl.ds(pl.multiple_of(8 * j, 8), 8), :], cap)
            return acc + mm(sel, keys[pl.ds(2 * j, 2)].reshape(chunk, LANES))

        kvf = lax.fori_loop(0, n // 8, pick, jnp.zeros((cap, LANES), F32)).astype(BF)
        play(f, midway)
        co, lse = cross_attend(start, norms, w_q, kvf, counts[f, 0:1, 0:1])
        rows = pl.ds(pl.multiple_of(f * LAT, LAT), LAT)
        h1_held[f] = start + mm(co, w_o[...]) + out_bias[0:1, :]
        pltpu.make_async_copy(h1_held.at[f], h1.at[rows, :], h1_sem.at[f]).start()
        kvf_out[f] = kvf
        co_out[rows, :] = co
        lse_out[f] = lse
        return carry

    lax.fori_loop(0, frames, attend, 0)
    gather.play("c11", "d10", "d11")

    big = (
        (up_one, m_up_one, at["w_up"], D, FF),
        (down_one, m_down_one, at["w_down"], FF, D),
        (qkv_w, m_qkv, at["w_qkv"], D, 3 * D),
        (so_w, m_so, at["w_so"], D, D),
        (up_two, m_up_two, at["w_up"] + D * FF // LANES, D, FF),
        (down_two, m_down_two, at["w_down"] + D * FF // LANES, FF, D),
    )
    outs = []
    for j, (out, held, row, rows, cols) in enumerate(big):
        relayout(whole, row, stage, held, rows, cols)
        outs.append(pltpu.make_async_copy(held, out, out_sem.at[j]))
        outs[-1].start()
    for copy in outs:
        copy.wait()
    for f in range(frames):
        pltpu.make_async_copy(h1_held.at[f], h1.at[f * LAT : (f + 1) * LAT, :], h1_sem.at[f]).wait()
    for copy in id_copies:
        copy.wait_send()
    exchange.finish()
    gather.finish()


def begin_all(master_rows, token_rows, ids, episodes, frames, cap):
    shard = master_rows.shape[0]
    tokens = token_rows.shape[0]
    total = 8 * tokens
    chunks = gather_chunks(shard)
    vmem = pl.BlockSpec(memory_space=pltpu.VMEM)
    anywhere = pl.BlockSpec(memory_space=pl.ANY)
    matrices = [(D, FF), (FF, D), (D, 3 * D), (D, D), (D, FF), (FF, D)]
    dma = pltpu.SemaphoreType.DMA
    return pl.pallas_call(
        functools.partial(begin_kernel, chunks),
        out_shape=[shaped(m, BF) for m in matrices]
        + [
            shaped((LAT, D), BF),
            shaped((8, D)),
            shaped((2, FF)),
            shaped((4, D)),
            shaped((D, LANES), BF),
            shaped((LANES, D), BF),
            shaped((DIN, LANES), BF),
            shaped((2, DIN)),
            shaped((tokens, DIN), BF),
            shaped((frames, 1, D)),
            shaped((frames, total // LANES, LANES), jnp.int32),
            shaped((frames, 8, LANES), jnp.int32),
            shaped((frames, cap, LANES), BF),
            shaped((frames * LAT, LANES), BF),
            shaped((frames, 1, LAT)),
            shaped((frames, 16, LANES)),
            shaped((frames * LAT, D)),
        ],
        in_specs=[vmem] * 4,
        out_specs=[anywhere] * 6 + [vmem] * 16 + [anywhere],
        scratch_shapes=[
            pltpu.VMEM((8 * shard, LANES), BF),
            pltpu.VMEM((2048, LANES), F32),
            pltpu.VMEM((8, tokens // LANES, LANES), jnp.int32),
            pltpu.VMEM((8, tokens, LANES), BF),
        ]
        + [pltpu.VMEM(m, BF) for m in matrices]
        + [
            pltpu.VMEM((8, D), F32),
            pltpu.VMEM((frames, LAT, D), F32),
            dma((frames,)),
            dma((7, len(chunks))), dma((7, len(chunks))), dma((8,)), dma((8,)), dma((7,)), dma((7,)), dma((6,)),
        ],
        compiler_params=pltpu.CompilerParams(
            collective_id=3, has_side_effects=True, vmem_limit_bytes=56 * MIB
        ),
    )(master_rows, token_rows, ids, episodes)


FCHUNK = 512


def to_flat(stage, matrix):
    rows, wide = matrix.shape[0], matrix.shape[1] // LANES
    for j in range(wide):
        stage[pl.ds(j, rows, stride=wide), :] = matrix[:, j * LANES : (j + 1) * LANES]
    return stage[0 : rows * wide, :]


def feed_forward(rows, gain, bias, up_bias, down_bias, w_up, w_down, act_ref, slope_ref, normed_ref, total_ref):
    xhat, rstd = norm_stats(rows)
    normed_ref[...] = (xhat * gain + bias).astype(BF)
    total_ref[...] = rows + down_bias

    for c in range(2):
        at = slice(c * FF // 2, (c + 1) * FF // 2)
        act, slope = gelu_pair(mm(normed_ref[...], w_up[:, at]) + up_bias[:, at])
        act = act.astype(BF)
        act_ref[:, at] = act
        slope_ref[:, at] = slope.astype(BF)
        total_ref[...] += mm(act, w_down[at, :])


def feed_back(grad_ref, normed_ref, xhat, rstd, gain, act, slope, w_up, w_down, acc_up, acc_down, dhid, dnorm, dout, work):
    work[...] = jnp.zeros(work.shape, F32)
    for c in range(FF // FCHUNK):
        at = slice(c * FCHUNK, (c + 1) * FCHUNK)
        dpre = (mm_t(grad_ref[...], w_down[at, :]) * slope[:, at].astype(F32)).astype(BF)
        dhid[:, at] += col_sum(dpre.astype(F32))
        work[...] += mm_t(dpre, w_up[:, at])
        acc_up[:, at] += t_mm(normed_ref[...], dpre)
        acc_down[at, :] += t_mm(act[:, at], grad_ref[...])
    grad_normed = work[...]
    dnorm[...] += jnp.concatenate([col_sum(grad_normed * xhat), col_sum(grad_normed)], axis=0)
    dout[...] += col_sum(grad_ref[...].astype(F32))
    return norm_back(grad_normed, xhat, rstd, gain)


def clear(first, refs):
    @pl.when(first)
    def _():
        for ref in refs:
            ref[...] = jnp.zeros_like(ref)


def flat_spans(row, count, shard, extra):
    spans, done = [], 0
    while done < count:
        part = min(count - done, shard - (row + done) % shard)
        spans.append((done, part, row + done + (row + done) // shard * extra))
        done += part
    return spans


def flatten(acc, stage, low, slot):
    wide = acc.shape[1] // LANES
    block = min(acc.shape[0], 2048 // wide // 128 * 128)
    span = block * wide

    def step(i, carry):
        part = acc[pl.ds(pl.multiple_of(i * block, block), block), :]
        for j in range(wide):
            stage[pl.ds(j, block, stride=wide), :] = part[:, j * LANES : (j + 1) * LANES]
        low[slot, pl.ds(pl.multiple_of(i * span, span), span), :] = stage[0:span, :].astype(BF)
        return carry

    lax.fori_loop(0, acc.shape[0] // block, step, 0)


def write_flat(flat, stage, low, pieces, sems, shard, extra):
    pending = {}
    for j, (acc, row) in enumerate(pieces):
        count = acc.shape[0] * acc.shape[1] // LANES
        slot = j % 2
        for copy in pending.get(slot, []):
            copy.wait()
        flatten(acc, stage, low, slot)
        pending[slot] = [
            pltpu.make_async_copy(low.at[slot, pl.ds(off, part), :], flat.at[pl.ds(at, part), :], sems.at[slot, k])
            for k, (off, part, at) in enumerate(flat_spans(row, count, shard, extra))
        ]
        for copy in pending[slot]:
            copy.start()
    for copies in pending.values():
        for copy in copies:
            copy.wait()


class FrameExchange:
    def __init__(self, place, source, grad, held, result, sems):
        self.p, self.source, self.grad, self.held, self.result = place, source, grad, held, result
        self.in_send, self.in_recv, self.out_send, self.out_recv, self.own_in, self.own_out = sems
        self.frames, self.rows = grad.shape[0], source.shape[1]

    @staticmethod
    def scratch(frames):
        dma = pltpu.SemaphoreType.DMA
        return [dma((frames, 7))] * 4 + [dma((frames,))] * 2

    def block(self, index):
        return pl.ds(pl.multiple_of(index * self.rows, 16), self.rows)

    def arriving(self, f, d):
        target = self.p.lat_other(d)
        src = self.source.at[target[1] * self.frames + f]
        dst = self.grad.at[f, self.block(self.p.me), :]
        return remote(src, dst, self.in_send.at[f, d - 1], self.in_recv.at[f, d - 1], target)

    def own_arriving(self, f):
        src = self.source.at[self.p.me * self.frames + f]
        return pltpu.make_async_copy(src, self.grad.at[f, self.block(self.p.me), :], self.own_in.at[f])

    def leaving(self, f, d):
        target = self.p.lat_other(d)
        src = self.held.at[f, self.block(target[1]), :]
        dst = self.result.at[self.p.me * self.frames + f]
        return remote(src, dst, self.out_send.at[f, d - 1], self.out_recv.at[f, d - 1], target)

    def own_leaving(self, f):
        dst = self.result.at[self.p.me * self.frames + f]
        return pltpu.make_async_copy(self.held.at[f, self.block(self.p.me), :], dst, self.own_out.at[f])

    def partners(self):
        return [self.p.lat_other(d) for d in range(1, 8)]

    def begin(self):
        met(self.partners())
        for f in range(self.frames):
            self.own_arriving(f).start()
            for d in range(1, 8):
                self.arriving(f, d).start()

    def await_frame(self, f):
        self.own_arriving(f).wait()
        for d in range(1, 8):
            self.arriving(f, d).wait_recv()

    def send_frame(self, f):
        self.own_leaving(f).start()
        for d in range(1, 8):
            self.leaving(f, d).start()

    def finish(self):
        def step(f, carry):
            self.own_leaving(f).wait()
            for d in range(1, 8):
                self.arriving(f, d).wait_send()
                self.leaving(f, d).wait()
            return carry

        lax.fori_loop(0, self.frames, step, 0)


class Flow:
    def __init__(self, step, steps, array, slots, sems):
        self.step, self.steps, self.array, self.slots, self.sems = step, steps, array, slots, sems
        self.rows = slots.shape[1]

    def here(self):
        return self.slots.at[lax.rem(self.step, 2)]

    def ends(self, step):
        slot = lax.rem(step, 2)
        rows = pl.ds(pl.multiple_of(step * self.rows, self.rows), self.rows)
        return self.array.at[rows, :], self.slots.at[slot], self.sems.at[slot]

    def load(self, step):
        outside, inside, sem = self.ends(step)
        return pltpu.make_async_copy(outside, inside, sem)

    def store(self, step):
        outside, inside, sem = self.ends(step)
        return pltpu.make_async_copy(inside, outside, sem)

    def fetch_ahead(self):
        pl.when(self.step == 0)(lambda: self.load(self.step).start())
        pl.when(self.step + 1 < self.steps)(lambda: self.load(self.step + 1).start())

    def arrived(self):
        self.load(self.step).wait()

    def free(self):
        pl.when(self.step >= 2)(lambda: self.store(self.step - 2).wait())

    def send(self):
        self.store(self.step).start()

    def drain(self):
        if self.steps > 1:
            self.store(self.step - 1).wait()
        self.store(self.step).wait()


def flow_slots(shape, dtype):
    return [pltpu.VMEM((2,) + shape, dtype), pltpu.SemaphoreType.DMA((2,))]


class Late:
    def __init__(self, step, sources, refs, sems):
        self.first = step == 0
        self.copies = [
            pltpu.make_async_copy(src, ref, sems.at[k]) for k, (src, ref) in enumerate(zip(sources, refs))
        ]

        @pl.when(self.first)
        def _():
            for copy in self.copies:
                copy.start()

    def need(self, *which):
        @pl.when(self.first)
        def _():
            for k in which:
                self.copies[k].wait()


def forward_kernel(
    reach, shard, extra, steps, h1, grad, norms, hid_bias, out_bias, up_one, down_one, *rest,
):
    forward_body(reach, shard, extra, steps, h1, grad, norms, hid_bias, out_bias, up_one, down_one, rest[:4], *rest[4:])


def forward_body(
    reach, shard, extra, steps, h1, grad, norms, hid_bias, out_bias, up_one, down_one, late_sources,
    h2_all, qkv_all, lse_out, mixed_all, act_all, slope_all, latents, g3, dhid, dnorm, dout, flat,
    act_two, slope_two, acc_up, acc_down, stage, low, normed, mixed_t, work, sems,
    w_qkv, w_so, up_two, down_two, late_sems,
    h2_slots, h2_sems, qkv_slots, qkv_sems, mixed_slots, mixed_sems, act_slots, act_sems, slope_slots, slope_sems, *shared,
):
    step = pl.program_id(0)
    late = Late(step, late_sources, (w_qkv, w_so, up_two, down_two), late_sems)
    flows = [
        Flow(step, steps, *parts)
        for parts in (
            (h2_all, h2_slots, h2_sems), (qkv_all, qkv_slots, qkv_sems), (mixed_all, mixed_slots, mixed_sems),
            (act_all, act_slots, act_sems), (slope_all, slope_slots, slope_sems),
        )
    ]
    for flow in flows:
        flow.free()
    h2_out, qkv, mixed_out, act_one, slope_one = (flow.here() for flow in flows)
    if reach:
        place = Place()
        traffic = FrameExchange(place, grad, shared[0], shared[1], latents, shared[2:])
        pl.when(step == 0)(lambda: greet(traffic.partners()))
        grad = shared[0].at[step]
    clear(step == 0, (acc_up, acc_down, dhid, dnorm, dout))
    feed_forward(
        h1[...], norms[2:3, :], norms[3:4, :], hid_bias.at[0:1], out_bias[1:2, :], up_one, down_one, act_one,
        slope_one, normed, h2_out,
    )
    xhat, unused = norm_stats(h2_out[...])
    normed[...] = (xhat * norms[4:5, :] + norms[5:6, :]).astype(BF)

    late.need(0)
    if reach:
        pl.when(step == 0)(traffic.begin)

    qkv[...] = mm(normed[...], w_qkv[...]).astype(BF)
    for k in (0, 1, 3, 4):
        flows[k].send()
    scale = jnp.asarray(0.125, BF)
    ones = jnp.ones((16, LAT), BF)
    group = 4
    width = group * HEAD_DIM
    for base in range(0, D, width):
        queries = by_head(qkv[:, base : base + width] * scale)
        value_t = qkv[:, 2 * D + base : 2 * D + base + width].T
        scores = mm_t(qkv[:, D + base : D + base + width], queries)
        top = jnp.max(scores, axis=0, keepdims=True)
        terms = jnp.exp(scores - top).astype(BF)
        for j in range(group):
            at = slice(j * LAT, (j + 1) * LAT)
            values = jnp.concatenate([value_t[j * HEAD_DIM : (j + 1) * HEAD_DIM, :], ones], axis=0)
            product = mm(values, terms[:, at])
            total = product[HEAD_DIM : HEAD_DIM + 1, :]
            head = base // HEAD_DIM + j
            lse_out[0, head : head + 1, :] = top[:, at] + jnp.log(total)
            mixed_t[head * HEAD_DIM : (head + 1) * HEAD_DIM, :] = product[0:HEAD_DIM, :] * (1.0 / total)
    late.need(1, 2, 3)
    mixed = mixed_t[...].T.astype(BF)
    mixed_out[...] = mixed
    flows[2].send()
    h3 = h2_out[...] + mm(mixed, w_so[...]) + out_bias[2:3, :]
    feed_forward(
        h3, norms[6:7, :], norms[7:8, :], hid_bias.at[1:2], out_bias[3:4, :], up_two, down_two, act_two, slope_two,
        normed, work,
    )
    if reach:
        shared[1][step] = work[...].astype(BF)
        traffic.send_frame(step)
        traffic.await_frame(step)
    else:
        latents[...] = work[...].astype(BF)
    xhat, rstd = norm_stats(h3)
    g3[...] = grad[...].astype(F32) + feed_back(
        grad, normed, xhat, rstd, norms[6:7, :], act_two, slope_two, up_two, down_two,
        acc_up, acc_down, dhid, dnorm, dout, work,
    )

    @pl.when(step == pl.num_programs(0) - 1)
    def _():
        at = flat_rows_of()
        half = D * FF // LANES
        write_flat(flat, stage, low, [(acc_up, at["w_up"] + half), (acc_down, at["w_down"] + half)], sems, shard, extra)
        if reach:
            traffic.finish()
        for flow in flows:
            flow.drain()


def backward_kernel(
    shard, extra, steps, qkv, lse, mixed, g3, h2_all, h1_all, act_all, slope_all, norms, w_so, src_qkv, src_up, src_down,
    latents_in, flat_in,
    g1, dhid, dnorm_sa, dnorm_one, dout_so, dout_one, latents_out, flat,
    dqkv, acc_up, acc_down, acc_qkv, acc_so, stage, low, normed, grad_mixed, grad_low, work, sems,
    w_qkv, up_one, down_one, late_sems,
    h2_slots, h2_sems, h1_slots, h1_sems, act_slots, act_sems, slope_slots, slope_sems, latents_held, pass_sem,
):
    step = pl.program_id(0)
    late = Late(step, (src_qkv, src_up, src_down), (w_qkv, up_one, down_one), late_sems)
    flows = [
        Flow(step, steps, *parts)
        for parts in (
            (h2_all, h2_slots, h2_sems), (h1_all, h1_slots, h1_sems), (act_all, act_slots, act_sems),
            (slope_all, slope_slots, slope_sems),
        )
    ]
    for flow in flows:
        flow.fetch_ahead()
    h2, h1, act_one, slope_one = (flow.here() for flow in flows)
    latents_load = pltpu.make_async_copy(latents_in, latents_held, pass_sem.at[0])
    latents_store = pltpu.make_async_copy(latents_held, latents_out, pass_sem.at[1])
    pl.when(step == 0)(lambda: latents_load.start())

    @pl.when(step == min(1, steps - 1))
    def _():
        latents_load.wait()
        latents_store.start()

    clear(
        step == 0,
        (acc_up, acc_down, acc_qkv, acc_so, dhid, dnorm_sa, dnorm_one, dout_so, dout_one),
    )
    scale = jnp.asarray(0.125, BF)
    grad_three = g3[...]
    grad_low[...] = grad_three.astype(BF)
    dout_so[...] += col_sum(grad_low[...].astype(F32))
    acc_so[...] += t_mm(mixed[...], grad_low[...])
    grad_mixed[...] = mm_t(grad_low[...], w_so[...]).astype(BF)

    for base in range(0, D, LANES):
        query_at = slice(base, base + LANES)
        key_at = slice(D + base, D + base + LANES)
        value_at = slice(2 * D + base, 2 * D + base + LANES)
        head = base // HEAD_DIM
        queries = by_head(qkv[:, query_at] * scale)
        grads = by_head(grad_mixed[:, query_at])
        keys = qkv[:, key_at]
        key_t = keys.T
        log_total = jnp.concatenate([lse[0, head : head + 1, :], lse[0, head + 1 : head + 2, :]], axis=1)
        prob = jnp.exp(mm_t(keys, queries) - log_total)
        dqkv[:, value_at] = mm(prob.astype(BF), grads).astype(BF)
        weighted = prob * mm_t(qkv[:, value_at], grads)
        grad_score = (weighted - prob * col_sum(weighted)).astype(BF)
        dqkv[:, key_at] = mm(grad_score, queries).astype(BF)
        query_t = [
            mm(key_t[j * HEAD_DIM : (j + 1) * HEAD_DIM, :], grad_score[:, j * LAT : (j + 1) * LAT]) for j in range(2)
        ]
        dqkv[:, query_at] = (jnp.concatenate(query_t, axis=0).T * 0.125).astype(BF)
    late.need(0, 1, 2)
    for flow in flows:
        flow.arrived()
    xhat, rstd = norm_stats(h2[...])
    normed[...] = (xhat * norms[4:5, :] + norms[5:6, :]).astype(BF)
    grad_in = mm_t(dqkv[...], w_qkv[...])
    acc_qkv[...] += t_mm(normed[...], dqkv[...])
    dnorm_sa[...] += jnp.concatenate([col_sum(grad_in * xhat), col_sum(grad_in)], axis=0)
    grad_two = grad_three + norm_back(grad_in, xhat, rstd, norms[4:5, :])

    xhat, rstd = norm_stats(h1[...])
    normed[...] = (xhat * norms[2:3, :] + norms[3:4, :]).astype(BF)
    grad_low[...] = grad_two.astype(BF)
    grad_one = grad_two + feed_back(
        grad_low, normed, xhat, rstd, norms[2:3, :], act_one, slope_one, up_one, down_one,
        acc_up, acc_down, dhid, dnorm_one, dout_one, work,
    )

    g1[...] = grad_one

    @pl.when(step == pl.num_programs(0) - 1)
    def _():
        at = flat_rows_of()
        write_flat(
            flat, stage, low,
            [(acc_up, at["w_up"]), (acc_down, at["w_down"]), (acc_qkv, at["w_qkv"]), (acc_so, at["w_so"])],
            sems, shard, extra,
        )
        latents_store.wait()


def cross_back_frame(
    grad_one, kvf, co, lse, rank_ref, count, episode_row, hot_column, latent, norms, w_q, w_o,
    acc_latent, acc_q, acc_o, acc_episode, dnorm, dout, dkv_t, pause=lambda: None,
):
    cap = kvf.shape[0]
    start = latent[...].astype(F32) + episode_row
    xhat, rstd = norm_stats(start)
    query_in = (xhat * norms[0:1, :] + norms[1:2, :]).astype(BF)
    queries = mm(query_in, w_q[...]).astype(BF) * jnp.asarray(0.125, BF)
    branch = grad_one.astype(BF)
    grad_co = mm_t(branch, w_o[...]).astype(BF)
    acc_o[...] += t_mm(co, branch)
    dout[...] += col_sum(branch.astype(F32))
    scores = cross_scores(kvf, queries, count)
    prob = jnp.exp(scores - lse)
    weighted = prob * mm_t(kvf, grad_co)
    grad_score = (weighted - prob * col_sum(weighted)).astype(BF)
    grad_kv = (mm(grad_score, queries) + mm(prob.astype(BF), grad_co)).astype(BF)
    grad_query = (t_mm(kvf, grad_score).T * 0.125).astype(BF)
    pause()
    acc_q[...] += t_mm(query_in, grad_query)
    grad_in = mm_t(grad_query, w_q[...])
    grad_start = grad_one + norm_back(grad_in, xhat, rstd, norms[0:1, :])
    dnorm[...] += jnp.concatenate([col_sum(grad_in * xhat), col_sum(grad_in)], axis=0)
    acc_latent[...] += grad_start
    acc_episode[...] += hot_column * col_sum(grad_start)
    grad_kv_t = grad_kv.T
    chunk = 8 * LANES

    def scatter(j, carry):
        sel = select_tokens(rank_ref[pl.ds(pl.multiple_of(j * 8, 8), 8), :], cap)
        at = pl.ds(pl.multiple_of(j * chunk, chunk), chunk)
        dkv_t[:, at] = added(dkv_t[:, at], mm(grad_kv_t, sel))
        return carry

    lax.fori_loop(0, dkv_t.shape[1] // chunk, scatter, 0)


def write_small(put, stage, low, latent_low, acc_latent, acc_q, acc_o, acc_episode, norm_grads, hid_grads, out_grads):
    at = flat_rows_of()
    flatten(acc_latent, stage, latent_low, 0)
    put(latent_low.at[0], 0)
    head = at["lat_norms"] - at["episode"]
    used = EPISODES * (D // LANES)
    rows = [to_flat(stage, acc_episode[...])[0:used, :], jnp.zeros((head - used, LANES), F32)]
    rows = jnp.concatenate(rows + [to_flat(stage, norm_grads)], axis=0)
    top = rows.shape[0]
    low[0, 0:top, :] = rows.astype(BF)
    put(low.at[0, pl.ds(0, top), :], at["episode"])
    stage[0:D, :] = acc_q[...]
    even = stage[pl.ds(0, D // 2, stride=2), :]
    odd = pltpu.roll(stage[pl.ds(1, D // 2, stride=2), :], CH, 1)
    low[0, top : top + D // 2, :] = jnp.where(lane_half(even.shape, 0), even, odd).astype(BF)
    both = D // 2 + CH * D // LANES
    low[0, top + D // 2 : top + both, :] = to_flat(stage, acc_o[CH : 2 * CH, :]).astype(BF)
    put(low.at[0, pl.ds(top, both), :], at["w_q"])
    hid = to_flat(stage, hid_grads)
    last = top + both
    low[0, last : last + hid.shape[0], :] = hid.astype(BF)
    end = hid.shape[0] + 4 * D // LANES
    low[0, last + hid.shape[0] : last + end, :] = to_flat(stage, out_grads).astype(BF)
    put(low.at[0, pl.ds(last, end), :], at["hid_bias"])


def cross_accumulators(total_keys):
    shapes = [(LAT, D), (D, LANES), (LANES, D), (16, D), (2, D), (1, D)]
    return [pltpu.VMEM(shape, F32) for shape in shapes] + [pltpu.VMEM((LANES, total_keys), BF)]


def small_buffers():
    return [pltpu.VMEM((2048, LANES), F32), pltpu.VMEM((1, 640, LANES), BF), pltpu.VMEM((1, 2048, LANES), BF)]


def stacked(*parts):
    return jnp.concatenate([part[...] for part in parts], axis=0)


def cross_bwd_kernel(
    kv_rows, g1, kvf, co, lse, rank, count, episode, hot, latent, norms, w_q, w_o,
    dnorm_one, dnorm_sa, dnorm_two, dhid_one, dhid_two, dout_one, dout_so, dout_two, flat_in, flat,
    acc_latent, acc_q, acc_o, acc_episode, dnorm, dout, dkv_t, stage, low, latent_low, kv_low, sems,
):
    step = pl.program_id(0)
    accs = (acc_latent, acc_q, acc_o, acc_episode, dnorm, dout, dkv_t)
    clear(step == 0, accs)
    cross_back_frame(
        g1[...], kvf[0], co[...], lse[0], rank.at[0], count[0, 0:1, 0:1], episode[0], hot[0, :, 0:1],
        latent, norms, w_q, w_o, *accs,
    )

    @pl.when(step == pl.num_programs(0) - 1)
    def _():
        copies = []

        def put(source, row):
            copies.append(
                pltpu.make_async_copy(source, flat.at[pl.ds(row, source.shape[0]), :], sems.at[len(copies)])
            )
            copies[-1].start()

        write_small(
            put, stage, low, latent_low, acc_latent, acc_q, acc_o, acc_episode,
            stacked(dnorm, dnorm_one, dnorm_sa, dnorm_two), stacked(dhid_one, dhid_two),
            stacked(dout, dout_one, dout_so, dout_two),
        )
        for copy in copies:
            copy.wait()
        tokens = kv_rows[1]
        for j in range(dkv_t.shape[1] // tokens):
            kv_low[...] = dkv_t[:, j * tokens : (j + 1) * tokens].T
            copy = pltpu.make_async_copy(kv_low, flat.at[pl.ds(kv_rows[0] + j * tokens, tokens), :], sems.at[0])
            copy.start()
            copy.wait()


def fixed(*shape):
    return pl.BlockSpec(shape, lambda i: (0,) * len(shape), pipeline_mode=pl.Buffered(1))


def kept(*shape):
    return pl.BlockSpec(shape, lambda i: (0,) * len(shape))


def rowed(rows, cols):
    return pl.BlockSpec((rows, cols), lambda i: (i, 0))


def framed(*shape):
    return pl.BlockSpec((1,) + shape, lambda i: (i,) + (0,) * len(shape))


def shaped(shape, dtype=F32):
    return jax.ShapeDtypeStruct(shape, dtype)


def call(kernel, grid, in_specs, outs, args, flops=0, trans=0, scratch=(), limit=56, aliases=None, collective=None):
    out_specs, out_shapes = zip(*outs)
    moved = sum(math.prod(a.shape) * a.dtype.itemsize for a in args)
    moved += sum(math.prod(s.shape) * s.dtype.itemsize for s in out_shapes)
    return pl.pallas_call(
        kernel,
        grid=(grid,),
        in_specs=in_specs,
        out_specs=list(out_specs),
        out_shape=list(out_shapes),
        scratch_shapes=list(scratch),
        input_output_aliases=aliases or {},
        compiler_params=pltpu.CompilerParams(
            dimension_semantics=("arbitrary",),
            vmem_limit_bytes=limit * MIB,
            collective_id=collective,
            has_side_effects=collective is not None,
        ),
        cost_estimate=pl.CostEstimate(flops=flops, bytes_accessed=moved, transcendentals=trans),
    )(*args)


def reduce_all(flat, shard, bias_owner, bias_row, tokens, tok_normed, w_kv, tok_norm, g1, cross):
    vmem = pl.BlockSpec(memory_space=pltpu.VMEM)
    anywhere = pl.BlockSpec(memory_space=pl.ANY)
    dma = pltpu.SemaphoreType.DMA
    first = [
        pltpu.VMEM((8, STAT_ROWS, LANES), F32), dma((7,)), dma((7,)), pltpu.VMEM((16, LANES), BF),
        pltpu.VMEM((DIN, LANES), BF), dma((2,)), pltpu.VMEM(g1.shape, F32), dma((g1.shape[0],)),
        pltpu.VMEM((8, tokens.shape[0], LANES), BF), dma((16,)),
    ]
    grads = flat.reshape(2, 2, 2, -1, LANES)
    return pl.pallas_call(
        functools.partial(reduce_kernel, shard, bias_owner, bias_row),
        out_shape=[
            shaped((shard, LANES), BF), shaped((STAT_ROWS, LANES)), shaped(tokens.shape, BF),
            shaped(grads.shape, BF),
        ],
        in_specs=[anywhere] + [vmem] * 4 + [anywhere] + [vmem] * len(cross),
        out_specs=[vmem, vmem, vmem, anywhere],
        scratch_shapes=first
        + cross_accumulators(8 * tokens.shape[0])
        + small_buffers()
        + Reduction.scratch(shard),
        input_output_aliases={0: 3},
        compiler_params=pltpu.CompilerParams(
            collective_id=1, has_side_effects=True, vmem_limit_bytes=56 * MIB
        ),
    )(grads, tokens, tok_normed, w_kv, tok_norm, g1, *cross)


def body(tokens, frame_ids, episodes, master, moment_one, moment_two, latent_grad):
    lat_count = lax.axis_size("lat")
    lat_index = lax.axis_index("lat")
    shard_len = master.shape[0]
    frame_total = episodes.shape[1]
    frames = frame_total // lat_count
    rows_total = frames * LAT
    total_keys = frame_ids.shape[1] * lat_count
    cap = total_keys // 8
    token_rows_count = total_keys // LANES

    reach = lat_count == 8 and lax.axis_size("kf") == 4
    shard_rows = shard_len // LANES
    master_rows = master.reshape(shard_rows, LANES)
    score_flops = rows_total * cap * LANES * 2
    select_flops = frames * cap * total_keys * LANES * 2
    if reach:
        (
            up_one, down_one, w_qkv, w_so, up_two, down_two,
            latent, norms, hid_bias, out_bias, w_q, w_o, w_kv, tok_norm, tok_normed, episode_rows, rank, counts,
            kvf, cross_out, cross_lse, hot_lanes, h1,
        ) = begin_all(master_rows, tokens[0], frame_ids.reshape(-1, LANES), episodes, frames, cap)
    else:
        own_episodes = lax.dynamic_slice_in_dim(episodes[0], lat_index * frames, frames, 0)
        episode_match = own_episodes[:, None] == jnp.arange(EPISODES, dtype=jnp.int32)[None, :]
        hot_lanes = jnp.broadcast_to(
            jnp.pad(episode_match.astype(F32), ((0, 0), (0, 16 - EPISODES)))[:, :, None], (frames, 16, LANES)
        )
        weights = split_flat(lax.all_gather(master.astype(BF), "lat", axis=0, tiled=True))
        norms = weights["lat_norms"].astype(F32)
        out_bias = weights["out_bias"].astype(F32)
        hid_bias = weights["hid_bias"].astype(F32)
        tok_norm = weights["tok_norm"].astype(F32)
        w_kv, w_qkv, w_so, latent = (weights[name] for name in ("w_kv", "w_qkv", "w_so", "latent"))
        up_one, up_two = weights["w_up"]
        down_one, down_two = weights["w_down"]
        frame_tag = lax.all_gather(frame_ids[0].astype(BF), "lat", axis=0, tiled=True).astype(jnp.int32)
        own_frames = lat_index * frames + jnp.arange(frames, dtype=jnp.int32)
        own_hit = frame_tag[None, :] == own_frames[:, None]
        rank = jnp.cumsum(own_hit.astype(jnp.int32), axis=1) - 1
        counts = jnp.broadcast_to(rank[:, -1][:, None, None] + 1, (frames, 8, LANES))
        rank = jnp.where(own_hit, rank, -1).reshape(frames, token_rows_count, LANES)
        tok_normed = layer_norm(tokens[0].astype(F32), tok_norm[0], tok_norm[1]).astype(BF)
        key_value = mm(tok_normed, w_kv).astype(BF)
        all_keys = lax.all_gather(key_value, "lat", axis=0, tiled=True)
        episode_rows = mm(episode_match.astype(BF), weights["episode"]).reshape(frames, 1, D)
        w_q = jnp.pad(weights["w_q"], ((0, 0), (0, LANES - CH)))
        w_o = jnp.pad(weights["w_o"], ((LANES - CH, 0), (0, 0)))
        h1, kvf, cross_out, cross_lse = call(
            cross_fwd_kernel,
            frames,
            [
                fixed(LAT, D), framed(1, D), fixed(8, D), fixed(D, LANES), fixed(LANES, D), fixed(4, D),
                fixed(total_keys, LANES), framed(token_rows_count, LANES), framed(8, LANES),
            ],
            [
                (rowed(LAT, D), shaped((rows_total, D))),
                (framed(cap, LANES), shaped((frames, cap, LANES), BF)),
                (rowed(LAT, LANES), shaped((rows_total, LANES), BF)),
                (framed(1, LAT), shaped((frames, 1, LAT))),
            ],
            (latent, episode_rows, norms, w_q, w_o, out_bias, all_keys, rank, counts),
            flops=2 * score_flops + select_flops,
            trans=rows_total * cap,
        )
    mlp_flops = 4 * rows_total * D * FF
    attn_flops = 4 * rows_total * LAT * D
    anywhere = pl.BlockSpec(memory_space=pl.ANY)
    token_count = frame_ids.shape[1]
    if reach:
        flat_shard, extra = shard_rows, token_count
        flat_shape = (lat_count * (shard_rows + extra), LANES)
        kv_rows = (shard_rows, token_count, shard_rows + extra)
        grad_in, grad_spec = latent_grad[0], anywhere
        latents_spec = (anywhere, shaped(latent_grad.shape[1:], BF))
        shared = [pltpu.VMEM((frames, LAT, D), BF)] * 2 + FrameExchange.scratch(frames)
    else:
        flat_shard, extra = NPARAM // LANES, 0
        flat_shape = (flat_shard + total_keys, LANES)
        kv_rows = (flat_shard, 512, 512)
        grad_in = lax.all_to_all(
            latent_grad[0], "lat", split_axis=0, concat_axis=1, tiled=True
        ).reshape(rows_total, D)
        grad_spec = rowed(LAT, D)
        latents_spec = (rowed(LAT, D), shaped((rows_total, D), BF))
        shared = []
    slab = D * FF // LANES
    h2, qkv, self_lse, mixed, act_one, slope_one, latents, g3, dhid_two, dnorm_two, dout_two, flat = call(
        functools.partial(forward_kernel, reach, flat_shard, extra, frames),
        frames,
        [
            rowed(LAT, D), grad_spec, fixed(8, D), fixed(2, FF), fixed(4, D), fixed(D, FF), fixed(FF, D),
        ]
        + [anywhere] * 4,
        [
            (anywhere, shaped((rows_total, D))),
            (anywhere, shaped((rows_total, 3 * D), BF)),
            (framed(HEADS, LAT), shaped((frames, HEADS, LAT))),
            (anywhere, shaped((rows_total, D), BF)),
            (anywhere, shaped((rows_total, FF), BF)),
            (anywhere, shaped((rows_total, FF), BF)),
            latents_spec,
            (rowed(LAT, D), shaped((rows_total, D))),
            (kept(1, FF), shaped((1, FF))),
            (kept(2, D), shaped((2, D))),
            (kept(1, D), shaped((1, D))),
            (anywhere, shaped(flat_shape, BF)),
        ],
        (h1, grad_in, norms, hid_bias, out_bias, up_one, down_one, w_qkv, w_so, up_two, down_two),
        flops=4 * mlp_flops + 4 * attn_flops,
        trans=4 * rows_total * FF,
        scratch=[
            pltpu.VMEM((LAT, FF), BF), pltpu.VMEM((LAT, FF), BF), pltpu.VMEM((D, FF), F32), pltpu.VMEM((FF, D), F32),
            pltpu.VMEM((2048, LANES), F32), pltpu.VMEM((2, slab, LANES), BF), pltpu.VMEM((LAT, D), BF),
            pltpu.VMEM((D, LAT), F32), pltpu.VMEM((LAT, D), F32), pltpu.SemaphoreType.DMA((2, 16)),
            pltpu.VMEM((D, 3 * D), BF), pltpu.VMEM((D, D), BF), pltpu.VMEM((D, FF), BF), pltpu.VMEM((FF, D), BF),
            pltpu.SemaphoreType.DMA((4,)),
        ]
        + flow_slots((LAT, D), F32)
        + flow_slots((LAT, 3 * D), BF)
        + flow_slots((LAT, D), BF)
        + flow_slots((LAT, FF), BF)
        + flow_slots((LAT, FF), BF)
        + shared,
        limit=62,
        collective=4 if reach else None,
    )
    g1, dhid_one, dnorm_sa, dnorm_one, dout_so, dout_one, latents, flat = call(
        functools.partial(backward_kernel, flat_shard, extra, frames),
        frames,
        [
            rowed(LAT, 3 * D), framed(HEADS, LAT), rowed(LAT, D), rowed(LAT, D), anywhere, anywhere, anywhere, anywhere,
            fixed(8, D), fixed(D, D),
        ]
        + [anywhere] * 5,
        [
            (rowed(LAT, D), shaped((rows_total, D))),
            (kept(1, FF), shaped((1, FF))),
            (kept(2, D), shaped((2, D))),
            (kept(2, D), shaped((2, D))),
            (kept(1, D), shaped((1, D))),
            (kept(1, D), shaped((1, D))),
            (anywhere, shaped(latents.shape, BF)),
            (anywhere, shaped(flat_shape, BF)),
        ],
        (
            qkv, self_lse, mixed, g3, h2, h1, act_one, slope_one, norms, w_so, w_qkv, up_one, down_one, latents, flat,
        ),
        flops=2 * mlp_flops + 10 * attn_flops,
        trans=rows_total * LAT * HEADS,
        scratch=[
            pltpu.VMEM((LAT, 3 * D), BF), pltpu.VMEM((D, FF), F32), pltpu.VMEM((FF, D), F32),
            pltpu.VMEM((D, 3 * D), F32), pltpu.VMEM((D, D), F32),
            pltpu.VMEM((2048, LANES), F32), pltpu.VMEM((2, slab, LANES), BF), pltpu.VMEM((LAT, D), BF),
            pltpu.VMEM((LAT, D), BF), pltpu.VMEM((LAT, D), BF), pltpu.VMEM((LAT, D), F32),
            pltpu.SemaphoreType.DMA((2, 16)),
            pltpu.VMEM((D, 3 * D), BF), pltpu.VMEM((D, FF), BF), pltpu.VMEM((FF, D), BF),
            pltpu.SemaphoreType.DMA((3,)),
        ]
        + flow_slots((LAT, D), F32)
        + flow_slots((LAT, D), F32)
        + flow_slots((LAT, FF), BF)
        + flow_slots((LAT, FF), BF)
        + [pltpu.VMEM(latents.shape, BF), pltpu.SemaphoreType.DMA((2,))],
        limit=60,
        aliases={14: 7},
    )
    if reach:
        latents_out = latents[None]
    else:
        latents_out = lax.all_to_all(
            latents.reshape(frames, LAT, D), "lat", split_axis=1, concat_axis=0, tiled=True
        )[None]
    cross = (
        kvf, cross_out, cross_lse, rank, counts, episode_rows, hot_lanes, latent, norms, w_q, w_o,
        dnorm_one, dnorm_sa, dnorm_two, dhid_one, dhid_two, dout_one, dout_so, dout_two,
    )
    layout = param_layout()
    starts, ends, offset, bias_offset = [], [], 0, 0
    for name, shape in layout:
        if name == "hid_bias":
            bias_offset = offset
        starts.append(offset // LANES)
        offset += math.prod(shape)
        ends.append(offset // LANES)
    pad = [0] * (16 - len(layout))
    starts, ends = (np.tile(np.array(v + pad, np.int32)[:, None], (1, LANES)) for v in (starts, ends))
    opt_rows = shard_rows // 2 if shard_rows % 16 == 0 else shard_rows
    opt_steps = shard_rows // opt_rows
    base = (lat_index * shard_rows).astype(jnp.int32).reshape(1)
    smem = pl.BlockSpec(memory_space=pltpu.SMEM)
    flat_rows = (shard_rows, LANES)
    bias_owner, bias_at = divmod(bias_offset, shard_len)
    if reach:
        summed, stats, token_grad, unused = reduce_all(
            flat, shard_rows, bias_owner, bias_at // LANES, tokens[0], tok_normed, w_kv, tok_norm,
            g1.reshape(frames, LAT, D), cross,
        )
    else:
        (flat,) = call(
            functools.partial(cross_bwd_kernel, kv_rows),
            frames,
            [
                rowed(LAT, D), framed(cap, LANES), rowed(LAT, LANES), framed(1, LAT), framed(token_rows_count, LANES),
                framed(8, LANES), framed(1, D), framed(16, LANES), fixed(LAT, D), fixed(8, D), fixed(D, LANES),
                fixed(LANES, D),
            ]
            + [fixed(*part.shape) for part in cross[11:]]
            + [anywhere],
            [(anywhere, shaped(flat_shape, BF))],
            (g1,) + cross + (flat,),
            flops=6 * score_flops,
            trans=rows_total * cap,
            scratch=cross_accumulators(total_keys)
            + small_buffers()
            + [pltpu.VMEM((kv_rows[1], LANES), BF), pltpu.SemaphoreType.DMA((8,))],
            aliases={20: 0},
        )
        grad_kv = lax.psum_scatter(flat[flat_shard:], "lat", scatter_dimension=0, tiled=True)
        flat = flat[:flat_shard]
        grad_w_kv = t_mm(tok_normed, grad_kv)
        grad_tok_normed = mm_t(grad_kv, w_kv)
        unused, token_pull = jax.vjp(layer_norm, tokens[0].astype(F32), tok_norm[0], tok_norm[1])
        grad_tokens, grad_tok_gain, grad_tok_bias = token_pull(grad_tok_normed)
        token_grad = grad_tokens.astype(BF)
        flat_at = flat_rows_of()
        tok_norm_grad = jnp.stack([grad_tok_gain, grad_tok_bias]).reshape(-1, LANES).astype(BF)
        flat = lax.dynamic_update_slice(flat, tok_norm_grad, (flat_at["tok_norm"], 0))
        flat = lax.dynamic_update_slice(flat, grad_w_kv.astype(BF), (flat_at["w_kv"], 0))
        local_flat = flat.reshape(-1)
        summed = lax.psum_scatter(local_flat, "lat", scatter_dimension=0, tiled=True)
        summed = lax.psum(summed, "kf").reshape(flat_rows)
        bias_rows = summed[bias_at // LANES : bias_at // LANES + 2 * FF // LANES].astype(F32)
        bias_rows = jnp.where(lat_index == bias_owner, bias_rows, 0.0)
        grad_sq = jnp.sum(jnp.square(summed.astype(F32)), axis=0, keepdims=True)
        stats = lax.psum(jnp.concatenate([grad_sq, jnp.zeros((7, LANES), F32), bias_rows]), "lat")
    grad_shard, lamb_update, new_one, new_two, norms_sq, bias_grad, token_grad = call(
        lamb_kernel,
        opt_steps,
        [smem, fixed(STAT_ROWS, LANES), fixed(16, LANES), fixed(16, LANES)] + [rowed(opt_rows, LANES)] * 4 + [fixed(*token_grad.shape)],
        [(rowed(opt_rows, LANES), shaped(flat_rows))] * 4
        + [(kept(16, 2 * LANES), shaped((16, 2 * LANES))), (kept(2, FF), shaped((2, FF)))]
        + [(kept(*token_grad.shape), shaped(token_grad.shape, BF))],
        (
            base, stats, starts, ends, summed, master_rows,
            moment_one.reshape(flat_rows), moment_two.reshape(flat_rows), token_grad,
        ),
    )
    if reach:
        vmem = pl.BlockSpec(memory_space=pltpu.VMEM)
        trust = pl.pallas_call(
            trust_kernel,
            out_shape=shaped((1, len(layout))),
            in_specs=[vmem],
            out_specs=vmem,
            scratch_shapes=[
                pltpu.VMEM((8, 16, 2 * LANES), F32),
                pltpu.SemaphoreType.DMA((7,)),
                pltpu.SemaphoreType.DMA((7,)),
            ],
            compiler_params=pltpu.CompilerParams(collective_id=2, has_side_effects=True),
        )(norms_sq).reshape(-1)
    else:
        sums = lax.psum(jnp.sum(norms_sq.reshape(16, 2, LANES), axis=2), "lat")[: len(layout)]
        trust = jnp.sqrt(sums[:, 1]) / (jnp.sqrt(sums[:, 0]) + 1e-06)
    return (
        latents_out,
        token_grad[None],
        grad_shard.reshape(-1),
        lamb_update.reshape(-1),
        new_one.reshape(-1),
        new_two.reshape(-1),
        trust,
        bias_grad,
    )


def solution(mesh):
    return jax.shard_map(
        body,
        mesh=mesh,
        in_specs=(
            P("kf", "lat", None),
            P("kf", "lat"),
            P("kf", None),
            P("lat"),
            P("lat"),
            P("lat"),
            P("kf", None, "lat", None),
        ),
        out_specs=(
            P("kf", None, "lat", None),
            P("kf", "lat", None),
            P("lat"),
            P("lat"),
            P("lat"),
            P("lat"),
            P(),
            P(),
        ),
        check_vma=False,
    )
```

```python
import functools
import math

import jax
import jax.numpy as jnp
import numpy as np
from jax import lax
from jax.experimental import pallas as pl
from jax.experimental.pallas import tpu as pltpu
from jax.sharding import PartitionSpec as P

DIN = 256
D = 512
LAT = 512
CH = 64
HEADS = 8
HEAD_DIM = 64
FF = 2048
FRAMES = 32
EPISODES = 11
NPARAM = 5619712
LANES = 128

norm_eps = 1e-05
masked_fill = -1e30
beta_one = 0.9
beta_two = 0.999
adam_eps = 1e-06
decay_rate = 0.01
clip_fraction = 0.5
lamb_step = 10.0

BF = jnp.bfloat16
F32 = jnp.float32
MIB = 1024 * 1024


def param_layout():
    return [
        ("latent", (LAT, D)),
        ("episode", (EPISODES, D)),
        ("tok_norm", (2, DIN)),
        ("lat_norms", (8, D)),
        ("w_kv", (DIN, 2 * CH)),
        ("w_q", (D, CH)),
        ("w_o", (CH, D)),
        ("w_qkv", (D, 3 * D)),
        ("w_so", (D, D)),
        ("w_up", (2, D, FF)),
        ("w_down", (2, FF, D)),
        ("hid_bias", (2, FF)),
        ("out_bias", (4, D)),
    ]


def split_flat(flat_vector):
    pieces = {}
    offset = 0
    for tensor_name, tensor_shape in param_layout():
        entries = math.prod(tensor_shape)
        pieces[tensor_name] = flat_vector[offset : offset + entries].reshape(tensor_shape)
        offset += entries
    return pieces


def layer_norm(inputs, norm_gain, norm_bias):
    row_mean = jnp.mean(inputs, axis=-1, keepdims=True)
    centered = inputs - row_mean
    row_var = jnp.mean(centered * centered, axis=-1, keepdims=True)
    return centered * lax.rsqrt(row_var + norm_eps) * norm_gain + norm_bias


def mm(left, right):
    return jnp.dot(left, right, preferred_element_type=F32)


def mm_t(left, right):
    return lax.dot_general(left, right, (((1,), (1,)), ((), ())), preferred_element_type=F32)


def t_mm(left, right):
    return lax.dot_general(left, right, (((0,), (0,)), ((), ())), preferred_element_type=F32)


def norm_stats(rows):
    mean = jnp.mean(rows, axis=-1, keepdims=True)
    centered = rows - mean
    var = jnp.mean(centered * centered, axis=-1, keepdims=True)
    rstd = lax.rsqrt(var + norm_eps)
    return centered * rstd, rstd


def norm_back(grad, xhat, rstd, gain):
    dxh = grad * gain
    first = jnp.mean(dxh, axis=-1, keepdims=True)
    second = jnp.mean(dxh * xhat, axis=-1, keepdims=True)
    return rstd * (dxh - first - xhat * second)


def col_sum(values):
    return jnp.sum(values, axis=0, keepdims=True)


def gelu_pair(x):
    cdf = 0.5 + 0.5 * lax.erf(x * (1.0 / math.sqrt(2.0)))
    density = jnp.exp(x * x * -0.5) * (1.0 / math.sqrt(2.0 * math.pi))
    return x * cdf, cdf + x * density


def accumulate(first, ref, value):
    @pl.when(first)
    def _():
        ref[...] = value

    @pl.when(jnp.logical_not(first))
    def _():
        ref[...] += value


def lane_half(shape, half):
    lane = lax.broadcasted_iota(jnp.int32, shape, 1)
    return (lane >= half * HEAD_DIM) & (lane < (half + 1) * HEAD_DIM)


def keep_half(values, half):
    return jnp.where(lane_half(values.shape, half), values, jnp.zeros_like(values))


def by_head(values):
    return jnp.concatenate([keep_half(values, h) for h in range(values.shape[1] // HEAD_DIM)], axis=0)


def select_tokens(rank_rows, cap):
    slot = lax.broadcasted_iota(jnp.int32, (cap, LANES), 0)
    parts = []
    for r in range(rank_rows.shape[0]):
        hit = slot == rank_rows[r : r + 1, :]
        parts.append(jnp.where(hit, 1.0, 0.0).astype(BF))
    return jnp.concatenate(parts, axis=1)


def cross_scores(kvf, queries_scaled, count):
    scores = mm_t(kvf, queries_scaled)
    slot = lax.broadcasted_iota(jnp.int32, scores.shape, 0)
    return jnp.where(slot < count, scores, masked_fill)


def cross_attend(start, norms, w_q, kvf, count):
    xhat, unused = norm_stats(start)
    query_in = (xhat * norms[0:1, :] + norms[1:2, :]).astype(BF)
    queries = mm(query_in, w_q[...]).astype(BF) * jnp.asarray(0.125, BF)
    scores = cross_scores(kvf, queries, count)
    top = jnp.max(scores, axis=0, keepdims=True)
    terms = jnp.exp(scores - top)
    total = jnp.sum(terms, axis=0, keepdims=True)
    prob = (terms * (1.0 / total)).astype(BF)
    return t_mm(kvf, prob).T.astype(BF), top + jnp.log(total)


def cross_fwd_kernel(latent, episode, norms, w_q, w_o, out_bias, kv, rank, count, h1, kvf_out, co_out, lse_out):
    cap = kvf_out.shape[1]
    start = latent[...].astype(F32) + episode[0]
    chunk = 8 * LANES
    chunks = kv.shape[0] // chunk

    def step(j, acc):
        sel = select_tokens(rank[0, pl.ds(pl.multiple_of(j * 8, 8), 8), :], cap)
        return acc + mm(sel, kv[pl.ds(pl.multiple_of(j * chunk, chunk), chunk), :])

    kvf = lax.fori_loop(0, chunks, step, jnp.zeros((cap, LANES), F32)).astype(BF)
    co, lse = cross_attend(start, norms, w_q, kvf, count[0, 0:1, 0:1])
    h1[...] = start + mm(co, w_o[...]) + out_bias[0:1, :]
    kvf_out[0] = kvf
    co_out[...] = co
    lse_out[0] = lse


def segment_hot(starts, ends, base, rows):
    row = lax.broadcasted_iota(jnp.int32, (16, rows), 1) + base
    return jnp.where((row >= starts[:, 0:1]) & (row < ends[:, 0:1]), 1.0, 0.0).astype(BF)


def segment_sums(hot, squares):
    high = squares.astype(BF)
    low = (squares - high.astype(F32)).astype(BF)
    return mm(hot, high) + mm(hot, low)


def lamb_kernel(
    base, stats, starts, ends, summed, master, one, two, token_in,
    grad_out, update_out, one_out, two_out, norms_sq, bias, token_out,
):
    i = pl.program_id(0)
    token_out[...] = token_in[...]
    rows = master.shape[0]
    hot = segment_hot(starts, ends, base[0] + i * rows, rows)
    total_sq = jnp.sum(stats[0:1, :], axis=1, keepdims=True)
    clip = jnp.minimum(1.0, clip_fraction * math.sqrt(NPARAM) / (jnp.sqrt(total_sq) + 1e-06))
    grad = summed[...].astype(F32)
    grad_out[...] = grad
    clipped = clip * grad
    new_one = beta_one * one[...] + (1.0 - beta_one) * clipped
    new_two = beta_two * two[...] + (1.0 - beta_two) * clipped * clipped
    one_out[...] = new_one
    two_out[...] = new_two
    first_hat = new_one * (1.0 / (1.0 - beta_one**lamb_step))
    second_hat = new_two * (1.0 / (1.0 - beta_two**lamb_step))
    update = first_hat / (jnp.sqrt(second_hat) + adam_eps) + decay_rate * master[...]
    update_out[...] = update
    accumulate(i == 0, norms_sq, segment_sums(hot, jnp.concatenate([update * update, master[...] * master[...]], axis=1)))
    for j in range(2 * FF // LANES):
        r, c = divmod(j, FF // LANES)
        bias[r : r + 1, c * LANES : (c + 1) * LANES] = stats[8 + j : 9 + j, :]


BATCH = 256
HALF = 128
QUARTER = 64
MESH = pl.DeviceIdType.MESH


class Place:
    def __init__(self):
        self.z = lax.axis_index("kf")
        self.me = lax.axis_index("lat")
        self.core = lax.rem(self.me, 2)
        self.x = lax.rem(self.me // 2, 2)
        self.y = self.me // 4
        self.z_low = lax.rem(self.z, 2)
        self.z_high = self.z // 2
        self.sibling = (self.z, self.me + 1 - 2 * self.core)
        self.x_side = (self.z, self.me + 2 - 4 * self.x)
        self.y_side = (self.z, self.me + 4 - 8 * self.y)
        self.z_near = (self.z + 1 - 2 * self.z_low, self.me)
        self.z_far = (self.z + 2 - 4 * self.z_high, self.me)

    def z_other(self, step):
        return (lax.rem(self.z + step, 4), self.me)

    def lat_other(self, step):
        return (self.z, lax.rem(self.me + step, 8))


def remote(src, dst, send, recv, device):
    return pltpu.make_async_remote_copy(
        src_ref=src, dst_ref=dst, send_sem=send, recv_sem=recv, device_id=device, device_id_type=MESH
    )


def greet(devices):
    barrier = pltpu.get_barrier_semaphore()
    for device in devices:
        pl.semaphore_signal(barrier, inc=1, device_id=device, device_id_type=MESH)


def met(devices):
    pl.semaphore_wait(pltpu.get_barrier_semaphore(), len(devices))


def added(left, right):
    return (left.astype(F32) + right.astype(F32)).astype(BF)


class Reduction:
    lags = (0, 1, 3, 5, 7, 9, 11)
    plane = 2

    def __init__(self, place, shard, grads, out, bufs, sems):
        self.p = place
        self.grads = grads
        self.out = out
        self.own, self.rc, self.r1, self.r2, self.r3, self.r4, self.res = bufs
        self.own_sem, self.send, self.rc_sem, self.r1_sem, self.r2_sem, self.r3_sem, self.r4_sem, self.res_sem = sems
        self.shard = shard
        self.full = pl.cdiv(shard, BATCH)
        self.batches = self.full + self.plane
        self.back = self.full * BATCH - shard
        self.held = flat_rows_of()["tok_norm"] // BATCH
        self.early = self.full - 1 - (self.held + 4)

    @staticmethod
    def scratch(shard):
        n = pl.cdiv(shard, BATCH) + Reduction.plane
        bufs = [
            pltpu.VMEM((2, 2, 2, BATCH, LANES), BF),
            pltpu.VMEM((n, 2, 2, BATCH, LANES), BF),
            pltpu.VMEM((n, 2, 2, HALF, LANES), BF),
            pltpu.VMEM((n, 2, HALF, LANES), BF),
            pltpu.VMEM((n, HALF, LANES), BF),
            pltpu.VMEM((n, QUARTER, LANES), BF),
            pltpu.VMEM((n, BATCH, LANES), BF),
        ]
        dma = pltpu.SemaphoreType.DMA
        sems = [dma((2,)), dma((10, 4)), dma((n,)), dma((n, 2)), dma((n, 2)), dma((n,)), dma((n,)), dma((n, 3))]
        return bufs + sems

    def from_on(self, i, first):
        return (i + 64 - first) // 64

    def row(self, i):
        n, held = self.full, self.held
        on = functools.partial(self.from_on, i)
        keys = on(self.early) - on(self.early + 2)
        shift = held + 4 + on(self.early + 2) * (-2) + on(self.early + 3) * (-n)
        shift = shift + on(self.early + 3 + held) * 2 + on(self.early + 5 + held) * (-4)
        b = i + shift
        row = keys * (self.shard + (i - self.early) * BATCH)
        row = row + (1 - keys) * (b * BATCH - (b // (n - 1)) * self.back)
        return pl.multiple_of(row, 16)

    def is_keys(self, i):
        return (i >= self.early) & (i < self.early + self.plane)

    def own_copy(self, i):
        slot = lax.rem(i, 2)
        src = self.grads.at[:, :, self.p.core, pl.ds(self.row(i), BATCH), :]
        return pltpu.make_async_copy(src, self.own.at[slot], self.own_sem.at[slot])

    def copies(self, stage, i):
        p, slot = self.p, lax.rem(i, 4)
        if stage == 0:
            src = self.grads.at[:, :, 1 - p.core, pl.ds(self.row(i), BATCH), :]
            return [remote(src, self.rc.at[i], self.send.at[0, slot], self.rc_sem.at[i], p.sibling)]
        if stage == 1:
            to_x = self.rc.at[i, :, 1 - p.x, pl.ds(0, HALF), :]
            to_y = self.rc.at[i, 1 - p.y, :, pl.ds(HALF, HALF), :]
            return [
                remote(to_x, self.r1.at[i, 0], self.send.at[1, slot], self.r1_sem.at[i, 0], p.x_side),
                remote(to_y, self.r1.at[i, 1], self.send.at[2, slot], self.r1_sem.at[i, 1], p.y_side),
            ]
        if stage == 2:
            to_y = self.r1.at[i, 0, 1 - p.y]
            to_x = self.r1.at[i, 1, 1 - p.x]
            return [
                remote(to_y, self.r2.at[i, 0], self.send.at[3, slot], self.r2_sem.at[i, 0], p.y_side),
                remote(to_x, self.r2.at[i, 1], self.send.at[4, slot], self.r2_sem.at[i, 1], p.x_side),
            ]
        if stage == 3:
            src = self.r2.at[i, 1 - p.z_low]
            return [remote(src, self.r3.at[i], self.send.at[5, slot], self.r3_sem.at[i], p.z_near)]
        if stage == 4:
            src = self.r3.at[i, pl.ds(pl.multiple_of((1 - p.z_high) * QUARTER, QUARTER), QUARTER), :]
            return [remote(src, self.r4.at[i], self.send.at[6, slot], self.r4_sem.at[i], p.z_far)]
        mine = self.res.at[i, pl.ds(pl.multiple_of(p.z_low * HALF + p.z_high * QUARTER, QUARTER), QUARTER), :]
        return [
            remote(mine, mine, self.send.at[6 + d, slot], self.res_sem.at[i, d - 1], p.z_other(d))
            for d in (1, 2, 3)
        ]

    def launch(self, stage, i):
        before = i - 4
        if stage >= 3:
            before = before - 4 * (self.from_on(before, self.early) - self.from_on(before, self.early + self.plane))

        @pl.when(i >= 4)
        def _():
            for copy in self.copies(stage, before):
                copy.wait_send()

        for copy in self.copies(stage, i):
            copy.start()

    def landed(self, stage, i):
        for copy in self.copies(stage, i):
            copy.wait_recv()

    def work(self, stage, i):
        p = self.p
        if stage == 0:
            self.own_copy(i).start()
        elif stage == 1:
            self.landed(0, i)
            self.own_copy(i).wait()
            self.rc[i] = added(self.rc[i], self.own[lax.rem(i, 2)])
        elif stage == 2:
            self.landed(1, i)
            self.r1[i, 0] = added(self.r1[i, 0], self.rc[i, :, p.x, 0:HALF, :])
            self.r1[i, 1] = added(self.r1[i, 1], self.rc[i, p.y, :, HALF:BATCH, :])
        elif stage == 3:
            self.landed(2, i)
            self.r2[i, 0] = added(self.r2[i, 0], self.r1[i, 0, p.y])
            self.r2[i, 1] = added(self.r2[i, 1], self.r1[i, 1, p.x])
        elif stage == 4:
            self.landed(3, i)
            self.r3[i] = added(self.r3[i], self.r2[i, p.z_low])
        elif stage == 5:
            self.landed(4, i)
            part = self.r3[i, pl.ds(pl.multiple_of(p.z_high * QUARTER, QUARTER), QUARTER), :]
            at = pl.multiple_of(p.z_low * HALF + p.z_high * QUARTER, QUARTER)
            self.res[i, pl.ds(at, QUARTER), :] = added(self.r4[i], part)
        else:
            self.landed(5, i)
            self.out[pl.ds(self.row(i), BATCH), :] = self.res[i]
        if stage == 3:
            pl.when(jnp.logical_not(self.is_keys(i)))(lambda: self.launch(stage, i))
        elif stage < 6:
            self.launch(stage, i)

    def tick(self, t):
        for stage, lag in enumerate(self.lags):
            i = t - lag

            inside = (i >= 0) & (i < self.batches)

            @pl.when(inside if stage < 4 else inside & jnp.logical_not(self.is_keys(i)))
            def _(stage=stage, i=i):
                self.work(stage, i)

    def ticks(self):
        return self.batches + self.lags[-1]

    def finish(self):
        for stage in range(6):
            for back in range(4):
                for copy in self.copies(stage, self.batches - 4 + back):
                    copy.wait_send()

    def partners(self):
        p = self.p
        return [p.sibling, p.x_side, p.y_side] + [p.z_other(d) for d in (1, 2, 3)]


def share_all(place, block, send, recv):
    mine = block.at[place.me]
    copies = [
        remote(mine, mine, send.at[d - 1], recv.at[d - 1], place.lat_other(d)) for d in range(1, 8)
    ]
    for copy in copies:
        copy.start()
    for copy in copies:
        copy.wait()


STAT_ROWS = 40


def token_backward(grad_kv, tokens, tok_normed, w_kv, tok_norm, token_grad, kv_grad, edge):
    kv_grad[...] = t_mm(tok_normed[...], grad_kv).astype(BF)
    grad = mm_t(grad_kv, w_kv[...])
    xhat, rstd = norm_stats(tokens[...].astype(F32))
    token_grad[...] = norm_back(grad, xhat, rstd, tok_norm[0:1, :]).astype(BF)
    gain, bias = col_sum(grad * xhat), col_sum(grad)
    parts = [half[:, j * LANES : (j + 1) * LANES] for half in (gain, bias) for j in range(DIN // LANES)]
    keep = edge.shape[0] - len(parts)
    edge[...] = jnp.concatenate([edge[...].astype(F32)[0:keep, :]] + parts, axis=0).astype(BF)


def reduce_kernel(
    shard, bias_owner, bias_at, unused_flat, tokens, tok_normed, w_kv, tok_norm,
    g1, kvf, co, lse, rank, count, episode, hot, latent, norms, w_q, w_o,
    dnorm_one, dnorm_sa, dnorm_two, dhid_one, dhid_two, dout_one, dout_so, dout_two,
    summed, stats, token_grad, grads, *scratch,
):
    place = Place()
    block, block_send, block_recv, edge, kv_grad, edge_sem, g1_held, g1_sem, kv_low, kv_sem = scratch[:10]
    accs, (stage, low, latent_low), engine = scratch[10:17], scratch[17:20], scratch[20:]
    acc_latent, acc_q, acc_o, acc_episode, dnorm, dout, dkv_t = accs
    frames = kvf.shape[0]
    red = Reduction(place, shard, grads, summed, engine[:7], engine[7:])
    frame_copies = [pltpu.make_async_copy(g1.at[f], g1_held.at[f], g1_sem.at[f]) for f in range(frames)]
    for copy in frame_copies:
        copy.start()
    partners = [place.lat_other(d) for d in range(1, 8)] + [place.z_other(d) for d in (1, 2, 3)]
    greet(partners)
    for ref in accs:
        ref[...] = jnp.zeros_like(ref)
    met(partners)

    def run(first, last):
        lax.fori_loop(first, last, lambda t, c: (red.tick(t), c)[1], 0)

    def frame(f, carry):
        red.tick(2 * f)
        pltpu.make_async_copy(g1.at[f], g1_held.at[f], g1_sem.at[f]).wait()
        rows = pl.ds(pl.multiple_of(f * LAT, LAT), LAT)
        cross_back_frame(
            g1_held[f], kvf[f], co[rows, :], lse[f], rank.at[f], count[f, 0:1, 0:1], episode[f], hot[f, :, 0:1],
            latent, norms, w_q, w_o, *accs, pause=lambda: red.tick(2 * f + 1),
        )
        return carry

    lax.fori_loop(0, frames, frame, 0)
    run(2 * frames, red.early)
    at = flat_rows_of()
    copies = []

    def put(source, row):
        owner, local = row if isinstance(row, tuple) else divmod(row, shard)
        dst = grads.at[owner // 4, owner // 2 % 2, owner % 2, pl.ds(local, source.shape[0]), :]
        copies.append(pltpu.make_async_copy(source, dst, kv_sem.at[len(copies)]))
        copies[-1].start()

    write_small(
        put, stage, low, latent_low, acc_latent, acc_q, acc_o, acc_episode,
        stacked(dnorm, dnorm_one, dnorm_sa, dnorm_two), stacked(dhid_one, dhid_two),
        stacked(dout, dout_one, dout_so, dout_two),
    )
    edge_row = at["tok_norm"] // 16 * 16
    edge[...] = low[0, edge_row - at["episode"] : edge_row - at["episode"] + 16, :]
    count_kv = tokens.shape[0]
    for j in range(8):
        kv_low[j] = dkv_t[:, j * count_kv : (j + 1) * count_kv].T
        put(kv_low.at[j], (j, shard))
    for copy in copies:
        copy.wait()
    ready = red.early + red.lags[3] + red.plane
    run(red.early, ready)
    grad_kv = jnp.concatenate([red.r2[red.early + i, h] for i in range(red.plane) for h in range(2)], axis=0)
    token_backward(grad_kv, tokens, tok_normed, w_kv, tok_norm, token_grad, kv_grad, edge)
    writes = [
        pltpu.make_async_copy(edge, grads.at[0, 0, 0, pl.ds(edge_row, 16), :], edge_sem.at[0]),
        pltpu.make_async_copy(kv_grad, grads.at[0, 0, 0, pl.ds(at["w_kv"], DIN), :], edge_sem.at[1]),
    ]
    for copy in writes:
        copy.start()
    run(ready, ready + 2)
    for copy in writes:
        copy.wait()
    run(ready + 2, red.ticks())
    grad_sq = jnp.zeros((1, LANES), F32)
    step = 784
    for j in range(shard // step):
        part = summed[j * step : (j + 1) * step, :].astype(F32)
        grad_sq = grad_sq + col_sum(part * part)
    bias = summed[bias_at : bias_at + 2 * FF // LANES, :].astype(F32)
    bias = jnp.where(place.me == bias_owner, bias, 0.0)
    head = jnp.concatenate([grad_sq, jnp.zeros((7, LANES), F32), bias], axis=0)
    block[pl.ds(place.me, 1)] = head[None]
    share_all(place, block, block_send, block_recv)
    total = block[0]
    for s in range(1, 8):
        total = total + block[s]
    stats[...] = total
    red.finish()


def trust_kernel(norms_sq, trust, block, send, recv):
    place = Place()
    partners = [place.lat_other(d) for d in range(1, 8)]
    greet(partners)
    block[pl.ds(place.me, 1)] = norms_sq[...][None]
    met(partners)
    share_all(place, block, send, recv)
    total = block[0]
    for s in range(1, 8):
        total = total + block[s]
    update_sq = jnp.sum(total[:, 0:LANES].T, axis=0, keepdims=True)
    weight_sq = jnp.sum(total[:, LANES : 2 * LANES].T, axis=0, keepdims=True)
    ratio = jnp.sqrt(weight_sq) / (jnp.sqrt(update_sq) + 1e-06)
    trust[...] = ratio[:, 0 : trust.shape[1]]


def relayout(whole, row, stage, dst, rows, cols):
    wide = cols // LANES
    block = min(rows, 2048 // wide // 128 * 128)

    def step(i, carry):
        at = pl.multiple_of(row + i * (block * wide), 16)
        stage[0 : block * wide, :] = whole[pl.ds(at, block * wide), :].astype(F32)
        for j in range(wide):
            part = stage[pl.ds(j, block, stride=wide), :]
            dst[pl.ds(pl.multiple_of(i * block, 16), block), j * LANES : (j + 1) * LANES] = part.astype(BF)
        return carry

    lax.fori_loop(0, rows // block, step, 0)


def small_matrix(whole, row, stage, rows, cols):
    wide = cols // LANES
    stage[0 : rows * wide, :] = whole[row : row + rows * wide, :].astype(F32)
    return jnp.concatenate([stage[pl.ds(j, rows, stride=wide), :] for j in range(wide)], axis=1)


class Gather:
    def __init__(self, place, whole, shard, chunks, send, recv):
        self.p, self.whole, self.shard, self.chunks, self.send, self.recv = place, whole, shard, chunks, send, recv
        p = place
        x_index, y_index = p.x_side[1], p.y_side[1]
        low = p.z_low
        self.first = x_index + low * (y_index - x_index)
        self.second = y_index + low * (x_index - y_index)
        self.diagonal = x_index + 4 - 8 * p.y

    def copy(self, kind, k):
        p = self.p
        block = (p.me, p.me, self.first, self.first, self.first, self.diagonal, self.second)[kind]
        target = (
            (p.z, self.first), p.sibling, (p.z, self.second), p.z_near, p.sibling, p.sibling, p.sibling
        )[kind]
        row, count = self.chunks[k]
        ref = self.whole.at[pl.ds(pl.multiple_of(block * self.shard + row, 16), count), :]
        return remote(ref, ref, self.send.at[kind, k], self.recv.at[kind, k], target)

    def play(self, *events):
        for event in events:
            kind, k = event[0], int(event[1:])
            if kind == "a":
                self.copy(0, k).start()
                self.copy(1, k).start()
            elif kind == "b":
                self.copy(0, k).wait_recv()
                for way in (2, 3, 4):
                    self.copy(way, k).start()
            elif kind == "c":
                for arrived, onward in ((2, 5), (3, 6)):
                    self.copy(arrived, k).wait_recv()
                    self.copy(onward, k).start()
            else:
                for way in (1, 4, 5, 6):
                    self.copy(way, k).wait_recv()

    def finish(self):
        for k in range(len(self.chunks)):
            for kind in range(7):
                self.copy(kind, k).wait_send()


class KeyExchange:
    def __init__(self, place, keys, send, recv):
        self.p, self.keys, self.send, self.recv = place, keys, send, recv
        self.x_index, self.y_index = place.x_side[1], place.y_side[1]
        self.diagonal = self.x_index + 4 - 8 * place.y

    def copy(self, kind):
        p = self.p
        half = self.keys.shape[1] // 2
        low, high, full = pl.ds(0, half), pl.ds(half, half), pl.ds(0, 2 * half)
        block, rows, target = (
            (p.me, full, p.x_side), (p.me, full, p.y_side), (p.me, full, p.sibling),
            (self.x_index, low, p.y_side), (self.y_index, high, p.x_side),
            (self.x_index, full, p.sibling), (self.y_index, full, p.sibling), (self.diagonal, full, p.sibling),
        )[kind]
        ref = self.keys.at[block, rows, :]
        return remote(ref, ref, self.send.at[kind], self.recv.at[kind], target)

    def step(self, s):
        if s == 0:
            waits, starts = (), (0, 1, 2)
        elif s == 1:
            waits, starts = (0, 1), (3, 4, 5, 6)
        elif s == 2:
            waits, starts = (3, 4), (7,)
        else:
            waits, starts = (2, 5, 6, 7), ()
        for kind in waits:
            self.copy(kind).wait_recv()
        for kind in starts:
            self.copy(kind).start()

    def finish(self):
        for kind in range(8):
            self.copy(kind).wait_send()


def flat_rows_of():
    rows, at = {}, 0
    for name, shape in param_layout():
        rows[name] = at // LANES
        at += math.prod(shape)
    return rows


def gather_chunks(shard):
    at = flat_rows_of()
    tail = at["hid_bias"] % shard // 16 * 16
    chunks = [(at["episode"], at["w_o"] - at["episode"]), (tail, shard - tail), (at["w_o"], at["w_qkv"] - at["w_o"])]
    for low, high in ((0, at["episode"]), (at["w_qkv"], tail)):
        while low < high:
            count = min(512, high - low)
            chunks.append((low, count))
            low += count
    return chunks


def begin_kernel(
    chunks, master, tokens, ids, episodes,
    up_one, down_one, qkv_w, so_w, up_two, down_two,
    latent, norms, hid_bias, out_bias, w_q, w_o, w_kv, tok_norm, tok_normed, episode, rank, counts,
    kvf_out, co_out, lse_out, hot_lanes, h1,
    whole, stage, all_ids, keys, m_up_one, m_down_one, m_qkv, m_so, m_up_two, m_down_two,
    episodes_held, h1_held, h1_sem, master_held, load_sem, send, recv, key_send, key_recv, id_send, id_recv, out_sem,
):
    place = Place()
    shard = master.shape[0]
    frames, cap = kvf_out.shape[0], kvf_out.shape[1]
    gather = Gather(place, whole, shard, chunks, send, recv)
    exchange = KeyExchange(place, keys, key_send, key_recv)
    at = flat_rows_of()
    loads = [
        pltpu.make_async_copy(master.at[pl.ds(row, count), :], master_held.at[pl.ds(row, count), :], load_sem.at[k])
        for k, (row, count) in enumerate(chunks)
    ]
    for copy in loads:
        copy.start()
    partners = [place.lat_other(d) for d in range(1, 8)] + [place.z_near]
    greet(partners)
    all_ids[pl.ds(place.me, 1)] = ids[...][None]
    id_copies = [
        remote(all_ids.at[place.me], all_ids.at[place.me], id_send.at[d - 1], id_recv.at[d - 1], place.lat_other(d))
        for d in range(1, 8)
    ]
    own_at = place.me * shard

    def cast(first, last):
        for k in range(first, last):
            row, count = chunks[k]
            loads[k].wait()
            at_row = pl.multiple_of(own_at + row, 16)
            whole[pl.ds(at_row, count), :] = master_held[row : row + count, :].astype(BF)

    cast(0, 5)
    met(partners)
    for copy in id_copies:
        copy.start()
    gather.play("a0", "a1", "a2", "a3", "a4")
    cast(5, len(chunks))

    for copy in id_copies:
        copy.wait_recv()
    tags = jnp.concatenate([all_ids[s] for s in range(8)], axis=0)
    low = lax.broadcasted_iota(jnp.int32, (LANES, LANES), 0)
    high = lax.broadcasted_iota(jnp.int32, (LANES, LANES), 1)
    upto = jnp.where(low <= high, 1.0, 0.0).astype(BF)
    n = tags.shape[0]
    below = jnp.where(
        lax.broadcasted_iota(jnp.int32, (n, n), 1) < lax.broadcasted_iota(jnp.int32, (n, n), 0), 1.0, 0.0
    ).astype(BF)
    for f in range(frames):
        hit = tags == place.me * frames + f
        hit_low = jnp.where(hit, 1.0, 0.0).astype(BF)
        inside = mm(hit_low, upto)
        row_total = jnp.broadcast_to(inside[:, LANES - 1 : LANES], (n, LANES))
        before = mm(below, row_total.astype(BF))
        place_in = (inside + before).astype(jnp.int32) - 1
        rank[f] = jnp.where(hit, place_in, -1)
        total = jnp.sum(row_total[:, 0:1], axis=0, keepdims=True).astype(jnp.int32)
        counts[f] = jnp.broadcast_to(total, (8, LANES))
    gather.play("b0", "b1", "a5", "b2", "c0", "c1", "a6", "d0", "d1")

    pair = whole[at["tok_norm"] // 16 * 16 : at["lat_norms"], :].astype(F32)
    pair = pair[at["tok_norm"] % 16 : at["tok_norm"] % 16 + 4, :]
    tok_norm[...] = jnp.concatenate(
        [
            jnp.concatenate([pair[0:1], pair[1:2]], axis=1),
            jnp.concatenate([pair[2:3], pair[3:4]], axis=1),
        ],
        axis=0,
    )
    w_kv[...] = whole[at["w_kv"] : at["w_kv"] + DIN, :]
    xhat, unused = norm_stats(tokens[...].astype(F32))
    normed = (xhat * tok_norm[0:1, :] + tok_norm[1:2, :]).astype(BF)
    tok_normed[...] = normed
    keys[pl.ds(place.me, 1)] = mm(normed, w_kv[...]).astype(BF)[None]
    exchange.step(0)
    gather.play("a7", "a8", "b3", "c2")
    norms[...] = small_matrix(whole, at["lat_norms"], stage, 8, D)
    hid_bias[...] = small_matrix(whole, at["hid_bias"], stage, 2, FF)
    out_bias[...] = small_matrix(whole, at["out_bias"], stage, 4, D)
    mine = lax.broadcasted_iota(jnp.int32, (16, FRAMES), 0) + place.me * frames
    mine = mine == lax.broadcasted_iota(jnp.int32, (16, FRAMES), 1)
    own = jnp.sum(jnp.where(mine, episodes[...].astype(F32), 0.0), axis=1, keepdims=True)
    hot = jnp.where(lax.broadcasted_iota(jnp.int32, (16, 16), 1).astype(F32) == own, 1.0, 0.0).astype(BF)
    for f in range(frames):
        row = lax.broadcasted_iota(jnp.int32, (16, LANES), 0).astype(F32)
        hot_lanes[f] = jnp.where(row == own[f : f + 1, 0:1], 1.0, 0.0)
    episode_rows = mm(hot, small_matrix(whole, at["episode"], stage, 16, D).astype(BF))
    gather.play("b4", "c3", "d2", "b5", "c4", "d3", "b6")
    exchange.step(1)
    gather.play("a9", "a10", "c5", "d4", "c6", "d5")
    packed = whole[at["w_q"] : at["w_q"] + D // 2, :].astype(F32)
    stage[pl.ds(0, D // 2, stride=2), :] = packed
    stage[pl.ds(1, D // 2, stride=2), :] = pltpu.roll(packed, CH, 1)
    w_q[...] = keep_half(stage[0:D, :], 0).astype(BF)
    w_o[0:CH, :] = jnp.zeros((CH, D), BF)
    w_o[CH : 2 * CH, :] = small_matrix(whole, at["w_o"], stage, CH, D).astype(BF)
    exchange.step(2)
    gather.play("a11", "b7", "d6")
    exchange.step(3)
    relayout(whole, 0, stage, latent, LAT, D)

    chunk = 8 * LANES
    episodes_held[...] = episode_rows[0:8, :]
    before = [("b8",), ("b9", "d7"), ("b10", "d8"), ("b11", "d9")]
    midway = [("c7",), ("c8",), ("c9",), ("c10",)]

    def play(frame, parts):
        for step, events in enumerate(parts):
            pl.when(frame == step)(functools.partial(gather.play, *events))

    def attend(f, carry):
        play(f, before)
        row = episodes_held[pl.ds(f, 1), :]
        start = latent[...].astype(F32) + row
        episode[pl.ds(f, 1)] = row[None]

        def pick(j, acc):
            sel = select_tokens(rank[f, pl.ds(pl.multiple_of(8 * j, 8), 8), :], cap)
            return acc + mm(sel, keys[pl.ds(2 * j, 2)].reshape(chunk, LANES))

        kvf = lax.fori_loop(0, n // 8, pick, jnp.zeros((cap, LANES), F32)).astype(BF)
        play(f, midway)
        co, lse = cross_attend(start, norms, w_q, kvf, counts[f, 0:1, 0:1])
        rows = pl.ds(pl.multiple_of(f * LAT, LAT), LAT)
        h1_held[f] = start + mm(co, w_o[...]) + out_bias[0:1, :]
        pltpu.make_async_copy(h1_held.at[f], h1.at[rows, :], h1_sem.at[f]).start()
        kvf_out[f] = kvf
        co_out[rows, :] = co
        lse_out[f] = lse
        return carry

    lax.fori_loop(0, frames, attend, 0)
    gather.play("c11", "d10", "d11")

    big = (
        (up_one, m_up_one, at["w_up"], D, FF),
        (down_one, m_down_one, at["w_down"], FF, D),
        (qkv_w, m_qkv, at["w_qkv"], D, 3 * D),
        (so_w, m_so, at["w_so"], D, D),
        (up_two, m_up_two, at["w_up"] + D * FF // LANES, D, FF),
        (down_two, m_down_two, at["w_down"] + D * FF // LANES, FF, D),
    )
    outs = []
    for j, (out, held, row, rows, cols) in enumerate(big):
        relayout(whole, row, stage, held, rows, cols)
        outs.append(pltpu.make_async_copy(held, out, out_sem.at[j]))
        outs[-1].start()
    for copy in outs:
        copy.wait()
    for f in range(frames):
        pltpu.make_async_copy(h1_held.at[f], h1.at[f * LAT : (f + 1) * LAT, :], h1_sem.at[f]).wait()
    for copy in id_copies:
        copy.wait_send()
    exchange.finish()
    gather.finish()


def begin_all(master_rows, token_rows, ids, episodes, frames, cap):
    shard = master_rows.shape[0]
    tokens = token_rows.shape[0]
    total = 8 * tokens
    chunks = gather_chunks(shard)
    vmem = pl.BlockSpec(memory_space=pltpu.VMEM)
    anywhere = pl.BlockSpec(memory_space=pl.ANY)
    matrices = [(D, FF), (FF, D), (D, 3 * D), (D, D), (D, FF), (FF, D)]
    dma = pltpu.SemaphoreType.DMA
    return pl.pallas_call(
        functools.partial(begin_kernel, chunks),
        out_shape=[shaped(m, BF) for m in matrices]
        + [
            shaped((LAT, D), BF),
            shaped((8, D)),
            shaped((2, FF)),
            shaped((4, D)),
            shaped((D, LANES), BF),
            shaped((LANES, D), BF),
            shaped((DIN, LANES), BF),
            shaped((2, DIN)),
            shaped((tokens, DIN), BF),
            shaped((frames, 1, D)),
            shaped((frames, total // LANES, LANES), jnp.int32),
            shaped((frames, 8, LANES), jnp.int32),
            shaped((frames, cap, LANES), BF),
            shaped((frames * LAT, LANES), BF),
            shaped((frames, 1, LAT)),
            shaped((frames, 16, LANES)),
            shaped((frames * LAT, D)),
        ],
        in_specs=[anywhere] + [vmem] * 3,
        out_specs=[anywhere] * 6 + [vmem] * 16 + [anywhere],
        scratch_shapes=[
            pltpu.VMEM((8 * shard, LANES), BF),
            pltpu.VMEM((2048, LANES), F32),
            pltpu.VMEM((8, tokens // LANES, LANES), jnp.int32),
            pltpu.VMEM((8, tokens, LANES), BF),
        ]
        + [pltpu.VMEM(m, BF) for m in matrices]
        + [
            pltpu.VMEM((8, D), F32),
            pltpu.VMEM((frames, LAT, D), F32),
            dma((frames,)),
            pltpu.VMEM((shard, LANES), F32),
            dma((len(chunks),)),
            dma((7, len(chunks))), dma((7, len(chunks))), dma((8,)), dma((8,)), dma((7,)), dma((7,)), dma((6,)),
        ],
        compiler_params=pltpu.CompilerParams(
            collective_id=3, has_side_effects=True, vmem_limit_bytes=56 * MIB
        ),
    )(master_rows, token_rows, ids, episodes)


FCHUNK = 1024


def to_flat(stage, matrix):
    rows, wide = matrix.shape[0], matrix.shape[1] // LANES
    for j in range(wide):
        stage[pl.ds(j, rows, stride=wide), :] = matrix[:, j * LANES : (j + 1) * LANES]
    return stage[0 : rows * wide, :]


def feed_forward(rows, gain, bias, up_bias, down_bias, w_up, w_down, act_ref, slope_ref, normed_ref, total_ref):
    xhat, rstd = norm_stats(rows)
    normed_ref[...] = (xhat * gain + bias).astype(BF)
    act, slope = gelu_pair(mm(normed_ref[...], w_up[...]) + up_bias[...])
    act = act.astype(BF)
    act_ref[...] = act
    slope_ref[...] = slope.astype(BF)
    total_ref[...] = rows + down_bias + mm(act, w_down[...])


def feed_back(grad_ref, normed_ref, xhat, rstd, gain, act, slope, w_up, w_down, acc_up, acc_down, dhid, dnorm, dout, work):
    work[...] = jnp.zeros(work.shape, F32)
    for c in range(FF // FCHUNK):
        at = slice(c * FCHUNK, (c + 1) * FCHUNK)
        dpre = (mm_t(grad_ref[...], w_down[at, :]) * slope[:, at].astype(F32)).astype(BF)
        dhid[:, at] += col_sum(dpre.astype(F32))
        work[...] += mm_t(dpre, w_up[:, at])
        acc_up[:, at] += t_mm(normed_ref[...], dpre)
        acc_down[at, :] += t_mm(act[:, at], grad_ref[...])
    grad_normed = work[...]
    dnorm[...] += jnp.concatenate([col_sum(grad_normed * xhat), col_sum(grad_normed)], axis=0)
    dout[...] += col_sum(grad_ref[...].astype(F32))
    return norm_back(grad_normed, xhat, rstd, gain)


def clear(first, refs):
    @pl.when(first)
    def _():
        for ref in refs:
            ref[...] = jnp.zeros_like(ref)


def flat_spans(row, count, shard, extra):
    spans, done = [], 0
    while done < count:
        part = min(count - done, shard - (row + done) % shard)
        spans.append((done, part, row + done + (row + done) // shard * extra))
        done += part
    return spans


def flatten(acc, stage, low, slot):
    wide = acc.shape[1] // LANES
    block = min(acc.shape[0], 2048 // wide // 128 * 128)
    span = block * wide

    def step(i, carry):
        part = acc[pl.ds(pl.multiple_of(i * block, block), block), :]
        for j in range(wide):
            stage[pl.ds(j, block, stride=wide), :] = part[:, j * LANES : (j + 1) * LANES]
        low[slot, pl.ds(pl.multiple_of(i * span, span), span), :] = stage[0:span, :].astype(BF)
        return carry

    lax.fori_loop(0, acc.shape[0] // block, step, 0)


def write_flat(flat, stage, low, pieces, sems, shard, extra):
    pending = {}
    for j, (acc, row) in enumerate(pieces):
        count = acc.shape[0] * acc.shape[1] // LANES
        slot = j % 2
        for copy in pending.get(slot, []):
            copy.wait()
        flatten(acc, stage, low, slot)
        pending[slot] = [
            pltpu.make_async_copy(low.at[slot, pl.ds(off, part), :], flat.at[pl.ds(at, part), :], sems.at[slot, k])
            for k, (off, part, at) in enumerate(flat_spans(row, count, shard, extra))
        ]
        for copy in pending[slot]:
            copy.start()
    for copies in pending.values():
        for copy in copies:
            copy.wait()


class FrameExchange:
    def __init__(self, place, source, grad, held, result, sems):
        self.p, self.source, self.grad, self.held, self.result = place, source, grad, held, result
        self.in_send, self.in_recv, self.out_send, self.out_recv, self.own_in, self.own_out = sems
        self.frames, self.rows = grad.shape[0], source.shape[1]

    @staticmethod
    def scratch(frames):
        dma = pltpu.SemaphoreType.DMA
        return [dma((frames, 7))] * 4 + [dma((frames,))] * 2

    def block(self, index):
        return pl.ds(pl.multiple_of(index * self.rows, 16), self.rows)

    def arriving(self, f, d):
        target = self.p.lat_other(d)
        src = self.source.at[target[1] * self.frames + f]
        dst = self.grad.at[f, self.block(self.p.me), :]
        return remote(src, dst, self.in_send.at[f, d - 1], self.in_recv.at[f, d - 1], target)

    def own_arriving(self, f):
        src = self.source.at[self.p.me * self.frames + f]
        return pltpu.make_async_copy(src, self.grad.at[f, self.block(self.p.me), :], self.own_in.at[f])

    def leaving(self, f, d):
        target = self.p.lat_other(d)
        src = self.held.at[f, self.block(target[1]), :]
        dst = self.result.at[self.p.me * self.frames + f]
        return remote(src, dst, self.out_send.at[f, d - 1], self.out_recv.at[f, d - 1], target)

    def own_leaving(self, f):
        dst = self.result.at[self.p.me * self.frames + f]
        return pltpu.make_async_copy(self.held.at[f, self.block(self.p.me), :], dst, self.own_out.at[f])

    def partners(self):
        return [self.p.lat_other(d) for d in range(1, 8)]

    def begin(self):
        met(self.partners())
        for f in range(self.frames):
            self.own_arriving(f).start()
            for d in range(1, 8):
                self.arriving(f, d).start()

    def await_frame(self, f):
        self.own_arriving(f).wait()
        for d in range(1, 8):
            self.arriving(f, d).wait_recv()

    def send_frame(self, f):
        self.own_leaving(f).start()
        for d in range(1, 8):
            self.leaving(f, d).start()

    def finish(self):
        def step(f, carry):
            self.own_leaving(f).wait()
            for d in range(1, 8):
                self.arriving(f, d).wait_send()
                self.leaving(f, d).wait()
            return carry

        lax.fori_loop(0, self.frames, step, 0)


class Flow:
    def __init__(self, step, steps, array, slots, sems):
        self.step, self.steps, self.array, self.slots, self.sems = step, steps, array, slots, sems
        self.rows = slots.shape[1]

    def here(self):
        return self.slots.at[lax.rem(self.step, 2)]

    def ends(self, step):
        slot = lax.rem(step, 2)
        rows = pl.ds(pl.multiple_of(step * self.rows, self.rows), self.rows)
        return self.array.at[rows, :], self.slots.at[slot], self.sems.at[slot]

    def load(self, step):
        outside, inside, sem = self.ends(step)
        return pltpu.make_async_copy(outside, inside, sem)

    def store(self, step):
        outside, inside, sem = self.ends(step)
        return pltpu.make_async_copy(inside, outside, sem)

    def fetch_ahead(self):
        pl.when(self.step == 0)(lambda: self.load(self.step).start())
        pl.when(self.step + 1 < self.steps)(lambda: self.load(self.step + 1).start())

    def arrived(self):
        self.load(self.step).wait()

    def free(self):
        pl.when(self.step >= 2)(lambda: self.store(self.step - 2).wait())

    def send(self):
        self.store(self.step).start()

    def drain(self):
        if self.steps > 1:
            self.store(self.step - 1).wait()
        self.store(self.step).wait()


def flow_slots(shape, dtype):
    return [pltpu.VMEM((2,) + shape, dtype), pltpu.SemaphoreType.DMA((2,))]


class Late:
    def __init__(self, step, sources, refs, sems):
        self.first = step == 0
        self.copies = [
            pltpu.make_async_copy(src, ref, sems.at[k]) for k, (src, ref) in enumerate(zip(sources, refs))
        ]

        @pl.when(self.first)
        def _():
            for copy in self.copies:
                copy.start()

    def need(self, *which):
        @pl.when(self.first)
        def _():
            for k in which:
                self.copies[k].wait()


def forward_kernel(
    reach, shard, extra, steps, h1, grad, norms, hid_bias, out_bias, up_one, down_one, *rest,
):
    forward_body(reach, shard, extra, steps, h1, grad, norms, hid_bias, out_bias, up_one, down_one, rest[:4], *rest[4:])


def forward_body(
    reach, shard, extra, steps, h1, grad, norms, hid_bias, out_bias, up_one, down_one, late_sources,
    h2_all, qkv_all, lse_out, mixed_all, act_all, slope_all, latents, g3, dhid, dnorm, dout, flat,
    act_two, slope_two, acc_up, acc_down, stage, low, normed, mixed_t, work, sems,
    w_qkv, w_so, up_two, down_two, late_sems,
    h2_slots, h2_sems, qkv_slots, qkv_sems, mixed_slots, mixed_sems, act_slots, act_sems, slope_slots, slope_sems, *shared,
):
    step = pl.program_id(0)
    late = Late(step, late_sources, (w_qkv, w_so, up_two, down_two), late_sems)
    flows = [
        Flow(step, steps, *parts)
        for parts in (
            (h2_all, h2_slots, h2_sems), (qkv_all, qkv_slots, qkv_sems), (mixed_all, mixed_slots, mixed_sems),
            (act_all, act_slots, act_sems), (slope_all, slope_slots, slope_sems),
        )
    ]
    for flow in flows:
        flow.free()
    h2_out, qkv, mixed_out, act_one, slope_one = (flow.here() for flow in flows)
    if reach:
        place = Place()
        traffic = FrameExchange(place, grad, shared[0], shared[1], latents, shared[2:])
        pl.when(step == 0)(lambda: greet(traffic.partners()))
        grad = shared[0].at[step]
    clear(step == 0, (acc_up, acc_down, dhid, dnorm, dout))
    feed_forward(
        h1[...], norms[2:3, :], norms[3:4, :], hid_bias.at[0:1], out_bias[1:2, :], up_one, down_one, act_one,
        slope_one, normed, h2_out,
    )
    xhat, unused = norm_stats(h2_out[...])
    normed[...] = (xhat * norms[4:5, :] + norms[5:6, :]).astype(BF)

    late.need(0)
    if reach:
        pl.when(step == 0)(traffic.begin)

    qkv[...] = mm(normed[...], w_qkv[...]).astype(BF)
    for k in (0, 1, 3, 4):
        flows[k].send()
    scale = jnp.asarray(0.125, BF)
    ones = jnp.ones((16, LAT), BF)
    group = 4
    width = group * HEAD_DIM
    for base in range(0, D, width):
        queries = by_head(qkv[:, base : base + width] * scale)
        value_t = qkv[:, 2 * D + base : 2 * D + base + width].T
        scores = mm_t(qkv[:, D + base : D + base + width], queries)
        top = jnp.max(scores, axis=0, keepdims=True)
        terms = jnp.exp(scores - top).astype(BF)
        for j in range(group):
            at = slice(j * LAT, (j + 1) * LAT)
            values = jnp.concatenate([value_t[j * HEAD_DIM : (j + 1) * HEAD_DIM, :], ones], axis=0)
            product = mm(values, terms[:, at])
            total = product[HEAD_DIM : HEAD_DIM + 1, :]
            head = base // HEAD_DIM + j
            lse_out[0, head : head + 1, :] = top[:, at] + jnp.log(total)
            mixed_t[head * HEAD_DIM : (head + 1) * HEAD_DIM, :] = product[0:HEAD_DIM, :] * (1.0 / total)
    late.need(1, 2, 3)
    mixed = mixed_t[...].T.astype(BF)
    mixed_out[...] = mixed
    flows[2].send()
    h3 = h2_out[...] + mm(mixed, w_so[...]) + out_bias[2:3, :]
    feed_forward(
        h3, norms[6:7, :], norms[7:8, :], hid_bias.at[1:2], out_bias[3:4, :], up_two, down_two, act_two, slope_two,
        normed, work,
    )
    if reach:
        shared[1][step] = work[...].astype(BF)
        traffic.send_frame(step)
        traffic.await_frame(step)
    else:
        latents[...] = work[...].astype(BF)
    xhat, rstd = norm_stats(h3)
    g3[...] = grad[...].astype(F32) + feed_back(
        grad, normed, xhat, rstd, norms[6:7, :], act_two, slope_two, up_two, down_two,
        acc_up, acc_down, dhid, dnorm, dout, work,
    )

    @pl.when(step == pl.num_programs(0) - 1)
    def _():
        at = flat_rows_of()
        half = D * FF // LANES
        write_flat(flat, stage, low, [(acc_up, at["w_up"] + half), (acc_down, at["w_down"] + half)], sems, shard, extra)
        if reach:
            traffic.finish()
        for flow in flows:
            flow.drain()


def backward_kernel(
    shard, extra, steps, qkv, lse, mixed, g3, h2_all, h1_all, act_all, slope_all, norms, w_so, src_qkv, src_up, src_down,
    latents_in, flat_in,
    g1, dhid, dnorm_sa, dnorm_one, dout_so, dout_one, latents_out, flat,
    dqkv, acc_up, acc_down, acc_qkv, acc_so, stage, low, normed, grad_mixed, grad_low, work, sems,
    w_qkv, up_one, down_one, late_sems,
    h2_slots, h2_sems, h1_slots, h1_sems, act_slots, act_sems, slope_slots, slope_sems, latents_held, pass_sem,
):
    step = pl.program_id(0)
    late = Late(step, (src_qkv, src_up, src_down), (w_qkv, up_one, down_one), late_sems)
    flows = [
        Flow(step, steps, *parts)
        for parts in (
            (h2_all, h2_slots, h2_sems), (h1_all, h1_slots, h1_sems), (act_all, act_slots, act_sems),
            (slope_all, slope_slots, slope_sems),
        )
    ]
    for flow in flows:
        flow.fetch_ahead()
    h2, h1, act_one, slope_one = (flow.here() for flow in flows)
    latents_load = pltpu.make_async_copy(latents_in, latents_held, pass_sem.at[0])
    latents_store = pltpu.make_async_copy(latents_held, latents_out, pass_sem.at[1])
    pl.when(step == 0)(lambda: latents_load.start())

    @pl.when(step == min(1, steps - 1))
    def _():
        latents_load.wait()
        latents_store.start()

    clear(
        step == 0,
        (acc_up, acc_down, acc_qkv, acc_so, dhid, dnorm_sa, dnorm_one, dout_so, dout_one),
    )
    scale = jnp.asarray(0.125, BF)
    grad_three = g3[...]
    grad_low[...] = grad_three.astype(BF)
    dout_so[...] += col_sum(grad_low[...].astype(F32))
    acc_so[...] += t_mm(mixed[...], grad_low[...])
    grad_mixed[...] = mm_t(grad_low[...], w_so[...]).astype(BF)

    for base in range(0, D, LANES):
        query_at = slice(base, base + LANES)
        key_at = slice(D + base, D + base + LANES)
        value_at = slice(2 * D + base, 2 * D + base + LANES)
        head = base // HEAD_DIM
        queries = by_head(qkv[:, query_at] * scale)
        grads = by_head(grad_mixed[:, query_at])
        keys = qkv[:, key_at]
        key_t = keys.T
        log_total = jnp.concatenate([lse[0, head : head + 1, :], lse[0, head + 1 : head + 2, :]], axis=1)
        prob = jnp.exp(mm_t(keys, queries) - log_total)
        dqkv[:, value_at] = mm(prob.astype(BF), grads).astype(BF)
        weighted = prob * mm_t(qkv[:, value_at], grads)
        grad_score = (weighted - prob * col_sum(weighted)).astype(BF)
        dqkv[:, key_at] = mm(grad_score, queries).astype(BF)
        query_t = [
            mm(key_t[j * HEAD_DIM : (j + 1) * HEAD_DIM, :], grad_score[:, j * LAT : (j + 1) * LAT]) for j in range(2)
        ]
        dqkv[:, query_at] = (jnp.concatenate(query_t, axis=0).T * 0.125).astype(BF)
    late.need(0, 1, 2)
    for flow in flows:
        flow.arrived()
    xhat, rstd = norm_stats(h2[...])
    normed[...] = (xhat * norms[4:5, :] + norms[5:6, :]).astype(BF)
    grad_in = mm_t(dqkv[...], w_qkv[...])
    acc_qkv[...] += t_mm(normed[...], dqkv[...])
    dnorm_sa[...] += jnp.concatenate([col_sum(grad_in * xhat), col_sum(grad_in)], axis=0)
    grad_two = grad_three + norm_back(grad_in, xhat, rstd, norms[4:5, :])

    xhat, rstd = norm_stats(h1[...])
    normed[...] = (xhat * norms[2:3, :] + norms[3:4, :]).astype(BF)
    grad_low[...] = grad_two.astype(BF)
    grad_one = grad_two + feed_back(
        grad_low, normed, xhat, rstd, norms[2:3, :], act_one, slope_one, up_one, down_one,
        acc_up, acc_down, dhid, dnorm_one, dout_one, work,
    )

    g1[...] = grad_one

    @pl.when(step == pl.num_programs(0) - 1)
    def _():
        at = flat_rows_of()
        write_flat(
            flat, stage, low,
            [(acc_up, at["w_up"]), (acc_down, at["w_down"]), (acc_qkv, at["w_qkv"]), (acc_so, at["w_so"])],
            sems, shard, extra,
        )
        latents_store.wait()


def cross_back_frame(
    grad_one, kvf, co, lse, rank_ref, count, episode_row, hot_column, latent, norms, w_q, w_o,
    acc_latent, acc_q, acc_o, acc_episode, dnorm, dout, dkv_t, pause=lambda: None,
):
    cap = kvf.shape[0]
    start = latent[...].astype(F32) + episode_row
    xhat, rstd = norm_stats(start)
    query_in = (xhat * norms[0:1, :] + norms[1:2, :]).astype(BF)
    queries = mm(query_in, w_q[...]).astype(BF) * jnp.asarray(0.125, BF)
    branch = grad_one.astype(BF)
    grad_co = mm_t(branch, w_o[...]).astype(BF)
    acc_o[...] += t_mm(co, branch)
    dout[...] += col_sum(branch.astype(F32))
    scores = cross_scores(kvf, queries, count)
    prob = jnp.exp(scores - lse)
    weighted = prob * mm_t(kvf, grad_co)
    grad_score = (weighted - prob * col_sum(weighted)).astype(BF)
    grad_kv = (mm(grad_score, queries) + mm(prob.astype(BF), grad_co)).astype(BF)
    grad_query = (t_mm(kvf, grad_score).T * 0.125).astype(BF)
    pause()
    acc_q[...] += t_mm(query_in, grad_query)
    grad_in = mm_t(grad_query, w_q[...])
    grad_start = grad_one + norm_back(grad_in, xhat, rstd, norms[0:1, :])
    dnorm[...] += jnp.concatenate([col_sum(grad_in * xhat), col_sum(grad_in)], axis=0)
    acc_latent[...] += grad_start
    acc_episode[...] += hot_column * col_sum(grad_start)
    grad_kv_t = grad_kv.T
    chunk = 8 * LANES

    def scatter(j, carry):
        sel = select_tokens(rank_ref[pl.ds(pl.multiple_of(j * 8, 8), 8), :], cap)
        at = pl.ds(pl.multiple_of(j * chunk, chunk), chunk)
        dkv_t[:, at] = added(dkv_t[:, at], mm(grad_kv_t, sel))
        return carry

    lax.fori_loop(0, dkv_t.shape[1] // chunk, scatter, 0)


def write_small(put, stage, low, latent_low, acc_latent, acc_q, acc_o, acc_episode, norm_grads, hid_grads, out_grads):
    at = flat_rows_of()
    flatten(acc_latent, stage, latent_low, 0)
    put(latent_low.at[0], 0)
    head = at["lat_norms"] - at["episode"]
    used = EPISODES * (D // LANES)
    rows = [to_flat(stage, acc_episode[...])[0:used, :], jnp.zeros((head - used, LANES), F32)]
    rows = jnp.concatenate(rows + [to_flat(stage, norm_grads)], axis=0)
    top = rows.shape[0]
    low[0, 0:top, :] = rows.astype(BF)
    put(low.at[0, pl.ds(0, top), :], at["episode"])
    stage[0:D, :] = acc_q[...]
    even = stage[pl.ds(0, D // 2, stride=2), :]
    odd = pltpu.roll(stage[pl.ds(1, D // 2, stride=2), :], CH, 1)
    low[0, top : top + D // 2, :] = jnp.where(lane_half(even.shape, 0), even, odd).astype(BF)
    both = D // 2 + CH * D // LANES
    low[0, top + D // 2 : top + both, :] = to_flat(stage, acc_o[CH : 2 * CH, :]).astype(BF)
    put(low.at[0, pl.ds(top, both), :], at["w_q"])
    hid = to_flat(stage, hid_grads)
    last = top + both
    low[0, last : last + hid.shape[0], :] = hid.astype(BF)
    end = hid.shape[0] + 4 * D // LANES
    low[0, last + hid.shape[0] : last + end, :] = to_flat(stage, out_grads).astype(BF)
    put(low.at[0, pl.ds(last, end), :], at["hid_bias"])


def cross_accumulators(total_keys):
    shapes = [(LAT, D), (D, LANES), (LANES, D), (16, D), (2, D), (1, D)]
    return [pltpu.VMEM(shape, F32) for shape in shapes] + [pltpu.VMEM((LANES, total_keys), BF)]


def small_buffers():
    return [pltpu.VMEM((2048, LANES), F32), pltpu.VMEM((1, 640, LANES), BF), pltpu.VMEM((1, 2048, LANES), BF)]


def stacked(*parts):
    return jnp.concatenate([part[...] for part in parts], axis=0)


def cross_bwd_kernel(
    kv_rows, g1, kvf, co, lse, rank, count, episode, hot, latent, norms, w_q, w_o,
    dnorm_one, dnorm_sa, dnorm_two, dhid_one, dhid_two, dout_one, dout_so, dout_two, flat_in, flat,
    acc_latent, acc_q, acc_o, acc_episode, dnorm, dout, dkv_t, stage, low, latent_low, kv_low, sems,
):
    step = pl.program_id(0)
    accs = (acc_latent, acc_q, acc_o, acc_episode, dnorm, dout, dkv_t)
    clear(step == 0, accs)
    cross_back_frame(
        g1[...], kvf[0], co[...], lse[0], rank.at[0], count[0, 0:1, 0:1], episode[0], hot[0, :, 0:1],
        latent, norms, w_q, w_o, *accs,
    )

    @pl.when(step == pl.num_programs(0) - 1)
    def _():
        copies = []

        def put(source, row):
            copies.append(
                pltpu.make_async_copy(source, flat.at[pl.ds(row, source.shape[0]), :], sems.at[len(copies)])
            )
            copies[-1].start()

        write_small(
            put, stage, low, latent_low, acc_latent, acc_q, acc_o, acc_episode,
            stacked(dnorm, dnorm_one, dnorm_sa, dnorm_two), stacked(dhid_one, dhid_two),
            stacked(dout, dout_one, dout_so, dout_two),
        )
        for copy in copies:
            copy.wait()
        tokens = kv_rows[1]
        for j in range(dkv_t.shape[1] // tokens):
            kv_low[...] = dkv_t[:, j * tokens : (j + 1) * tokens].T
            copy = pltpu.make_async_copy(kv_low, flat.at[pl.ds(kv_rows[0] + j * tokens, tokens), :], sems.at[0])
            copy.start()
            copy.wait()


def fixed(*shape):
    return pl.BlockSpec(shape, lambda i: (0,) * len(shape), pipeline_mode=pl.Buffered(1))


def kept(*shape):
    return pl.BlockSpec(shape, lambda i: (0,) * len(shape))


def rowed(rows, cols):
    return pl.BlockSpec((rows, cols), lambda i: (i, 0))


def framed(*shape):
    return pl.BlockSpec((1,) + shape, lambda i: (i,) + (0,) * len(shape))


def shaped(shape, dtype=F32):
    return jax.ShapeDtypeStruct(shape, dtype)


def call(kernel, grid, in_specs, outs, args, flops=0, trans=0, scratch=(), limit=56, aliases=None, collective=None):
    out_specs, out_shapes = zip(*outs)
    moved = sum(math.prod(a.shape) * a.dtype.itemsize for a in args)
    moved += sum(math.prod(s.shape) * s.dtype.itemsize for s in out_shapes)
    return pl.pallas_call(
        kernel,
        grid=(grid,),
        in_specs=in_specs,
        out_specs=list(out_specs),
        out_shape=list(out_shapes),
        scratch_shapes=list(scratch),
        input_output_aliases=aliases or {},
        compiler_params=pltpu.CompilerParams(
            dimension_semantics=("arbitrary",),
            vmem_limit_bytes=limit * MIB,
            collective_id=collective,
            has_side_effects=collective is not None,
        ),
        cost_estimate=pl.CostEstimate(flops=flops, bytes_accessed=moved, transcendentals=trans),
    )(*args)


def reduce_all(flat, shard, bias_owner, bias_row, tokens, tok_normed, w_kv, tok_norm, g1, cross):
    vmem = pl.BlockSpec(memory_space=pltpu.VMEM)
    anywhere = pl.BlockSpec(memory_space=pl.ANY)
    dma = pltpu.SemaphoreType.DMA
    first = [
        pltpu.VMEM((8, STAT_ROWS, LANES), F32), dma((7,)), dma((7,)), pltpu.VMEM((16, LANES), BF),
        pltpu.VMEM((DIN, LANES), BF), dma((2,)), pltpu.VMEM(g1.shape, F32), dma((g1.shape[0],)),
        pltpu.VMEM((8, tokens.shape[0], LANES), BF), dma((16,)),
    ]
    grads = flat.reshape(2, 2, 2, -1, LANES)
    return pl.pallas_call(
        functools.partial(reduce_kernel, shard, bias_owner, bias_row),
        out_shape=[
            shaped((shard, LANES), BF), shaped((STAT_ROWS, LANES)), shaped(tokens.shape, BF),
            shaped(grads.shape, BF),
        ],
        in_specs=[anywhere] + [vmem] * 4 + [anywhere] + [vmem] * len(cross),
        out_specs=[vmem, vmem, vmem, anywhere],
        scratch_shapes=first
        + cross_accumulators(8 * tokens.shape[0])
        + small_buffers()
        + Reduction.scratch(shard),
        input_output_aliases={0: 3},
        compiler_params=pltpu.CompilerParams(
            collective_id=1, has_side_effects=True, vmem_limit_bytes=56 * MIB
        ),
    )(grads, tokens, tok_normed, w_kv, tok_norm, g1, *cross)


def body(tokens, frame_ids, episodes, master, moment_one, moment_two, latent_grad):
    lat_count = lax.axis_size("lat")
    lat_index = lax.axis_index("lat")
    shard_len = master.shape[0]
    frame_total = episodes.shape[1]
    frames = frame_total // lat_count
    rows_total = frames * LAT
    total_keys = frame_ids.shape[1] * lat_count
    cap = total_keys // 8
    token_rows_count = total_keys // LANES

    reach = lat_count == 8 and lax.axis_size("kf") == 4
    shard_rows = shard_len // LANES
    master_rows = master.reshape(shard_rows, LANES)
    score_flops = rows_total * cap * LANES * 2
    select_flops = frames * cap * total_keys * LANES * 2
    if reach:
        (
            up_one, down_one, w_qkv, w_so, up_two, down_two,
            latent, norms, hid_bias, out_bias, w_q, w_o, w_kv, tok_norm, tok_normed, episode_rows, rank, counts,
            kvf, cross_out, cross_lse, hot_lanes, h1,
        ) = begin_all(master_rows, tokens[0], frame_ids.reshape(-1, LANES), episodes, frames, cap)
    else:
        own_episodes = lax.dynamic_slice_in_dim(episodes[0], lat_index * frames, frames, 0)
        episode_match = own_episodes[:, None] == jnp.arange(EPISODES, dtype=jnp.int32)[None, :]
        hot_lanes = jnp.broadcast_to(
            jnp.pad(episode_match.astype(F32), ((0, 0), (0, 16 - EPISODES)))[:, :, None], (frames, 16, LANES)
        )
        weights = split_flat(lax.all_gather(master.astype(BF), "lat", axis=0, tiled=True))
        norms = weights["lat_norms"].astype(F32)
        out_bias = weights["out_bias"].astype(F32)
        hid_bias = weights["hid_bias"].astype(F32)
        tok_norm = weights["tok_norm"].astype(F32)
        w_kv, w_qkv, w_so, latent = (weights[name] for name in ("w_kv", "w_qkv", "w_so", "latent"))
        up_one, up_two = weights["w_up"]
        down_one, down_two = weights["w_down"]
        frame_tag = lax.all_gather(frame_ids[0].astype(BF), "lat", axis=0, tiled=True).astype(jnp.int32)
        own_frames = lat_index * frames + jnp.arange(frames, dtype=jnp.int32)
        own_hit = frame_tag[None, :] == own_frames[:, None]
        rank = jnp.cumsum(own_hit.astype(jnp.int32), axis=1) - 1
        counts = jnp.broadcast_to(rank[:, -1][:, None, None] + 1, (frames, 8, LANES))
        rank = jnp.where(own_hit, rank, -1).reshape(frames, token_rows_count, LANES)
        tok_normed = layer_norm(tokens[0].astype(F32), tok_norm[0], tok_norm[1]).astype(BF)
        key_value = mm(tok_normed, w_kv).astype(BF)
        all_keys = lax.all_gather(key_value, "lat", axis=0, tiled=True)
        episode_rows = mm(episode_match.astype(BF), weights["episode"]).reshape(frames, 1, D)
        w_q = jnp.pad(weights["w_q"], ((0, 0), (0, LANES - CH)))
        w_o = jnp.pad(weights["w_o"], ((LANES - CH, 0), (0, 0)))
        h1, kvf, cross_out, cross_lse = call(
            cross_fwd_kernel,
            frames,
            [
                fixed(LAT, D), framed(1, D), fixed(8, D), fixed(D, LANES), fixed(LANES, D), fixed(4, D),
                fixed(total_keys, LANES), framed(token_rows_count, LANES), framed(8, LANES),
            ],
            [
                (rowed(LAT, D), shaped((rows_total, D))),
                (framed(cap, LANES), shaped((frames, cap, LANES), BF)),
                (rowed(LAT, LANES), shaped((rows_total, LANES), BF)),
                (framed(1, LAT), shaped((frames, 1, LAT))),
            ],
            (latent, episode_rows, norms, w_q, w_o, out_bias, all_keys, rank, counts),
            flops=2 * score_flops + select_flops,
            trans=rows_total * cap,
        )
    mlp_flops = 4 * rows_total * D * FF
    attn_flops = 4 * rows_total * LAT * D
    anywhere = pl.BlockSpec(memory_space=pl.ANY)
    token_count = frame_ids.shape[1]
    if reach:
        flat_shard, extra = shard_rows, token_count
        flat_shape = (lat_count * (shard_rows + extra), LANES)
        kv_rows = (shard_rows, token_count, shard_rows + extra)
        grad_in, grad_spec = latent_grad[0], anywhere
        latents_spec = (anywhere, shaped(latent_grad.shape[1:], BF))
        shared = [pltpu.VMEM((frames, LAT, D), BF)] * 2 + FrameExchange.scratch(frames)
    else:
        flat_shard, extra = NPARAM // LANES, 0
        flat_shape = (flat_shard + total_keys, LANES)
        kv_rows = (flat_shard, 512, 512)
        grad_in = lax.all_to_all(
            latent_grad[0], "lat", split_axis=0, concat_axis=1, tiled=True
        ).reshape(rows_total, D)
        grad_spec = rowed(LAT, D)
        latents_spec = (rowed(LAT, D), shaped((rows_total, D), BF))
        shared = []
    slab = D * FF // LANES
    h2, qkv, self_lse, mixed, act_one, slope_one, latents, g3, dhid_two, dnorm_two, dout_two, flat = call(
        functools.partial(forward_kernel, reach, flat_shard, extra, frames),
        frames,
        [
            rowed(LAT, D), grad_spec, fixed(8, D), fixed(2, FF), fixed(4, D), fixed(D, FF), fixed(FF, D),
        ]
        + [anywhere] * 4,
        [
            (anywhere, shaped((rows_total, D))),
            (anywhere, shaped((rows_total, 3 * D), BF)),
            (framed(HEADS, LAT), shaped((frames, HEADS, LAT))),
            (anywhere, shaped((rows_total, D), BF)),
            (anywhere, shaped((rows_total, FF), BF)),
            (anywhere, shaped((rows_total, FF), BF)),
            latents_spec,
            (rowed(LAT, D), shaped((rows_total, D))),
            (kept(1, FF), shaped((1, FF))),
            (kept(2, D), shaped((2, D))),
            (kept(1, D), shaped((1, D))),
            (anywhere, shaped(flat_shape, BF)),
        ],
        (h1, grad_in, norms, hid_bias, out_bias, up_one, down_one, w_qkv, w_so, up_two, down_two),
        flops=4 * mlp_flops + 4 * attn_flops,
        trans=4 * rows_total * FF,
        scratch=[
            pltpu.VMEM((LAT, FF), BF), pltpu.VMEM((LAT, FF), BF), pltpu.VMEM((D, FF), F32), pltpu.VMEM((FF, D), F32),
            pltpu.VMEM((2048, LANES), F32), pltpu.VMEM((2, slab, LANES), BF), pltpu.VMEM((LAT, D), BF),
            pltpu.VMEM((D, LAT), F32), pltpu.VMEM((LAT, D), F32), pltpu.SemaphoreType.DMA((2, 16)),
            pltpu.VMEM((D, 3 * D), BF), pltpu.VMEM((D, D), BF), pltpu.VMEM((D, FF), BF), pltpu.VMEM((FF, D), BF),
            pltpu.SemaphoreType.DMA((4,)),
        ]
        + flow_slots((LAT, D), F32)
        + flow_slots((LAT, 3 * D), BF)
        + flow_slots((LAT, D), BF)
        + flow_slots((LAT, FF), BF)
        + flow_slots((LAT, FF), BF)
        + shared,
        limit=62,
        collective=4 if reach else None,
    )
    g1, dhid_one, dnorm_sa, dnorm_one, dout_so, dout_one, latents, flat = call(
        functools.partial(backward_kernel, flat_shard, extra, frames),
        frames,
        [
            rowed(LAT, 3 * D), framed(HEADS, LAT), rowed(LAT, D), rowed(LAT, D), anywhere, anywhere, anywhere, anywhere,
            fixed(8, D), fixed(D, D),
        ]
        + [anywhere] * 5,
        [
            (rowed(LAT, D), shaped((rows_total, D))),
            (kept(1, FF), shaped((1, FF))),
            (kept(2, D), shaped((2, D))),
            (kept(2, D), shaped((2, D))),
            (kept(1, D), shaped((1, D))),
            (kept(1, D), shaped((1, D))),
            (anywhere, shaped(latents.shape, BF)),
            (anywhere, shaped(flat_shape, BF)),
        ],
        (
            qkv, self_lse, mixed, g3, h2, h1, act_one, slope_one, norms, w_so, w_qkv, up_one, down_one, latents, flat,
        ),
        flops=2 * mlp_flops + 10 * attn_flops,
        trans=rows_total * LAT * HEADS,
        scratch=[
            pltpu.VMEM((LAT, 3 * D), BF), pltpu.VMEM((D, FF), F32), pltpu.VMEM((FF, D), F32),
            pltpu.VMEM((D, 3 * D), F32), pltpu.VMEM((D, D), F32),
            pltpu.VMEM((2048, LANES), F32), pltpu.VMEM((2, slab, LANES), BF), pltpu.VMEM((LAT, D), BF),
            pltpu.VMEM((LAT, D), BF), pltpu.VMEM((LAT, D), BF), pltpu.VMEM((LAT, D), F32),
            pltpu.SemaphoreType.DMA((2, 16)),
            pltpu.VMEM((D, 3 * D), BF), pltpu.VMEM((D, FF), BF), pltpu.VMEM((FF, D), BF),
            pltpu.SemaphoreType.DMA((3,)),
        ]
        + flow_slots((LAT, D), F32)
        + flow_slots((LAT, D), F32)
        + flow_slots((LAT, FF), BF)
        + flow_slots((LAT, FF), BF)
        + [pltpu.VMEM(latents.shape, BF), pltpu.SemaphoreType.DMA((2,))],
        limit=60,
        aliases={14: 7},
    )
    if reach:
        latents_out = latents[None]
    else:
        latents_out = lax.all_to_all(
            latents.reshape(frames, LAT, D), "lat", split_axis=1, concat_axis=0, tiled=True
        )[None]
    cross = (
        kvf, cross_out, cross_lse, rank, counts, episode_rows, hot_lanes, latent, norms, w_q, w_o,
        dnorm_one, dnorm_sa, dnorm_two, dhid_one, dhid_two, dout_one, dout_so, dout_two,
    )
    layout = param_layout()
    starts, ends, offset, bias_offset = [], [], 0, 0
    for name, shape in layout:
        if name == "hid_bias":
            bias_offset = offset
        starts.append(offset // LANES)
        offset += math.prod(shape)
        ends.append(offset // LANES)
    pad = [0] * (16 - len(layout))
    starts, ends = (np.tile(np.array(v + pad, np.int32)[:, None], (1, LANES)) for v in (starts, ends))
    opt_rows = shard_rows // 2 if shard_rows % 16 == 0 else shard_rows
    opt_steps = shard_rows // opt_rows
    base = (lat_index * shard_rows).astype(jnp.int32).reshape(1)
    smem = pl.BlockSpec(memory_space=pltpu.SMEM)
    flat_rows = (shard_rows, LANES)
    bias_owner, bias_at = divmod(bias_offset, shard_len)
    if reach:
        summed, stats, token_grad, unused = reduce_all(
            flat, shard_rows, bias_owner, bias_at // LANES, tokens[0], tok_normed, w_kv, tok_norm,
            g1.reshape(frames, LAT, D), cross,
        )
    else:
        (flat,) = call(
            functools.partial(cross_bwd_kernel, kv_rows),
            frames,
            [
                rowed(LAT, D), framed(cap, LANES), rowed(LAT, LANES), framed(1, LAT), framed(token_rows_count, LANES),
                framed(8, LANES), framed(1, D), framed(16, LANES), fixed(LAT, D), fixed(8, D), fixed(D, LANES),
                fixed(LANES, D),
            ]
            + [fixed(*part.shape) for part in cross[11:]]
            + [anywhere],
            [(anywhere, shaped(flat_shape, BF))],
            (g1,) + cross + (flat,),
            flops=6 * score_flops,
            trans=rows_total * cap,
            scratch=cross_accumulators(total_keys)
            + small_buffers()
            + [pltpu.VMEM((kv_rows[1], LANES), BF), pltpu.SemaphoreType.DMA((8,))],
            aliases={20: 0},
        )
        grad_kv = lax.psum_scatter(flat[flat_shard:], "lat", scatter_dimension=0, tiled=True)
        flat = flat[:flat_shard]
        grad_w_kv = t_mm(tok_normed, grad_kv)
        grad_tok_normed = mm_t(grad_kv, w_kv)
        unused, token_pull = jax.vjp(layer_norm, tokens[0].astype(F32), tok_norm[0], tok_norm[1])
        grad_tokens, grad_tok_gain, grad_tok_bias = token_pull(grad_tok_normed)
        token_grad = grad_tokens.astype(BF)
        flat_at = flat_rows_of()
        tok_norm_grad = jnp.stack([grad_tok_gain, grad_tok_bias]).reshape(-1, LANES).astype(BF)
        flat = lax.dynamic_update_slice(flat, tok_norm_grad, (flat_at["tok_norm"], 0))
        flat = lax.dynamic_update_slice(flat, grad_w_kv.astype(BF), (flat_at["w_kv"], 0))
        local_flat = flat.reshape(-1)
        summed = lax.psum_scatter(local_flat, "lat", scatter_dimension=0, tiled=True)
        summed = lax.psum(summed, "kf").reshape(flat_rows)
        bias_rows = summed[bias_at // LANES : bias_at // LANES + 2 * FF // LANES].astype(F32)
        bias_rows = jnp.where(lat_index == bias_owner, bias_rows, 0.0)
        grad_sq = jnp.sum(jnp.square(summed.astype(F32)), axis=0, keepdims=True)
        stats = lax.psum(jnp.concatenate([grad_sq, jnp.zeros((7, LANES), F32), bias_rows]), "lat")
    grad_shard, lamb_update, new_one, new_two, norms_sq, bias_grad, token_grad = call(
        lamb_kernel,
        opt_steps,
        [smem, fixed(STAT_ROWS, LANES), fixed(16, LANES), fixed(16, LANES)] + [rowed(opt_rows, LANES)] * 4 + [fixed(*token_grad.shape)],
        [(rowed(opt_rows, LANES), shaped(flat_rows))] * 4
        + [(kept(16, 2 * LANES), shaped((16, 2 * LANES))), (kept(2, FF), shaped((2, FF)))]
        + [(kept(*token_grad.shape), shaped(token_grad.shape, BF))],
        (
            base, stats, starts, ends, summed, master_rows,
            moment_one.reshape(flat_rows), moment_two.reshape(flat_rows), token_grad,
        ),
    )
    if reach:
        vmem = pl.BlockSpec(memory_space=pltpu.VMEM)
        trust = pl.pallas_call(
            trust_kernel,
            out_shape=shaped((1, len(layout))),
            in_specs=[vmem],
            out_specs=vmem,
            scratch_shapes=[
                pltpu.VMEM((8, 16, 2 * LANES), F32),
                pltpu.SemaphoreType.DMA((7,)),
                pltpu.SemaphoreType.DMA((7,)),
            ],
            compiler_params=pltpu.CompilerParams(collective_id=2, has_side_effects=True),
        )(norms_sq).reshape(-1)
    else:
        sums = lax.psum(jnp.sum(norms_sq.reshape(16, 2, LANES), axis=2), "lat")[: len(layout)]
        trust = jnp.sqrt(sums[:, 1]) / (jnp.sqrt(sums[:, 0]) + 1e-06)
    return (
        latents_out,
        token_grad[None],
        grad_shard.reshape(-1),
        lamb_update.reshape(-1),
        new_one.reshape(-1),
        new_two.reshape(-1),
        trust,
        bias_grad,
    )


def solution(mesh):
    return jax.shard_map(
        body,
        mesh=mesh,
        in_specs=(
            P("kf", "lat", None),
            P("kf", "lat"),
            P("kf", None),
            P("lat"),
            P("lat"),
            P("lat"),
            P("kf", None, "lat", None),
        ),
        out_specs=(
            P("kf", None, "lat", None),
            P("kf", "lat", None),
            P("lat"),
            P("lat"),
            P("lat"),
            P("lat"),
            P(),
            P(),
        ),
        check_vma=False,
    )
```

```python
import functools
import math

import jax
import jax.numpy as jnp
import numpy as np
from jax import lax
from jax.experimental import pallas as pl
from jax.experimental.pallas import tpu as pltpu
from jax.sharding import PartitionSpec as P

DIN = 256
D = 512
LAT = 512
CH = 64
HEADS = 8
HEAD_DIM = 64
FF = 2048
FRAMES = 32
EPISODES = 11
NPARAM = 5619712
LANES = 128

norm_eps = 1e-05
masked_fill = -1e30
beta_one = 0.9
beta_two = 0.999
adam_eps = 1e-06
decay_rate = 0.01
clip_fraction = 0.5
lamb_step = 10.0

BF = jnp.bfloat16
F32 = jnp.float32
MIB = 1024 * 1024


def param_layout():
    return [
        ("latent", (LAT, D)),
        ("episode", (EPISODES, D)),
        ("tok_norm", (2, DIN)),
        ("lat_norms", (8, D)),
        ("w_kv", (DIN, 2 * CH)),
        ("w_q", (D, CH)),
        ("w_o", (CH, D)),
        ("w_qkv", (D, 3 * D)),
        ("w_so", (D, D)),
        ("w_up", (2, D, FF)),
        ("w_down", (2, FF, D)),
        ("hid_bias", (2, FF)),
        ("out_bias", (4, D)),
    ]


def split_flat(flat_vector):
    pieces = {}
    offset = 0
    for tensor_name, tensor_shape in param_layout():
        entries = math.prod(tensor_shape)
        pieces[tensor_name] = flat_vector[offset : offset + entries].reshape(tensor_shape)
        offset += entries
    return pieces


def layer_norm(inputs, norm_gain, norm_bias):
    row_mean = jnp.mean(inputs, axis=-1, keepdims=True)
    centered = inputs - row_mean
    row_var = jnp.mean(centered * centered, axis=-1, keepdims=True)
    return centered * lax.rsqrt(row_var + norm_eps) * norm_gain + norm_bias


def mm(left, right):
    return jnp.dot(left, right, preferred_element_type=F32)


def mm_t(left, right):
    return lax.dot_general(left, right, (((1,), (1,)), ((), ())), preferred_element_type=F32)


def t_mm(left, right):
    return lax.dot_general(left, right, (((0,), (0,)), ((), ())), preferred_element_type=F32)


def norm_stats(rows):
    mean = jnp.mean(rows, axis=-1, keepdims=True)
    centered = rows - mean
    var = jnp.mean(centered * centered, axis=-1, keepdims=True)
    rstd = lax.rsqrt(var + norm_eps)
    return centered * rstd, rstd


def norm_back(grad, xhat, rstd, gain):
    dxh = grad * gain
    first = jnp.mean(dxh, axis=-1, keepdims=True)
    second = jnp.mean(dxh * xhat, axis=-1, keepdims=True)
    return rstd * (dxh - first - xhat * second)


def col_sum(values):
    return jnp.sum(values, axis=0, keepdims=True)


def gelu_pair(x):
    cdf = 0.5 + 0.5 * lax.erf(x * (1.0 / math.sqrt(2.0)))
    density = jnp.exp(x * x * -0.5) * (1.0 / math.sqrt(2.0 * math.pi))
    return x * cdf, cdf + x * density


def accumulate(first, ref, value):
    @pl.when(first)
    def _():
        ref[...] = value

    @pl.when(jnp.logical_not(first))
    def _():
        ref[...] += value


def lane_half(shape, half):
    lane = lax.broadcasted_iota(jnp.int32, shape, 1)
    return (lane >= half * HEAD_DIM) & (lane < (half + 1) * HEAD_DIM)


def keep_half(values, half):
    return jnp.where(lane_half(values.shape, half), values, jnp.zeros_like(values))


def by_head(values):
    return jnp.concatenate([keep_half(values, h) for h in range(values.shape[1] // HEAD_DIM)], axis=0)


def select_tokens(rank_rows, cap):
    slot = lax.broadcasted_iota(jnp.int32, (cap, LANES), 0)
    parts = []
    for r in range(rank_rows.shape[0]):
        hit = slot == rank_rows[r : r + 1, :]
        parts.append(jnp.where(hit, 1.0, 0.0).astype(BF))
    return jnp.concatenate(parts, axis=1)


def cross_scores(kvf, queries_scaled, count):
    scores = mm_t(kvf, queries_scaled)
    slot = lax.broadcasted_iota(jnp.int32, scores.shape, 0)
    return jnp.where(slot < count, scores, masked_fill)


def cross_attend(start, norms, w_q, kvf, count):
    xhat, unused = norm_stats(start)
    query_in = (xhat * norms[0:1, :] + norms[1:2, :]).astype(BF)
    queries = mm(query_in, w_q[...]).astype(BF) * jnp.asarray(0.125, BF)
    scores = cross_scores(kvf, queries, count)
    top = jnp.max(scores, axis=0, keepdims=True)
    terms = jnp.exp(scores - top)
    total = jnp.sum(terms, axis=0, keepdims=True)
    prob = (terms * (1.0 / total)).astype(BF)
    return t_mm(kvf, prob).T.astype(BF), top + jnp.log(total)


def cross_fwd_kernel(latent, episode, norms, w_q, w_o, out_bias, kv, rank, count, h1, kvf_out, co_out, lse_out):
    cap = kvf_out.shape[1]
    start = latent[...].astype(F32) + episode[0]
    chunk = 8 * LANES
    chunks = kv.shape[0] // chunk

    def step(j, acc):
        sel = select_tokens(rank[0, pl.ds(pl.multiple_of(j * 8, 8), 8), :], cap)
        return acc + mm(sel, kv[pl.ds(pl.multiple_of(j * chunk, chunk), chunk), :])

    kvf = lax.fori_loop(0, chunks, step, jnp.zeros((cap, LANES), F32)).astype(BF)
    co, lse = cross_attend(start, norms, w_q, kvf, count[0, 0:1, 0:1])
    h1[...] = start + mm(co, w_o[...]) + out_bias[0:1, :]
    kvf_out[0] = kvf
    co_out[...] = co
    lse_out[0] = lse


def segment_hot(starts, ends, base, rows):
    row = lax.broadcasted_iota(jnp.int32, (16, rows), 1) + base
    return jnp.where((row >= starts[:, 0:1]) & (row < ends[:, 0:1]), 1.0, 0.0).astype(BF)


def segment_sums(hot, squares):
    high = squares.astype(BF)
    low = (squares - high.astype(F32)).astype(BF)
    return mm(hot, high) + mm(hot, low)


def lamb_kernel(
    base, stats, starts, ends, summed, master, one, two, token_in,
    grad_out, update_out, one_out, two_out, norms_sq, bias, token_out,
):
    i = pl.program_id(0)
    token_out[...] = token_in[...]
    rows = master.shape[0]
    hot = segment_hot(starts, ends, base[0] + i * rows, rows)
    total_sq = jnp.sum(stats[0:1, :], axis=1, keepdims=True)
    clip = jnp.minimum(1.0, clip_fraction * math.sqrt(NPARAM) / (jnp.sqrt(total_sq) + 1e-06))
    grad = summed[...].astype(F32)
    grad_out[...] = grad
    clipped = clip * grad
    new_one = beta_one * one[...] + (1.0 - beta_one) * clipped
    new_two = beta_two * two[...] + (1.0 - beta_two) * clipped * clipped
    one_out[...] = new_one
    two_out[...] = new_two
    first_hat = new_one * (1.0 / (1.0 - beta_one**lamb_step))
    second_hat = new_two * (1.0 / (1.0 - beta_two**lamb_step))
    update = first_hat / (jnp.sqrt(second_hat) + adam_eps) + decay_rate * master[...]
    update_out[...] = update
    accumulate(i == 0, norms_sq, segment_sums(hot, jnp.concatenate([update * update, master[...] * master[...]], axis=1)))
    for j in range(2 * FF // LANES):
        r, c = divmod(j, FF // LANES)
        bias[r : r + 1, c * LANES : (c + 1) * LANES] = stats[8 + j : 9 + j, :]


BATCH = 256
HALF = 128
QUARTER = 64
MESH = pl.DeviceIdType.MESH


class Place:
    def __init__(self):
        self.z = lax.axis_index("kf")
        self.me = lax.axis_index("lat")
        self.core = lax.rem(self.me, 2)
        self.x = lax.rem(self.me // 2, 2)
        self.y = self.me // 4
        self.z_low = lax.rem(self.z, 2)
        self.z_high = self.z // 2
        self.sibling = (self.z, self.me + 1 - 2 * self.core)
        self.x_side = (self.z, self.me + 2 - 4 * self.x)
        self.y_side = (self.z, self.me + 4 - 8 * self.y)
        self.z_near = (self.z + 1 - 2 * self.z_low, self.me)
        self.z_far = (self.z + 2 - 4 * self.z_high, self.me)

    def z_other(self, step):
        return (lax.rem(self.z + step, 4), self.me)

    def lat_other(self, step):
        return (self.z, lax.rem(self.me + step, 8))


def remote(src, dst, send, recv, device):
    return pltpu.make_async_remote_copy(
        src_ref=src, dst_ref=dst, send_sem=send, recv_sem=recv, device_id=device, device_id_type=MESH
    )


def greet(devices):
    barrier = pltpu.get_barrier_semaphore()
    for device in devices:
        pl.semaphore_signal(barrier, inc=1, device_id=device, device_id_type=MESH)


def met(devices):
    pl.semaphore_wait(pltpu.get_barrier_semaphore(), len(devices))


def added(left, right):
    return (left.astype(F32) + right.astype(F32)).astype(BF)


class Reduction:
    lags = (0, 1, 3, 5, 7, 9, 11)
    plane = 2

    def __init__(self, place, shard, grads, out, bufs, sems):
        self.p = place
        self.grads = grads
        self.out = out
        self.own, self.rc, self.r1, self.r2, self.r3, self.r4, self.res = bufs
        self.own_sem, self.send, self.rc_sem, self.r1_sem, self.r2_sem, self.r3_sem, self.r4_sem, self.res_sem = sems
        self.shard = shard
        self.full = pl.cdiv(shard, BATCH)
        self.batches = self.full + self.plane
        self.back = self.full * BATCH - shard
        self.held = flat_rows_of()["tok_norm"] // BATCH
        self.early = self.full - 1 - (self.held + 4)

    @staticmethod
    def scratch(shard):
        n = pl.cdiv(shard, BATCH) + Reduction.plane
        bufs = [
            pltpu.VMEM((2, 2, 2, BATCH, LANES), BF),
            pltpu.VMEM((n, 2, 2, BATCH, LANES), BF),
            pltpu.VMEM((n, 2, 2, HALF, LANES), BF),
            pltpu.VMEM((n, 2, HALF, LANES), BF),
            pltpu.VMEM((n, HALF, LANES), BF),
            pltpu.VMEM((n, QUARTER, LANES), BF),
            pltpu.VMEM((n, BATCH, LANES), BF),
        ]
        dma = pltpu.SemaphoreType.DMA
        sems = [dma((2,)), dma((10, 4)), dma((n,)), dma((n, 2)), dma((n, 2)), dma((n,)), dma((n,)), dma((n, 3))]
        return bufs + sems

    def from_on(self, i, first):
        return (i + 64 - first) // 64

    def row(self, i):
        n, held = self.full, self.held
        on = functools.partial(self.from_on, i)
        keys = on(self.early) - on(self.early + 2)
        shift = held + 4 + on(self.early + 2) * (-2) + on(self.early + 3) * (-n)
        shift = shift + on(self.early + 3 + held) * 2 + on(self.early + 5 + held) * (-4)
        b = i + shift
        row = keys * (self.shard + (i - self.early) * BATCH)
        row = row + (1 - keys) * (b * BATCH - (b // (n - 1)) * self.back)
        return pl.multiple_of(row, 16)

    def is_keys(self, i):
        return (i >= self.early) & (i < self.early + self.plane)

    def own_copy(self, i):
        slot = lax.rem(i, 2)
        src = self.grads.at[:, :, self.p.core, pl.ds(self.row(i), BATCH), :]
        return pltpu.make_async_copy(src, self.own.at[slot], self.own_sem.at[slot])

    def copies(self, stage, i):
        p, slot = self.p, lax.rem(i, 4)
        if stage == 0:
            src = self.grads.at[:, :, 1 - p.core, pl.ds(self.row(i), BATCH), :]
            return [remote(src, self.rc.at[i], self.send.at[0, slot], self.rc_sem.at[i], p.sibling)]
        if stage == 1:
            to_x = self.rc.at[i, :, 1 - p.x, pl.ds(0, HALF), :]
            to_y = self.rc.at[i, 1 - p.y, :, pl.ds(HALF, HALF), :]
            return [
                remote(to_x, self.r1.at[i, 0], self.send.at[1, slot], self.r1_sem.at[i, 0], p.x_side),
                remote(to_y, self.r1.at[i, 1], self.send.at[2, slot], self.r1_sem.at[i, 1], p.y_side),
            ]
        if stage == 2:
            to_y = self.r1.at[i, 0, 1 - p.y]
            to_x = self.r1.at[i, 1, 1 - p.x]
            return [
                remote(to_y, self.r2.at[i, 0], self.send.at[3, slot], self.r2_sem.at[i, 0], p.y_side),
                remote(to_x, self.r2.at[i, 1], self.send.at[4, slot], self.r2_sem.at[i, 1], p.x_side),
            ]
        if stage == 3:
            src = self.r2.at[i, 1 - p.z_low]
            return [remote(src, self.r3.at[i], self.send.at[5, slot], self.r3_sem.at[i], p.z_near)]
        if stage == 4:
            src = self.r3.at[i, pl.ds(pl.multiple_of((1 - p.z_high) * QUARTER, QUARTER), QUARTER), :]
            return [remote(src, self.r4.at[i], self.send.at[6, slot], self.r4_sem.at[i], p.z_far)]
        mine = self.res.at[i, pl.ds(pl.multiple_of(p.z_low * HALF + p.z_high * QUARTER, QUARTER), QUARTER), :]
        return [
            remote(mine, mine, self.send.at[6 + d, slot], self.res_sem.at[i, d - 1], p.z_other(d))
            for d in (1, 2, 3)
        ]

    def launch(self, stage, i):
        before = i - 4
        if stage >= 3:
            before = before - 4 * (self.from_on(before, self.early) - self.from_on(before, self.early + self.plane))

        @pl.when(i >= 4)
        def _():
            for copy in self.copies(stage, before):
                copy.wait_send()

        for copy in self.copies(stage, i):
            copy.start()

    def landed(self, stage, i):
        for copy in self.copies(stage, i):
            copy.wait_recv()

    def work(self, stage, i):
        p = self.p
        if stage == 0:
            self.own_copy(i).start()
        elif stage == 1:
            self.landed(0, i)
            self.own_copy(i).wait()
            self.rc[i] = added(self.rc[i], self.own[lax.rem(i, 2)])
        elif stage == 2:
            self.landed(1, i)
            self.r1[i, 0] = added(self.r1[i, 0], self.rc[i, :, p.x, 0:HALF, :])
            self.r1[i, 1] = added(self.r1[i, 1], self.rc[i, p.y, :, HALF:BATCH, :])
        elif stage == 3:
            self.landed(2, i)
            self.r2[i, 0] = added(self.r2[i, 0], self.r1[i, 0, p.y])
            self.r2[i, 1] = added(self.r2[i, 1], self.r1[i, 1, p.x])
        elif stage == 4:
            self.landed(3, i)
            self.r3[i] = added(self.r3[i], self.r2[i, p.z_low])
        elif stage == 5:
            self.landed(4, i)
            part = self.r3[i, pl.ds(pl.multiple_of(p.z_high * QUARTER, QUARTER), QUARTER), :]
            at = pl.multiple_of(p.z_low * HALF + p.z_high * QUARTER, QUARTER)
            self.res[i, pl.ds(at, QUARTER), :] = added(self.r4[i], part)
        else:
            self.landed(5, i)
            self.out[pl.ds(self.row(i), BATCH), :] = self.res[i]
        if stage == 3:
            pl.when(jnp.logical_not(self.is_keys(i)))(lambda: self.launch(stage, i))
        elif stage < 6:
            self.launch(stage, i)

    def tick(self, t):
        for stage, lag in enumerate(self.lags):
            i = t - lag

            inside = (i >= 0) & (i < self.batches)

            @pl.when(inside if stage < 4 else inside & jnp.logical_not(self.is_keys(i)))
            def _(stage=stage, i=i):
                self.work(stage, i)

    def ticks(self):
        return self.batches + self.lags[-1]

    def finish(self):
        for stage in range(6):
            for back in range(4):
                for copy in self.copies(stage, self.batches - 4 + back):
                    copy.wait_send()

    def partners(self):
        p = self.p
        return [p.sibling, p.x_side, p.y_side] + [p.z_other(d) for d in (1, 2, 3)]


def share_all(place, block, send, recv):
    mine = block.at[place.me]
    copies = [
        remote(mine, mine, send.at[d - 1], recv.at[d - 1], place.lat_other(d)) for d in range(1, 8)
    ]
    for copy in copies:
        copy.start()
    for copy in copies:
        copy.wait()


STAT_ROWS = 40


def token_backward(grad_kv, tokens, tok_normed, w_kv, tok_norm, token_grad, kv_grad, edge):
    kv_grad[...] = t_mm(tok_normed[...], grad_kv).astype(BF)
    grad = mm_t(grad_kv, w_kv[...])
    xhat, rstd = norm_stats(tokens[...].astype(F32))
    token_grad[...] = norm_back(grad, xhat, rstd, tok_norm[0:1, :]).astype(BF)
    gain, bias = col_sum(grad * xhat), col_sum(grad)
    parts = [half[:, j * LANES : (j + 1) * LANES] for half in (gain, bias) for j in range(DIN // LANES)]
    keep = edge.shape[0] - len(parts)
    edge[...] = jnp.concatenate([edge[...].astype(F32)[0:keep, :]] + parts, axis=0).astype(BF)


def reduce_kernel(
    shard, bias_owner, bias_at, unused_flat, tokens, tok_normed, w_kv, tok_norm,
    g1, kvf, co, lse, rank, count, episode, hot, latent, norms, w_q, w_o,
    dnorm_one, dnorm_sa, dnorm_two, dhid_one, dhid_two, dout_one, dout_so, dout_two,
    summed, stats, token_grad, grads, *scratch,
):
    place = Place()
    block, block_send, block_recv, edge, kv_grad, edge_sem, g1_held, g1_sem, kv_low, kv_sem = scratch[:10]
    accs, (stage, low, latent_low), engine = scratch[10:17], scratch[17:20], scratch[20:]
    acc_latent, acc_q, acc_o, acc_episode, dnorm, dout, dkv_t = accs
    frames = kvf.shape[0]
    red = Reduction(place, shard, grads, summed, engine[:7], engine[7:])
    frame_copies = [pltpu.make_async_copy(g1.at[f], g1_held.at[f], g1_sem.at[f]) for f in range(frames)]
    for copy in frame_copies:
        copy.start()
    partners = [place.lat_other(d) for d in range(1, 8)] + [place.z_other(d) for d in (1, 2, 3)]
    greet(partners)
    for ref in accs:
        ref[...] = jnp.zeros_like(ref)
    met(partners)

    def run(first, last):
        lax.fori_loop(first, last, lambda t, c: (red.tick(t), c)[1], 0)

    def frame(f, carry):
        red.tick(2 * f)
        pltpu.make_async_copy(g1.at[f], g1_held.at[f], g1_sem.at[f]).wait()
        rows = pl.ds(pl.multiple_of(f * LAT, LAT), LAT)
        cross_back_frame(
            g1_held[f], kvf[f], co[rows, :], lse[f], rank.at[f], count[f, 0:1, 0:1], episode[f], hot[f, :, 0:1],
            latent, norms, w_q, w_o, *accs, pause=lambda: red.tick(2 * f + 1),
        )
        return carry

    lax.fori_loop(0, frames, frame, 0)
    run(2 * frames, red.early)
    at = flat_rows_of()
    copies = []

    def put(source, row):
        owner, local = row if isinstance(row, tuple) else divmod(row, shard)
        dst = grads.at[owner // 4, owner // 2 % 2, owner % 2, pl.ds(local, source.shape[0]), :]
        copies.append(pltpu.make_async_copy(source, dst, kv_sem.at[len(copies)]))
        copies[-1].start()

    write_small(
        put, stage, low, latent_low, acc_latent, acc_q, acc_o, acc_episode,
        stacked(dnorm, dnorm_one, dnorm_sa, dnorm_two), stacked(dhid_one, dhid_two),
        stacked(dout, dout_one, dout_so, dout_two),
    )
    edge_row = at["tok_norm"] // 16 * 16
    edge[...] = low[0, edge_row - at["episode"] : edge_row - at["episode"] + 16, :]
    count_kv = tokens.shape[0]
    for j in range(8):
        kv_low[j] = dkv_t[:, j * count_kv : (j + 1) * count_kv].T
        put(kv_low.at[j], (j, shard))
    for copy in copies:
        copy.wait()
    ready = red.early + red.lags[3] + red.plane
    run(red.early, ready)
    grad_kv = jnp.concatenate([red.r2[red.early + i, h] for i in range(red.plane) for h in range(2)], axis=0)
    token_backward(grad_kv, tokens, tok_normed, w_kv, tok_norm, token_grad, kv_grad, edge)
    writes = [
        pltpu.make_async_copy(edge, grads.at[0, 0, 0, pl.ds(edge_row, 16), :], edge_sem.at[0]),
        pltpu.make_async_copy(kv_grad, grads.at[0, 0, 0, pl.ds(at["w_kv"], DIN), :], edge_sem.at[1]),
    ]
    for copy in writes:
        copy.start()
    run(ready, ready + 2)
    for copy in writes:
        copy.wait()
    run(ready + 2, red.ticks())
    grad_sq = jnp.zeros((1, LANES), F32)
    step = 784
    for j in range(shard // step):
        part = summed[j * step : (j + 1) * step, :].astype(F32)
        grad_sq = grad_sq + col_sum(part * part)
    bias = summed[bias_at : bias_at + 2 * FF // LANES, :].astype(F32)
    bias = jnp.where(place.me == bias_owner, bias, 0.0)
    head = jnp.concatenate([grad_sq, jnp.zeros((7, LANES), F32), bias], axis=0)
    block[pl.ds(place.me, 1)] = head[None]
    share_all(place, block, block_send, block_recv)
    total = block[0]
    for s in range(1, 8):
        total = total + block[s]
    stats[...] = total
    red.finish()


def trust_kernel(norms_sq, trust, block, send, recv):
    place = Place()
    partners = [place.lat_other(d) for d in range(1, 8)]
    greet(partners)
    block[pl.ds(place.me, 1)] = norms_sq[...][None]
    met(partners)
    share_all(place, block, send, recv)
    total = block[0]
    for s in range(1, 8):
        total = total + block[s]
    update_sq = jnp.sum(total[:, 0:LANES].T, axis=0, keepdims=True)
    weight_sq = jnp.sum(total[:, LANES : 2 * LANES].T, axis=0, keepdims=True)
    ratio = jnp.sqrt(weight_sq) / (jnp.sqrt(update_sq) + 1e-06)
    trust[...] = ratio[:, 0 : trust.shape[1]]


def relayout(whole, row, stage, dst, rows, cols):
    wide = cols // LANES
    block = min(rows, 2048 // wide // 128 * 128)

    def step(i, carry):
        at = pl.multiple_of(row + i * (block * wide), 16)
        stage[0 : block * wide, :] = whole[pl.ds(at, block * wide), :].astype(F32)
        for j in range(wide):
            part = stage[pl.ds(j, block, stride=wide), :]
            dst[pl.ds(pl.multiple_of(i * block, 16), block), j * LANES : (j + 1) * LANES] = part.astype(BF)
        return carry

    lax.fori_loop(0, rows // block, step, 0)


def small_matrix(whole, row, stage, rows, cols):
    wide = cols // LANES
    stage[0 : rows * wide, :] = whole[row : row + rows * wide, :].astype(F32)
    return jnp.concatenate([stage[pl.ds(j, rows, stride=wide), :] for j in range(wide)], axis=1)


class Gather:
    def __init__(self, place, whole, shard, chunks, send, recv):
        self.p, self.whole, self.shard, self.chunks, self.send, self.recv = place, whole, shard, chunks, send, recv
        p = place
        x_index, y_index = p.x_side[1], p.y_side[1]
        low = p.z_low
        self.first = x_index + low * (y_index - x_index)
        self.second = y_index + low * (x_index - y_index)
        self.diagonal = x_index + 4 - 8 * p.y

    def copy(self, kind, k):
        p = self.p
        block = (p.me, p.me, self.first, self.first, self.first, self.diagonal, self.second)[kind]
        target = (
            (p.z, self.first), p.sibling, (p.z, self.second), p.z_near, p.sibling, p.sibling, p.sibling
        )[kind]
        row, count = self.chunks[k]
        ref = self.whole.at[pl.ds(pl.multiple_of(block * self.shard + row, 16), count), :]
        return remote(ref, ref, self.send.at[kind, k], self.recv.at[kind, k], target)

    def play(self, *events):
        for event in events:
            kind, k = event[0], int(event[1:])
            if kind == "a":
                self.copy(0, k).start()
                self.copy(1, k).start()
            elif kind == "b":
                self.copy(0, k).wait_recv()
                for way in (2, 3, 4):
                    self.copy(way, k).start()
            elif kind == "c":
                for arrived, onward in ((2, 5), (3, 6)):
                    self.copy(arrived, k).wait_recv()
                    self.copy(onward, k).start()
            else:
                for way in (1, 4, 5, 6):
                    self.copy(way, k).wait_recv()

    def finish(self):
        for k in range(len(self.chunks)):
            for kind in range(7):
                self.copy(kind, k).wait_send()


class KeyExchange:
    def __init__(self, place, keys, send, recv):
        self.p, self.keys, self.send, self.recv = place, keys, send, recv
        self.x_index, self.y_index = place.x_side[1], place.y_side[1]
        self.diagonal = self.x_index + 4 - 8 * place.y

    def copy(self, kind):
        p = self.p
        half = self.keys.shape[1] // 2
        low, high, full = pl.ds(0, half), pl.ds(half, half), pl.ds(0, 2 * half)
        block, rows, target = (
            (p.me, full, p.x_side), (p.me, full, p.y_side), (p.me, full, p.sibling),
            (self.x_index, low, p.y_side), (self.y_index, high, p.x_side),
            (self.x_index, full, p.sibling), (self.y_index, full, p.sibling), (self.diagonal, full, p.sibling),
        )[kind]
        ref = self.keys.at[block, rows, :]
        return remote(ref, ref, self.send.at[kind], self.recv.at[kind], target)

    def step(self, s):
        if s == 0:
            waits, starts = (), (0, 1, 2)
        elif s == 1:
            waits, starts = (0, 1), (3, 4, 5, 6)
        elif s == 2:
            waits, starts = (3, 4), (7,)
        else:
            waits, starts = (2, 5, 6, 7), ()
        for kind in waits:
            self.copy(kind).wait_recv()
        for kind in starts:
            self.copy(kind).start()

    def finish(self):
        for kind in range(8):
            self.copy(kind).wait_send()


def flat_rows_of():
    rows, at = {}, 0
    for name, shape in param_layout():
        rows[name] = at // LANES
        at += math.prod(shape)
    return rows


def gather_chunks(shard):
    at = flat_rows_of()
    tail = at["hid_bias"] % shard // 16 * 16
    chunks = [(at["episode"], at["w_o"] - at["episode"]), (tail, shard - tail), (at["w_o"], at["w_qkv"] - at["w_o"])]
    for low, high in ((0, at["episode"]), (at["w_qkv"], tail)):
        while low < high:
            count = min(512, high - low)
            chunks.append((low, count))
            low += count
    return chunks


def begin_kernel(
    chunks, master, tokens, ids, episodes,
    up_one, down_one, qkv_w, so_w, up_two, down_two,
    latent, norms, hid_bias, out_bias, w_q, w_o, w_kv, tok_norm, tok_normed, episode, rank, counts,
    kvf_out, co_out, lse_out, hot_lanes, h1,
    whole, stage, all_ids, keys, m_up_one, m_down_one, m_qkv, m_so, m_up_two, m_down_two,
    episodes_held, h1_held, h1_sem, master_held, load_sem, send, recv, key_send, key_recv, id_send, id_recv, out_sem,
):
    place = Place()
    shard = master.shape[0]
    frames, cap = kvf_out.shape[0], kvf_out.shape[1]
    gather = Gather(place, whole, shard, chunks, send, recv)
    exchange = KeyExchange(place, keys, key_send, key_recv)
    at = flat_rows_of()
    loads = [
        pltpu.make_async_copy(master.at[pl.ds(row, count), :], master_held.at[pl.ds(row, count), :], load_sem.at[k])
        for k, (row, count) in enumerate(chunks)
    ]
    for copy in loads:
        copy.start()
    partners = [place.lat_other(d) for d in range(1, 8)] + [place.z_near]
    greet(partners)
    all_ids[pl.ds(place.me, 1)] = ids[...][None]
    id_copies = [
        remote(all_ids.at[place.me], all_ids.at[place.me], id_send.at[d - 1], id_recv.at[d - 1], place.lat_other(d))
        for d in range(1, 8)
    ]
    own_at = place.me * shard

    def cast(first, last):
        for k in range(first, last):
            row, count = chunks[k]
            loads[k].wait()
            at_row = pl.multiple_of(own_at + row, 16)
            whole[pl.ds(at_row, count), :] = master_held[row : row + count, :].astype(BF)

    cast(0, 5)
    met(partners)
    for copy in id_copies:
        copy.start()
    gather.play("a0", "a1", "a2", "a3", "a4")
    cast(5, len(chunks))

    for copy in id_copies:
        copy.wait_recv()
    tags = jnp.concatenate([all_ids[s] for s in range(8)], axis=0)
    low = lax.broadcasted_iota(jnp.int32, (LANES, LANES), 0)
    high = lax.broadcasted_iota(jnp.int32, (LANES, LANES), 1)
    upto = jnp.where(low <= high, 1.0, 0.0).astype(BF)
    n = tags.shape[0]
    below = jnp.where(
        lax.broadcasted_iota(jnp.int32, (n, n), 1) < lax.broadcasted_iota(jnp.int32, (n, n), 0), 1.0, 0.0
    ).astype(BF)
    for f in range(frames):
        hit = tags == place.me * frames + f
        hit_low = jnp.where(hit, 1.0, 0.0).astype(BF)
        inside = mm(hit_low, upto)
        row_total = jnp.broadcast_to(inside[:, LANES - 1 : LANES], (n, LANES))
        before = mm(below, row_total.astype(BF))
        place_in = (inside + before).astype(jnp.int32) - 1
        rank[f] = jnp.where(hit, place_in, -1)
        total = jnp.sum(row_total[:, 0:1], axis=0, keepdims=True).astype(jnp.int32)
        counts[f] = jnp.broadcast_to(total, (8, LANES))
    gather.play("b0", "b1", "a5", "b2", "c0", "c1", "a6", "d0", "d1")

    pair = whole[at["tok_norm"] // 16 * 16 : at["lat_norms"], :].astype(F32)
    pair = pair[at["tok_norm"] % 16 : at["tok_norm"] % 16 + 4, :]
    tok_norm[...] = jnp.concatenate(
        [
            jnp.concatenate([pair[0:1], pair[1:2]], axis=1),
            jnp.concatenate([pair[2:3], pair[3:4]], axis=1),
        ],
        axis=0,
    )
    w_kv[...] = whole[at["w_kv"] : at["w_kv"] + DIN, :]
    xhat, unused = norm_stats(tokens[...].astype(F32))
    normed = (xhat * tok_norm[0:1, :] + tok_norm[1:2, :]).astype(BF)
    tok_normed[...] = normed
    keys[pl.ds(place.me, 1)] = mm(normed, w_kv[...]).astype(BF)[None]
    exchange.step(0)
    gather.play("a7", "a8", "b3", "c2")
    norms[...] = small_matrix(whole, at["lat_norms"], stage, 8, D)
    hid_bias[...] = small_matrix(whole, at["hid_bias"], stage, 2, FF)
    out_bias[...] = small_matrix(whole, at["out_bias"], stage, 4, D)
    mine = lax.broadcasted_iota(jnp.int32, (16, FRAMES), 0) + place.me * frames
    mine = mine == lax.broadcasted_iota(jnp.int32, (16, FRAMES), 1)
    own = jnp.sum(jnp.where(mine, episodes[...].astype(F32), 0.0), axis=1, keepdims=True)
    hot = jnp.where(lax.broadcasted_iota(jnp.int32, (16, 16), 1).astype(F32) == own, 1.0, 0.0).astype(BF)
    for f in range(frames):
        row = lax.broadcasted_iota(jnp.int32, (16, LANES), 0).astype(F32)
        hot_lanes[f] = jnp.where(row == own[f : f + 1, 0:1], 1.0, 0.0)
    episode_rows = mm(hot, small_matrix(whole, at["episode"], stage, 16, D).astype(BF))
    gather.play("b4", "c3", "d2", "b5", "c4", "d3", "b6")
    exchange.step(1)
    gather.play("a9", "a10", "c5", "d4", "c6", "d5")
    packed = whole[at["w_q"] : at["w_q"] + D // 2, :].astype(F32)
    stage[pl.ds(0, D // 2, stride=2), :] = packed
    stage[pl.ds(1, D // 2, stride=2), :] = pltpu.roll(packed, CH, 1)
    w_q[...] = keep_half(stage[0:D, :], 0).astype(BF)
    w_o[0:CH, :] = jnp.zeros((CH, D), BF)
    w_o[CH : 2 * CH, :] = small_matrix(whole, at["w_o"], stage, CH, D).astype(BF)
    exchange.step(2)
    gather.play("a11", "b7", "d6")
    exchange.step(3)
    relayout(whole, 0, stage, latent, LAT, D)

    chunk = 8 * LANES
    episodes_held[...] = episode_rows[0:8, :]
    before = [("b8",), ("b9", "d7"), ("b10", "d8"), ("b11", "d9")]
    midway = [("c7",), ("c8",), ("c9",), ("c10",)]

    def play(frame, parts):
        for step, events in enumerate(parts):
            pl.when(frame == step)(functools.partial(gather.play, *events))

    def attend(f, carry):
        play(f, before)
        row = episodes_held[pl.ds(f, 1), :]
        start = latent[...].astype(F32) + row
        episode[pl.ds(f, 1)] = row[None]

        def pick(j, acc):
            sel = select_tokens(rank[f, pl.ds(pl.multiple_of(8 * j, 8), 8), :], cap)
            return acc + mm(sel, keys[pl.ds(2 * j, 2)].reshape(chunk, LANES))

        kvf = lax.fori_loop(0, n // 8, pick, jnp.zeros((cap, LANES), F32)).astype(BF)
        play(f, midway)
        co, lse = cross_attend(start, norms, w_q, kvf, counts[f, 0:1, 0:1])
        rows = pl.ds(pl.multiple_of(f * LAT, LAT), LAT)
        h1_held[f] = start + mm(co, w_o[...]) + out_bias[0:1, :]
        pltpu.make_async_copy(h1_held.at[f], h1.at[rows, :], h1_sem.at[f]).start()
        kvf_out[f] = kvf
        co_out[rows, :] = co
        lse_out[f] = lse
        return carry

    lax.fori_loop(0, frames, attend, 0)
    gather.play("c11", "d10", "d11")

    big = (
        (up_one, m_up_one, at["w_up"], D, FF),
        (down_one, m_down_one, at["w_down"], FF, D),
        (up_two, m_up_two, at["w_up"] + D * FF // LANES, D, FF),
        (down_two, m_down_two, at["w_down"] + D * FF // LANES, FF, D),
        (qkv_w, m_qkv, at["w_qkv"], D, 3 * D),
        (so_w, m_so, at["w_so"], D, D),
    )
    outs = []
    for j, (out, held, row, rows, cols) in enumerate(big):
        relayout(whole, row, stage, held, rows, cols)
        outs.append(pltpu.make_async_copy(held, out, out_sem.at[j]))
        outs[-1].start()
    for copy in outs:
        copy.wait()
    for f in range(frames):
        pltpu.make_async_copy(h1_held.at[f], h1.at[f * LAT : (f + 1) * LAT, :], h1_sem.at[f]).wait()
    for copy in id_copies:
        copy.wait_send()
    exchange.finish()
    gather.finish()


def begin_all(master_rows, token_rows, ids, episodes, frames, cap):
    shard = master_rows.shape[0]
    tokens = token_rows.shape[0]
    total = 8 * tokens
    chunks = gather_chunks(shard)
    vmem = pl.BlockSpec(memory_space=pltpu.VMEM)
    anywhere = pl.BlockSpec(memory_space=pl.ANY)
    matrices = [(D, FF), (FF, D), (D, 3 * D), (D, D), (D, FF), (FF, D)]
    dma = pltpu.SemaphoreType.DMA
    return pl.pallas_call(
        functools.partial(begin_kernel, chunks),
        out_shape=[shaped(m, BF) for m in matrices]
        + [
            shaped((LAT, D), BF),
            shaped((8, D)),
            shaped((2, FF)),
            shaped((4, D)),
            shaped((D, LANES), BF),
            shaped((LANES, D), BF),
            shaped((DIN, LANES), BF),
            shaped((2, DIN)),
            shaped((tokens, DIN), BF),
            shaped((frames, 1, D)),
            shaped((frames, total // LANES, LANES), jnp.int32),
            shaped((frames, 8, LANES), jnp.int32),
            shaped((frames, cap, LANES), BF),
            shaped((frames * LAT, LANES), BF),
            shaped((frames, 1, LAT)),
            shaped((frames, 16, LANES)),
            shaped((frames * LAT, D)),
        ],
        in_specs=[anywhere] + [vmem] * 3,
        out_specs=[anywhere] * 6 + [vmem] * 16 + [anywhere],
        scratch_shapes=[
            pltpu.VMEM((8 * shard, LANES), BF),
            pltpu.VMEM((2048, LANES), F32),
            pltpu.VMEM((8, tokens // LANES, LANES), jnp.int32),
            pltpu.VMEM((8, tokens, LANES), BF),
        ]
        + [pltpu.VMEM(m, BF) for m in matrices]
        + [
            pltpu.VMEM((8, D), F32),
            pltpu.VMEM((frames, LAT, D), F32),
            dma((frames,)),
            pltpu.VMEM((shard, LANES), F32),
            dma((len(chunks),)),
            dma((7, len(chunks))), dma((7, len(chunks))), dma((8,)), dma((8,)), dma((7,)), dma((7,)), dma((6,)),
        ],
        compiler_params=pltpu.CompilerParams(
            collective_id=3, has_side_effects=True, vmem_limit_bytes=56 * MIB
        ),
    )(master_rows, token_rows, ids, episodes)


FCHUNK = 1024


def to_flat(stage, matrix):
    rows, wide = matrix.shape[0], matrix.shape[1] // LANES
    for j in range(wide):
        stage[pl.ds(j, rows, stride=wide), :] = matrix[:, j * LANES : (j + 1) * LANES]
    return stage[0 : rows * wide, :]


def feed_forward(rows, gain, bias, up_bias, down_bias, w_up, w_down, act_ref, slope_ref, normed_ref, total_ref):
    xhat, rstd = norm_stats(rows)
    normed_ref[...] = (xhat * gain + bias).astype(BF)
    act, slope = gelu_pair(mm(normed_ref[...], w_up[...]) + up_bias[...])
    act = act.astype(BF)
    act_ref[...] = act
    slope_ref[...] = slope.astype(BF)
    total_ref[...] = rows + down_bias + mm(act, w_down[...])


def feed_back(grad_ref, normed_ref, xhat, rstd, gain, act, slope, w_up, w_down, acc_up, acc_down, dhid, dnorm, dout, work):
    work[...] = jnp.zeros(work.shape, F32)
    for c in range(FF // FCHUNK):
        at = slice(c * FCHUNK, (c + 1) * FCHUNK)
        dpre = (mm_t(grad_ref[...], w_down[at, :]) * slope[:, at].astype(F32)).astype(BF)
        dhid[:, at] += col_sum(dpre.astype(F32))
        work[...] += mm_t(dpre, w_up[:, at])
        acc_up[:, at] += t_mm(normed_ref[...], dpre)
        acc_down[at, :] += t_mm(act[:, at], grad_ref[...])
    grad_normed = work[...]
    dnorm[...] += jnp.concatenate([col_sum(grad_normed * xhat), col_sum(grad_normed)], axis=0)
    dout[...] += col_sum(grad_ref[...].astype(F32))
    return norm_back(grad_normed, xhat, rstd, gain)


def clear(first, refs):
    @pl.when(first)
    def _():
        for ref in refs:
            ref[...] = jnp.zeros_like(ref)


def flat_spans(row, count, shard, extra):
    spans, done = [], 0
    while done < count:
        part = min(count - done, shard - (row + done) % shard)
        spans.append((done, part, row + done + (row + done) // shard * extra))
        done += part
    return spans


def flatten(acc, stage, low, slot):
    wide = acc.shape[1] // LANES
    block = min(acc.shape[0], 2048 // wide // 128 * 128)
    span = block * wide

    def step(i, carry):
        part = acc[pl.ds(pl.multiple_of(i * block, block), block), :]
        for j in range(wide):
            stage[pl.ds(j, block, stride=wide), :] = part[:, j * LANES : (j + 1) * LANES]
        low[slot, pl.ds(pl.multiple_of(i * span, span), span), :] = stage[0:span, :].astype(BF)
        return carry

    lax.fori_loop(0, acc.shape[0] // block, step, 0)


def write_flat(flat, stage, low, pieces, sems, shard, extra):
    pending = {}
    for j, (acc, row) in enumerate(pieces):
        count = acc.shape[0] * acc.shape[1] // LANES
        slot = j % 2
        for copy in pending.get(slot, []):
            copy.wait()
        flatten(acc, stage, low, slot)
        pending[slot] = [
            pltpu.make_async_copy(low.at[slot, pl.ds(off, part), :], flat.at[pl.ds(at, part), :], sems.at[slot, k])
            for k, (off, part, at) in enumerate(flat_spans(row, count, shard, extra))
        ]
        for copy in pending[slot]:
            copy.start()
    for copies in pending.values():
        for copy in copies:
            copy.wait()


class FrameExchange:
    def __init__(self, place, source, grad, held, result, sems):
        self.p, self.source, self.grad, self.held, self.result = place, source, grad, held, result
        self.in_send, self.in_recv, self.out_send, self.out_recv, self.own_in, self.own_out = sems
        self.frames, self.rows = grad.shape[0], source.shape[1]

    @staticmethod
    def scratch(frames):
        dma = pltpu.SemaphoreType.DMA
        return [dma((frames, 7))] * 4 + [dma((frames,))] * 2

    def block(self, index):
        return pl.ds(pl.multiple_of(index * self.rows, 16), self.rows)

    def arriving(self, f, d):
        target = self.p.lat_other(d)
        src = self.source.at[target[1] * self.frames + f]
        dst = self.grad.at[f, self.block(self.p.me), :]
        return remote(src, dst, self.in_send.at[f, d - 1], self.in_recv.at[f, d - 1], target)

    def own_arriving(self, f):
        src = self.source.at[self.p.me * self.frames + f]
        return pltpu.make_async_copy(src, self.grad.at[f, self.block(self.p.me), :], self.own_in.at[f])

    def leaving(self, f, d):
        target = self.p.lat_other(d)
        src = self.held.at[f, self.block(target[1]), :]
        dst = self.result.at[self.p.me * self.frames + f]
        return remote(src, dst, self.out_send.at[f, d - 1], self.out_recv.at[f, d - 1], target)

    def own_leaving(self, f):
        dst = self.result.at[self.p.me * self.frames + f]
        return pltpu.make_async_copy(self.held.at[f, self.block(self.p.me), :], dst, self.own_out.at[f])

    def partners(self):
        return [self.p.lat_other(d) for d in range(1, 8)]

    def begin(self):
        met(self.partners())
        for f in range(self.frames):
            self.own_arriving(f).start()
            for d in range(1, 8):
                self.arriving(f, d).start()

    def await_frame(self, f):
        self.own_arriving(f).wait()
        for d in range(1, 8):
            self.arriving(f, d).wait_recv()

    def send_frame(self, f):
        self.own_leaving(f).start()
        for d in range(1, 8):
            self.leaving(f, d).start()

    def finish(self):
        def step(f, carry):
            self.own_leaving(f).wait()
            for d in range(1, 8):
                self.arriving(f, d).wait_send()
                self.leaving(f, d).wait()
            return carry

        lax.fori_loop(0, self.frames, step, 0)


class Flow:
    def __init__(self, step, steps, array, slots, sems):
        self.step, self.steps, self.array, self.slots, self.sems = step, steps, array, slots, sems
        self.rows = slots.shape[1]

    def here(self):
        return self.slots.at[lax.rem(self.step, 2)]

    def ends(self, step):
        slot = lax.rem(step, 2)
        rows = pl.ds(pl.multiple_of(step * self.rows, self.rows), self.rows)
        return self.array.at[rows, :], self.slots.at[slot], self.sems.at[slot]

    def load(self, step):
        outside, inside, sem = self.ends(step)
        return pltpu.make_async_copy(outside, inside, sem)

    def store(self, step):
        outside, inside, sem = self.ends(step)
        return pltpu.make_async_copy(inside, outside, sem)

    def fetch_ahead(self):
        pl.when(self.step == 0)(lambda: self.load(self.step).start())
        pl.when(self.step + 1 < self.steps)(lambda: self.load(self.step + 1).start())

    def arrived(self):
        self.load(self.step).wait()

    def free(self):
        pl.when(self.step >= 2)(lambda: self.store(self.step - 2).wait())

    def send(self):
        self.store(self.step).start()

    def drain(self):
        if self.steps > 1:
            self.store(self.step - 1).wait()
        self.store(self.step).wait()


def flow_slots(shape, dtype):
    return [pltpu.VMEM((2,) + shape, dtype), pltpu.SemaphoreType.DMA((2,))]


class Late:
    def __init__(self, step, sources, refs, sems):
        self.first = step == 0
        self.copies = [
            pltpu.make_async_copy(src, ref, sems.at[k]) for k, (src, ref) in enumerate(zip(sources, refs))
        ]

        @pl.when(self.first)
        def _():
            for copy in self.copies:
                copy.start()

    def need(self, *which):
        @pl.when(self.first)
        def _():
            for k in which:
                self.copies[k].wait()


def forward_kernel(
    reach, shard, extra, steps, h1, grad, norms, hid_bias, out_bias, up_one, down_one, *rest,
):
    forward_body(reach, shard, extra, steps, h1, grad, norms, hid_bias, out_bias, up_one, down_one, rest[:4], *rest[4:])


def forward_body(
    reach, shard, extra, steps, h1, grad, norms, hid_bias, out_bias, up_one, down_one, late_sources,
    h2_all, qkv_all, lse_out, mixed_all, act_all, slope_all, latents, g3, dhid, dnorm, dout, flat,
    act_two, slope_two, acc_up, acc_down, stage, low, normed, mixed_t, work, sems,
    w_qkv, w_so, up_two, down_two, late_sems,
    h2_slots, h2_sems, qkv_slots, qkv_sems, mixed_slots, mixed_sems, act_slots, act_sems, slope_slots, slope_sems, *shared,
):
    step = pl.program_id(0)
    late = Late(step, late_sources, (w_qkv, w_so, up_two, down_two), late_sems)
    flows = [
        Flow(step, steps, *parts)
        for parts in (
            (h2_all, h2_slots, h2_sems), (qkv_all, qkv_slots, qkv_sems), (mixed_all, mixed_slots, mixed_sems),
            (act_all, act_slots, act_sems), (slope_all, slope_slots, slope_sems),
        )
    ]
    for flow in flows:
        flow.free()
    h2_out, qkv, mixed_out, act_one, slope_one = (flow.here() for flow in flows)
    if reach:
        place = Place()
        traffic = FrameExchange(place, grad, shared[0], shared[1], latents, shared[2:])
        pl.when(step == 0)(lambda: greet(traffic.partners()))
        grad = shared[0].at[step]
    clear(step == 0, (acc_up, acc_down, dhid, dnorm, dout))
    feed_forward(
        h1[...], norms[2:3, :], norms[3:4, :], hid_bias.at[0:1], out_bias[1:2, :], up_one, down_one, act_one,
        slope_one, normed, h2_out,
    )
    xhat, unused = norm_stats(h2_out[...])
    normed[...] = (xhat * norms[4:5, :] + norms[5:6, :]).astype(BF)

    late.need(0)
    if reach:
        pl.when(step == 0)(traffic.begin)

    qkv[...] = mm(normed[...], w_qkv[...]).astype(BF)
    for k in (0, 1, 3, 4):
        flows[k].send()
    scale = jnp.asarray(0.125, BF)
    ones = jnp.ones((16, LAT), BF)
    group = 4
    width = group * HEAD_DIM
    for base in range(0, D, width):
        queries = by_head(qkv[:, base : base + width] * scale)
        value_t = qkv[:, 2 * D + base : 2 * D + base + width].T
        scores = mm_t(qkv[:, D + base : D + base + width], queries)
        top = jnp.max(scores, axis=0, keepdims=True)
        terms = jnp.exp(scores - top).astype(BF)
        for j in range(group):
            at = slice(j * LAT, (j + 1) * LAT)
            values = jnp.concatenate([value_t[j * HEAD_DIM : (j + 1) * HEAD_DIM, :], ones], axis=0)
            product = mm(values, terms[:, at])
            total = product[HEAD_DIM : HEAD_DIM + 1, :]
            head = base // HEAD_DIM + j
            lse_out[0, head : head + 1, :] = top[:, at] + jnp.log(total)
            mixed_t[head * HEAD_DIM : (head + 1) * HEAD_DIM, :] = product[0:HEAD_DIM, :] * (1.0 / total)
    late.need(1, 2, 3)
    mixed = mixed_t[...].T.astype(BF)
    mixed_out[...] = mixed
    flows[2].send()
    h3 = h2_out[...] + mm(mixed, w_so[...]) + out_bias[2:3, :]
    feed_forward(
        h3, norms[6:7, :], norms[7:8, :], hid_bias.at[1:2], out_bias[3:4, :], up_two, down_two, act_two, slope_two,
        normed, work,
    )
    if reach:
        shared[1][step] = work[...].astype(BF)
        traffic.send_frame(step)
        traffic.await_frame(step)
    else:
        latents[...] = work[...].astype(BF)
    xhat, rstd = norm_stats(h3)
    g3[...] = grad[...].astype(F32) + feed_back(
        grad, normed, xhat, rstd, norms[6:7, :], act_two, slope_two, up_two, down_two,
        acc_up, acc_down, dhid, dnorm, dout, work,
    )

    @pl.when(step == pl.num_programs(0) - 1)
    def _():
        at = flat_rows_of()
        half = D * FF // LANES
        write_flat(flat, stage, low, [(acc_up, at["w_up"] + half), (acc_down, at["w_down"] + half)], sems, shard, extra)
        if reach:
            traffic.finish()
        for flow in flows:
            flow.drain()


def backward_kernel(
    shard, extra, steps, qkv, lse, mixed, g3, h2_all, h1_all, act_all, slope_all, norms, w_so, src_qkv, src_up, src_down,
    latents_in, flat_in,
    g1, dhid, dnorm_sa, dnorm_one, dout_so, dout_one, latents_out, flat,
    dqkv, acc_up, acc_down, acc_qkv, acc_so, stage, low, normed, grad_mixed, grad_low, work, sems,
    w_qkv, up_one, down_one, late_sems,
    h2_slots, h2_sems, h1_slots, h1_sems, act_slots, act_sems, slope_slots, slope_sems, latents_held, pass_sem,
):
    step = pl.program_id(0)
    late = Late(step, (src_qkv, src_up, src_down), (w_qkv, up_one, down_one), late_sems)
    flows = [
        Flow(step, steps, *parts)
        for parts in (
            (h2_all, h2_slots, h2_sems), (h1_all, h1_slots, h1_sems), (act_all, act_slots, act_sems),
            (slope_all, slope_slots, slope_sems),
        )
    ]
    for flow in flows:
        flow.fetch_ahead()
    h2, h1, act_one, slope_one = (flow.here() for flow in flows)
    latents_load = pltpu.make_async_copy(latents_in, latents_held, pass_sem.at[0])
    latents_store = pltpu.make_async_copy(latents_held, latents_out, pass_sem.at[1])
    pl.when(step == 0)(lambda: latents_load.start())

    @pl.when(step == min(1, steps - 1))
    def _():
        latents_load.wait()
        latents_store.start()

    clear(
        step == 0,
        (acc_up, acc_down, acc_qkv, acc_so, dhid, dnorm_sa, dnorm_one, dout_so, dout_one),
    )
    scale = jnp.asarray(0.125, BF)
    grad_three = g3[...]
    grad_low[...] = grad_three.astype(BF)
    dout_so[...] += col_sum(grad_low[...].astype(F32))
    acc_so[...] += t_mm(mixed[...], grad_low[...])
    grad_mixed[...] = mm_t(grad_low[...], w_so[...]).astype(BF)

    for base in range(0, D, LANES):
        query_at = slice(base, base + LANES)
        key_at = slice(D + base, D + base + LANES)
        value_at = slice(2 * D + base, 2 * D + base + LANES)
        head = base // HEAD_DIM
        queries = by_head(qkv[:, query_at] * scale)
        grads = by_head(grad_mixed[:, query_at])
        keys = qkv[:, key_at]
        key_t = keys.T
        log_total = jnp.concatenate([lse[0, head : head + 1, :], lse[0, head + 1 : head + 2, :]], axis=1)
        prob = jnp.exp(mm_t(keys, queries) - log_total)
        dqkv[:, value_at] = mm(prob.astype(BF), grads).astype(BF)
        weighted = prob * mm_t(qkv[:, value_at], grads)
        grad_score = (weighted - prob * col_sum(weighted)).astype(BF)
        dqkv[:, key_at] = mm(grad_score, queries).astype(BF)
        query_t = [
            mm(key_t[j * HEAD_DIM : (j + 1) * HEAD_DIM, :], grad_score[:, j * LAT : (j + 1) * LAT]) for j in range(2)
        ]
        dqkv[:, query_at] = (jnp.concatenate(query_t, axis=0).T * 0.125).astype(BF)
    late.need(0, 1, 2)
    for flow in flows:
        flow.arrived()
    xhat, rstd = norm_stats(h2[...])
    normed[...] = (xhat * norms[4:5, :] + norms[5:6, :]).astype(BF)
    grad_in = mm_t(dqkv[...], w_qkv[...])
    acc_qkv[...] += t_mm(normed[...], dqkv[...])
    dnorm_sa[...] += jnp.concatenate([col_sum(grad_in * xhat), col_sum(grad_in)], axis=0)
    grad_two = grad_three + norm_back(grad_in, xhat, rstd, norms[4:5, :])

    xhat, rstd = norm_stats(h1[...])
    normed[...] = (xhat * norms[2:3, :] + norms[3:4, :]).astype(BF)
    grad_low[...] = grad_two.astype(BF)
    grad_one = grad_two + feed_back(
        grad_low, normed, xhat, rstd, norms[2:3, :], act_one, slope_one, up_one, down_one,
        acc_up, acc_down, dhid, dnorm_one, dout_one, work,
    )

    g1[...] = grad_one

    @pl.when(step == pl.num_programs(0) - 1)
    def _():
        at = flat_rows_of()
        write_flat(
            flat, stage, low,
            [(acc_up, at["w_up"]), (acc_down, at["w_down"]), (acc_qkv, at["w_qkv"]), (acc_so, at["w_so"])],
            sems, shard, extra,
        )
        latents_store.wait()


def cross_back_frame(
    grad_one, kvf, co, lse, rank_ref, count, episode_row, hot_column, latent, norms, w_q, w_o,
    acc_latent, acc_q, acc_o, acc_episode, dnorm, dout, dkv_t, pause=lambda: None,
):
    cap = kvf.shape[0]
    start = latent[...].astype(F32) + episode_row
    xhat, rstd = norm_stats(start)
    query_in = (xhat * norms[0:1, :] + norms[1:2, :]).astype(BF)
    queries = mm(query_in, w_q[...]).astype(BF) * jnp.asarray(0.125, BF)
    branch = grad_one.astype(BF)
    grad_co = mm_t(branch, w_o[...]).astype(BF)
    acc_o[...] += t_mm(co, branch)
    dout[...] += col_sum(branch.astype(F32))
    scores = cross_scores(kvf, queries, count)
    prob = jnp.exp(scores - lse)
    weighted = prob * mm_t(kvf, grad_co)
    grad_score = (weighted - prob * col_sum(weighted)).astype(BF)
    grad_kv = (mm(grad_score, queries) + mm(prob.astype(BF), grad_co)).astype(BF)
    grad_query = (t_mm(kvf, grad_score).T * 0.125).astype(BF)
    pause()
    acc_q[...] += t_mm(query_in, grad_query)
    grad_in = mm_t(grad_query, w_q[...])
    grad_start = grad_one + norm_back(grad_in, xhat, rstd, norms[0:1, :])
    dnorm[...] += jnp.concatenate([col_sum(grad_in * xhat), col_sum(grad_in)], axis=0)
    acc_latent[...] += grad_start
    acc_episode[...] += hot_column * col_sum(grad_start)
    grad_kv_t = grad_kv.T
    chunk = 8 * LANES

    def scatter(j, carry):
        sel = select_tokens(rank_ref[pl.ds(pl.multiple_of(j * 8, 8), 8), :], cap)
        at = pl.ds(pl.multiple_of(j * chunk, chunk), chunk)
        dkv_t[:, at] = added(dkv_t[:, at], mm(grad_kv_t, sel))
        return carry

    lax.fori_loop(0, dkv_t.shape[1] // chunk, scatter, 0)


def write_small(put, stage, low, latent_low, acc_latent, acc_q, acc_o, acc_episode, norm_grads, hid_grads, out_grads):
    at = flat_rows_of()
    flatten(acc_latent, stage, latent_low, 0)
    put(latent_low.at[0], 0)
    head = at["lat_norms"] - at["episode"]
    used = EPISODES * (D // LANES)
    rows = [to_flat(stage, acc_episode[...])[0:used, :], jnp.zeros((head - used, LANES), F32)]
    rows = jnp.concatenate(rows + [to_flat(stage, norm_grads)], axis=0)
    top = rows.shape[0]
    low[0, 0:top, :] = rows.astype(BF)
    put(low.at[0, pl.ds(0, top), :], at["episode"])
    stage[0:D, :] = acc_q[...]
    even = stage[pl.ds(0, D // 2, stride=2), :]
    odd = pltpu.roll(stage[pl.ds(1, D // 2, stride=2), :], CH, 1)
    low[0, top : top + D // 2, :] = jnp.where(lane_half(even.shape, 0), even, odd).astype(BF)
    both = D // 2 + CH * D // LANES
    low[0, top + D // 2 : top + both, :] = to_flat(stage, acc_o[CH : 2 * CH, :]).astype(BF)
    put(low.at[0, pl.ds(top, both), :], at["w_q"])
    hid = to_flat(stage, hid_grads)
    last = top + both
    low[0, last : last + hid.shape[0], :] = hid.astype(BF)
    end = hid.shape[0] + 4 * D // LANES
    low[0, last + hid.shape[0] : last + end, :] = to_flat(stage, out_grads).astype(BF)
    put(low.at[0, pl.ds(last, end), :], at["hid_bias"])


def cross_accumulators(total_keys):
    shapes = [(LAT, D), (D, LANES), (LANES, D), (16, D), (2, D), (1, D)]
    return [pltpu.VMEM(shape, F32) for shape in shapes] + [pltpu.VMEM((LANES, total_keys), BF)]


def small_buffers():
    return [pltpu.VMEM((2048, LANES), F32), pltpu.VMEM((1, 640, LANES), BF), pltpu.VMEM((1, 2048, LANES), BF)]


def stacked(*parts):
    return jnp.concatenate([part[...] for part in parts], axis=0)


def cross_bwd_kernel(
    kv_rows, g1, kvf, co, lse, rank, count, episode, hot, latent, norms, w_q, w_o,
    dnorm_one, dnorm_sa, dnorm_two, dhid_one, dhid_two, dout_one, dout_so, dout_two, flat_in, flat,
    acc_latent, acc_q, acc_o, acc_episode, dnorm, dout, dkv_t, stage, low, latent_low, kv_low, sems,
):
    step = pl.program_id(0)
    accs = (acc_latent, acc_q, acc_o, acc_episode, dnorm, dout, dkv_t)
    clear(step == 0, accs)
    cross_back_frame(
        g1[...], kvf[0], co[...], lse[0], rank.at[0], count[0, 0:1, 0:1], episode[0], hot[0, :, 0:1],
        latent, norms, w_q, w_o, *accs,
    )

    @pl.when(step == pl.num_programs(0) - 1)
    def _():
        copies = []

        def put(source, row):
            copies.append(
                pltpu.make_async_copy(source, flat.at[pl.ds(row, source.shape[0]), :], sems.at[len(copies)])
            )
            copies[-1].start()

        write_small(
            put, stage, low, latent_low, acc_latent, acc_q, acc_o, acc_episode,
            stacked(dnorm, dnorm_one, dnorm_sa, dnorm_two), stacked(dhid_one, dhid_two),
            stacked(dout, dout_one, dout_so, dout_two),
        )
        for copy in copies:
            copy.wait()
        tokens = kv_rows[1]
        for j in range(dkv_t.shape[1] // tokens):
            kv_low[...] = dkv_t[:, j * tokens : (j + 1) * tokens].T
            copy = pltpu.make_async_copy(kv_low, flat.at[pl.ds(kv_rows[0] + j * tokens, tokens), :], sems.at[0])
            copy.start()
            copy.wait()


def fixed(*shape):
    return pl.BlockSpec(shape, lambda i: (0,) * len(shape), pipeline_mode=pl.Buffered(1))


def kept(*shape):
    return pl.BlockSpec(shape, lambda i: (0,) * len(shape))


def rowed(rows, cols):
    return pl.BlockSpec((rows, cols), lambda i: (i, 0))


def framed(*shape):
    return pl.BlockSpec((1,) + shape, lambda i: (i,) + (0,) * len(shape))


def shaped(shape, dtype=F32):
    return jax.ShapeDtypeStruct(shape, dtype)


def call(kernel, grid, in_specs, outs, args, flops=0, trans=0, scratch=(), limit=56, aliases=None, collective=None):
    out_specs, out_shapes = zip(*outs)
    moved = sum(math.prod(a.shape) * a.dtype.itemsize for a in args)
    moved += sum(math.prod(s.shape) * s.dtype.itemsize for s in out_shapes)
    return pl.pallas_call(
        kernel,
        grid=(grid,),
        in_specs=in_specs,
        out_specs=list(out_specs),
        out_shape=list(out_shapes),
        scratch_shapes=list(scratch),
        input_output_aliases=aliases or {},
        compiler_params=pltpu.CompilerParams(
            dimension_semantics=("arbitrary",),
            vmem_limit_bytes=limit * MIB,
            collective_id=collective,
            has_side_effects=collective is not None,
        ),
        cost_estimate=pl.CostEstimate(flops=flops, bytes_accessed=moved, transcendentals=trans),
    )(*args)


def reduce_all(flat, shard, bias_owner, bias_row, tokens, tok_normed, w_kv, tok_norm, g1, cross):
    vmem = pl.BlockSpec(memory_space=pltpu.VMEM)
    anywhere = pl.BlockSpec(memory_space=pl.ANY)
    dma = pltpu.SemaphoreType.DMA
    first = [
        pltpu.VMEM((8, STAT_ROWS, LANES), F32), dma((7,)), dma((7,)), pltpu.VMEM((16, LANES), BF),
        pltpu.VMEM((DIN, LANES), BF), dma((2,)), pltpu.VMEM(g1.shape, F32), dma((g1.shape[0],)),
        pltpu.VMEM((8, tokens.shape[0], LANES), BF), dma((16,)),
    ]
    grads = flat.reshape(2, 2, 2, -1, LANES)
    return pl.pallas_call(
        functools.partial(reduce_kernel, shard, bias_owner, bias_row),
        out_shape=[
            shaped((shard, LANES), BF), shaped((STAT_ROWS, LANES)), shaped(tokens.shape, BF),
            shaped(grads.shape, BF),
        ],
        in_specs=[anywhere] + [vmem] * 4 + [anywhere] + [vmem] * len(cross),
        out_specs=[vmem, vmem, vmem, anywhere],
        scratch_shapes=first
        + cross_accumulators(8 * tokens.shape[0])
        + small_buffers()
        + Reduction.scratch(shard),
        input_output_aliases={0: 3},
        compiler_params=pltpu.CompilerParams(
            collective_id=1, has_side_effects=True, vmem_limit_bytes=56 * MIB
        ),
    )(grads, tokens, tok_normed, w_kv, tok_norm, g1, *cross)


def body(tokens, frame_ids, episodes, master, moment_one, moment_two, latent_grad):
    lat_count = lax.axis_size("lat")
    lat_index = lax.axis_index("lat")
    shard_len = master.shape[0]
    frame_total = episodes.shape[1]
    frames = frame_total // lat_count
    rows_total = frames * LAT
    total_keys = frame_ids.shape[1] * lat_count
    cap = total_keys // 8
    token_rows_count = total_keys // LANES

    reach = lat_count == 8 and lax.axis_size("kf") == 4
    shard_rows = shard_len // LANES
    master_rows = master.reshape(shard_rows, LANES)
    score_flops = rows_total * cap * LANES * 2
    select_flops = frames * cap * total_keys * LANES * 2
    if reach:
        (
            up_one, down_one, w_qkv, w_so, up_two, down_two,
            latent, norms, hid_bias, out_bias, w_q, w_o, w_kv, tok_norm, tok_normed, episode_rows, rank, counts,
            kvf, cross_out, cross_lse, hot_lanes, h1,
        ) = begin_all(master_rows, tokens[0], frame_ids.reshape(-1, LANES), episodes, frames, cap)
    else:
        own_episodes = lax.dynamic_slice_in_dim(episodes[0], lat_index * frames, frames, 0)
        episode_match = own_episodes[:, None] == jnp.arange(EPISODES, dtype=jnp.int32)[None, :]
        hot_lanes = jnp.broadcast_to(
            jnp.pad(episode_match.astype(F32), ((0, 0), (0, 16 - EPISODES)))[:, :, None], (frames, 16, LANES)
        )
        weights = split_flat(lax.all_gather(master.astype(BF), "lat", axis=0, tiled=True))
        norms = weights["lat_norms"].astype(F32)
        out_bias = weights["out_bias"].astype(F32)
        hid_bias = weights["hid_bias"].astype(F32)
        tok_norm = weights["tok_norm"].astype(F32)
        w_kv, w_qkv, w_so, latent = (weights[name] for name in ("w_kv", "w_qkv", "w_so", "latent"))
        up_one, up_two = weights["w_up"]
        down_one, down_two = weights["w_down"]
        frame_tag = lax.all_gather(frame_ids[0].astype(BF), "lat", axis=0, tiled=True).astype(jnp.int32)
        own_frames = lat_index * frames + jnp.arange(frames, dtype=jnp.int32)
        own_hit = frame_tag[None, :] == own_frames[:, None]
        rank = jnp.cumsum(own_hit.astype(jnp.int32), axis=1) - 1
        counts = jnp.broadcast_to(rank[:, -1][:, None, None] + 1, (frames, 8, LANES))
        rank = jnp.where(own_hit, rank, -1).reshape(frames, token_rows_count, LANES)
        tok_normed = layer_norm(tokens[0].astype(F32), tok_norm[0], tok_norm[1]).astype(BF)
        key_value = mm(tok_normed, w_kv).astype(BF)
        all_keys = lax.all_gather(key_value, "lat", axis=0, tiled=True)
        episode_rows = mm(episode_match.astype(BF), weights["episode"]).reshape(frames, 1, D)
        w_q = jnp.pad(weights["w_q"], ((0, 0), (0, LANES - CH)))
        w_o = jnp.pad(weights["w_o"], ((LANES - CH, 0), (0, 0)))
        h1, kvf, cross_out, cross_lse = call(
            cross_fwd_kernel,
            frames,
            [
                fixed(LAT, D), framed(1, D), fixed(8, D), fixed(D, LANES), fixed(LANES, D), fixed(4, D),
                fixed(total_keys, LANES), framed(token_rows_count, LANES), framed(8, LANES),
            ],
            [
                (rowed(LAT, D), shaped((rows_total, D))),
                (framed(cap, LANES), shaped((frames, cap, LANES), BF)),
                (rowed(LAT, LANES), shaped((rows_total, LANES), BF)),
                (framed(1, LAT), shaped((frames, 1, LAT))),
            ],
            (latent, episode_rows, norms, w_q, w_o, out_bias, all_keys, rank, counts),
            flops=2 * score_flops + select_flops,
            trans=rows_total * cap,
        )
    mlp_flops = 4 * rows_total * D * FF
    attn_flops = 4 * rows_total * LAT * D
    anywhere = pl.BlockSpec(memory_space=pl.ANY)
    token_count = frame_ids.shape[1]
    if reach:
        flat_shard, extra = shard_rows, token_count
        flat_shape = (lat_count * (shard_rows + extra), LANES)
        kv_rows = (shard_rows, token_count, shard_rows + extra)
        grad_in, grad_spec = latent_grad[0], anywhere
        latents_spec = (anywhere, shaped(latent_grad.shape[1:], BF))
        shared = [pltpu.VMEM((frames, LAT, D), BF)] * 2 + FrameExchange.scratch(frames)
    else:
        flat_shard, extra = NPARAM // LANES, 0
        flat_shape = (flat_shard + total_keys, LANES)
        kv_rows = (flat_shard, 512, 512)
        grad_in = lax.all_to_all(
            latent_grad[0], "lat", split_axis=0, concat_axis=1, tiled=True
        ).reshape(rows_total, D)
        grad_spec = rowed(LAT, D)
        latents_spec = (rowed(LAT, D), shaped((rows_total, D), BF))
        shared = []
    slab = D * FF // LANES
    h2, qkv, self_lse, mixed, act_one, slope_one, latents, g3, dhid_two, dnorm_two, dout_two, flat = call(
        functools.partial(forward_kernel, reach, flat_shard, extra, frames),
        frames,
        [
            rowed(LAT, D), grad_spec, fixed(8, D), fixed(2, FF), fixed(4, D), fixed(D, FF), fixed(FF, D),
        ]
        + [anywhere] * 4,
        [
            (anywhere, shaped((rows_total, D))),
            (anywhere, shaped((rows_total, 3 * D), BF)),
            (framed(HEADS, LAT), shaped((frames, HEADS, LAT))),
            (anywhere, shaped((rows_total, D), BF)),
            (anywhere, shaped((rows_total, FF), BF)),
            (anywhere, shaped((rows_total, FF), BF)),
            latents_spec,
            (rowed(LAT, D), shaped((rows_total, D))),
            (kept(1, FF), shaped((1, FF))),
            (kept(2, D), shaped((2, D))),
            (kept(1, D), shaped((1, D))),
            (anywhere, shaped(flat_shape, BF)),
        ],
        (h1, grad_in, norms, hid_bias, out_bias, up_one, down_one, w_qkv, w_so, up_two, down_two),
        flops=4 * mlp_flops + 4 * attn_flops,
        trans=4 * rows_total * FF,
        scratch=[
            pltpu.VMEM((LAT, FF), BF), pltpu.VMEM((LAT, FF), BF), pltpu.VMEM((D, FF), F32), pltpu.VMEM((FF, D), F32),
            pltpu.VMEM((2048, LANES), F32), pltpu.VMEM((2, slab, LANES), BF), pltpu.VMEM((LAT, D), BF),
            pltpu.VMEM((D, LAT), F32), pltpu.VMEM((LAT, D), F32), pltpu.SemaphoreType.DMA((2, 16)),
            pltpu.VMEM((D, 3 * D), BF), pltpu.VMEM((D, D), BF), pltpu.VMEM((D, FF), BF), pltpu.VMEM((FF, D), BF),
            pltpu.SemaphoreType.DMA((4,)),
        ]
        + flow_slots((LAT, D), F32)
        + flow_slots((LAT, 3 * D), BF)
        + flow_slots((LAT, D), BF)
        + flow_slots((LAT, FF), BF)
        + flow_slots((LAT, FF), BF)
        + shared,
        limit=62,
        collective=4 if reach else None,
    )
    g1, dhid_one, dnorm_sa, dnorm_one, dout_so, dout_one, latents, flat = call(
        functools.partial(backward_kernel, flat_shard, extra, frames),
        frames,
        [
            rowed(LAT, 3 * D), framed(HEADS, LAT), rowed(LAT, D), rowed(LAT, D), anywhere, anywhere, anywhere, anywhere,
            fixed(8, D), fixed(D, D),
        ]
        + [anywhere] * 5,
        [
            (rowed(LAT, D), shaped((rows_total, D))),
            (kept(1, FF), shaped((1, FF))),
            (kept(2, D), shaped((2, D))),
            (kept(2, D), shaped((2, D))),
            (kept(1, D), shaped((1, D))),
            (kept(1, D), shaped((1, D))),
            (anywhere, shaped(latents.shape, BF)),
            (anywhere, shaped(flat_shape, BF)),
        ],
        (
            qkv, self_lse, mixed, g3, h2, h1, act_one, slope_one, norms, w_so, w_qkv, up_one, down_one, latents, flat,
        ),
        flops=2 * mlp_flops + 10 * attn_flops,
        trans=rows_total * LAT * HEADS,
        scratch=[
            pltpu.VMEM((LAT, 3 * D), BF), pltpu.VMEM((D, FF), F32), pltpu.VMEM((FF, D), F32),
            pltpu.VMEM((D, 3 * D), F32), pltpu.VMEM((D, D), F32),
            pltpu.VMEM((2048, LANES), F32), pltpu.VMEM((2, slab, LANES), BF), pltpu.VMEM((LAT, D), BF),
            pltpu.VMEM((LAT, D), BF), pltpu.VMEM((LAT, D), BF), pltpu.VMEM((LAT, D), F32),
            pltpu.SemaphoreType.DMA((2, 16)),
            pltpu.VMEM((D, 3 * D), BF), pltpu.VMEM((D, FF), BF), pltpu.VMEM((FF, D), BF),
            pltpu.SemaphoreType.DMA((3,)),
        ]
        + flow_slots((LAT, D), F32)
        + flow_slots((LAT, D), F32)
        + flow_slots((LAT, FF), BF)
        + flow_slots((LAT, FF), BF)
        + [pltpu.VMEM(latents.shape, BF), pltpu.SemaphoreType.DMA((2,))],
        limit=60,
        aliases={14: 7},
    )
    if reach:
        latents_out = latents[None]
    else:
        latents_out = lax.all_to_all(
            latents.reshape(frames, LAT, D), "lat", split_axis=1, concat_axis=0, tiled=True
        )[None]
    cross = (
        kvf, cross_out, cross_lse, rank, counts, episode_rows, hot_lanes, latent, norms, w_q, w_o,
        dnorm_one, dnorm_sa, dnorm_two, dhid_one, dhid_two, dout_one, dout_so, dout_two,
    )
    layout = param_layout()
    starts, ends, offset, bias_offset = [], [], 0, 0
    for name, shape in layout:
        if name == "hid_bias":
            bias_offset = offset
        starts.append(offset // LANES)
        offset += math.prod(shape)
        ends.append(offset // LANES)
    pad = [0] * (16 - len(layout))
    starts, ends = (np.tile(np.array(v + pad, np.int32)[:, None], (1, LANES)) for v in (starts, ends))
    opt_rows = shard_rows // 2 if shard_rows % 16 == 0 else shard_rows
    opt_steps = shard_rows // opt_rows
    base = (lat_index * shard_rows).astype(jnp.int32).reshape(1)
    smem = pl.BlockSpec(memory_space=pltpu.SMEM)
    flat_rows = (shard_rows, LANES)
    bias_owner, bias_at = divmod(bias_offset, shard_len)
    if reach:
        summed, stats, token_grad, unused = reduce_all(
            flat, shard_rows, bias_owner, bias_at // LANES, tokens[0], tok_normed, w_kv, tok_norm,
            g1.reshape(frames, LAT, D), cross,
        )
    else:
        (flat,) = call(
            functools.partial(cross_bwd_kernel, kv_rows),
            frames,
            [
                rowed(LAT, D), framed(cap, LANES), rowed(LAT, LANES), framed(1, LAT), framed(token_rows_count, LANES),
                framed(8, LANES), framed(1, D), framed(16, LANES), fixed(LAT, D), fixed(8, D), fixed(D, LANES),
                fixed(LANES, D),
            ]
            + [fixed(*part.shape) for part in cross[11:]]
            + [anywhere],
            [(anywhere, shaped(flat_shape, BF))],
            (g1,) + cross + (flat,),
            flops=6 * score_flops,
            trans=rows_total * cap,
            scratch=cross_accumulators(total_keys)
            + small_buffers()
            + [pltpu.VMEM((kv_rows[1], LANES), BF), pltpu.SemaphoreType.DMA((8,))],
            aliases={20: 0},
        )
        grad_kv = lax.psum_scatter(flat[flat_shard:], "lat", scatter_dimension=0, tiled=True)
        flat = flat[:flat_shard]
        grad_w_kv = t_mm(tok_normed, grad_kv)
        grad_tok_normed = mm_t(grad_kv, w_kv)
        unused, token_pull = jax.vjp(layer_norm, tokens[0].astype(F32), tok_norm[0], tok_norm[1])
        grad_tokens, grad_tok_gain, grad_tok_bias = token_pull(grad_tok_normed)
        token_grad = grad_tokens.astype(BF)
        flat_at = flat_rows_of()
        tok_norm_grad = jnp.stack([grad_tok_gain, grad_tok_bias]).reshape(-1, LANES).astype(BF)
        flat = lax.dynamic_update_slice(flat, tok_norm_grad, (flat_at["tok_norm"], 0))
        flat = lax.dynamic_update_slice(flat, grad_w_kv.astype(BF), (flat_at["w_kv"], 0))
        local_flat = flat.reshape(-1)
        summed = lax.psum_scatter(local_flat, "lat", scatter_dimension=0, tiled=True)
        summed = lax.psum(summed, "kf").reshape(flat_rows)
        bias_rows = summed[bias_at // LANES : bias_at // LANES + 2 * FF // LANES].astype(F32)
        bias_rows = jnp.where(lat_index == bias_owner, bias_rows, 0.0)
        grad_sq = jnp.sum(jnp.square(summed.astype(F32)), axis=0, keepdims=True)
        stats = lax.psum(jnp.concatenate([grad_sq, jnp.zeros((7, LANES), F32), bias_rows]), "lat")
    grad_shard, lamb_update, new_one, new_two, norms_sq, bias_grad, token_grad = call(
        lamb_kernel,
        opt_steps,
        [smem, fixed(STAT_ROWS, LANES), fixed(16, LANES), fixed(16, LANES)] + [rowed(opt_rows, LANES)] * 4 + [fixed(*token_grad.shape)],
        [(rowed(opt_rows, LANES), shaped(flat_rows))] * 4
        + [(kept(16, 2 * LANES), shaped((16, 2 * LANES))), (kept(2, FF), shaped((2, FF)))]
        + [(kept(*token_grad.shape), shaped(token_grad.shape, BF))],
        (
            base, stats, starts, ends, summed, master_rows,
            moment_one.reshape(flat_rows), moment_two.reshape(flat_rows), token_grad,
        ),
    )
    if reach:
        vmem = pl.BlockSpec(memory_space=pltpu.VMEM)
        trust = pl.pallas_call(
            trust_kernel,
            out_shape=shaped((1, len(layout))),
            in_specs=[vmem],
            out_specs=vmem,
            scratch_shapes=[
                pltpu.VMEM((8, 16, 2 * LANES), F32),
                pltpu.SemaphoreType.DMA((7,)),
                pltpu.SemaphoreType.DMA((7,)),
            ],
            compiler_params=pltpu.CompilerParams(collective_id=2, has_side_effects=True),
        )(norms_sq).reshape(-1)
    else:
        sums = lax.psum(jnp.sum(norms_sq.reshape(16, 2, LANES), axis=2), "lat")[: len(layout)]
        trust = jnp.sqrt(sums[:, 1]) / (jnp.sqrt(sums[:, 0]) + 1e-06)
    return (
        latents_out,
        token_grad[None],
        grad_shard.reshape(-1),
        lamb_update.reshape(-1),
        new_one.reshape(-1),
        new_two.reshape(-1),
        trust,
        bias_grad,
    )


def solution(mesh):
    return jax.shard_map(
        body,
        mesh=mesh,
        in_specs=(
            P("kf", "lat", None),
            P("kf", "lat"),
            P("kf", None),
            P("lat"),
            P("lat"),
            P("lat"),
            P("kf", None, "lat", None),
        ),
        out_specs=(
            P("kf", None, "lat", None),
            P("kf", "lat", None),
            P("lat"),
            P("lat"),
            P("lat"),
            P("lat"),
            P(),
            P(),
        ),
        check_vma=False,
    )
```
